32 devices in a mesh: rep: 16 (over z, y, core), shard: 2 (over x).
Axes of the slice: x: 2, y: 2, z: 4, core: 2. Of those that a mesh axis runs over, the one named last changes fastest.
Arguments:
- prompt_in: bfloat16 [2, 16, 1024, 1024], P(None, 'rep', 'shard'), may hold values from -6 to 6
- cont_in: bfloat16 [2, 16, 2, 128, 1024], P(None, 'rep', 'shard'), may hold values from -6 to 6
- prompt_cot: bfloat16 [2, 16, 1024, 1024], P(None, 'rep', 'shard'), may hold values from -6 to 6
- cont_cot: bfloat16 [2, 16, 2, 128, 1024], P(None, 'rep', 'shard'), may hold values from -6 to 6
- ln1_gain: bfloat16 [1024], P('shard'), may hold values from 0.099609375 to 1.8984375
- ln1_bias: bfloat16 [1024], P('shard'), may hold values from -3 to 3
- ln2_gain: bfloat16 [1024], P('shard'), may hold values from 0.099609375 to 1.8984375
- ln2_bias: bfloat16 [1024], P('shard'), may hold values from -3 to 3
- qkv_weight: bfloat16 [1024, 3072], P('shard'), may hold values from -0.25 to 0.25
- qkv_bias: bfloat16 [3072], P('shard'), may hold values from -3 to 3
- out_weight: bfloat16 [1024, 1024], P('shard'), may hold values from -0.75 to 0.75
- out_bias: bfloat16 [1024], P('shard'), may hold values from -3 to 3
- up_weight: bfloat16 [1024, 4096], P('shard'), may hold values from -0.1875 to 0.1875
- up_bias: bfloat16 [4096], P('shard'), may hold values from -3 to 3
- down_weight: bfloat16 [4096, 1024], P('shard'), may hold values from -0.09375 to 0.09375
- down_bias: bfloat16 [1024], P('shard'), may hold values from -3 to 3
Outputs:
- prompt_out: bfloat16 [2, 16, 1024, 1024], P(None, 'rep', 'shard')
- cont_out: bfloat16 [2, 16, 2, 128, 1024], P(None, 'rep', 'shard')
- prompt_grad: float32 [2, 16, 1024, 1024], P(None, 'rep', 'shard')
- cont_grad: float32 [2, 16, 2, 128, 1024], P(None, 'rep', 'shard')
- ln1_gain_grad: float32 [1024], P('shard')
- ln1_bias_grad: float32 [1024], P('shard')
- ln2_gain_grad: float32 [1024], P('shard')
- ln2_bias_grad: float32 [1024], P('shard')
- qkv_weight_grad: float32 [1024, 3072], P('shard')
- qkv_bias_grad: float32 [3072], P('shard')
- out_weight_grad: float32 [1024, 1024], P('shard')
- out_bias_grad: float32 [1024], P('shard')
- up_weight_grad: float32 [1024, 4096], P('shard')
- up_bias_grad: float32 [4096], P('shard')
- down_weight_grad: float32 [4096, 1024], P('shard')
- down_bias_grad: float32 [1024], P('shard')
The draws below stay inside these ranges and needn't reach their ends.
All inputs are finite; a program needn't handle non-finite values.
Results may differ from the reference program's by a relative error of at most 0.018.
Values may be sent and summed in bfloat16 or wider, within the bound.
No kernel may reach another device: no remote copies, remote signals or barrier semaphores. Data moves between devices by JAX's collectives and lax.ppermute only.
A program may use at most 448 MiB of HBM per device.

```python
import math
import jax
import jax.numpy as jnp
from jax import lax

D = 1024
H = 16
HD = 64
ROT = 16
FF = 4096
PROMPT = 1024
CONT = 128
MB = 2
GROUPS = 16
CONTS = 2


def block_levels(stream_key, shape, shards, least, high):
    def one(axis_at, parts):
        draws = jax.random.uniform(jax.random.fold_in(jax.random.fold_in(stream_key, 6), axis_at), (parts,), jnp.float32, least / len(shards), high / len(shards))
        return jnp.repeat(jnp.exp(draws), shape[axis_at] // parts).reshape((-1,) + (1,) * (len(shape) - axis_at - 1))

    factor_of = one(*shards[0])
    for cut in shards[1:]:
        factor_of = factor_of * one(*cut)
    return factor_of


def normal_values(stream_key, shape, width, reach, shards=(), kind=jnp.bfloat16):
    array = jax.random.normal(stream_key, shape, jnp.float32) * width
    if len(shards) > 0:
        array = block_levels(stream_key, shape, shards, -0.22, 0.18) * array
    return jnp.clip(array, min=-reach, max=reach).astype(kind)


def setup_inputs(seed: int = 0) -> dict:
    key_of = jax.random.split(jax.random.key(seed), 17)
    prompt_in = normal_values(key_of[0], (MB, GROUPS, PROMPT, D), 1.0, 6.0, ((1, 16), (2, 2)))
    cont_in = normal_values(key_of[1], (MB, GROUPS, CONTS, CONT, D), 1.0, 6.0, ((1, 16), (2, 2)))
    prompt_cot = normal_values(key_of[2], (MB, GROUPS, PROMPT, D), 1.0, 6.0, ((1, 16), (2, 2)))
    cont_cot = normal_values(key_of[3], (MB, GROUPS, CONTS, CONT, D), 1.0, 6.0, ((1, 16), (2, 2)))
    ln1_gain = jnp.clip(1.0 + 0.18 * jax.random.normal(key_of[4], (D,), jnp.float32), 0.099609375, 1.8984375).astype(jnp.bfloat16)
    ln1_bias = normal_values(key_of[5], (D,), 0.5, 3.0, ((0, 2),))
    ln2_gain = jnp.clip(1.0 + 0.18 * jax.random.normal(key_of[6], (D,), jnp.float32), 0.099609375, 1.8984375).astype(jnp.bfloat16)
    ln2_bias = normal_values(key_of[7], (D,), 0.5, 3.0, ((0, 2),))
    qkv_weight = normal_values(key_of[8], (D, 3 * D), (D // 2) ** -0.5, 0.25, ((0, 2),))
    qkv_bias = normal_values(key_of[9], (3 * D,), 0.5, 3.0, ((0, 2),))
    out_weight = normal_values(key_of[10], (D, D), (D // 16) ** -0.5, 0.75, ((0, 2),))
    out_bias = normal_values(key_of[11], (D,), 0.5, 3.0, ((0, 2),))
    up_weight = normal_values(key_of[12], (D, FF), D ** -0.5, 0.1875, ((0, 2),))
    up_bias = normal_values(key_of[13], (FF,), 0.5, 3.0, ((0, 2),))
    down_weight = normal_values(key_of[14], (FF, D), FF ** -0.5, 0.09375, ((0, 2),))
    down_bias = normal_values(key_of[15], (D,), 0.5, 3.0, ((0, 2),))
    return {"prompt_in": prompt_in, "cont_in": cont_in, "prompt_cot": prompt_cot, "cont_cot": cont_cot, "ln1_gain": ln1_gain, "ln1_bias": ln1_bias, "ln2_gain": ln2_gain, "ln2_bias": ln2_bias, "qkv_weight": qkv_weight, "qkv_bias": qkv_bias, "out_weight": out_weight, "out_bias": out_bias, "up_weight": up_weight, "up_bias": up_bias, "down_weight": down_weight, "down_bias": down_bias}


@jax.custom_vjp
def low(v):
    return lax.optimization_barrier(v.astype(jnp.bfloat16)).astype(jnp.float32)

@jax.custom_vjp
def low_back(v):
    return v

def low_keep(v):
    return (low(v), None)

def low_pass(kept, grad):
    return (grad,)

def back_keep(v):
    return (v, None)

def back_low(kept, grad):
    return (low(grad),)
low.defvjp(low_keep, low_pass)
low_back.defvjp(back_keep, back_low)
highest = lax.Precision.HIGHEST

def layer_norm(tokens, norm_gain, norm_bias):
    mean_val = lax.optimization_barrier(jnp.mean(tokens, axis=-1, keepdims=True))
    centred = tokens - mean_val
    variance = lax.optimization_barrier(jnp.mean(centred * centred, axis=-1, keepdims=True))
    return centred * lax.rsqrt(variance + 1e-05) * norm_gain + norm_bias

def rotary_tables(positions):
    half_rot = ROT // 2
    inverse_freq = jnp.exp(jnp.arange(half_rot, dtype=jnp.float32) * (-2.0 * math.log(10000.0) / ROT))
    angles = positions[:, None] * inverse_freq[None, :]
    return (jnp.cos(angles), jnp.sin(angles))

def rotate(head_vals, cosine_table, sine_table):
    half_rot = ROT // 2
    front_half = head_vals[..., :half_rot]
    back_half = head_vals[..., half_rot:ROT]
    cos_part = cosine_table[:, None, :]
    sin_part = sine_table[:, None, :]
    return jnp.concatenate([front_half * cos_part - back_half * sin_part, back_half * cos_part + front_half * sin_part, head_vals[..., ROT:]], axis=-1)

def attend(queries, keys_in, values_in, allowed):
    scores = low_back(jnp.einsum('qhd,khd->hqk', queries, keys_in, precision=highest) * HD ** (-0.5))
    scores = jnp.where(allowed[None], scores, -1e+30)
    probability = low(jax.nn.softmax(scores, axis=-1))
    return low(low_back(jnp.einsum('hqk,khd->qhd', probability, values_in, precision=highest)))

def group_forward(prompt_rows, cont_rows, params):
    ln1_gain, ln1_bias, ln2_gain, ln2_bias, qkv_weight, qkv_bias, out_weight, out_bias, up_weight, up_bias, down_weight, down_bias = params
    count = PROMPT + CONTS * CONT
    tokens = jnp.concatenate([prompt_rows, cont_rows.reshape(CONTS * CONT, D)], axis=0)
    positions = jnp.concatenate([jnp.arange(PROMPT, dtype=jnp.float32), jnp.tile(jnp.arange(CONT, dtype=jnp.float32) + PROMPT, CONTS)])
    cosine_table, sine_table = rotary_tables(positions)
    hidden_one = low(layer_norm(tokens, ln1_gain, ln1_bias))
    hidden_two = low(layer_norm(tokens, ln2_gain, ln2_bias))
    linear = low_back(jnp.dot(hidden_one, qkv_weight, precision=highest) + qkv_bias)
    queries = low(rotate(linear[:, :D].reshape(count, H, HD), cosine_table, sine_table))
    keys_all = low(rotate(linear[:, D:2 * D].reshape(count, H, HD), cosine_table, sine_table))
    values_all = low(linear[:, 2 * D:].reshape(count, H, HD))
    prompt_mask = jnp.arange(PROMPT)[:, None] >= jnp.arange(PROMPT)[None, :]
    prompt_context = attend(queries[:PROMPT], keys_all[:PROMPT], values_all[:PROMPT], prompt_mask)
    cont_mask = jnp.concatenate([jnp.ones((CONT, PROMPT), dtype=jnp.bool_), jnp.arange(CONT)[:, None] >= jnp.arange(CONT)[None, :]], axis=1)

    def one_cont(query_block, key_block, value_block):
        return attend(query_block, jnp.concatenate([keys_all[:PROMPT], key_block], axis=0), jnp.concatenate([values_all[:PROMPT], value_block], axis=0), cont_mask)
    cont_context = jax.vmap(one_cont)(queries[PROMPT:].reshape(CONTS, CONT, H, HD), keys_all[PROMPT:].reshape(CONTS, CONT, H, HD), values_all[PROMPT:].reshape(CONTS, CONT, H, HD))
    context = jnp.concatenate([prompt_context, cont_context.reshape(CONTS * CONT, H, HD)], axis=0).reshape(count, D)
    attended = jnp.dot(context, out_weight, precision=highest) + out_bias
    pre_act = low_back(jnp.dot(hidden_two, up_weight, precision=highest) + up_bias)
    activated = low(jax.nn.gelu(pre_act, approximate=False))
    result = tokens + attended + jnp.dot(activated, down_weight, precision=highest) + down_bias
    return (result[:PROMPT], result[PROMPT:].reshape(CONTS, CONT, D))

def reference(prompt_in, cont_in, prompt_cot, cont_cot, ln1_gain, ln1_bias, ln2_gain, ln2_bias, qkv_weight, qkv_bias, out_weight, out_bias, up_weight, up_bias, down_weight, down_bias):
    params = tuple((weight.astype(jnp.float32) for weight in (ln1_gain, ln1_bias, ln2_gain, ln2_bias, qkv_weight, qkv_bias, out_weight, out_bias, up_weight, up_bias, down_weight, down_bias)))
    items = (prompt_in.reshape(MB * GROUPS, PROMPT, D), cont_in.reshape(MB * GROUPS, CONTS, CONT, D), prompt_cot.reshape(MB * GROUPS, PROMPT, D), cont_cot.reshape(MB * GROUPS, CONTS, CONT, D))

    def one_group(totals, group_item):
        prompt_rows, cont_rows, prompt_dy, cont_dy = group_item
        outputs, pullback = jax.vjp(group_forward, prompt_rows.astype(jnp.float32), cont_rows.astype(jnp.float32), params)
        prompt_back, cont_back, param_grads = pullback((prompt_dy.astype(jnp.float32), cont_dy.astype(jnp.float32)))
        totals = jax.tree.map(jnp.add, totals, param_grads)
        return (totals, (outputs[0].astype(jnp.bfloat16), outputs[1].astype(jnp.bfloat16), prompt_back, cont_back))
    zeros_init = tuple((jnp.zeros_like(param) for param in params))
    totals, (prompt_out, cont_out, prompt_grad, cont_grad) = lax.scan(one_group, zeros_init, items)
    return (prompt_out.reshape(MB, GROUPS, PROMPT, D), cont_out.reshape(MB, GROUPS, CONTS, CONT, D), prompt_grad.reshape(MB, GROUPS, PROMPT, D), cont_grad.reshape(MB, GROUPS, CONTS, CONT, D), totals[0], totals[1], totals[2], totals[3], totals[4], totals[5], totals[6], totals[7], totals[8], totals[9], totals[10], totals[11])
```

```python
import functools
import math

import jax
import jax.numpy as jnp
import numpy as np
from jax import lax
from jax.experimental import pallas as pl
from jax.experimental.pallas import tpu as pltpu
from jax.sharding import PartitionSpec as P

H = 16
HD = 64
ROT = 16
EPS = 1e-05
F32 = jnp.float32
BF = jnp.bfloat16
MIB = 1024 * 1024
SD = jax.ShapeDtypeStruct


def dnn(a, b):
    return lax.dot_general(a, b, (((1,), (0,)), ((), ())), preferred_element_type=F32)


def dnt(a, b):
    return lax.dot_general(a, b, (((1,), (1,)), ((), ())), preferred_element_type=F32)


def dtn(a, b):
    return lax.dot_general(a, b, (((0,), (0,)), ((), ())), preferred_element_type=F32)


def normed(rows):
    x = rows.astype(F32)
    c = x - jnp.mean(x, axis=-1, keepdims=True)
    inv = lax.rsqrt(jnp.mean(c * c, axis=-1, keepdims=True) + EPS)
    return c * inv, inv


def tile(i, n):
    return pl.ds(pl.multiple_of(i * n, n), n)


def rows_tile(n, most):
    t = most
    while n % t:
        t -= 8
    return t


def mlp_kernel(rt, x_ref, dy_ref, wu_ref, bu_ref, wd_ref, gb_ref, act_ref, dpre_ref, h_ref, yp_ref, g2_ref, ln_ref, bu_out, yacc, dacc):
    f = pl.program_id(0)
    last = pl.num_programs(0) - 1
    rows = x_ref.shape[0]

    @pl.when(f == 0)
    def _():
        @pl.loop(0, rows // 128)
        def _(i):
            r = tile(i, 128)
            xh, _ = normed(x_ref[r, :])
            h_ref[r, :] = (xh * gb_ref[0:1, :] + gb_ref[1:2, :]).astype(BF)
            yacc[r, :] = jnp.zeros((128, yacc.shape[1]), F32)
            dacc[r, :] = jnp.zeros((128, dacc.shape[1]), F32)

    def step(i, bsum):
        r = tile(i, rt)
        pre = dnn(h_ref[r, :], wu_ref[...]) + bu_ref[...]
        da = dnt(dy_ref[r, :], wd_ref[...])
        cdf = 0.5 * (1.0 + lax.erf(pre * 0.7071067811865476))
        act = (pre * cdf).astype(BF)
        dpre = (da * (cdf + pre * jnp.exp(-0.5 * pre * pre) * 0.3989422804014327)).astype(BF)
        act_ref[r, :] = act
        dpre_ref[r, :] = dpre
        yacc[r, :] += dnn(act, wd_ref[...])
        dacc[r, :] += dnt(dpre, wu_ref[...])
        return bsum + jnp.sum(dpre.astype(F32), axis=0, keepdims=True)

    bu_out[...] = lax.fori_loop(0, rows // rt, step, jnp.zeros(bu_out.shape, F32))

    @pl.when(f == last)
    def _():
        ln_ref[...] = jnp.zeros_like(ln_ref)

        @pl.loop(0, rows // 128)
        def _(i):
            r = tile(i, 128)
            xh, _ = normed(x_ref[r, :])
            dh = dacc[r, :]
            yp_ref[r, :] = yacc[r, :].astype(BF)
            g2_ref[r, :] = (dh * gb_ref[0:1, :]).astype(BF)
            ln_ref[0:1, :] += jnp.sum(dh * xh, axis=0, keepdims=True)
            ln_ref[1:2, :] += jnp.sum(dh, axis=0, keepdims=True)


def mlp_rows(x, dy, wu, bu, wd, gb):
    rows, width = x.shape
    hidden = wu.shape[1]
    fb = min(512, hidden)
    full = lambda s: pl.BlockSpec(s, lambda f: (0,) * len(s))
    return pl.pallas_call(
        functools.partial(mlp_kernel, rows_tile(rows, 640)),
        grid=(hidden // fb,),
        in_specs=[
            full((rows, width)),
            full((rows, width)),
            pl.BlockSpec((width, fb), lambda f: (0, f)),
            pl.BlockSpec((1, fb), lambda f: (0, f)),
            pl.BlockSpec((fb, width), lambda f: (f, 0)),
            full((2, width)),
        ],
        out_specs=[
            pl.BlockSpec((rows, fb), lambda f: (0, f)),
            pl.BlockSpec((rows, fb), lambda f: (0, f)),
            full((rows, width)),
            full((rows, width)),
            full((rows, width)),
            full((2, width)),
            pl.BlockSpec((1, fb), lambda f: (0, f)),
        ],
        out_shape=[
            SD((rows, hidden), BF),
            SD((rows, hidden), BF),
            SD((rows, width), BF),
            SD((rows, width), BF),
            SD((rows, width), BF),
            SD((2, width), F32),
            SD((1, hidden), F32),
        ],
        scratch_shapes=[pltpu.VMEM((rows, width), F32)] * 2,
        compiler_params=pltpu.CompilerParams(vmem_limit_bytes=60 * MIB),
        cost_estimate=pl.CostEstimate(
            flops=8 * rows * width * hidden,
            bytes_accessed=4 * (width * hidden + rows * hidden) + 10 * rows * width,
            transcendentals=2 * rows * hidden,
        ),
    )(x, dy, wu, bu, wd, gb)


def roll8(x, left):
    w = x.shape[-1]
    return pltpu.roll(x, (w - 8) if left else 8, 1)


def attn_kernel(S, PD, CL, QB, HG, adding, me_ref, *refs):
    it = iter(refs)
    take = lambda n: [next(it) for _ in range(n)]
    xs = take(S)
    dys = take(S)
    yps = take(S * adding)
    g2s = take(S * adding)
    wq, wk, wv = take(3)
    bq, bk, bv = take(3)
    wo, gb = take(2)
    cr, s1r, s2r = take(3)
    ys = take(S)
    gs = take(S)
    dl, ctx, h1, dyc, ln, db = take(6)
    yacc, dacc, q_s, k_s, v_s, dc_s, kT, vT, dk_s, dv_s = take(10)
    g = pl.program_id(0)
    last = pl.num_programs(0) - 1
    me = me_ref[0]
    N, _ = xs[0].shape
    T = N * S
    PR = PD * S
    CR = N - PD
    W = HG * HD

    def each_slot(fn):
        for s in range(S):
            for j in range(S):

                @pl.when(lax.rem(me + j, S) == s)
                def _():
                    fn(s, j)

    def spans(s):
        return ((0, PD, s * PD), (PD, CR, PR + s * CR))

    @pl.when(g == 0)
    def _():
        def load(s, j):
            for a, n, c in spans(s):
                xh, _ = normed(xs[j][a : a + n, :])
                h1[c : c + n, :] = (xh * gb[0:1, :] + gb[1:2, :]).astype(BF)
                dyc[c : c + n, :] = dys[j][a : a + n, :]

        each_slot(load)

    RT = T // 2

    def proj(i, _):
        r = tile(i, RT)
        c = cr[r, :]
        s1 = s1r[r, :]
        s2 = s2r[r, :]

        def rot(y, scale):
            out = []
            for p in range(W // 128):
                z = y[:, p * 128 : (p + 1) * 128]
                z = (z * c + roll8(z, True) * s1 + roll8(z, False) * s2).astype(BF)
                out.append(z * jnp.asarray(scale, BF))
            return jnp.concatenate(out, axis=1) if len(out) > 1 else out[0]

        hh = h1[r, :]
        q_s[r, :] = rot(dnn(hh, wq[...]) + bq[...], HD**-0.5)
        k_s[r, :] = rot(dnn(hh, wk[...]) + bk[...], 1.0)
        v_s[r, :] = (dnn(hh, wv[...]) + bv[...]).astype(BF)
        dc_s[r, :] = dnt(dyc[r, :], wo[...]).astype(BF)
        return 0

    lax.fori_loop(0, 2, proj, 0)
    lane = lax.broadcasted_iota(jnp.int32, (1, 128), 1)
    row_i = lax.broadcasted_iota(jnp.int32, (QB, QB), 0)
    col_i = lax.broadcasted_iota(jnp.int32, (QB, QB), 1)
    causal = row_i <= col_i
    cmask = causal & ((row_i // CL) == (col_i // CL))
    blocks = []
    for i in range(PR // QB):
        blocks.append((i * QB, [(0, i * QB, None)] * (i > 0) + [(i * QB, QB, causal)]))
    for c in range((T - PR) // QB):
        blocks.append((PR + c * QB, [(0, PR, None), (PR + c * QB, QB, cmask)]))

    @pl.loop(0, W // 128)
    def _(p):
        lanes = tile(p, 128)
        kT[...] = k_s[:, lanes].T
        vT[...] = v_s[:, lanes].T
        dk_s[...] = jnp.zeros_like(dk_s)
        dv_s[...] = jnp.zeros_like(dv_s)
        for q0, parts in blocks:
            rq = pl.ds(q0, QB)
            qb = q_s[rq, lanes]
            dcb = dc_s[rq, lanes]
            P_, DS, qh, dch, cT, dqT = [], [], [], [], [], []
            for h in range(2):
                sel = (lane >= HD * h) & (lane < HD * h + HD)
                qm = jnp.where(sel, qb, jnp.zeros_like(qb))
                dm = jnp.where(sel, dcb, jnp.zeros_like(dcb))
                qh.append(qm)
                dch.append(dm)
                ss = []
                for k0, n, mask in parts:
                    s = dnt(k_s[k0 : k0 + n, lanes], qm)
                    if mask is not None:
                        s = jnp.where(mask, s, -1e30)
                    ss.append(s)
                m = functools.reduce(jnp.maximum, [jnp.max(s, axis=0, keepdims=True) for s in ss])
                es = [jnp.exp(s - m) for s in ss]
                rl = 1.0 / sum(jnp.sum(e, axis=0, keepdims=True) for e in es)
                ps = [e * rl for e in es]
                dps = [dnt(v_s[k0 : k0 + n, lanes], dm) for k0, n, _ in parts]
                delta = sum(jnp.sum(a * b, axis=0, keepdims=True) for a, b in zip(ps, dps))
                P_.append([a.astype(BF) for a in ps])
                DS.append([(a * (b - delta)).astype(BF) for a, b in zip(ps, dps)])
                hr = slice(HD * h, HD * h + HD)
                cT.append(sum(dnn(vT[hr, k0 : k0 + n], a) for (k0, n, _), a in zip(parts, P_[h])))
                dqT.append(sum(dnn(kT[hr, k0 : k0 + n], a) for (k0, n, _), a in zip(parts, DS[h])))
            q2 = jnp.concatenate(qh, axis=0)
            dc2 = jnp.concatenate(dch, axis=0)
            for i, (k0, n, _) in enumerate(parts):
                dv_s[k0 : k0 + n, :] += dnn(jnp.concatenate([P_[0][i], P_[1][i]], axis=1), dc2)
                dk_s[k0 : k0 + n, :] += dnn(jnp.concatenate([DS[0][i], DS[1][i]], axis=1), q2)
            ctx[rq, lanes] = jnp.concatenate(cT, axis=0).T.astype(BF)
            z = jnp.concatenate(dqT, axis=0).T * (HD**-0.5)
            z = z * cr[rq, :] - roll8(z, True) * s1r[rq, :] - roll8(z, False) * s2r[rq, :]
            dl[0, rq, lanes] = z.astype(BF)
        z = dk_s[...]
        z = z * cr[...] - roll8(z, True) * s1r[...] - roll8(z, False) * s2r[...]
        dl[1, :, lanes] = z.astype(BF)
        dl[2, :, lanes] = dv_s[...].astype(BF)

    for c in range(3):
        db[c : c + 1, :] = jnp.sum(dl[c].astype(F32), axis=0, keepdims=True)

    def post(i, first):
        r = tile(i, RT)
        y = dnn(ctx[r, :], wo[...])
        d = dnt(dl[0, r, :], wq[...]) + dnt(dl[1, r, :], wk[...]) + dnt(dl[2, r, :], wv[...])
        if first:
            yacc[r, :] = y
            dacc[r, :] = d
        else:
            yacc[r, :] += y
            dacc[r, :] += d

    @pl.when(g == 0)
    def _():
        @pl.loop(0, 2)
        def _(i):
            post(i, True)

    @pl.when(g > 0)
    def _():
        @pl.loop(0, 2)
        def _(i):
            post(i, False)

    @pl.when(g == last)
    def _():
        ln[...] = jnp.zeros_like(ln)

        def store(s, j):
            for a, n, c in spans(s):
                xh, _ = normed(xs[j][a : a + n, :])
                d = dacc[c : c + n, :]
                y = yacc[c : c + n, :]
                gg = d * gb[0:1, :]
                if adding:
                    y = y + yps[j][a : a + n, :].astype(F32)
                    gg = gg + g2s[j][a : a + n, :].astype(F32)
                ys[j][a : a + n, :] = y.astype(BF)
                gs[j][a : a + n, :] = gg.astype(BF)
                ln[0:1, :] += jnp.sum(d * xh, axis=0, keepdims=True)
                ln[1:2, :] += jnp.sum(d, axis=0, keepdims=True)

        each_slot(store)


def attn_group(S, PD, CL, me, xs, dys, yps, g2s, wqkv, bqkv, wo, gb, tabs):
    N, D = xs[0].shape
    CW = wo.shape[0]
    T = N * S
    HG = 4 if CW % 256 == 0 else 2
    QB = 256
    W = HG * HD
    G = CW // W
    full = lambda s: pl.BlockSpec(s, lambda g, m: (0,) * len(s), pipeline_mode=pl.Buffered(1))
    keep = lambda s: pl.BlockSpec(s, lambda g, m: (0,) * len(s))
    tok = full((N, D))
    adding = int(T * D <= 1536 * 1024)
    if not adding:
        others = (yps, g2s)
        yps, g2s = [], []
    wspec = lambda c: pl.BlockSpec((D, W), lambda g, m: (0, c * G + g))
    bspec = lambda c: pl.BlockSpec((1, W), lambda g, m: (0, c * G + g))
    outs = pl.pallas_call(
        functools.partial(attn_kernel, S, PD, CL, QB, HG, adding),
        grid_spec=pltpu.PrefetchScalarGridSpec(
            num_scalar_prefetch=1,
            grid=(G,),
            in_specs=[tok] * ((2 + 2 * adding) * S)
            + [wspec(0), wspec(1), wspec(2), bspec(0), bspec(1), bspec(2)]
            + [pl.BlockSpec((W, D), lambda g, m: (g, 0)), full((2, D))]
            + [full((T, 128))] * 3,
            out_specs=[keep((N, D))] * (2 * S)
            + [
                pl.BlockSpec((3, T, W), lambda g, m: (0, 0, g)),
                pl.BlockSpec((T, W), lambda g, m: (0, g)),
                keep((T, D)),
                keep((T, D)),
                keep((2, D)),
                pl.BlockSpec((3, W), lambda g, m: (0, g)),
            ],
            scratch_shapes=[pltpu.VMEM((T, D), F32)] * 2
            + [pltpu.VMEM((T, W), BF)] * 4
            + [pltpu.VMEM((128, T), BF)] * 2
            + [pltpu.VMEM((T, 128), F32)] * 2,
        ),
        out_shape=[SD((N, D), BF)] * (2 * S)
        + [SD((3, T, CW), BF), SD((T, CW), BF), SD((T, D), BF), SD((T, D), BF), SD((2, D), F32), SD((3, CW), F32)],
        compiler_params=pltpu.CompilerParams(vmem_limit_bytes=62 * MIB),
        cost_estimate=pl.CostEstimate(
            flops=16 * T * D * CW + 48 * T * T * CW, bytes_accessed=16 * T * D + 12 * T * CW + 8 * D * CW, transcendentals=T * T * CW // HD
        ),
    )(me, *xs, *dys, *yps, *g2s, wqkv, wqkv, wqkv, bqkv, bqkv, bqkv, wo, gb, *tabs)
    ys, gs = outs[:S], outs[S : 2 * S]
    if not adding:
        ys, gs = [[a + b for a, b in zip(p, q)] for p, q in zip((ys, gs), others)]
    return ys, gs, outs[2 * S :]


def tn_kernel(n, wide, *refs):
    a = refs[:n]
    b = refs[n : 2 * n]
    o = refs[2 * n]
    if wide == 0:
        o[...] = sum(dtn(x[...], y[...]) for x, y in zip(a, b)).astype(BF)
    else:
        w = b[0].shape[2]
        for c in range(wide):
            o[:, c * w : (c + 1) * w] = sum(dtn(x[...], y[c]) for x, y in zip(a, b)).astype(BF)


def tn_sum(a, b, block):
    n = len(a)
    rows, da = a[0].shape
    block = min(block, da)
    wide = b[0].shape[0] if b[0].ndim == 3 else 0
    db = b[0].shape[-1] * max(wide, 1)
    keep = lambda s: pl.BlockSpec(s, lambda i: (0,) * len(s), pipeline_mode=pl.Buffered(1))
    return pl.pallas_call(
        functools.partial(tn_kernel, n, wide),
        grid=(da // block,),
        in_specs=[pl.BlockSpec((rows, block), lambda i: (0, i))] * n + [keep(b[0].shape)] * n,
        out_specs=pl.BlockSpec((block, db), lambda i: (i, 0)),
        out_shape=SD((da, db), BF),
        compiler_params=pltpu.CompilerParams(vmem_limit_bytes=60 * MIB),
        cost_estimate=pl.CostEstimate(flops=2 * n * rows * da * db, bytes_accessed=2 * (n * rows * (da + db) + da * db), transcendentals=0),
    )(*a, *b)


def final_kernel(S, first, PT, *refs):
    it = iter(refs)
    take = lambda n: [next(it) for _ in range(n)]
    x, dy = take(2)
    ys = take(S)
    gs = take(S)
    (vb,) = take(1)
    if not first:
        take(4)
    po, co, pg, cg = take(4)
    i = pl.program_id(0)
    xv = x[...].astype(F32)
    xh, inv = normed(xv)
    y = xv + vb[0:1, :] + sum(r[...].astype(F32) for r in ys) + vb[1:2, :]
    gsum = sum(r[...].astype(F32) for r in gs)
    dx = (gsum - jnp.mean(gsum, axis=-1, keepdims=True) - xh * jnp.mean(gsum * xh, axis=-1, keepdims=True)) * inv
    out = y.astype(BF)
    grad = dy[...].astype(F32) + dx

    @pl.when(i < PT)
    def _():
        po[0] = out
        pg[0] = grad

    @pl.when(i >= PT)
    def _():
        co[0] = out
        cg[0] = grad


def final_rows(m, MB, PD, x, dy, ys, gs, vb, prior):
    S = len(ys)
    N, D = x.shape
    CR = N - PD
    RT = 128
    PT = PD // RT
    first = prior is None
    row = pl.BlockSpec((RT, D), lambda i: (i, 0))
    pspec = pl.BlockSpec((1, RT, D), lambda i: (m, jnp.minimum(i, PT - 1), 0))
    cspec = pl.BlockSpec((1, RT, D), lambda i: (m, jnp.maximum(i - PT, 0), 0))
    hbm = pl.BlockSpec(memory_space=pl.ANY)
    n_in = 2 * S + 3
    return pl.pallas_call(
        functools.partial(final_kernel, S, first, PT),
        grid=(N // RT,),
        in_specs=[row] * (2 * S + 2) + [pl.BlockSpec((2, D), lambda i: (0, 0))] + ([] if first else [hbm] * 4),
        out_specs=[pspec, cspec, pspec, cspec],
        out_shape=[SD((MB, PD, D), BF), SD((MB, CR, D), BF), SD((MB, PD, D), F32), SD((MB, CR, D), F32)],
        input_output_aliases={} if first else {n_in + k: k for k in range(4)},
        compiler_params=pltpu.CompilerParams(vmem_limit_bytes=32 * MIB),
        cost_estimate=pl.CostEstimate(flops=20 * N * D, bytes_accessed=(4 * S + 10) * N * D, transcendentals=0),
    )(x, dy, *ys, *gs, vb, *(() if first else prior))


def shifted(value, S, j):
    return lax.ppermute(value, "shard", [(i, (i + j) % S) for i in range(S)])


def canonical(slots, me, S, back):
    if S == 1:
        return slots
    stacked = jnp.stack(slots, axis=0)
    return [
        lax.dynamic_index_in_dim(stacked, lax.rem((me - s if back else s - me) + S, S), 0, keepdims=False) for s in range(S)
    ]


def columns_for(weight, me, S, j, parts):
    rows, cols = weight.shape
    w = weight.reshape(rows, parts, S, cols // (parts * S))
    w = lax.dynamic_index_in_dim(w, lax.rem(me + j, S), 2, keepdims=False)
    return w.reshape(rows, cols // S)


def my_columns(weight, me, S, R, parts):
    rows = weight.shape[0]
    own = columns_for(weight, me, S, 0, parts)
    if S == 1:
        return own
    rep = lax.axis_index("rep")
    chunk = rows // R
    got = []
    for j in range(1, S):
        piece = columns_for(weight, me, S, j, parts)
        piece = lax.dynamic_slice_in_dim(piece, rep * chunk, chunk, 0)
        got.append(shifted(piece, S, j))
    others = lax.all_gather(jnp.stack(got, axis=0), "rep", axis=1, tiled=True)
    return jnp.concatenate(canonical([own] + [others[j] for j in range(S - 1)], me, S, True), axis=0)


def reduce_rows(grad):
    part = lax.psum_scatter(grad, "rep", scatter_dimension=0, tiled=True)
    return lax.all_gather(part, "rep", axis=0, tiled=True).astype(F32)


def reduce_columns(grad, me, S, parts):
    rows, cols = grad.shape
    part = lax.psum_scatter(grad.reshape(S, rows // S, cols), "rep", scatter_dimension=1, tiled=True)
    slots = [lax.dynamic_index_in_dim(part, me, 0, keepdims=False)]
    for j in range(1, S):
        slots.append(shifted(lax.dynamic_index_in_dim(part, lax.rem(me + j, S), 0, keepdims=False), S, j))
    slots = [s.reshape(s.shape[0], parts, cols // parts) for s in slots]
    whole = jnp.stack(canonical(slots, me, S, True), axis=2).reshape(-1, S * cols)
    return lax.all_gather(whole, "rep", axis=0, tiled=True).astype(F32)


def rotary_tables(PR, CR, CL):
    pos = np.concatenate([np.arange(PR), PR + np.arange(CR) % CL]).astype(np.float32)
    half = ROT // 2
    freq = np.exp(np.arange(half, dtype=np.float32) * np.float32(-2.0 * math.log(10000.0) / ROT)).astype(np.float32)
    ang = (pos[:, None] * freq[None, :]).astype(np.float32)
    c = np.cos(ang)
    s = np.sin(ang)
    n = pos.shape[0]
    one = np.ones((n, HD - ROT), np.float32)
    zero = np.zeros((n, HD - ROT), np.float32)
    z8 = np.zeros((n, half), np.float32)
    tabs = ([c, c, one], [-s, z8, zero], [z8, s, zero])
    return [jnp.asarray(np.tile(np.concatenate(t, axis=1), (1, 128 // HD)), F32) for t in tabs]


def per_device(
    prompt_in,
    cont_in,
    prompt_cot,
    cont_cot,
    ln1_gain,
    ln1_bias,
    ln2_gain,
    ln2_bias,
    qkv_weight,
    qkv_bias,
    out_weight,
    out_bias,
    up_weight,
    up_bias,
    down_weight,
    down_bias,
):
    S = lax.axis_size("shard")
    R = lax.axis_size("rep")
    me = lax.axis_index("shard")
    MB, _, PD, D = prompt_in.shape
    CD, CL = cont_in.shape[2:4]
    CR = CD * CL
    N = PD + CR
    CW = D // S
    FL = up_weight.shape[1] // S
    me_arr = jnp.reshape(me, (1,)).astype(jnp.int32)

    small = jnp.concatenate([ln1_gain, ln1_bias, ln2_gain, ln2_bias, out_bias, down_bias, qkv_bias])
    slots = [small] + [shifted(small, S, j) for j in range(1, S)]
    whole = jnp.stack(canonical(slots, me, S, True), axis=0).astype(F32)
    vec = whole[:, : 6 * CW].reshape(S, 6, CW).transpose(1, 0, 2).reshape(6, D)
    gb1 = vec[0:2]
    gb2 = vec[2:4]
    vb = vec[4:6]
    bqkv = whole[:, 6 * CW :].reshape(3, S, CW)
    bqkv = lax.dynamic_index_in_dim(bqkv, me, 1, keepdims=False).reshape(1, 3 * CW)
    bup = up_bias.astype(F32).reshape(1, FL)

    w_up = my_columns(up_weight, me, S, R, 1)
    w_qkv = my_columns(qkv_weight, me, S, R, 3)

    X = [[jnp.concatenate([prompt_in[m, 0], cont_in[m, 0].reshape(CR, D)], axis=0)] for m in range(MB)]
    DY = [[jnp.concatenate([prompt_cot[m, 0], cont_cot[m, 0].reshape(CR, D)], axis=0)] for m in range(MB)]
    for m in range(MB):
        for j in range(1, S):
            X[m].append(shifted(X[m][0], S, S - j))
            DY[m].append(shifted(DY[m][0], S, S - j))

    tabs = rotary_tables(PD * S, CR * S, CL)
    ff = [[None] * S for _ in range(MB)]
    for m in range(MB):
        ff[m][0] = mlp_rows(X[m][0], DY[m][0], w_up, bup, down_weight, gb2)
    y_own, g_own, rest = [], [], []
    y_got, g_got = [], []
    for m in range(MB):
        for j in range(1, S):
            ff[m][j] = mlp_rows(X[m][j], DY[m][j], w_up, bup, down_weight, gb2)
        ys, gs, more = attn_group(
            S, PD, CL, me_arr, X[m], DY[m], [f[3] for f in ff[m]], [f[4] for f in ff[m]], w_qkv, bqkv, out_weight, gb1, tabs
        )
        rest.append(more)
        y_got.append([ys[0]] + [shifted(ys[j], S, j) for j in range(1, S)])
        g_got.append([gs[0]] + [shifted(gs[j], S, j) for j in range(1, S)])

    every = [ff[m][j] for m in range(MB) for j in range(S)]
    dys = [DY[m][j] for m in range(MB) for j in range(S)]
    d_down = tn_sum([f[0] for f in every], dys, 256)
    d_up = tn_sum([f[2] for f in every], [f[1] for f in every], 256)
    d_qkv = tn_sum([r[2] for r in rest], [r[0] for r in rest], 256)
    d_out = tn_sum([r[1] for r in rest], [r[3] for r in rest], 256)

    g_down = reduce_rows(d_down)
    g_up = reduce_columns(d_up, me, S, 1)
    g_out = reduce_rows(d_out)
    g_qkv = reduce_columns(d_qkv, me, S, 3)

    ln1 = sum(r[4] for r in rest).reshape(2 * D)
    ln2 = sum(f[5] for f in every).reshape(2 * D)
    db_out = sum(jnp.sum(DY[m][0].astype(F32), axis=0) for m in range(MB))
    mine = (jnp.arange(S) == me).astype(F32)
    db_qkv = (sum(r[5] for r in rest)[:, None, :] * mine[None, :, None]).reshape(3 * D)
    db_up = (sum(f[6] for f in every) * mine[:, None]).reshape(S * FL)
    tot = lax.psum(jnp.concatenate([ln1, ln2, db_out, db_qkv, db_up]), ("rep", "shard"))
    own = lambda a, n: lax.dynamic_slice_in_dim(tot, a + me * n, n, 0)
    v_ln1g, v_ln1b, v_ln2g, v_ln2b, v_out = [own(k * D, CW) for k in range(5)]
    v_qkv = own(5 * D, 3 * CW)
    v_up = own(8 * D, FL)

    prior = None
    for m in range(MB):
        prior = final_rows(m, MB, PD, X[m][0], DY[m][0], y_got[m], g_got[m], vb, prior)
    po, co, pg, cg = prior
    return (
        po.reshape(MB, 1, PD, D),
        co.reshape(MB, 1, CD, CL, D),
        pg.reshape(MB, 1, PD, D),
        cg.reshape(MB, 1, CD, CL, D),
        v_ln1g,
        v_ln1b,
        v_ln2g,
        v_ln2b,
        g_qkv,
        v_qkv,
        g_out,
        v_out,
        g_up,
        v_up,
        g_down,
        v_out,
    )


def solution(mesh):
    tokens = (
        P(None, "rep", "shard", None),
        P(None, "rep", "shard", None, None),
        P(None, "rep", "shard", None),
        P(None, "rep", "shard", None, None),
    )
    vec = P("shard")
    mat = P("shard", None)
    params = (vec, vec, vec, vec, mat, vec, mat, vec, mat, vec, mat, vec)
    return jax.shard_map(
        per_device, mesh=mesh, in_specs=tokens + params, out_specs=tokens + params, check_vma=False
    )
```

```python
import functools
import math

import jax
import jax.numpy as jnp
import numpy as np
from jax import lax
from jax.experimental import pallas as pl
from jax.experimental.pallas import tpu as pltpu
from jax.sharding import PartitionSpec as P

H = 16
HD = 64
ROT = 16
EPS = 1e-05
F32 = jnp.float32
BF = jnp.bfloat16
MIB = 1024 * 1024
SD = jax.ShapeDtypeStruct


def dnn(a, b):
    return lax.dot_general(a, b, (((1,), (0,)), ((), ())), preferred_element_type=F32)


def dnt(a, b):
    return lax.dot_general(a, b, (((1,), (1,)), ((), ())), preferred_element_type=F32)


def dtn(a, b):
    return lax.dot_general(a, b, (((0,), (0,)), ((), ())), preferred_element_type=F32)


def normed(rows):
    x = rows.astype(F32)
    c = x - jnp.mean(x, axis=-1, keepdims=True)
    inv = lax.rsqrt(jnp.mean(c * c, axis=-1, keepdims=True) + EPS)
    return c * inv, inv


def tile(i, n):
    return pl.ds(pl.multiple_of(i * n, n), n)


def rows_tile(n, most):
    t = most
    while n % t:
        t -= 8
    return t


def mlp_kernel(rt, x_ref, dy_ref, wu_ref, bu_ref, wd_ref, gb_ref, act_ref, dpre_ref, h_ref, yp_ref, g2_ref, ln_ref, bu_out, yacc, dacc):
    f = pl.program_id(0)
    last = pl.num_programs(0) - 1
    rows = x_ref.shape[0]

    @pl.when(f == 0)
    def _():
        @pl.loop(0, rows // 128)
        def _(i):
            r = tile(i, 128)
            xh, _ = normed(x_ref[r, :])
            h_ref[r, :] = (xh * gb_ref[0:1, :] + gb_ref[1:2, :]).astype(BF)
            yacc[r, :] = jnp.zeros((128, yacc.shape[1]), F32)
            dacc[r, :] = jnp.zeros((128, dacc.shape[1]), F32)

    def step(i, bsum):
        r = tile(i, rt)
        pre = dnn(h_ref[r, :], wu_ref[...]) + bu_ref[...]
        da = dnt(dy_ref[r, :], wd_ref[...])
        cdf = 0.5 * (1.0 + lax.erf(pre * 0.7071067811865476))
        act = (pre * cdf).astype(BF)
        dpre = (da * (cdf + pre * jnp.exp(-0.5 * pre * pre) * 0.3989422804014327)).astype(BF)
        act_ref[r, :] = act
        dpre_ref[r, :] = dpre
        yacc[r, :] += dnn(act, wd_ref[...])
        dacc[r, :] += dnt(dpre, wu_ref[...])
        return bsum + jnp.sum(dpre.astype(F32), axis=0, keepdims=True)

    bu_out[...] = lax.fori_loop(0, rows // rt, step, jnp.zeros(bu_out.shape, F32))

    @pl.when(f == last)
    def _():
        ln_ref[...] = jnp.zeros_like(ln_ref)

        @pl.loop(0, rows // 128)
        def _(i):
            r = tile(i, 128)
            xh, _ = normed(x_ref[r, :])
            dh = dacc[r, :]
            yp_ref[r, :] = yacc[r, :].astype(BF)
            g2_ref[r, :] = (dh * gb_ref[0:1, :]).astype(BF)
            ln_ref[0:1, :] += jnp.sum(dh * xh, axis=0, keepdims=True)
            ln_ref[1:2, :] += jnp.sum(dh, axis=0, keepdims=True)


def mlp_rows(x, dy, wu, bu, wd, gb):
    rows, width = x.shape
    hidden = wu.shape[1]
    fb = min(512, hidden)
    full = lambda s: pl.BlockSpec(s, lambda f: (0,) * len(s))
    return pl.pallas_call(
        functools.partial(mlp_kernel, rows_tile(rows, 640)),
        grid=(hidden // fb,),
        in_specs=[
            full((rows, width)),
            full((rows, width)),
            pl.BlockSpec((width, fb), lambda f: (0, f)),
            pl.BlockSpec((1, fb), lambda f: (0, f)),
            pl.BlockSpec((fb, width), lambda f: (f, 0)),
            full((2, width)),
        ],
        out_specs=[
            pl.BlockSpec((rows, fb), lambda f: (0, f)),
            pl.BlockSpec((rows, fb), lambda f: (0, f)),
            full((rows, width)),
            full((rows, width)),
            full((rows, width)),
            full((2, width)),
            pl.BlockSpec((1, fb), lambda f: (0, f)),
        ],
        out_shape=[
            SD((rows, hidden), BF),
            SD((rows, hidden), BF),
            SD((rows, width), BF),
            SD((rows, width), BF),
            SD((rows, width), BF),
            SD((2, width), F32),
            SD((1, hidden), F32),
        ],
        scratch_shapes=[pltpu.VMEM((rows, width), F32)] * 2,
        compiler_params=pltpu.CompilerParams(vmem_limit_bytes=60 * MIB),
        cost_estimate=pl.CostEstimate(
            flops=8 * rows * width * hidden,
            bytes_accessed=4 * (width * hidden + rows * hidden) + 10 * rows * width,
            transcendentals=2 * rows * hidden,
        ),
    )(x, dy, wu, bu, wd, gb)


def roll8(x, left):
    w = x.shape[-1]
    return pltpu.roll(x, (w - 8) if left else 8, 1)


def attn_kernel(S, PD, CL, QB, HG, adding, me_ref, *refs):
    it = iter(refs)
    take = lambda n: [next(it) for _ in range(n)]
    stacked = S > 2
    per = 1 if stacked else S
    xs = take(per)
    dys = take(per)
    yps = take(per * adding)
    g2s = take(per * adding)
    wq, wk, wv = take(3)
    bq, bk, bv = take(3)
    wo, gb = take(2)
    cr, s1r, s2r = take(3)
    ys = take(per)
    gs = take(per)
    dl, ctx, h1, ln, db = take(5)
    yacc, dacc, q_s, k_s, v_s, dc_s, kT, vT, dk_s, dv_s = take(10)
    g = pl.program_id(0)
    last = pl.num_programs(0) - 1
    me = me_ref[0]
    N = xs[0].shape[-2]
    T = N * S
    PR = PD * S
    CR = N - PD
    W = HG * HD

    def every_slot(fn):
        if stacked:

            @pl.loop(0, S)
            def _(j):
                fn(j, lambda refs: refs[0].at[j])

        else:
            for j in range(S):
                fn(j, lambda refs: refs[j])

    def slot_rows(start, n):
        if start < PR:
            s, off = start // PD, start % PD
        else:
            s, off = (start - PR) // CR, PD + (start - PR) % CR
        return pl.ds(pl.multiple_of(lax.rem(s - me + S, S) * N + off, 128), n)

    def pieces(start, n):
        step = min(n, PD if start < PR else CR)
        return [(i, step) for i in range(0, n, step)]

    @pl.when(g == 0)
    def _():
        def load(j, of):
            x = of(xs)

            @pl.loop(0, N // 128)
            def _(i):
                xh, _ = normed(x[tile(i, 128), :])
                h1[pl.ds(pl.multiple_of(j * N + i * 128, 128), 128), :] = (xh * gb[0:1, :] + gb[1:2, :]).astype(BF)

        every_slot(load)

    def rot(y, r, scale):
        c = cr[r, :]
        s1 = s1r[r, :]
        s2 = s2r[r, :]
        out = []
        for p in range(W // 128):
            z = y[:, p * 128 : (p + 1) * 128]
            z = (z * c + roll8(z, True) * s1 + roll8(z, False) * s2).astype(BF)
            out.append(z * jnp.asarray(scale, BF) if scale != 1.0 else z)
        return jnp.concatenate(out, axis=1) if len(out) > 1 else out[0]

    def proj(j, of):
        s = lax.rem(me + j, S)
        rp = pl.ds(pl.multiple_of(s * PD, 128), PD)
        rc = pl.ds(pl.multiple_of(PR + s * CR, 128), CR)
        hh = h1[pl.ds(pl.multiple_of(j * N, 128), N), :]
        y = dnn(hh, wq[...]) + bq[...]
        q_s[rp, :] = rot(y[:PD], rp, HD**-0.5)
        q_s[rc, :] = rot(y[PD:], rc, HD**-0.5)
        y = dnn(hh, wk[...]) + bk[...]
        k_s[rp, :] = rot(y[:PD], rp, 1.0)
        k_s[rc, :] = rot(y[PD:], rc, 1.0)
        y = (dnn(hh, wv[...]) + bv[...]).astype(BF)
        v_s[rp, :] = y[:PD]
        v_s[rc, :] = y[PD:]
        y = dnt(of(dys)[...], wo[...]).astype(BF)
        dc_s[rp, :] = y[:PD]
        dc_s[rc, :] = y[PD:]
        if adding:
            nb = of(yps).shape[0]
            r = pl.ds(pl.multiple_of(g * nb, 16), nb)
            of(ys)[r, :] = of(yps)[...]
            of(gs)[r, :] = of(g2s)[...]

    every_slot(proj)
    lane = lax.broadcasted_iota(jnp.int32, (1, 128), 1)
    row_i = lax.broadcasted_iota(jnp.int32, (QB, QB), 0)
    col_i = lax.broadcasted_iota(jnp.int32, (QB, QB), 1)
    causal = row_i <= col_i
    cmask = causal & ((row_i // CL) == (col_i // CL))
    blocks = []
    for i in range(PR // QB):
        blocks.append((i * QB, [(0, i * QB, None)] * (i > 0) + [(i * QB, QB, causal)]))
    for c in range((T - PR) // QB):
        blocks.append((PR + c * QB, [(0, PR, None), (PR + c * QB, QB, cmask)]))

    @pl.loop(0, W // 128)
    def _(p):
        lanes = tile(p, 128)
        kT[...] = k_s[:, lanes].T
        vT[...] = v_s[:, lanes].T
        dk_s[...] = jnp.zeros_like(dk_s)
        dv_s[...] = jnp.zeros_like(dv_s)
        def begin(q0, parts):
            qb = q_s[pl.ds(q0, QB), lanes]
            dcb = dc_s[pl.ds(q0, QB), lanes]
            out = []
            for h in range(2):
                sel = (lane >= HD * h) & (lane < HD * h + HD)
                qm = jnp.where(sel, qb, jnp.zeros_like(qb))
                dm = jnp.where(sel, dcb, jnp.zeros_like(dcb))
                ss = []
                for k0, n, mask in parts:
                    s = dnt(k_s[k0 : k0 + n, lanes], qm)
                    ss.append(s if mask is None else jnp.where(mask, s, -1e30))
                out.append((qm, dm, ss, [dnt(v_s[k0 : k0 + n, lanes], dm) for k0, n, _ in parts]))
            return out

        ahead = begin(*blocks[0])
        for b, (q0, parts) in enumerate(blocks):
            now = ahead
            if b + 1 < len(blocks):
                ahead = begin(*blocks[b + 1])
            rq = pl.ds(q0, QB)
            P_, DS, cT, dqT = [], [], [], []
            qh = [t[0] for t in now]
            dch = [t[1] for t in now]
            for h in range(2):
                _, _, ss, dps = now[h]
                m = functools.reduce(jnp.maximum, [jnp.max(s, axis=0, keepdims=True) for s in ss])
                es = [jnp.exp(s - m) for s in ss]
                rl = 1.0 / sum(jnp.sum(e, axis=0, keepdims=True) for e in es)
                ps = [e * rl for e in es]
                delta = sum(jnp.sum(a * b, axis=0, keepdims=True) for a, b in zip(ps, dps))
                P_.append([a.astype(BF) for a in ps])
                DS.append([(a * (b - delta)).astype(BF) for a, b in zip(ps, dps)])
                hr = slice(HD * h, HD * h + HD)
                cT.append(sum(dnn(vT[hr, k0 : k0 + n], a) for (k0, n, _), a in zip(parts, P_[h])))
                dqT.append(sum(dnn(kT[hr, k0 : k0 + n], a) for (k0, n, _), a in zip(parts, DS[h])))
            q2 = jnp.concatenate(qh, axis=0)
            dc2 = jnp.concatenate(dch, axis=0)
            for i, (k0, n, _) in enumerate(parts):
                dv_s[k0 : k0 + n, :] += dnn(jnp.concatenate([P_[0][i], P_[1][i]], axis=1), dc2)
                dk_s[k0 : k0 + n, :] += dnn(jnp.concatenate([DS[0][i], DS[1][i]], axis=1), q2)
            co = jnp.concatenate(cT, axis=0).T.astype(BF)
            z = jnp.concatenate(dqT, axis=0).T * (HD**-0.5)
            z = (z * cr[rq, :] - roll8(z, True) * s1r[rq, :] - roll8(z, False) * s2r[rq, :]).astype(BF)
            for o, n in pieces(q0, QB):
                ctx[slot_rows(q0 + o, n), lanes] = co[o : o + n]
                dl[0, slot_rows(q0 + o, n), lanes] = z[o : o + n]

        @pl.loop(0, S)
        def _(s):
            to = lax.rem(s - me + S, S) * N
            for src, off, n in ((s * PD, 0, PD), (PR + s * CR, PD, CR)):
                r = pl.ds(pl.multiple_of(src, 128), n)
                w = pl.ds(pl.multiple_of(to + off, 128), n)
                z = dk_s[r, :]
                z = z * cr[r, :] - roll8(z, True) * s1r[r, :] - roll8(z, False) * s2r[r, :]
                dl[1, w, lanes] = z.astype(BF)
                dl[2, w, lanes] = dv_s[r, :].astype(BF)

    for c in range(3):
        db[c : c + 1, :] = jnp.sum(dl[c].astype(F32), axis=0, keepdims=True)

    @pl.loop(0, S)
    def _(j):
        r = pl.ds(pl.multiple_of(j * N, 128), N)
        y = dnn(ctx[r, :], wo[...])
        d = dnt(dl[0, r, :], wq[...]) + dnt(dl[1, r, :], wk[...]) + dnt(dl[2, r, :], wv[...])

        @pl.when(g == 0)
        def _():
            yacc[r, :] = y
            dacc[r, :] = d

        @pl.when(g > 0)
        def _():
            yacc[r, :] += y
            dacc[r, :] += d

    @pl.when(g == last)
    def _():
        ln[...] = jnp.zeros_like(ln)

        def store(j, of):
            x, yo, go = of(xs), of(ys), of(gs)

            @pl.loop(0, N // 128)
            def _(i):
                r = tile(i, 128)
                w = pl.ds(pl.multiple_of(j * N + i * 128, 128), 128)
                xh, _ = normed(x[r, :])
                d = dacc[w, :]
                y = yacc[w, :]
                gg = d * gb[0:1, :]
                if adding:
                    y = y + yo[r, :].astype(F32)
                    gg = gg + go[r, :].astype(F32)
                yo[r, :] = y.astype(BF)
                go[r, :] = gg.astype(BF)
                ln[0:1, :] += jnp.sum(d * xh, axis=0, keepdims=True)
                ln[1:2, :] += jnp.sum(d, axis=0, keepdims=True)

        every_slot(store)


def attn_group(S, PD, CL, me, xs, dys, yps, g2s, wqkv, bqkv, wo, gb, tabs):
    N, D = xs[0].shape
    CW = wo.shape[0]
    T = N * S
    HG = 4 if CW % 256 == 0 else 2
    QB = 256
    W = HG * HD
    G = CW // W
    full = lambda s: pl.BlockSpec(s, lambda g, m: (0,) * len(s), pipeline_mode=pl.Buffered(1))
    keep = lambda s: pl.BlockSpec(s, lambda g, m: (0,) * len(s))
    tok, tok_out, per = full((N, D)), keep((N, D)), S
    adding = int(T * D <= 1536 * 1024)
    others = (yps, g2s)
    if not adding:
        yps, g2s = [], []
    out_tok = SD((N, D), BF)
    if S > 2:
        xs, dys, yps, g2s = [[jnp.stack(v, axis=0)] if v else v for v in (xs, dys, yps, g2s)]
        tok, tok_out, per = full((S, N, D)), keep((S, N, D)), 1
        out_tok = SD((S, N, D), BF)
        part = pl.BlockSpec((S, N // G, D), lambda g, m: (0, g, 0))
    else:
        part = pl.BlockSpec((N // G, D), lambda g, m: (g, 0))
    wspec = lambda c: pl.BlockSpec((D, W), lambda g, m: (0, c * G + g))
    bspec = lambda c: pl.BlockSpec((1, W), lambda g, m: (0, c * G + g))
    outs = pl.pallas_call(
        functools.partial(attn_kernel, S, PD, CL, QB, HG, adding),
        grid_spec=pltpu.PrefetchScalarGridSpec(
            num_scalar_prefetch=1,
            grid=(G,),
            in_specs=[tok] * (2 * per)
            + [part] * (2 * adding * per)
            + [wspec(0), wspec(1), wspec(2), bspec(0), bspec(1), bspec(2)]
            + [pl.BlockSpec((W, D), lambda g, m: (g, 0)), full((2, D))]
            + [full((T, 128))] * 3,
            out_specs=[tok_out] * (2 * per)
            + [
                pl.BlockSpec((3, T, W), lambda g, m: (0, 0, g)),
                pl.BlockSpec((T, W), lambda g, m: (0, g)),
                keep((T, D)),
                keep((2, D)),
                pl.BlockSpec((3, W), lambda g, m: (0, g)),
            ],
            scratch_shapes=[pltpu.VMEM((T, D), F32)] * 2
            + [pltpu.VMEM((T, W), BF)] * 4
            + [pltpu.VMEM((128, T), BF)] * 2
            + [pltpu.VMEM((T, 128), F32)] * 2,
        ),
        out_shape=[out_tok] * (2 * per)
        + [SD((3, T, CW), BF), SD((T, CW), BF), SD((T, D), BF), SD((2, D), F32), SD((3, CW), F32)],
        compiler_params=pltpu.CompilerParams(vmem_limit_bytes=62 * MIB),
        cost_estimate=pl.CostEstimate(
            flops=16 * T * D * CW + 40 * T * T * CW,
            bytes_accessed=12 * T * D + 12 * T * CW + 8 * D * CW,
            transcendentals=T * T * CW // HD,
        ),
    )(me, *xs, *dys, *yps, *g2s, wqkv, wqkv, wqkv, bqkv, bqkv, bqkv, wo, gb, *tabs)
    ys, gs = outs[:per], outs[per : 2 * per]
    if S > 2:
        ys, gs = [[v[0][j] for j in range(S)] for v in (ys, gs)]
    if not adding:
        ys, gs = [[a + b for a, b in zip(p, q)] for p, q in zip((ys, gs), others)]
    return ys, gs, outs[2 * per :]


def tn_kernel(n, wide, *refs):
    a = refs[:n]
    b = refs[n : 2 * n]
    o = refs[2 * n]
    if wide == 0:
        o[...] = sum(dtn(x[...], y[...]) for x, y in zip(a, b)).astype(BF)
    else:
        w = b[0].shape[2]
        for c in range(wide):
            o[:, c * w : (c + 1) * w] = sum(dtn(x[...], y[c]) for x, y in zip(a, b)).astype(BF)


def tn_sum(a, b, block):
    n = len(a)
    rows, da = a[0].shape
    block = min(block, da)
    wide = b[0].shape[0] if b[0].ndim == 3 else 0
    db = b[0].shape[-1] * max(wide, 1)
    keep = lambda s: pl.BlockSpec(s, lambda i: (0,) * len(s), pipeline_mode=pl.Buffered(1))
    return pl.pallas_call(
        functools.partial(tn_kernel, n, wide),
        grid=(da // block,),
        in_specs=[pl.BlockSpec((rows, block), lambda i: (0, i))] * n + [keep(b[0].shape)] * n,
        out_specs=pl.BlockSpec((block, db), lambda i: (i, 0)),
        out_shape=SD((da, db), BF),
        compiler_params=pltpu.CompilerParams(vmem_limit_bytes=60 * MIB),
        cost_estimate=pl.CostEstimate(flops=2 * n * rows * da * db, bytes_accessed=2 * (n * rows * (da + db) + da * db), transcendentals=0),
    )(*a, *b)


def joined(refs):
    return jnp.concatenate([r[...] for r in refs], axis=0)


def down_kernel(n, *refs):
    a = refs[:n]
    b = refs[n : 2 * n]
    o = refs[-1]
    o[...] = dtn(joined(a), joined(b)).astype(BF).reshape(o.shape)


def up_kernel(n, *refs):
    a = refs[:n]
    b = refs[n : 2 * n]
    o = refs[-1]
    c, rows, w = o.shape
    k = b[0].shape[1] // w
    t = dtn(joined(a), joined(b)).astype(BF)
    for i in range(k):
        o[:, i * (rows // k) : (i + 1) * (rows // k), :] = t[:, i * w : (i + 1) * w].reshape(c, rows // k, w)


def mlp_grads(S, R, acts, dys, hs, dpres):
    n = len(acts)
    rows, FL = acts[0].shape
    D = dys[0].shape[1]
    DR = D // S
    blk = 256
    rd = FL // R
    ru = DR // R
    k = FL // D
    per = rd + S * ru * k
    one = pl.Buffered(1)
    keep = lambda s: pl.BlockSpec(s, lambda i: (0,) * len(s), pipeline_mode=one)
    cost = pl.CostEstimate(flops=2 * n * rows * D * FL, bytes_accessed=2 * (n * rows * (D + FL) + D * FL), transcendentals=0)
    params = pltpu.CompilerParams(vmem_limit_bytes=60 * MIB)
    g = pl.pallas_call(
        functools.partial(down_kernel, n),
        grid=(FL // blk,),
        in_specs=[pl.BlockSpec((rows, blk), lambda i: (0, i))] * n + [keep((rows, D))] * n,
        out_specs=pl.BlockSpec((blk // rd, rd, D), lambda i: (i, 0, 0)),
        out_shape=SD((R, per, D), BF),
        compiler_params=params,
        cost_estimate=cost,
    )(*acts, *dys)
    steps = DR // blk
    return pl.pallas_call(
        functools.partial(up_kernel, n),
        grid=(D // blk,),
        in_specs=[pl.BlockSpec((rows, blk), lambda i: (0, i))] * n + [keep((rows, FL))] * n + [pl.BlockSpec(memory_space=pl.ANY)],
        out_specs=pl.BlockSpec((blk // ru, ru * k, D), lambda i: (i % steps, rd // (ru * k) + i // steps, 0)),
        out_shape=SD((R, per, D), BF),
        input_output_aliases={2 * n: 0},
        compiler_params=params,
        cost_estimate=cost,
    )(*hs, *dpres, g)


def mlp_finish_kernel(S, rd, ru, g, down, up):
    D = g.shape[2]
    k = (g.shape[1] - rd) // (S * ru)
    down[...] = g[0, :rd, :].astype(F32)
    for t in range(S):
        for i in range(k):
            a = rd + (t * k + i) * ru
            up[:, (t * k + i) * D : (t * k + i + 1) * D] = g[0, a : a + ru, :].astype(F32)


def mlp_finish(S, g, FL):
    R, per, D = g.shape
    rd = FL // R
    ru = D // S // R
    return pl.pallas_call(
        functools.partial(mlp_finish_kernel, S, rd, ru),
        grid=(R,),
        in_specs=[pl.BlockSpec((1, per, D), lambda c: (c, 0, 0))],
        out_specs=[pl.BlockSpec((rd, D), lambda c: (c, 0)), pl.BlockSpec((ru, S * FL), lambda c: (c, 0))],
        out_shape=[SD((FL, D), F32), SD((D // S, S * FL), F32)],
        cost_estimate=pl.CostEstimate(flops=0, bytes_accessed=6 * R * per * D, transcendentals=0),
    )(g)


def attn_grads_kernel(n, S, R, q_ref, *refs):
    h = refs[:n]
    dl = refs[n : 2 * n]
    ctx = refs[2 * n : 3 * n]
    dy = refs[3 * n : -1]
    o = refs[-1]
    i = pl.program_id(0)
    q = q_ref[0]
    blk = h[0].shape[1]
    D = dy[0].shape[1]
    DR = D // S
    CW = dl[0].shape[2]
    ru = DR // R
    k = D // CW
    steps = DR // blk
    s = i // steps
    base = (i % steps) * (blk // ru)
    for p in range(3):
        t = dtn(joined(h), jnp.concatenate([y[p] for y in dl], axis=0)).astype(BF)
        for c in range(blk // ru):
            o[(base + c) ^ q, pl.ds(k * ru + s * 3 * ru + p * ru, ru), :] = t[c * ru : (c + 1) * ru, :]
    t = dtn(joined(ctx), joined(dy)).astype(BF)
    m = ctx[0].shape[1] // ru
    for c in range(m):
        for j in range(k):
            o[(i * m + c) ^ q, j * ru : (j + 1) * ru, :] = t[c * ru : (c + 1) * ru, j * CW : (j + 1) * CW]


def attn_grads(S, R, q, hs, dls, ctxs, dys):
    n = len(hs)
    T, D = hs[0].shape
    CW = ctxs[0].shape[1]
    DR = D // S
    ru = DR // R
    blk = 256
    G = D // blk
    per = (D // CW) * ru + S * 3 * ru
    keep = lambda s: pl.BlockSpec(s, lambda i, q: (0,) * len(s), pipeline_mode=pl.Buffered(1))
    return pl.pallas_call(
        functools.partial(attn_grads_kernel, n, S, R),
        grid_spec=pltpu.PrefetchScalarGridSpec(
            num_scalar_prefetch=1,
            grid=(G,),
            in_specs=[pl.BlockSpec((T, blk), lambda i, q: (0, i))] * n
            + [keep((3, T, CW))] * n
            + [pl.BlockSpec((T, CW // G), lambda i, q: (0, i))] * n
            + [keep(dys[0].shape)] * len(dys),
            out_specs=pl.BlockSpec((R, per, CW), lambda i, q: (0, 0, 0)),
        ),
        out_shape=SD((R, per, CW), BF),
        compiler_params=pltpu.CompilerParams(vmem_limit_bytes=60 * MIB),
        cost_estimate=pl.CostEstimate(flops=8 * n * T * D * CW, bytes_accessed=2 * n * T * (2 * D + 4 * CW) + 8 * D * CW, transcendentals=0),
    )(q, *hs, *dls, *ctxs, *dys)


def attn_finish_kernel(S, ru, k, q_ref, g, out, qkv):
    CW = g.shape[2]
    D = out.shape[1]
    for j in range(k):
        out[:, j * CW : (j + 1) * CW] = g[0, j * ru : (j + 1) * ru, :].astype(F32)
    for t in range(S):
        for p in range(3):
            a = k * ru + (t * 3 + p) * ru
            qkv[:, p * D + t * CW : p * D + (t + 1) * CW] = g[0, a : a + ru, :].astype(F32)


def attn_finish(S, q, g):
    R, per, CW = g.shape
    D = CW * S
    ru = D // S // R
    return pl.pallas_call(
        functools.partial(attn_finish_kernel, S, ru, S),
        grid_spec=pltpu.PrefetchScalarGridSpec(
            num_scalar_prefetch=1,
            grid=(R,),
            in_specs=[pl.BlockSpec((1, per, CW), lambda c, q: (c ^ q[0], 0, 0))],
            out_specs=[pl.BlockSpec((ru, D), lambda c, q: (c, 0)), pl.BlockSpec((ru, 3 * D), lambda c, q: (c, 0))],
        ),
        out_shape=[SD((CW, D), F32), SD((D // S, 3 * D), F32)],
        cost_estimate=pl.CostEstimate(flops=0, bytes_accessed=6 * R * per * CW, transcendentals=0),
    )(q, g)


def final_kernel(S, first, PT, *refs):
    it = iter(refs)
    take = lambda n: [next(it) for _ in range(n)]
    x, dy = take(2)
    ys = take(S)
    gs = take(S)
    (vb,) = take(1)
    if not first:
        take(4)
    po, co, pg, cg = take(4)
    i = pl.program_id(0)
    xv = x[...].astype(F32)
    xh, inv = normed(xv)
    y = xv + vb[0:1, :] + sum(r[...].astype(F32) for r in ys) + vb[1:2, :]
    gsum = sum(r[...].astype(F32) for r in gs)
    dx = (gsum - jnp.mean(gsum, axis=-1, keepdims=True) - xh * jnp.mean(gsum * xh, axis=-1, keepdims=True)) * inv
    out = y.astype(BF)
    grad = dy[...].astype(F32) + dx

    @pl.when(i < PT)
    def _():
        po[0] = out
        pg[0] = grad

    @pl.when(i >= PT)
    def _():
        co[0] = out
        cg[0] = grad


def final_rows(m, MB, PD, x, dy, ys, gs, vb, prior):
    S = len(ys)
    N, D = x.shape
    CR = N - PD
    RT = 128
    PT = PD // RT
    first = prior is None
    row = pl.BlockSpec((RT, D), lambda i: (i, 0))
    pspec = pl.BlockSpec((1, RT, D), lambda i: (m, jnp.minimum(i, PT - 1), 0))
    cspec = pl.BlockSpec((1, RT, D), lambda i: (m, jnp.maximum(i - PT, 0), 0))
    hbm = pl.BlockSpec(memory_space=pl.ANY)
    n_in = 2 * S + 3
    return pl.pallas_call(
        functools.partial(final_kernel, S, first, PT),
        grid=(N // RT,),
        in_specs=[row] * (2 * S + 2) + [pl.BlockSpec((2, D), lambda i: (0, 0))] + ([] if first else [hbm] * 4),
        out_specs=[pspec, cspec, pspec, cspec],
        out_shape=[SD((MB, PD, D), BF), SD((MB, CR, D), BF), SD((MB, PD, D), F32), SD((MB, CR, D), F32)],
        input_output_aliases={} if first else {n_in + k: k for k in range(4)},
        compiler_params=pltpu.CompilerParams(vmem_limit_bytes=32 * MIB),
        cost_estimate=pl.CostEstimate(flops=20 * N * D, bytes_accessed=(4 * S + 10) * N * D, transcendentals=0),
    )(x, dy, *ys, *gs, vb, *(() if first else prior))


def shifted(value, S, j):
    return lax.ppermute(value, "shard", [(i, (i + j) % S) for i in range(S)])


def canonical(slots, me, S, back):
    if S == 1:
        return slots
    if S == 2:
        a, b = slots
        return [jnp.where(me == 0, a, b), jnp.where(me == 0, b, a)]
    stacked = jnp.stack(slots, axis=0)
    return [
        lax.dynamic_index_in_dim(stacked, lax.rem((me - s if back else s - me) + S, S), 0, keepdims=False) for s in range(S)
    ]


def exchanged(value, R, bit):
    return lax.ppermute(value, "rep", [(i, i ^ bit) for i in range(R)])


def columns_for(weight, me, S, j, parts, row=0, rows=None):
    cols = weight.shape[1] // parts
    rows = weight.shape[0] if rows is None else rows
    w = cols // S
    at = lax.rem(me + j, S) * w
    got = [lax.dynamic_slice(weight, (row, p * cols + at), (rows, w)) for p in range(parts)]
    return got[0] if parts == 1 else jnp.concatenate(got, axis=1)


def my_columns_halves(weight, me, S, R):
    rows = weight.shape[0]
    half = rows // 2
    core = lax.rem(lax.axis_index("rep"), 2)
    slots = [columns_for(weight, me, S, 0, 1)]
    for j in range(1, S):
        piece = shifted(columns_for(weight, me, S, j, 1, core * half, half), S, j)
        other = exchanged(piece, R, 1)
        first = core == 0
        slots.append(jnp.concatenate([jnp.where(first, piece, other), jnp.where(first, other, piece)], axis=0))
    return jnp.concatenate(canonical(slots, me, S, True), axis=0), piece


def my_columns(weight, me, S, R, parts):
    rows = weight.shape[0]
    own = columns_for(weight, me, S, 0, parts)
    if S == 1:
        return own
    rep = lax.axis_index("rep")
    chunk = rows // R
    got = []
    for j in range(1, S):
        got.append(shifted(columns_for(weight, me, S, j, parts, rep * chunk, chunk), S, j))
    others = lax.all_gather(jnp.stack(got, axis=0), "rep", axis=1, tiled=True)
    return jnp.concatenate(canonical([own] + [others[j] for j in range(S - 1)], me, S, True), axis=0)


def add_low(a, b):
    return (a.astype(F32) + b.astype(F32)).astype(BF)


def halving(g, v, R, beside):
    bit = 1
    while bit < R:
        h = g.shape[0] // 2
        got = exchanged(g[h:], R, bit)
        v = v + exchanged(v, R, bit)
        got, v = lax.optimization_barrier((got, v))
        if bit in beside:
            got, beside[bit] = lax.optimization_barrier((got, beside[bit]))
        g = add_low(g[:h], got)
        bit *= 2
    return g[0], v


def doubling(part, R, beside):
    g = part[None]
    bit = R // 2
    while bit:
        got = exchanged(g, R, bit)
        if bit in beside:
            got, beside[bit] = lax.optimization_barrier((got, beside[bit]))
        g = jnp.concatenate([g, got], axis=0)
        bit //= 2
    return g


def sum_all(v, S, R):
    bit = 1
    while bit < R:
        v = v + exchanged(v, R, bit)
        bit *= 2
    return v


def swap_shards(part, me, S, head):
    n = (part.shape[0] - head) // S
    slots = []
    for j in range(S):
        b = lax.dynamic_slice_in_dim(part, head + lax.rem(me + j, S) * n, n, 0)
        slots.append(shifted(b, S, j) if j else b)
    return jnp.concatenate([part[:head]] + canonical(slots, me, S, True), axis=0)


def reduce_rows(grad):
    part = lax.psum_scatter(grad, "rep", scatter_dimension=0, tiled=True)
    return lax.all_gather(part, "rep", axis=0, tiled=True).astype(F32)


def reduce_columns(grad, me, S, parts):
    rows, cols = grad.shape
    part = lax.psum_scatter(grad.reshape(S, rows // S, cols), "rep", scatter_dimension=1, tiled=True)
    slots = [lax.dynamic_index_in_dim(part, me, 0, keepdims=False)]
    for j in range(1, S):
        slots.append(shifted(lax.dynamic_index_in_dim(part, lax.rem(me + j, S), 0, keepdims=False), S, j))
    slots = [s.reshape(s.shape[0], parts, cols // parts) for s in slots]
    whole = jnp.stack(canonical(slots, me, S, True), axis=2).reshape(-1, S * cols)
    return lax.all_gather(whole, "rep", axis=0, tiled=True).astype(F32)


def rotary_tables(PR, CR, CL):
    pos = np.concatenate([np.arange(PR), PR + np.arange(CR) % CL]).astype(np.float32)
    half = ROT // 2
    freq = np.exp(np.arange(half, dtype=np.float32) * np.float32(-2.0 * math.log(10000.0) / ROT)).astype(np.float32)
    ang = (pos[:, None] * freq[None, :]).astype(np.float32)
    c = np.cos(ang)
    s = np.sin(ang)
    n = pos.shape[0]
    one = np.ones((n, HD - ROT), np.float32)
    zero = np.zeros((n, HD - ROT), np.float32)
    z8 = np.zeros((n, half), np.float32)
    tabs = ([c, c, one], [-s, z8, zero], [z8, s, zero])
    return [jnp.asarray(np.tile(np.concatenate(t, axis=1), (1, 128 // HD)), F32) for t in tabs]


def per_device(
    prompt_in,
    cont_in,
    prompt_cot,
    cont_cot,
    ln1_gain,
    ln1_bias,
    ln2_gain,
    ln2_bias,
    qkv_weight,
    qkv_bias,
    out_weight,
    out_bias,
    up_weight,
    up_bias,
    down_weight,
    down_bias,
):
    S = lax.axis_size("shard")
    R = lax.axis_size("rep")
    me = lax.axis_index("shard")
    MB, _, PD, D = prompt_in.shape
    CD, CL = cont_in.shape[2:4]
    CR = CD * CL
    N = PD + CR
    CW = D // S
    FL = up_weight.shape[1] // S
    me_arr = jnp.reshape(me, (1,)).astype(jnp.int32)

    one = lambda v: v.astype(F32).reshape(-1, CW)
    small = jnp.concatenate([one(v) for v in (ln1_gain, ln1_bias, ln2_gain, ln2_bias, out_bias, down_bias, qkv_bias)], axis=0)
    w_up, brought = my_columns_halves(up_weight, me, S, R)
    slots = [small] + [shifted(small, S, j) for j in range(1, S)]
    whole = jnp.stack(canonical(slots, me, S, True), axis=0)
    vec = whole[:, :6].transpose(1, 0, 2).reshape(6, D)
    gb1 = vec[0:2]
    gb2 = vec[2:4]
    vb = vec[4:6]
    bqkv = whole[:, 6:].reshape(3, S, CW)
    bqkv = lax.dynamic_index_in_dim(bqkv, me, 1, keepdims=False).reshape(1, 3 * CW)
    bup = up_bias.astype(F32).reshape(1, FL)

    w_qkv = my_columns(qkv_weight, me, S, R, 3)

    X = [[jnp.concatenate([prompt_in[m, 0], cont_in[m, 0].reshape(CR, D)], axis=0)] for m in range(MB)]
    DY = [[jnp.concatenate([prompt_cot[m, 0], cont_cot[m, 0].reshape(CR, D)], axis=0)] for m in range(MB)]
    tabs = rotary_tables(PD * S, CR * S, CL)
    src = [(X[m][0], DY[m][0]) for m in range(MB)]
    src[1:], brought = lax.optimization_barrier((src[1:], brought))
    for m in range(MB):
        for j in range(1, S):
            X[m].append(shifted(src[m][0], S, S - j))
            DY[m].append(shifted(src[m][1], S, S - j))

    ff = [[None] * S for _ in range(MB)]

    def mlp(m, j):
        ff[m][j] = mlp_rows(X[m][j], DY[m][j], w_up, bup, down_weight, gb2)

    for m in range(MB):
        mlp(m, 0)
    rest = []
    y_got, g_got = [], []

    def attend(m):
        ys, gs, more = attn_group(
            S, PD, CL, me_arr, X[m], DY[m], [f[3] for f in ff[m]], [f[4] for f in ff[m]], w_qkv, bqkv, out_weight, gb1, tabs
        )
        rest.append(list(more))
        y_got.append([ys[0]] + [shifted(ys[j], S, j) for j in range(1, S)])
        g_got.append([gs[0]] + [shifted(gs[j], S, j) for j in range(1, S)])

    chunked = (D // S // R) % 16 == 0 and R & (R - 1) == 0
    for m in range(MB):
        for j in range(1, S):
            mlp(m, j)
        if m + 1 < MB:
            attend(m)
            w_up, rest[m][3] = lax.optimization_barrier((w_up, rest[m][3]))
    every = [ff[m][j] for m in range(MB) for j in range(S)]
    dys = [DY[m][j] for m in range(MB) for j in range(S)]
    acts, dpres, hs = [[f[k] for f in every] for k in range(3)]
    if chunked:
        gmlp = mlp_grads(S, R, acts, dys, hs, dpres)
        part = lax.psum_scatter(gmlp, "rep", scatter_dimension=0, tiled=True)[0]
    else:
        gmlp = tn_sum(acts, dys, 256)
        g_down = reduce_rows(gmlp)
        g_up = reduce_columns(tn_sum(hs, dpres, 256), me, S, 1)
    w_qkv, gmlp = lax.optimization_barrier((w_qkv, gmlp))
    attend(MB - 1)
    ln1 = sum(r[3] for r in rest).reshape(-1, CW)
    ln2 = sum(f[5] for f in every).reshape(-1, CW)
    db_out = sum(jnp.sum(DY[m][0].astype(F32), axis=0) for m in range(MB)).reshape(-1, CW)
    mine = (jnp.arange(S) == me).astype(F32)
    db_qkv = (sum(r[4] for r in rest)[:, None, :] * mine[None, :, None]).reshape(-1, CW)
    db_up = (sum(f[6] for f in every) * mine[:, None]).reshape(-1, CW)
    vecs = jnp.concatenate([ln1, ln2, db_out, db_qkv, db_up], axis=0)

    finals = lambda m, prior: final_rows(m, MB, PD, X[m][0], DY[m][0], y_got[m], g_got[m], vb, prior)
    hs, dls, ctxs = [[r[k] for r in rest] for k in (2, 0, 1)]
    if chunked:
        rep = lax.axis_index("rep")
        q = jnp.zeros((), jnp.int32)
        for b in range(R.bit_length() - 1):
            q = 2 * q + ((rep >> b) & 1)
        q = q.reshape(1).astype(jnp.int32)
        hs, y_got[:-1], g_got[:-1] = lax.optimization_barrier((hs, y_got[:-1], g_got[:-1]))
        gatt = attn_grads(S, R, q, hs, dls, ctxs, dys)
        gatt, part = lax.optimization_barrier((gatt, part))
        gmlp_all = lax.all_gather(swap_shards(part, me, S, FL // R), "rep", axis=0, tiled=False)
        early = None
        for m in range(MB - 1):
            early = finals(m, early)
        beside = {2: early}
        half, vecs = halving(gatt, vecs, R, beside)
        early = beside[2]
        half, y_got[-1], g_got[-1] = lax.optimization_barrier((half, y_got[-1], g_got[-1]))
        outs = finals(MB - 1, early)
        beside = {2: outs}
        gatt_all = doubling(swap_shards(half, me, S, D // R), R, beside)
        outs = beside[2]
        g_out, g_qkv = attn_finish(S, q, gatt_all)
        g_down, g_up = mlp_finish(S, gmlp_all, FL)
    else:
        dycs = [jnp.concatenate(DY[m], axis=0) for m in range(MB)]
        g_out = reduce_rows(tn_sum(ctxs, dycs, 256))
        g_qkv = reduce_columns(tn_sum(hs, dls, 256), me, S, 3)
        vecs = sum_all(vecs, S, R)
        outs = None
        for m in range(MB):
            outs = finals(m, outs)
    tot = vecs + sum(shifted(vecs, S, j) for j in range(1, S))
    own = lambda a, n: lax.dynamic_slice_in_dim(tot, a + me * n, n, 0).reshape(-1)
    v_ln1g, v_ln1b, v_ln2g, v_ln2b, v_out = [own(k * S, 1) for k in range(5)]
    v_qkv = own(5 * S, 3)
    v_up = own(8 * S, FL // CW)

    po, co, pg, cg = outs
    return (
        po.reshape(MB, 1, PD, D),
        co.reshape(MB, 1, CD, CL, D),
        pg.reshape(MB, 1, PD, D),
        cg.reshape(MB, 1, CD, CL, D),
        v_ln1g,
        v_ln1b,
        v_ln2g,
        v_ln2b,
        g_qkv,
        v_qkv,
        g_out,
        v_out,
        g_up,
        v_up,
        g_down,
        v_out,
    )


def solution(mesh):
    tokens = (
        P(None, "rep", "shard", None),
        P(None, "rep", "shard", None, None),
        P(None, "rep", "shard", None),
        P(None, "rep", "shard", None, None),
    )
    vec = P("shard")
    mat = P("shard", None)
    params = (vec, vec, vec, vec, mat, vec, mat, vec, mat, vec, mat, vec)
    return jax.shard_map(
        per_device, mesh=mesh, in_specs=tokens + params, out_specs=tokens + params, check_vma=False
    )
```

```python
import functools
import math

import jax
import jax.numpy as jnp
import numpy as np
from jax import lax
from jax.experimental import pallas as pl
from jax.experimental.pallas import tpu as pltpu
from jax.sharding import PartitionSpec as P

H = 16
HD = 64
ROT = 16
EPS = 1e-05
F32 = jnp.float32
BF = jnp.bfloat16
MIB = 1024 * 1024
SD = jax.ShapeDtypeStruct


def dnn(a, b):
    return lax.dot_general(a, b, (((1,), (0,)), ((), ())), preferred_element_type=F32)


def dnt(a, b):
    return lax.dot_general(a, b, (((1,), (1,)), ((), ())), preferred_element_type=F32)


def dtn(a, b):
    return lax.dot_general(a, b, (((0,), (0,)), ((), ())), preferred_element_type=F32)


def normed(rows):
    x = rows.astype(F32)
    c = x - jnp.mean(x, axis=-1, keepdims=True)
    inv = lax.rsqrt(jnp.mean(c * c, axis=-1, keepdims=True) + EPS)
    return c * inv, inv


def tile(i, n):
    return pl.ds(pl.multiple_of(i * n, n), n)


def rows_tile(n, most):
    t = most
    while n % t:
        t -= 8
    return t


def mlp_kernel(rt, x_ref, dy_ref, wu_ref, bu_ref, wd_ref, gb_ref, act_ref, dpre_ref, h_ref, yp_ref, g2_ref, ln_ref, bu_out, yacc, dacc):
    f = pl.program_id(0)
    last = pl.num_programs(0) - 1
    rows = x_ref.shape[0]

    @pl.when(f == 0)
    def _():
        @pl.loop(0, rows // 128)
        def _(i):
            r = tile(i, 128)
            xh, _ = normed(x_ref[r, :])
            h_ref[r, :] = (xh * gb_ref[0:1, :] + gb_ref[1:2, :]).astype(BF)
            yacc[r, :] = jnp.zeros((128, yacc.shape[1]), F32)
            dacc[r, :] = jnp.zeros((128, dacc.shape[1]), F32)

    def step(i, bsum):
        r = tile(i, rt)
        pre = dnn(h_ref[r, :], wu_ref[...]) + bu_ref[...]
        da = dnt(dy_ref[r, :], wd_ref[...])
        cdf = 0.5 * (1.0 + lax.erf(pre * 0.7071067811865476))
        act = (pre * cdf).astype(BF)
        dpre = (da * (cdf + pre * jnp.exp(-0.5 * pre * pre) * 0.3989422804014327)).astype(BF)
        act_ref[r, :] = act
        dpre_ref[r, :] = dpre
        yacc[r, :] += dnn(act, wd_ref[...])
        dacc[r, :] += dnt(dpre, wu_ref[...])
        return bsum + jnp.sum(dpre.astype(F32), axis=0, keepdims=True)

    bu_out[...] = lax.fori_loop(0, rows // rt, step, jnp.zeros(bu_out.shape, F32))

    @pl.when(f == last)
    def _():
        ln_ref[...] = jnp.zeros_like(ln_ref)

        @pl.loop(0, rows // 128)
        def _(i):
            r = tile(i, 128)
            xh, _ = normed(x_ref[r, :])
            dh = dacc[r, :]
            yp_ref[r, :] = yacc[r, :].astype(BF)
            g2_ref[r, :] = (dh * gb_ref[0:1, :]).astype(BF)
            ln_ref[0:1, :] += jnp.sum(dh * xh, axis=0, keepdims=True)
            ln_ref[1:2, :] += jnp.sum(dh, axis=0, keepdims=True)


def mlp_rows(x, dy, wu, bu, wd, gb):
    rows, width = x.shape
    hidden = wu.shape[1]
    fb = min(512, hidden)
    full = lambda s: pl.BlockSpec(s, lambda f: (0,) * len(s))
    return pl.pallas_call(
        functools.partial(mlp_kernel, rows_tile(rows, 640)),
        grid=(hidden // fb,),
        in_specs=[
            full((rows, width)),
            full((rows, width)),
            pl.BlockSpec((width, fb), lambda f: (0, f)),
            pl.BlockSpec((1, fb), lambda f: (0, f)),
            pl.BlockSpec((fb, width), lambda f: (f, 0)),
            full((2, width)),
        ],
        out_specs=[
            pl.BlockSpec((rows, fb), lambda f: (0, f)),
            pl.BlockSpec((rows, fb), lambda f: (0, f)),
            full((rows, width)),
            full((rows, width)),
            full((rows, width)),
            full((2, width)),
            pl.BlockSpec((1, fb), lambda f: (0, f)),
        ],
        out_shape=[
            SD((rows, hidden), BF),
            SD((rows, hidden), BF),
            SD((rows, width), BF),
            SD((rows, width), BF),
            SD((rows, width), BF),
            SD((2, width), F32),
            SD((1, hidden), F32),
        ],
        scratch_shapes=[pltpu.VMEM((rows, width), F32)] * 2,
        compiler_params=pltpu.CompilerParams(vmem_limit_bytes=60 * MIB),
        cost_estimate=pl.CostEstimate(
            flops=8 * rows * width * hidden,
            bytes_accessed=4 * (width * hidden + rows * hidden) + 10 * rows * width,
            transcendentals=2 * rows * hidden,
        ),
    )(x, dy, wu, bu, wd, gb)


def roll8(x, left):
    w = x.shape[-1]
    return pltpu.roll(x, (w - 8) if left else 8, 1)


def attn_kernel(S, PD, CL, QB, HG, adding, me_ref, *refs):
    it = iter(refs)
    take = lambda n: [next(it) for _ in range(n)]
    stacked = S > 2
    per = 1 if stacked else S
    xs = take(per)
    dys = take(per)
    yps = take(per * adding)
    g2s = take(per * adding)
    wq, wk, wv = take(3)
    bq, bk, bv = take(3)
    wo, gb = take(2)
    cr, s1r, s2r = take(3)
    ys = take(per)
    gs = take(per)
    dl, ctx, h1, ln, db = take(5)
    yacc, dacc, q_s, k_s, v_s, dc_s, kT, vT, dk_s, dv_s = take(10)
    g = pl.program_id(0)
    last = pl.num_programs(0) - 1
    me = me_ref[0]
    N = xs[0].shape[-2]
    T = N * S
    PR = PD * S
    CR = N - PD
    W = HG * HD

    def every_slot(fn):
        if stacked:

            @pl.loop(0, S)
            def _(j):
                fn(j, lambda refs: refs[0].at[j])

        else:
            for j in range(S):
                fn(j, lambda refs: refs[j])

    def slot_rows(start, n):
        if start < PR:
            s, off = start // PD, start % PD
        else:
            s, off = (start - PR) // CR, PD + (start - PR) % CR
        return pl.ds(pl.multiple_of(lax.rem(s - me + S, S) * N + off, 128), n)

    def pieces(start, n):
        step = min(n, PD if start < PR else CR)
        return [(i, step) for i in range(0, n, step)]

    @pl.when(g == 0)
    def _():
        def load(j, of):
            x = of(xs)

            @pl.loop(0, N // 128)
            def _(i):
                xh, _ = normed(x[tile(i, 128), :])
                h1[pl.ds(pl.multiple_of(j * N + i * 128, 128), 128), :] = (xh * gb[0:1, :] + gb[1:2, :]).astype(BF)

        every_slot(load)

    def rot(y, r, scale):
        c = cr[r, :]
        s1 = s1r[r, :]
        s2 = s2r[r, :]
        out = []
        for p in range(W // 128):
            z = y[:, p * 128 : (p + 1) * 128]
            z = (z * c + roll8(z, True) * s1 + roll8(z, False) * s2).astype(BF)
            out.append(z * jnp.asarray(scale, BF) if scale != 1.0 else z)
        return jnp.concatenate(out, axis=1) if len(out) > 1 else out[0]

    def proj(j, of):
        s = lax.rem(me + j, S)
        rp = pl.ds(pl.multiple_of(s * PD, 128), PD)
        rc = pl.ds(pl.multiple_of(PR + s * CR, 128), CR)
        hh = h1[pl.ds(pl.multiple_of(j * N, 128), N), :]
        y = dnn(hh, wq[...]) + bq[...]
        q_s[rp, :] = rot(y[:PD], rp, HD**-0.5)
        q_s[rc, :] = rot(y[PD:], rc, HD**-0.5)
        y = dnn(hh, wk[...]) + bk[...]
        k_s[rp, :] = rot(y[:PD], rp, 1.0)
        k_s[rc, :] = rot(y[PD:], rc, 1.0)
        y = (dnn(hh, wv[...]) + bv[...]).astype(BF)
        v_s[rp, :] = y[:PD]
        v_s[rc, :] = y[PD:]
        y = dnt(of(dys)[...], wo[...]).astype(BF)
        dc_s[rp, :] = y[:PD]
        dc_s[rc, :] = y[PD:]
        if adding:
            nb = of(yps).shape[0]
            r = pl.ds(pl.multiple_of(g * nb, 16), nb)
            of(ys)[r, :] = of(yps)[...]
            of(gs)[r, :] = of(g2s)[...]

    every_slot(proj)
    lane = lax.broadcasted_iota(jnp.int32, (1, 128), 1)
    row_i = lax.broadcasted_iota(jnp.int32, (QB, QB), 0)
    col_i = lax.broadcasted_iota(jnp.int32, (QB, QB), 1)
    causal = row_i <= col_i
    cmask = causal & ((row_i // CL) == (col_i // CL))
    blocks = []
    for i in range(PR // QB):
        blocks.append((i * QB, [(0, i * QB, None)] * (i > 0) + [(i * QB, QB, causal)]))
    for c in range((T - PR) // QB):
        blocks.append((PR + c * QB, [(0, PR, None), (PR + c * QB, QB, cmask)]))

    @pl.loop(0, W // 128)
    def _(p):
        lanes = tile(p, 128)
        kT[...] = k_s[:, lanes].T
        vT[...] = v_s[:, lanes].T
        dk_s[...] = jnp.zeros_like(dk_s)
        dv_s[...] = jnp.zeros_like(dv_s)
        def begin(q0, parts):
            qb = q_s[pl.ds(q0, QB), lanes]
            dcb = dc_s[pl.ds(q0, QB), lanes]
            out = []
            for h in range(2):
                sel = (lane >= HD * h) & (lane < HD * h + HD)
                qm = jnp.where(sel, qb, jnp.zeros_like(qb))
                dm = jnp.where(sel, dcb, jnp.zeros_like(dcb))
                ss = []
                for k0, n, mask in parts:
                    s = dnt(k_s[k0 : k0 + n, lanes], qm)
                    ss.append(s if mask is None else jnp.where(mask, s, -1e30))
                out.append((qm, dm, ss, [dnt(v_s[k0 : k0 + n, lanes], dm) for k0, n, _ in parts]))
            return out

        ahead = begin(*blocks[0])
        for b, (q0, parts) in enumerate(blocks):
            now = ahead
            if b + 1 < len(blocks):
                ahead = begin(*blocks[b + 1])
            rq = pl.ds(q0, QB)
            P_, DS, cT, dqT = [], [], [], []
            qh = [t[0] for t in now]
            dch = [t[1] for t in now]
            for h in range(2):
                _, _, ss, dps = now[h]
                m = functools.reduce(jnp.maximum, [jnp.max(s, axis=0, keepdims=True) for s in ss])
                es = [jnp.exp(s - m) for s in ss]
                rl = 1.0 / sum(jnp.sum(e, axis=0, keepdims=True) for e in es)
                ps = [e * rl for e in es]
                delta = sum(jnp.sum(a * b, axis=0, keepdims=True) for a, b in zip(ps, dps))
                P_.append([a.astype(BF) for a in ps])
                DS.append([(a * (b - delta)).astype(BF) for a, b in zip(ps, dps)])
                hr = slice(HD * h, HD * h + HD)
                cT.append(sum(dnn(vT[hr, k0 : k0 + n], a) for (k0, n, _), a in zip(parts, P_[h])))
                dqT.append(sum(dnn(kT[hr, k0 : k0 + n], a) for (k0, n, _), a in zip(parts, DS[h])))
            q2 = jnp.concatenate(qh, axis=0)
            dc2 = jnp.concatenate(dch, axis=0)
            for i, (k0, n, _) in enumerate(parts):
                dv_s[k0 : k0 + n, :] += dnn(jnp.concatenate([P_[0][i], P_[1][i]], axis=1), dc2)
                dk_s[k0 : k0 + n, :] += dnn(jnp.concatenate([DS[0][i], DS[1][i]], axis=1), q2)
            co = jnp.concatenate(cT, axis=0).T.astype(BF)
            z = jnp.concatenate(dqT, axis=0).T * (HD**-0.5)
            z = (z * cr[rq, :] - roll8(z, True) * s1r[rq, :] - roll8(z, False) * s2r[rq, :]).astype(BF)
            for o, n in pieces(q0, QB):
                ctx[slot_rows(q0 + o, n), lanes] = co[o : o + n]
                dl[0, slot_rows(q0 + o, n), lanes] = z[o : o + n]

        @pl.loop(0, S)
        def _(s):
            to = lax.rem(s - me + S, S) * N
            for src, off, n in ((s * PD, 0, PD), (PR + s * CR, PD, CR)):
                r = pl.ds(pl.multiple_of(src, 128), n)
                w = pl.ds(pl.multiple_of(to + off, 128), n)
                z = dk_s[r, :]
                z = z * cr[r, :] - roll8(z, True) * s1r[r, :] - roll8(z, False) * s2r[r, :]
                dl[1, w, lanes] = z.astype(BF)
                dl[2, w, lanes] = dv_s[r, :].astype(BF)

    for c in range(3):
        db[c : c + 1, :] = jnp.sum(dl[c].astype(F32), axis=0, keepdims=True)

    @pl.loop(0, S)
    def _(j):
        r = pl.ds(pl.multiple_of(j * N, 128), N)
        y = dnn(ctx[r, :], wo[...])
        d = dnt(dl[0, r, :], wq[...]) + dnt(dl[1, r, :], wk[...]) + dnt(dl[2, r, :], wv[...])

        @pl.when(g == 0)
        def _():
            yacc[r, :] = y
            dacc[r, :] = d

        @pl.when(g > 0)
        def _():
            yacc[r, :] += y
            dacc[r, :] += d

    @pl.when(g == last)
    def _():
        ln[...] = jnp.zeros_like(ln)

        def store(j, of):
            x, yo, go = of(xs), of(ys), of(gs)

            @pl.loop(0, N // 128)
            def _(i):
                r = tile(i, 128)
                w = pl.ds(pl.multiple_of(j * N + i * 128, 128), 128)
                xh, _ = normed(x[r, :])
                d = dacc[w, :]
                y = yacc[w, :]
                gg = d * gb[0:1, :]
                if adding:
                    y = y + yo[r, :].astype(F32)
                    gg = gg + go[r, :].astype(F32)
                yo[r, :] = y.astype(BF)
                go[r, :] = gg.astype(BF)
                ln[0:1, :] += jnp.sum(d * xh, axis=0, keepdims=True)
                ln[1:2, :] += jnp.sum(d, axis=0, keepdims=True)

        every_slot(store)


def attn_group(S, PD, CL, me, xs, dys, yps, g2s, wqkv, bqkv, wo, gb, tabs):
    N, D = xs[0].shape
    CW = wo.shape[0]
    T = N * S
    HG = 4 if CW % 256 == 0 else 2
    QB = 256
    W = HG * HD
    G = CW // W
    full = lambda s: pl.BlockSpec(s, lambda g, m: (0,) * len(s), pipeline_mode=pl.Buffered(1))
    keep = lambda s: pl.BlockSpec(s, lambda g, m: (0,) * len(s))
    tok, tok_out, per = full((N, D)), keep((N, D)), S
    adding = int(T * D <= 1536 * 1024)
    others = (yps, g2s)
    if not adding:
        yps, g2s = [], []
    out_tok = SD((N, D), BF)
    if S > 2:
        xs, dys, yps, g2s = [[jnp.stack(v, axis=0)] if v else v for v in (xs, dys, yps, g2s)]
        tok, tok_out, per = full((S, N, D)), keep((S, N, D)), 1
        out_tok = SD((S, N, D), BF)
        part = pl.BlockSpec((S, N // G, D), lambda g, m: (0, g, 0))
    else:
        part = pl.BlockSpec((N // G, D), lambda g, m: (g, 0))
    wspec = lambda c: pl.BlockSpec((D, W), lambda g, m: (0, c * G + g))
    bspec = lambda c: pl.BlockSpec((1, W), lambda g, m: (0, c * G + g))
    outs = pl.pallas_call(
        functools.partial(attn_kernel, S, PD, CL, QB, HG, adding),
        grid_spec=pltpu.PrefetchScalarGridSpec(
            num_scalar_prefetch=1,
            grid=(G,),
            in_specs=[tok] * (2 * per)
            + [part] * (2 * adding * per)
            + [wspec(0), wspec(1), wspec(2), bspec(0), bspec(1), bspec(2)]
            + [pl.BlockSpec((W, D), lambda g, m: (g, 0)), full((2, D))]
            + [full((T, 128))] * 3,
            out_specs=[tok_out] * (2 * per)
            + [
                pl.BlockSpec((3, T, W), lambda g, m: (0, 0, g)),
                pl.BlockSpec((T, W), lambda g, m: (0, g)),
                keep((T, D)),
                keep((2, D)),
                pl.BlockSpec((3, W), lambda g, m: (0, g)),
            ],
            scratch_shapes=[pltpu.VMEM((T, D), F32)] * 2
            + [pltpu.VMEM((T, W), BF)] * 4
            + [pltpu.VMEM((128, T), BF)] * 2
            + [pltpu.VMEM((T, 128), F32)] * 2,
        ),
        out_shape=[out_tok] * (2 * per)
        + [SD((3, T, CW), BF), SD((T, CW), BF), SD((T, D), BF), SD((2, D), F32), SD((3, CW), F32)],
        compiler_params=pltpu.CompilerParams(vmem_limit_bytes=62 * MIB),
        cost_estimate=pl.CostEstimate(
            flops=16 * T * D * CW + 40 * T * T * CW,
            bytes_accessed=12 * T * D + 12 * T * CW + 8 * D * CW,
            transcendentals=T * T * CW // HD,
        ),
    )(me, *xs, *dys, *yps, *g2s, wqkv, wqkv, wqkv, bqkv, bqkv, bqkv, wo, gb, *tabs)
    ys, gs = outs[:per], outs[per : 2 * per]
    if S > 2:
        ys, gs = [[v[0][j] for j in range(S)] for v in (ys, gs)]
    if not adding:
        ys, gs = [[a + b for a, b in zip(p, q)] for p, q in zip((ys, gs), others)]
    return ys, gs, outs[2 * per :]


def tn_kernel(n, wide, *refs):
    a = refs[:n]
    b = refs[n : 2 * n]
    o = refs[2 * n]
    if wide == 0:
        o[...] = sum(dtn(x[...], y[...]) for x, y in zip(a, b)).astype(BF)
    else:
        w = b[0].shape[2]
        for c in range(wide):
            o[:, c * w : (c + 1) * w] = sum(dtn(x[...], y[c]) for x, y in zip(a, b)).astype(BF)


def tn_sum(a, b, block):
    n = len(a)
    rows, da = a[0].shape
    block = min(block, da)
    wide = b[0].shape[0] if b[0].ndim == 3 else 0
    db = b[0].shape[-1] * max(wide, 1)
    keep = lambda s: pl.BlockSpec(s, lambda i: (0,) * len(s), pipeline_mode=pl.Buffered(1))
    return pl.pallas_call(
        functools.partial(tn_kernel, n, wide),
        grid=(da // block,),
        in_specs=[pl.BlockSpec((rows, block), lambda i: (0, i))] * n + [keep(b[0].shape)] * n,
        out_specs=pl.BlockSpec((block, db), lambda i: (i, 0)),
        out_shape=SD((da, db), BF),
        compiler_params=pltpu.CompilerParams(vmem_limit_bytes=60 * MIB),
        cost_estimate=pl.CostEstimate(flops=2 * n * rows * da * db, bytes_accessed=2 * (n * rows * (da + db) + da * db), transcendentals=0),
    )(*a, *b)


def joined(refs):
    return jnp.concatenate([r[...] for r in refs], axis=0)


def down_kernel(n, more, *refs):
    o = refs[-1]
    t = dtn(joined(refs[:n]), joined(refs[n : 2 * n])).reshape(o.shape)
    o[...] = (t + refs[2 * n][...].astype(F32) if more else t).astype(BF)


def up_kernel(n, more, *refs):
    o = refs[-1]
    c, rows, w = o.shape
    t = dtn(joined(refs[:n]), joined(refs[n : 2 * n]))
    k = t.shape[1] // w
    for i in range(k):
        r = slice(i * (rows // k), (i + 1) * (rows // k))
        p = t[:, i * w : (i + 1) * w].reshape(c, rows // k, w)
        o[:, r, :] = (p + refs[2 * n][:, r, :].astype(F32) if more else p).astype(BF)


def mlp_grads(S, R, acts, dys, hs, dpres, g=None):
    n = len(acts)
    rows, FL = acts[0].shape
    D = dys[0].shape[1]
    DR = D // S
    blk = 256
    rd = FL // R
    ru = DR // R
    k = FL // D
    per = rd + S * ru * k
    keep = lambda s: pl.BlockSpec(s, lambda i: (0,) * len(s), pipeline_mode=pl.Buffered(1))
    steps = DR // blk
    more = g is not None
    hbm = pl.BlockSpec(memory_space=pl.ANY)

    def call(kernel, a, b, spec, g):
        width = b[0].shape[1]
        prior = [] if g is None else [g]
        return pl.pallas_call(
            functools.partial(kernel, n, more),
            grid=(a[0].shape[1] // blk,),
            in_specs=[pl.BlockSpec((rows, blk), lambda i: (0, i))] * n
            + [keep((rows, width))] * n
            + ([spec if more else hbm] if prior else []),
            out_specs=spec,
            out_shape=SD((R, per, D), BF),
            input_output_aliases={2 * n: 0} if prior else {},
            compiler_params=pltpu.CompilerParams(vmem_limit_bytes=60 * MIB),
            cost_estimate=pl.CostEstimate(
                flops=2 * n * rows * D * FL, bytes_accessed=2 * (n * rows * (D + FL) + (1 + more) * D * FL), transcendentals=0
            ),
        )(*a, *b, *prior)

    g = call(down_kernel, acts, dys, pl.BlockSpec((blk // rd, rd, D), lambda i: (i, 0, 0)), g)
    spec = pl.BlockSpec((blk // ru, ru * k, D), lambda i: (i % steps, rd // (ru * k) + i // steps, 0))
    return call(up_kernel, hs, dpres, spec, g)


def mlp_finish_kernel(S, rd, ru, g, down, up):
    n, per, D = g.shape
    k = (per - rd) // (S * ru)
    for c in range(n):
        down[c * rd : (c + 1) * rd, :] = g[c, :rd, :].astype(F32)
        for t in range(S * k):
            a = rd + t * ru
            up[c * ru : (c + 1) * ru, t * D : (t + 1) * D] = g[c, a : a + ru, :].astype(F32)


def mlp_finish(S, g, FL):
    R, per, D = g.shape
    rd = FL // R
    ru = D // S // R
    n = 4
    return pl.pallas_call(
        functools.partial(mlp_finish_kernel, S, rd, ru),
        grid=(R // n,),
        in_specs=[pl.BlockSpec((n, per, D), lambda c: (c, 0, 0))],
        out_specs=[pl.BlockSpec((n * rd, D), lambda c: (c, 0)), pl.BlockSpec((n * ru, S * FL), lambda c: (c, 0))],
        out_shape=[SD((FL, D), F32), SD((D // S, S * FL), F32)],
        compiler_params=pltpu.CompilerParams(vmem_limit_bytes=40 * MIB),
        cost_estimate=pl.CostEstimate(flops=0, bytes_accessed=6 * R * per * D, transcendentals=0),
    )(g)


def attn_grads_kernel(n, S, R, q_ref, *refs):
    h = refs[:n]
    dl = refs[n : 2 * n]
    ctx = refs[2 * n : 3 * n]
    dy = refs[3 * n : -2]
    first, second = refs[-2:]
    i = pl.program_id(0)
    q1 = q_ref[0]
    q2 = q_ref[1]
    blk = h[0].shape[1]
    D = dy[0].shape[1]
    DR = D // S
    CW = dl[0].shape[2]
    ru = DR // R
    k = D // CW
    steps = DR // blk
    s = i // steps
    base = (i % steps) * (blk // ru)
    for p in range(3):
        t = dtn(joined(h), jnp.concatenate([y[p] for y in dl], axis=0)).astype(BF)
        for c in range(blk // ru):
            v = t[c * ru : (c + 1) * ru, :]
            if p < 2:
                first[(base + c) ^ q1, pl.ds(s * 2 * ru + p * ru, ru), :] = v
            else:
                second[(base + c) ^ q2, pl.ds(k * ru + s * ru, ru), :] = v
    t = dtn(joined(ctx), joined(dy)).astype(BF)
    m = ctx[0].shape[1] // ru
    for c in range(m):
        for j in range(k):
            second[(i * m + c) ^ q2, j * ru : (j + 1) * ru, :] = t[c * ru : (c + 1) * ru, j * CW : (j + 1) * CW]


def attn_grads(S, R, q, hs, dls, ctxs, dys):
    n = len(hs)
    T, D = hs[0].shape
    CW = ctxs[0].shape[1]
    DR = D // S
    ru = DR // R
    blk = 256
    G = D // blk
    keep = lambda s: pl.BlockSpec(s, lambda i, q: (0,) * len(s), pipeline_mode=pl.Buffered(1))
    shapes = [(R, S * 2 * ru, CW), (R, (D // CW + S) * ru, CW)]
    return pl.pallas_call(
        functools.partial(attn_grads_kernel, n, S, R),
        grid_spec=pltpu.PrefetchScalarGridSpec(
            num_scalar_prefetch=1,
            grid=(G,),
            in_specs=[pl.BlockSpec((T, blk), lambda i, q: (0, i))] * n
            + [keep((3, T, CW))] * n
            + [pl.BlockSpec((T, CW // G), lambda i, q: (0, i))] * n
            + [keep(dys[0].shape)] * len(dys),
            out_specs=[pl.BlockSpec(s, lambda i, q: (0, 0, 0)) for s in shapes],
        ),
        out_shape=[SD(s, BF) for s in shapes],
        compiler_params=pltpu.CompilerParams(vmem_limit_bytes=60 * MIB),
        cost_estimate=pl.CostEstimate(flops=8 * n * T * D * CW, bytes_accessed=2 * n * T * (2 * D + 4 * CW) + 8 * D * CW, transcendentals=0),
    )(q, *hs, *dls, *ctxs, *dys)


def attn_finish_kernel(S, ru, k, n, q_ref, *refs):
    firsts, seconds = refs[:n], refs[n : 2 * n]
    out, qkv = refs[2 * n :]
    CW = seconds[0].shape[2]
    D = out.shape[1]
    for c in range(n):
        r = slice(c * ru, (c + 1) * ru)
        for j in range(k):
            out[r, j * CW : (j + 1) * CW] = seconds[c][0, j * ru : (j + 1) * ru, :].astype(F32)
        for t in range(S):
            for p in range(3):
                a = (t * 2 + p) * ru if p < 2 else (k + t) * ru
                v = (firsts if p < 2 else seconds)[c][0, a : a + ru, :]
                qkv[r, p * D + t * CW : p * D + (t + 1) * CW] = v.astype(F32)


def attn_finish(S, q, g1, g2):
    R, per1, CW = g1.shape
    per2 = g2.shape[1]
    D = CW * S
    ru = D // S // R
    n = 4
    block = lambda per, k, c: pl.BlockSpec((1, per, CW), lambda i, q: ((i * n + c) ^ q[k], 0, 0))
    return pl.pallas_call(
        functools.partial(attn_finish_kernel, S, ru, S, n),
        grid_spec=pltpu.PrefetchScalarGridSpec(
            num_scalar_prefetch=1,
            grid=(R // n,),
            in_specs=[block(per1, 0, c) for c in range(n)] + [block(per2, 1, c) for c in range(n)],
            out_specs=[pl.BlockSpec((n * ru, D), lambda c, q: (c, 0)), pl.BlockSpec((n * ru, 3 * D), lambda c, q: (c, 0))],
        ),
        out_shape=[SD((CW, D), F32), SD((D // S, 3 * D), F32)],
        compiler_params=pltpu.CompilerParams(vmem_limit_bytes=40 * MIB),
        cost_estimate=pl.CostEstimate(flops=0, bytes_accessed=6 * R * (per1 + per2) * CW, transcendentals=0),
    )(q, *[g1] * n, *[g2] * n)


def final_kernel(S, first, PT, *refs):
    it = iter(refs)
    take = lambda n: [next(it) for _ in range(n)]
    x, dy = take(2)
    ys = take(S)
    gs = take(S)
    (vb,) = take(1)
    if not first:
        take(4)
    po, co, pg, cg = take(4)
    i = pl.program_id(0)
    xv = x[...].astype(F32)
    xh, inv = normed(xv)
    y = xv + vb[0:1, :] + sum(r[...].astype(F32) for r in ys) + vb[1:2, :]
    gsum = sum(r[...].astype(F32) for r in gs)
    dx = (gsum - jnp.mean(gsum, axis=-1, keepdims=True) - xh * jnp.mean(gsum * xh, axis=-1, keepdims=True)) * inv
    out = y.astype(BF)
    grad = dy[...].astype(F32) + dx

    @pl.when(i < PT)
    def _():
        po[0] = out
        pg[0] = grad

    @pl.when(i >= PT)
    def _():
        co[0] = out
        cg[0] = grad


def final_rows(m, MB, PD, x, dy, ys, gs, vb, prior):
    S = len(ys)
    N, D = x.shape
    CR = N - PD
    RT = 128
    PT = PD // RT
    first = prior is None
    row = pl.BlockSpec((RT, D), lambda i: (i, 0))
    pspec = pl.BlockSpec((1, RT, D), lambda i: (m, jnp.minimum(i, PT - 1), 0))
    cspec = pl.BlockSpec((1, RT, D), lambda i: (m, jnp.maximum(i - PT, 0), 0))
    hbm = pl.BlockSpec(memory_space=pl.ANY)
    n_in = 2 * S + 3
    return pl.pallas_call(
        functools.partial(final_kernel, S, first, PT),
        grid=(N // RT,),
        in_specs=[row] * (2 * S + 2) + [pl.BlockSpec((2, D), lambda i: (0, 0))] + ([] if first else [hbm] * 4),
        out_specs=[pspec, cspec, pspec, cspec],
        out_shape=[SD((MB, PD, D), BF), SD((MB, CR, D), BF), SD((MB, PD, D), F32), SD((MB, CR, D), F32)],
        input_output_aliases={} if first else {n_in + k: k for k in range(4)},
        compiler_params=pltpu.CompilerParams(vmem_limit_bytes=32 * MIB),
        cost_estimate=pl.CostEstimate(flops=20 * N * D, bytes_accessed=(4 * S + 10) * N * D, transcendentals=0),
    )(x, dy, *ys, *gs, vb, *(() if first else prior))


def shifted(value, S, j):
    return lax.ppermute(value, "shard", [(i, (i + j) % S) for i in range(S)])


def canonical(slots, me, S, back):
    if S == 1:
        return slots
    if S == 2:
        a, b = slots
        return [jnp.where(me == 0, a, b), jnp.where(me == 0, b, a)]
    stacked = jnp.stack(slots, axis=0)
    return [
        lax.dynamic_index_in_dim(stacked, lax.rem((me - s if back else s - me) + S, S), 0, keepdims=False) for s in range(S)
    ]


def exchanged(value, R, bit):
    return lax.ppermute(value, "rep", [(i, i ^ bit) for i in range(R)])


def columns_for(weight, me, S, j, parts, row=0, rows=None):
    cols = weight.shape[1] // parts
    rows = weight.shape[0] if rows is None else rows
    w = cols // S
    at = lax.rem(me + j, S) * w
    got = [lax.dynamic_slice(weight, (row, p * cols + at), (rows, w)) for p in range(parts)]
    return got[0] if parts == 1 else jnp.concatenate(got, axis=1)


def my_columns_halves(weight, me, S, R):
    rows = weight.shape[0]
    rep = lax.axis_index("rep")
    core = rep % 2
    y = (rep // 2) % 2
    n = rows // 4
    cut = [columns_for(weight, me, S, j, 1, (2 * core + y) * n, n) for j in range(1, S)]
    slots = [columns_for(weight, me, S, 0, 1)]

    def both(piece, other, first):
        return jnp.concatenate([jnp.where(first, piece, other), jnp.where(first, other, piece)], axis=0)

    for j in range(1, S):
        piece = shifted(cut[j - 1], S, j)
        pair = both(piece, exchanged(piece, R, 2), y == 0)
        slots.append(both(pair, exchanged(pair, R, 1), core == 0))
    return jnp.concatenate(canonical(slots, me, S, True), axis=0), piece, cut[0]


def my_columns(weight, me, S, R, parts):
    rows = weight.shape[0]
    own = columns_for(weight, me, S, 0, parts)
    if S == 1:
        return own
    rep = lax.axis_index("rep")
    chunk = rows // R
    got = []
    for j in range(1, S):
        got.append(shifted(columns_for(weight, me, S, j, parts, rep * chunk, chunk), S, j))
    others = lax.all_gather(jnp.stack(got, axis=0), "rep", axis=1, tiled=True)
    return jnp.concatenate(canonical([own] + [others[j] for j in range(S - 1)], me, S, True), axis=0)


def add_low(a, b):
    return (a.astype(F32) + b.astype(F32)).astype(BF)


def orders(R):
    bits = [1 << i for i in range(R.bit_length() - 1)]
    return bits, bits[:1] + bits[2:] + bits[1:2]


def place(rep, order):
    q = jnp.zeros((), jnp.int32)
    for bit in order:
        q = 2 * q + (rep & bit) // bit
    return q


def beside_it(got, key, beside):
    if key in beside:
        got, beside[key] = lax.optimization_barrier((got, beside[key]))
    return got


def halving(pair, v, R, beside):
    pair = list(pair)
    for i, bits in enumerate(zip(*orders(R))):
        h = pair[0].shape[0] // 2
        got = [exchanged(g[h:], R, bit) for g, bit in zip(pair, bits)]
        v = v + exchanged(v, R, bits[0])
        got, v = lax.optimization_barrier((got, v))
        got = beside_it(got, i, beside)
        pair = [add_low(g[:h], t) for g, t in zip(pair, got)]
    return [g[0] for g in pair], v


def doubling(parts, R, beside):
    pair = [p[None] for p in parts]
    for i, bits in reversed(list(enumerate(zip(*orders(R))))):
        got = [exchanged(g, R, bit) for g, bit in zip(pair, bits)]
        got = beside_it(got, i, beside)
        pair = [jnp.concatenate([g, t], axis=0) for g, t in zip(pair, got)]
    return pair


def sum_all(v, S, R):
    bit = 1
    while bit < R:
        v = v + exchanged(v, R, bit)
        bit *= 2
    return v


def swap_shards(part, me, S, head):
    n = (part.shape[0] - head) // S
    slots = []
    for j in range(S):
        b = lax.dynamic_slice_in_dim(part, head + lax.rem(me + j, S) * n, n, 0)
        slots.append(shifted(b, S, j) if j else b)
    return jnp.concatenate(([part[:head]] if head else []) + canonical(slots, me, S, True), axis=0)


def reduce_rows(grad):
    part = lax.psum_scatter(grad, "rep", scatter_dimension=0, tiled=True)
    return lax.all_gather(part, "rep", axis=0, tiled=True).astype(F32)


def reduce_columns(grad, me, S, parts):
    rows, cols = grad.shape
    part = lax.psum_scatter(grad.reshape(S, rows // S, cols), "rep", scatter_dimension=1, tiled=True)
    slots = [lax.dynamic_index_in_dim(part, me, 0, keepdims=False)]
    for j in range(1, S):
        slots.append(shifted(lax.dynamic_index_in_dim(part, lax.rem(me + j, S), 0, keepdims=False), S, j))
    slots = [s.reshape(s.shape[0], parts, cols // parts) for s in slots]
    whole = jnp.stack(canonical(slots, me, S, True), axis=2).reshape(-1, S * cols)
    return lax.all_gather(whole, "rep", axis=0, tiled=True).astype(F32)


def rotary_tables(PR, CR, CL):
    pos = np.concatenate([np.arange(PR), PR + np.arange(CR) % CL]).astype(np.float32)
    half = ROT // 2
    freq = np.exp(np.arange(half, dtype=np.float32) * np.float32(-2.0 * math.log(10000.0) / ROT)).astype(np.float32)
    ang = (pos[:, None] * freq[None, :]).astype(np.float32)
    c = np.cos(ang)
    s = np.sin(ang)
    n = pos.shape[0]
    one = np.ones((n, HD - ROT), np.float32)
    zero = np.zeros((n, HD - ROT), np.float32)
    z8 = np.zeros((n, half), np.float32)
    tabs = ([c, c, one], [-s, z8, zero], [z8, s, zero])
    return [jnp.asarray(np.tile(np.concatenate(t, axis=1), (1, 128 // HD)), F32) for t in tabs]


def per_device(
    prompt_in,
    cont_in,
    prompt_cot,
    cont_cot,
    ln1_gain,
    ln1_bias,
    ln2_gain,
    ln2_bias,
    qkv_weight,
    qkv_bias,
    out_weight,
    out_bias,
    up_weight,
    up_bias,
    down_weight,
    down_bias,
):
    S = lax.axis_size("shard")
    R = lax.axis_size("rep")
    me = lax.axis_index("shard")
    MB, _, PD, D = prompt_in.shape
    CD, CL = cont_in.shape[2:4]
    CR = CD * CL
    N = PD + CR
    CW = D // S
    FL = up_weight.shape[1] // S
    me_arr = jnp.reshape(me, (1,)).astype(jnp.int32)

    one = lambda v: v.astype(F32).reshape(-1, CW)
    small = jnp.concatenate([one(v) for v in (ln1_gain, ln1_bias, ln2_gain, ln2_bias, out_bias, down_bias, qkv_bias)], axis=0)
    w_up, brought, cut = my_columns_halves(up_weight, me, S, R)
    (small, qkv_weight), cut = lax.optimization_barrier(((small, qkv_weight), cut))
    slots = [small] + [shifted(small, S, j) for j in range(1, S)]
    whole = jnp.stack(canonical(slots, me, S, True), axis=0)
    vec = whole[:, :6].transpose(1, 0, 2).reshape(6, D)
    gb1 = vec[0:2]
    gb2 = vec[2:4]
    vb = vec[4:6]
    bqkv = whole[:, 6:].reshape(3, S, CW)
    bqkv = lax.dynamic_index_in_dim(bqkv, me, 1, keepdims=False).reshape(1, 3 * CW)
    bup = up_bias.astype(F32).reshape(1, FL)

    w_qkv = my_columns(qkv_weight, me, S, R, 3)

    X = [[jnp.concatenate([prompt_in[m, 0], cont_in[m, 0].reshape(CR, D)], axis=0)] for m in range(MB)]
    DY = [[jnp.concatenate([prompt_cot[m, 0], cont_cot[m, 0].reshape(CR, D)], axis=0)] for m in range(MB)]
    tabs = rotary_tables(PD * S, CR * S, CL)
    src = [(X[m][0], DY[m][0]) for m in range(MB)]
    src[1:], brought = lax.optimization_barrier((src[1:], brought))
    for m in range(MB):
        for j in range(1, S):
            X[m].append(shifted(src[m][0], S, S - j))
            DY[m].append(shifted(src[m][1], S, S - j))

    ff = [[None] * S for _ in range(MB)]

    def mlp(m, j):
        ff[m][j] = mlp_rows(X[m][j], DY[m][j], w_up, bup, down_weight, gb2)

    for m in range(MB):
        mlp(m, 0)
    rest = []
    y_got, g_got = [], []

    def attend(m):
        ys, gs, more = attn_group(
            S, PD, CL, me_arr, X[m], DY[m], [f[3] for f in ff[m]], [f[4] for f in ff[m]], w_qkv, bqkv, out_weight, gb1, tabs
        )
        rest.append(list(more))
        y_got.append([ys[0]] + [shifted(ys[j], S, j) for j in range(1, S)])
        g_got.append([gs[0]] + [shifted(gs[j], S, j) for j in range(1, S)])

    chunked = (D // S // R) % 16 == 0 and R & (R - 1) == 0
    rep = lax.axis_index("rep")
    late = [(MB - 1, j) for j in range(1, S)]
    early = [(m, j) for m in range(MB) for j in range(S) if (m, j) not in late]
    of = lambda set_, k: [ff[m][j][k] for m, j in set_]
    for m, j in early:
        if j:
            mlp(m, j)
    if chunked:
        gmlp = mlp_grads(S, R, of(early, 0), [DY[m][j] for m, j in early], of(early, 2), of(early, 1))
        w_up, gmlp = lax.optimization_barrier((w_up, gmlp))
    for m, j in late:
        mlp(m, j)
    if chunked:
        if late:
            gmlp = mlp_grads(S, R, of(late, 0), [DY[m][j] for m, j in late], of(late, 2), of(late, 1), gmlp)
        part = lax.psum_scatter(gmlp, "rep", scatter_dimension=0, tiled=True)[0]
        w_qkv, gmlp = lax.optimization_barrier((w_qkv, gmlp))
    for m in range(MB):
        attend(m)
        if m + 1 < MB:
            w_qkv, rest[m][3] = lax.optimization_barrier((w_qkv, rest[m][3]))
    every = early + late
    ln1 = sum(r[3] for r in rest).reshape(-1, CW)
    ln2 = sum(of(every, 5)).reshape(-1, CW)
    db_out = sum(jnp.sum(DY[m][0].astype(F32), axis=0) for m in range(MB)).reshape(-1, CW)
    mine = (jnp.arange(S) == me).astype(F32)
    db_qkv = (sum(r[4] for r in rest)[:, None, :] * mine[None, :, None]).reshape(-1, CW)
    db_up = (sum(of(every, 6)) * mine[:, None]).reshape(-1, CW)
    vecs = jnp.concatenate([ln1, ln2, db_out, db_qkv, db_up], axis=0)

    finals = lambda m, prior: final_rows(m, MB, PD, X[m][0], DY[m][0], y_got[m], g_got[m], vb, prior)
    hs, dls, ctxs = [[r[k] for r in rest] for k in (2, 0, 1)]
    if chunked:
        q = jnp.stack([place(rep, order) for order in orders(R)]).astype(jnp.int32)
        hs, y_got[:-1], g_got[:-1] = lax.optimization_barrier((hs, y_got[:-1], g_got[:-1]))
        gatt = attn_grads(S, R, q, hs, dls, ctxs, [DY[m][j] for m in range(MB) for j in range(S)])
        outs = None
        for m in range(MB - 1):
            outs = finals(m, outs)
        part = swap_shards(part, me, S, FL // R)
        beside = {0: part, 1: outs, 2: (y_got[-1], g_got[-1])}
        half, vecs = halving(gatt, vecs, R, beside)
        part, outs, (y_got[-1], g_got[-1]) = beside[0], beside[1], beside[2]
        gmlp_all = lax.all_gather(part, "rep", axis=0, tiled=False)
        outs = finals(MB - 1, outs)
        k = D // CW * (D // S // R)
        beside = {2: outs, 1: mlp_finish(S, gmlp_all, FL)}
        g1, g2 = doubling([swap_shards(half[0], me, S, 0), swap_shards(half[1], me, S, k)], R, beside)
        outs = beside[2]
        g_down, g_up = beside[1]
        g_out, g_qkv = attn_finish(S, q, g1, g2)
    else:
        dls, ctxs, hs = [[r[k] for r in rest] for k in (0, 1, 2)]
        g_down = reduce_rows(tn_sum(of(every, 0), [DY[m][j] for m, j in every], 256))
        g_up = reduce_columns(tn_sum(of(every, 2), of(every, 1), 256), me, S, 1)
        dycs = [jnp.concatenate(DY[m], axis=0) for m in range(MB)]
        g_out = reduce_rows(tn_sum(ctxs, dycs, 256))
        g_qkv = reduce_columns(tn_sum(hs, dls, 256), me, S, 3)
        vecs = sum_all(vecs, S, R)
        outs = None
        for m in range(MB):
            outs = finals(m, outs)
    tot = vecs + sum(shifted(vecs, S, j) for j in range(1, S))
    own = lambda a, n: lax.dynamic_slice_in_dim(tot, a + me * n, n, 0).reshape(-1)
    v_ln1g, v_ln1b, v_ln2g, v_ln2b, v_out = [own(k * S, 1) for k in range(5)]
    v_qkv = own(5 * S, 3)
    v_up = own(8 * S, FL // CW)

    po, co, pg, cg = outs
    return (
        po.reshape(MB, 1, PD, D),
        co.reshape(MB, 1, CD, CL, D),
        pg.reshape(MB, 1, PD, D),
        cg.reshape(MB, 1, CD, CL, D),
        v_ln1g,
        v_ln1b,
        v_ln2g,
        v_ln2b,
        g_qkv,
        v_qkv,
        g_out,
        v_out,
        g_up,
        v_up,
        g_down,
        v_out,
    )


def solution(mesh):
    tokens = (
        P(None, "rep", "shard", None),
        P(None, "rep", "shard", None, None),
        P(None, "rep", "shard", None),
        P(None, "rep", "shard", None, None),
    )
    vec = P("shard")
    mat = P("shard", None)
    params = (vec, vec, vec, vec, mat, vec, mat, vec, mat, vec, mat, vec)
    return jax.shard_map(
        per_device, mesh=mesh, in_specs=tokens + params, out_specs=tokens + params, check_vma=False
    )
```

```python
import functools
import math

import jax
import jax.numpy as jnp
import numpy as np
from jax import lax
from jax.experimental import pallas as pl
from jax.experimental.pallas import tpu as pltpu
from jax.sharding import PartitionSpec as P

H = 16
HD = 64
ROT = 16
EPS = 1e-05
F32 = jnp.float32
BF = jnp.bfloat16
MIB = 1024 * 1024
SD = jax.ShapeDtypeStruct


def dnn(a, b):
    return lax.dot_general(a, b, (((1,), (0,)), ((), ())), preferred_element_type=F32)


def dnt(a, b):
    return lax.dot_general(a, b, (((1,), (1,)), ((), ())), preferred_element_type=F32)


def dtn(a, b):
    return lax.dot_general(a, b, (((0,), (0,)), ((), ())), preferred_element_type=F32)


def normed(rows):
    x = rows.astype(F32)
    c = x - jnp.mean(x, axis=-1, keepdims=True)
    inv = lax.rsqrt(jnp.mean(c * c, axis=-1, keepdims=True) + EPS)
    return c * inv, inv


def tile(i, n):
    return pl.ds(pl.multiple_of(i * n, n), n)


def rows_tile(n, most):
    t = most
    while n % t:
        t -= 8
    return t


def mlp_kernel(rt, x_ref, dy_ref, wu_ref, bu_ref, wd_ref, gb_ref, act_ref, dpre_ref, h_ref, bu_out, *back):
    f = pl.program_id(0)
    if back:
        yp_ref, g2_ref, ln_ref, yacc, dacc = back
    last = pl.num_programs(0) - 1
    rows = x_ref.shape[0]

    @pl.when(f == 0)
    def _():
        @pl.loop(0, rows // 128)
        def _(i):
            r = tile(i, 128)
            xh, _ = normed(x_ref[r, :])
            h_ref[r, :] = (xh * gb_ref[0:1, :] + gb_ref[1:2, :]).astype(BF)
            if back:
                yacc[r, :] = jnp.zeros((128, yacc.shape[1]), F32)
                dacc[r, :] = jnp.zeros((128, dacc.shape[1]), F32)

    def step(i, bsum):
        r = tile(i, rt)
        pre = dnn(h_ref[r, :], wu_ref[...]) + bu_ref[...]
        da = dnt(dy_ref[r, :], wd_ref[...])
        cdf = 0.5 * (1.0 + lax.erf(pre * 0.7071067811865476))
        act = (pre * cdf).astype(BF)
        dpre = (da * (cdf + pre * jnp.exp(-0.5 * pre * pre) * 0.3989422804014327)).astype(BF)
        act_ref[r, :] = act
        dpre_ref[r, :] = dpre
        if back:
            yacc[r, :] += dnn(act, wd_ref[...])
            dacc[r, :] += dnt(dpre, wu_ref[...])
        return bsum + jnp.sum(dpre.astype(F32), axis=0, keepdims=True)

    bu_out[...] = lax.fori_loop(0, rows // rt, step, jnp.zeros(bu_out.shape, F32))
    if not back:
        return

    @pl.when(f == last)
    def _():
        ln_ref[...] = jnp.zeros_like(ln_ref)

        @pl.loop(0, rows // 128)
        def _(i):
            r = tile(i, 128)
            xh, _ = normed(x_ref[r, :])
            dh = dacc[r, :]
            yp_ref[r, :] = yacc[r, :].astype(BF)
            g2_ref[r, :] = (dh * gb_ref[0:1, :]).astype(BF)
            ln_ref[0:1, :] += jnp.sum(dh * xh, axis=0, keepdims=True)
            ln_ref[1:2, :] += jnp.sum(dh, axis=0, keepdims=True)


def mlp_rows(x, dy, wu, bu, wd, gb, back):
    rows, width = x.shape
    hidden = wu.shape[1]
    fb = min(512, hidden)
    full = lambda s: pl.BlockSpec(s, lambda f: (0,) * len(s))
    return pl.pallas_call(
        functools.partial(mlp_kernel, rows_tile(rows, 640)),
        grid=(hidden // fb,),
        in_specs=[
            full((rows, width)),
            full((rows, width)),
            pl.BlockSpec((width, fb), lambda f: (0, f)),
            pl.BlockSpec((1, fb), lambda f: (0, f)),
            pl.BlockSpec((fb, width), lambda f: (f, 0)),
            full((2, width)),
        ],
        out_specs=[
            pl.BlockSpec((rows, fb), lambda f: (0, f)),
            pl.BlockSpec((rows, fb), lambda f: (0, f)),
            full((rows, width)),
            pl.BlockSpec((1, fb), lambda f: (0, f)),
        ]
        + [full((rows, width)), full((rows, width)), full((2, width))] * back,
        out_shape=[SD((rows, hidden), BF), SD((rows, hidden), BF), SD((rows, width), BF), SD((1, hidden), F32)]
        + [SD((rows, width), BF), SD((rows, width), BF), SD((2, width), F32)] * back,
        scratch_shapes=[pltpu.VMEM((rows, width), F32)] * (2 * back),
        compiler_params=pltpu.CompilerParams(vmem_limit_bytes=60 * MIB),
        cost_estimate=pl.CostEstimate(
            flops=4 * (1 + back) * rows * width * hidden,
            bytes_accessed=4 * (width * hidden + rows * hidden) + (6 + 4 * back) * rows * width,
            transcendentals=2 * rows * hidden,
        ),
    )(x, dy, wu, bu, wd, gb)


def roll8(x, left):
    w = x.shape[-1]
    return pltpu.roll(x, (w - 8) if left else 8, 1)


def attn_kernel(S, PD, CL, QB, HG, adding, me_ref, *refs):
    it = iter(refs)
    take = lambda n: [next(it) for _ in range(n)]
    stacked = S > 2
    per = 1 if stacked else S
    xs = take(per)
    dys = take(per)
    far = 1 if stacked else S - 1
    yps = take(far * adding)
    g2s = take(far * adding)
    wq, wk, wv = take(3)
    bq, bk, bv = take(3)
    wo, gb = take(2)
    cr, s1r, s2r = take(3)
    ys = take(far)
    gs = take(far)
    dl, ctx, h1, ln, db = take(5)
    yacc, dacc, q_s, k_s, v_s, dc_s, kT, vT, dk_s, dv_s = take(10)
    g = pl.program_id(0)
    last = pl.num_programs(0) - 1
    me = me_ref[0]
    N = xs[0].shape[-2]
    T = N * S
    PR = PD * S
    CR = N - PD
    W = HG * HD

    def every_slot(fn, start=0):
        if stacked:

            @pl.loop(start, S)
            def _(j):
                fn(j, lambda refs: refs[0].at[j], lambda refs: refs[0].at[j - 1])

        else:
            for j in range(start, S):
                fn(j, lambda refs: refs[j], lambda refs: refs[j - 1])

    def slot_rows(start, n):
        if start < PR:
            s, off = start // PD, start % PD
        else:
            s, off = (start - PR) // CR, PD + (start - PR) % CR
        return pl.ds(pl.multiple_of(lax.rem(s - me + S, S) * N + off, 128), n)

    def pieces(start, n):
        step = min(n, PD if start < PR else CR)
        return [(i, step) for i in range(0, n, step)]

    @pl.when(g == 0)
    def _():
        def load(j, of, away):
            x = of(xs)

            @pl.loop(0, N // 128)
            def _(i):
                xh, _ = normed(x[tile(i, 128), :])
                h1[pl.ds(pl.multiple_of(j * N + i * 128, 128), 128), :] = (xh * gb[0:1, :] + gb[1:2, :]).astype(BF)

        every_slot(load)

    def rot(y, r, scale):
        c = cr[r, :]
        s1 = s1r[r, :]
        s2 = s2r[r, :]
        out = []
        for p in range(W // 128):
            z = y[:, p * 128 : (p + 1) * 128]
            z = (z * c + roll8(z, True) * s1 + roll8(z, False) * s2).astype(BF)
            out.append(z * jnp.asarray(scale, BF) if scale != 1.0 else z)
        return jnp.concatenate(out, axis=1) if len(out) > 1 else out[0]

    def proj(j, of, away):
        s = lax.rem(me + j, S)
        rp = pl.ds(pl.multiple_of(s * PD, 128), PD)
        rc = pl.ds(pl.multiple_of(PR + s * CR, 128), CR)
        hh = h1[pl.ds(pl.multiple_of(j * N, 128), N), :]
        y = dnn(hh, wq[...]) + bq[...]
        q_s[rp, :] = rot(y[:PD], rp, HD**-0.5)
        q_s[rc, :] = rot(y[PD:], rc, HD**-0.5)
        y = dnn(hh, wk[...]) + bk[...]
        k_s[rp, :] = rot(y[:PD], rp, 1.0)
        k_s[rc, :] = rot(y[PD:], rc, 1.0)
        y = (dnn(hh, wv[...]) + bv[...]).astype(BF)
        v_s[rp, :] = y[:PD]
        v_s[rc, :] = y[PD:]
        y = dnt(of(dys)[...], wo[...]).astype(BF)
        dc_s[rp, :] = y[:PD]
        dc_s[rc, :] = y[PD:]

    def bring(j, of, away):
        nb = away(yps).shape[0]
        r = pl.ds(pl.multiple_of(g * nb, 16), nb)
        away(ys)[r, :] = away(yps)[...]
        away(gs)[r, :] = away(g2s)[...]

    every_slot(proj)
    if adding:
        every_slot(bring, 1)
    lane = lax.broadcasted_iota(jnp.int32, (1, 128), 1)
    row_i = lax.broadcasted_iota(jnp.int32, (QB, QB), 0)
    col_i = lax.broadcasted_iota(jnp.int32, (QB, QB), 1)
    causal = row_i <= col_i
    cmask = causal & ((row_i // CL) == (col_i // CL))
    blocks = []
    for i in range(PR // QB):
        blocks.append((i * QB, [(0, i * QB, None)] * (i > 0) + [(i * QB, QB, causal)]))
    for c in range((T - PR) // QB):
        blocks.append((PR + c * QB, [(0, PR, None), (PR + c * QB, QB, cmask)]))

    @pl.loop(0, W // 128)
    def _(p):
        lanes = tile(p, 128)
        kT[...] = k_s[:, lanes].T
        vT[...] = v_s[:, lanes].T
        dk_s[...] = jnp.zeros_like(dk_s)
        dv_s[...] = jnp.zeros_like(dv_s)
        def begin(q0, parts):
            qb = q_s[pl.ds(q0, QB), lanes]
            dcb = dc_s[pl.ds(q0, QB), lanes]
            out = []
            for h in range(2):
                sel = (lane >= HD * h) & (lane < HD * h + HD)
                qm = jnp.where(sel, qb, jnp.zeros_like(qb))
                dm = jnp.where(sel, dcb, jnp.zeros_like(dcb))
                ss = []
                for k0, n, mask in parts:
                    s = dnt(k_s[k0 : k0 + n, lanes], qm)
                    ss.append(s if mask is None else jnp.where(mask, s, -1e30))
                out.append((qm, dm, ss, [dnt(v_s[k0 : k0 + n, lanes], dm) for k0, n, _ in parts]))
            return out

        ahead = begin(*blocks[0])
        for b, (q0, parts) in enumerate(blocks):
            now = ahead
            if b + 1 < len(blocks):
                ahead = begin(*blocks[b + 1])
            rq = pl.ds(q0, QB)
            P_, DS, cT, dqT = [], [], [], []
            qh = [t[0] for t in now]
            dch = [t[1] for t in now]
            for h in range(2):
                _, _, ss, dps = now[h]
                m = functools.reduce(jnp.maximum, [jnp.max(s, axis=0, keepdims=True) for s in ss])
                es = [jnp.exp(s - m) for s in ss]
                rl = 1.0 / sum(jnp.sum(e, axis=0, keepdims=True) for e in es)
                ps = [e * rl for e in es]
                delta = sum(jnp.sum(a * b, axis=0, keepdims=True) for a, b in zip(ps, dps))
                P_.append([a.astype(BF) for a in ps])
                DS.append([(a * (b - delta)).astype(BF) for a, b in zip(ps, dps)])
                hr = slice(HD * h, HD * h + HD)
                cT.append(sum(dnn(vT[hr, k0 : k0 + n], a) for (k0, n, _), a in zip(parts, P_[h])))
                dqT.append(sum(dnn(kT[hr, k0 : k0 + n], a) for (k0, n, _), a in zip(parts, DS[h])))
            q2 = jnp.concatenate(qh, axis=0)
            dc2 = jnp.concatenate(dch, axis=0)
            for i, (k0, n, _) in enumerate(parts):
                dv_s[k0 : k0 + n, :] += dnn(jnp.concatenate([P_[0][i], P_[1][i]], axis=1), dc2)
                dk_s[k0 : k0 + n, :] += dnn(jnp.concatenate([DS[0][i], DS[1][i]], axis=1), q2)
            co = jnp.concatenate(cT, axis=0).T.astype(BF)
            z = jnp.concatenate(dqT, axis=0).T * (HD**-0.5)
            z = (z * cr[rq, :] - roll8(z, True) * s1r[rq, :] - roll8(z, False) * s2r[rq, :]).astype(BF)
            for o, n in pieces(q0, QB):
                ctx[slot_rows(q0 + o, n), lanes] = co[o : o + n]
                dl[0, slot_rows(q0 + o, n), lanes] = z[o : o + n]

        @pl.loop(0, S)
        def _(s):
            to = lax.rem(s - me + S, S) * N
            for src, off, n in ((s * PD, 0, PD), (PR + s * CR, PD, CR)):
                r = pl.ds(pl.multiple_of(src, 128), n)
                w = pl.ds(pl.multiple_of(to + off, 128), n)
                z = dk_s[r, :]
                z = z * cr[r, :] - roll8(z, True) * s1r[r, :] - roll8(z, False) * s2r[r, :]
                dl[1, w, lanes] = z.astype(BF)
                dl[2, w, lanes] = dv_s[r, :].astype(BF)

    for c in range(3):
        db[c : c + 1, :] = jnp.sum(dl[c].astype(F32), axis=0, keepdims=True)

    @pl.loop(1, S)
    def _(j):
        r = pl.ds(pl.multiple_of(j * N, 128), N)
        w = pl.ds(pl.multiple_of((j - 1) * N, 128), N)
        y = dnn(ctx[r, :], wo[...])
        d = dnt(dl[0, r, :], wq[...]) + dnt(dl[1, r, :], wk[...]) + dnt(dl[2, r, :], wv[...])

        @pl.when(g == 0)
        def _():
            yacc[w, :] = y
            dacc[w, :] = d

        @pl.when(g > 0)
        def _():
            yacc[w, :] += y
            dacc[w, :] += d

    @pl.when(g == last)
    def _():
        ln[...] = jnp.zeros_like(ln)

        def store(j, of, away):
            x, yo, go = of(xs), away(ys), away(gs)

            @pl.loop(0, N // 128)
            def _(i):
                r = tile(i, 128)
                w = pl.ds(pl.multiple_of((j - 1) * N + i * 128, 128), 128)
                xh, _ = normed(x[r, :])
                d = dacc[w, :]
                y = yacc[w, :]
                gg = d * gb[0:1, :]
                if adding:
                    y = y + yo[r, :].astype(F32)
                    gg = gg + go[r, :].astype(F32)
                yo[r, :] = y.astype(BF)
                go[r, :] = gg.astype(BF)
                ln[0:1, :] += jnp.sum(d * xh, axis=0, keepdims=True)
                ln[1:2, :] += jnp.sum(d, axis=0, keepdims=True)

        every_slot(store, 1)


def attn_group(S, PD, CL, me, xs, dys, yps, g2s, wqkv, bqkv, wo, gb, tabs):
    N, D = xs[0].shape
    CW = wo.shape[0]
    T = N * S
    HG = 4 if CW % 256 == 0 else 2
    QB = 256
    W = HG * HD
    G = CW // W
    full = lambda s: pl.BlockSpec(s, lambda g, m: (0,) * len(s), pipeline_mode=pl.Buffered(1))
    keep = lambda s: pl.BlockSpec(s, lambda g, m: (0,) * len(s))
    tok, tok_out, per, far = full((N, D)), keep((N, D)), S, S - 1
    adding = int(T * D <= 1536 * 1024)
    others = (yps, g2s)
    if not adding:
        yps, g2s = [], []
    out_tok = SD((N, D), BF)
    part = pl.BlockSpec((N // G, D), lambda g, m: (g, 0))
    if S > 2:
        xs, dys, yps, g2s = [[jnp.stack(v, axis=0)] if v else v for v in (xs, dys, yps, g2s)]
        tok, tok_out, per, far = full((S, N, D)), keep((S - 1, N, D)), 1, 1
        out_tok = SD((S - 1, N, D), BF)
        part = pl.BlockSpec((S - 1, N // G, D), lambda g, m: (0, g, 0))
    wspec = lambda c: pl.BlockSpec((D, W), lambda g, m: (0, c * G + g))
    bspec = lambda c: pl.BlockSpec((1, W), lambda g, m: (0, c * G + g))
    outs = pl.pallas_call(
        functools.partial(attn_kernel, S, PD, CL, QB, HG, adding),
        grid_spec=pltpu.PrefetchScalarGridSpec(
            num_scalar_prefetch=1,
            grid=(G,),
            in_specs=[tok] * (2 * per)
            + [part] * (2 * adding * far)
            + [wspec(0), wspec(1), wspec(2), bspec(0), bspec(1), bspec(2)]
            + [pl.BlockSpec((W, D), lambda g, m: (g, 0)), full((2, D))]
            + [full((T, 128))] * 3,
            out_specs=[tok_out] * (2 * far)
            + [
                pl.BlockSpec((3, T, W), lambda g, m: (0, 0, g)),
                pl.BlockSpec((T, W), lambda g, m: (0, g)),
                keep((T, D)),
                keep((2, D)),
                pl.BlockSpec((3, W), lambda g, m: (0, g)),
            ],
            scratch_shapes=[pltpu.VMEM((T - N, D), F32)] * 2
            + [pltpu.VMEM((T, W), BF)] * 4
            + [pltpu.VMEM((128, T), BF)] * 2
            + [pltpu.VMEM((T, 128), F32)] * 2,
        ),
        out_shape=[out_tok] * (2 * far)
        + [SD((3, T, CW), BF), SD((T, CW), BF), SD((T, D), BF), SD((2, D), F32), SD((3, CW), F32)],
        compiler_params=pltpu.CompilerParams(vmem_limit_bytes=62 * MIB),
        cost_estimate=pl.CostEstimate(
            flops=16 * T * D * CW + 40 * T * T * CW,
            bytes_accessed=12 * T * D + 12 * T * CW + 8 * D * CW,
            transcendentals=T * T * CW // HD,
        ),
    )(me, *xs, *dys, *yps, *g2s, wqkv, wqkv, wqkv, bqkv, bqkv, bqkv, wo, gb, *tabs)
    ys, gs = outs[:far], outs[far : 2 * far]
    if S > 2:
        ys, gs = [[v[0][j] for j in range(S - 1)] for v in (ys, gs)]
    if not adding:
        ys, gs = [[a + b for a, b in zip(p, q)] for p, q in zip((ys, gs), others)]
    return ys, gs, outs[2 * far :]


def tn_kernel(n, wide, *refs):
    a = refs[:n]
    b = refs[n : 2 * n]
    o = refs[2 * n]
    if wide == 0:
        o[...] = sum(dtn(x[...], y[...]) for x, y in zip(a, b)).astype(BF)
    else:
        w = b[0].shape[2]
        for c in range(wide):
            o[:, c * w : (c + 1) * w] = sum(dtn(x[...], y[c]) for x, y in zip(a, b)).astype(BF)


def tn_sum(a, b, block):
    n = len(a)
    rows, da = a[0].shape
    block = min(block, da)
    wide = b[0].shape[0] if b[0].ndim == 3 else 0
    db = b[0].shape[-1] * max(wide, 1)
    keep = lambda s: pl.BlockSpec(s, lambda i: (0,) * len(s), pipeline_mode=pl.Buffered(1))
    return pl.pallas_call(
        functools.partial(tn_kernel, n, wide),
        grid=(da // block,),
        in_specs=[pl.BlockSpec((rows, block), lambda i: (0, i))] * n + [keep(b[0].shape)] * n,
        out_specs=pl.BlockSpec((block, db), lambda i: (i, 0)),
        out_shape=SD((da, db), BF),
        compiler_params=pltpu.CompilerParams(vmem_limit_bytes=60 * MIB),
        cost_estimate=pl.CostEstimate(flops=2 * n * rows * da * db, bytes_accessed=2 * (n * rows * (da + db) + da * db), transcendentals=0),
    )(*a, *b)


def joined(refs):
    return jnp.concatenate([r[...] for r in refs], axis=0)


def down_kernel(n, more, *refs):
    o = refs[-1]
    t = dtn(joined(refs[:n]), joined(refs[n : 2 * n])).reshape(o.shape)
    o[...] = (t + refs[2 * n][...].astype(F32) if more else t).astype(BF)


def up_kernel(n, more, *refs):
    o = refs[-1]
    c, rows, w = o.shape
    t = dtn(joined(refs[:n]), joined(refs[n : 2 * n]))
    k = t.shape[1] // w
    for i in range(k):
        r = slice(i * (rows // k), (i + 1) * (rows // k))
        p = t[:, i * w : (i + 1) * w].reshape(c, rows // k, w)
        o[:, r, :] = (p + refs[2 * n][:, r, :].astype(F32) if more else p).astype(BF)


def mlp_grads(S, R, acts, dys, hs, dpres, g=None):
    n = len(acts)
    rows, FL = acts[0].shape
    D = dys[0].shape[1]
    DR = D // S
    blk = 256
    rd = FL // R
    ru = DR // R
    k = FL // D
    per = rd + S * ru * k
    keep = lambda s: pl.BlockSpec(s, lambda i: (0,) * len(s), pipeline_mode=pl.Buffered(1))
    steps = DR // blk
    more = g is not None
    hbm = pl.BlockSpec(memory_space=pl.ANY)

    def call(kernel, a, b, spec, g):
        width = b[0].shape[1]
        prior = [] if g is None else [g]
        return pl.pallas_call(
            functools.partial(kernel, n, more),
            grid=(a[0].shape[1] // blk,),
            in_specs=[pl.BlockSpec((rows, blk), lambda i: (0, i))] * n
            + [keep((rows, width))] * n
            + ([spec if more else hbm] if prior else []),
            out_specs=spec,
            out_shape=SD((R, per, D), BF),
            input_output_aliases={2 * n: 0} if prior else {},
            compiler_params=pltpu.CompilerParams(vmem_limit_bytes=60 * MIB),
            cost_estimate=pl.CostEstimate(
                flops=2 * n * rows * D * FL, bytes_accessed=2 * (n * rows * (D + FL) + (1 + more) * D * FL), transcendentals=0
            ),
        )(*a, *b, *prior)

    g = call(down_kernel, acts, dys, pl.BlockSpec((blk // rd, rd, D), lambda i: (i, 0, 0)), g)
    spec = pl.BlockSpec((blk // ru, ru * k, D), lambda i: (i % steps, rd // (ru * k) + i // steps, 0))
    return call(up_kernel, hs, dpres, spec, g)


def mlp_finish_kernel(S, rd, ru, g, down, up):
    n, per, D = g.shape
    k = (per - rd) // (S * ru)
    for c in range(n):
        down[c * rd : (c + 1) * rd, :] = g[c, :rd, :].astype(F32)
        for t in range(S * k):
            a = rd + t * ru
            up[c * ru : (c + 1) * ru, t * D : (t + 1) * D] = g[c, a : a + ru, :].astype(F32)


def mlp_finish(S, g, FL):
    R, per, D = g.shape
    rd = FL // R
    ru = D // S // R
    n = 4
    return pl.pallas_call(
        functools.partial(mlp_finish_kernel, S, rd, ru),
        grid=(R // n,),
        in_specs=[pl.BlockSpec((n, per, D), lambda c: (c, 0, 0))],
        out_specs=[pl.BlockSpec((n * rd, D), lambda c: (c, 0)), pl.BlockSpec((n * ru, S * FL), lambda c: (c, 0))],
        out_shape=[SD((FL, D), F32), SD((D // S, S * FL), F32)],
        compiler_params=pltpu.CompilerParams(vmem_limit_bytes=40 * MIB),
        cost_estimate=pl.CostEstimate(flops=0, bytes_accessed=6 * R * per * D, transcendentals=0),
    )(g)


def attn_grads_kernel(n, S, R, q_ref, *refs):
    h = refs[:n]
    dl = refs[n : 2 * n]
    ctx = refs[2 * n : 3 * n]
    dy = refs[3 * n : -2]
    first, second = refs[-2:]
    i = pl.program_id(0)
    q1 = q_ref[0]
    q2 = q_ref[1]
    blk = h[0].shape[1]
    D = dy[0].shape[1]
    DR = D // S
    CW = dl[0].shape[2]
    ru = DR // R
    k = D // CW
    steps = DR // blk
    s = i // steps
    base = (i % steps) * (blk // ru)
    for p in range(3):
        t = dtn(joined(h), jnp.concatenate([y[p] for y in dl], axis=0)).astype(BF)
        for c in range(blk // ru):
            v = t[c * ru : (c + 1) * ru, :]
            if p < 2:
                first[(base + c) ^ q1, pl.ds(s * 2 * ru + p * ru, ru), :] = v
            else:
                second[(base + c) ^ q2, pl.ds(k * ru + s * ru, ru), :] = v
    t = dtn(joined(ctx), joined(dy)).astype(BF)
    m = ctx[0].shape[1] // ru
    for c in range(m):
        for j in range(k):
            second[(i * m + c) ^ q2, j * ru : (j + 1) * ru, :] = t[c * ru : (c + 1) * ru, j * CW : (j + 1) * CW]


def attn_grads(S, R, q, hs, dls, ctxs, dys):
    n = len(hs)
    T, D = hs[0].shape
    CW = ctxs[0].shape[1]
    DR = D // S
    ru = DR // R
    blk = 256
    G = D // blk
    keep = lambda s: pl.BlockSpec(s, lambda i, q: (0,) * len(s), pipeline_mode=pl.Buffered(1))
    shapes = [(R, S * 2 * ru, CW), (R, (D // CW + S) * ru, CW)]
    return pl.pallas_call(
        functools.partial(attn_grads_kernel, n, S, R),
        grid_spec=pltpu.PrefetchScalarGridSpec(
            num_scalar_prefetch=1,
            grid=(G,),
            in_specs=[pl.BlockSpec((T, blk), lambda i, q: (0, i))] * n
            + [keep((3, T, CW))] * n
            + [pl.BlockSpec((T, CW // G), lambda i, q: (0, i))] * n
            + [keep(dys[0].shape)] * len(dys),
            out_specs=[pl.BlockSpec(s, lambda i, q: (0, 0, 0)) for s in shapes],
        ),
        out_shape=[SD(s, BF) for s in shapes],
        compiler_params=pltpu.CompilerParams(vmem_limit_bytes=60 * MIB),
        cost_estimate=pl.CostEstimate(flops=8 * n * T * D * CW, bytes_accessed=2 * n * T * (2 * D + 4 * CW) + 8 * D * CW, transcendentals=0),
    )(q, *hs, *dls, *ctxs, *dys)


def attn_finish_kernel(S, ru, k, n, q_ref, *refs):
    firsts, seconds = refs[:n], refs[n : 2 * n]
    out, qkv = refs[2 * n :]
    CW = seconds[0].shape[2]
    D = out.shape[1]
    for c in range(n):
        r = slice(c * ru, (c + 1) * ru)
        for j in range(k):
            out[r, j * CW : (j + 1) * CW] = seconds[c][0, j * ru : (j + 1) * ru, :].astype(F32)
        for t in range(S):
            for p in range(3):
                a = (t * 2 + p) * ru if p < 2 else (k + t) * ru
                v = (firsts if p < 2 else seconds)[c][0, a : a + ru, :]
                qkv[r, p * D + t * CW : p * D + (t + 1) * CW] = v.astype(F32)


def attn_finish(S, q, g1, g2):
    R, per1, CW = g1.shape
    per2 = g2.shape[1]
    D = CW * S
    ru = D // S // R
    n = 4
    block = lambda per, k, c: pl.BlockSpec((1, per, CW), lambda i, q: ((i * n + c) ^ q[k], 0, 0))
    return pl.pallas_call(
        functools.partial(attn_finish_kernel, S, ru, S, n),
        grid_spec=pltpu.PrefetchScalarGridSpec(
            num_scalar_prefetch=1,
            grid=(R // n,),
            in_specs=[block(per1, 0, c) for c in range(n)] + [block(per2, 1, c) for c in range(n)],
            out_specs=[pl.BlockSpec((n * ru, D), lambda c, q: (c, 0)), pl.BlockSpec((n * ru, 3 * D), lambda c, q: (c, 0))],
        ),
        out_shape=[SD((CW, D), F32), SD((D // S, 3 * D), F32)],
        compiler_params=pltpu.CompilerParams(vmem_limit_bytes=40 * MIB),
        cost_estimate=pl.CostEstimate(flops=0, bytes_accessed=6 * R * (per1 + per2) * CW, transcendentals=0),
    )(q, *[g1] * n, *[g2] * n)


def own_kernel(act, dpre, wu, wd, dl, ctx, wqkv, wo, x, gb, y, g, ln, yacc, d1, d2):
    f = pl.program_id(0)
    last = pl.num_programs(0) - 1
    N = x.shape[0]
    CW = ctx.shape[1]

    @pl.when(f == 0)
    def _():
        yacc[...] = dnn(ctx[...], wo[...])
        d1[...] = sum(dnt(dl[p], wqkv[:, p * CW : (p + 1) * CW]) for p in range(3))
        d2[...] = jnp.zeros_like(d2)

    yacc[...] += dnn(act[...], wd[...])
    d2[...] += dnt(dpre[...], wu[...])

    @pl.when(f == last)
    def _():
        ln[...] = jnp.zeros_like(ln)

        @pl.loop(0, N // 128)
        def _(i):
            r = tile(i, 128)
            xh, _ = normed(x[r, :])
            a = d1[r, :]
            b = d2[r, :]
            y[r, :] = yacc[r, :].astype(BF)
            g[r, :] = (a * gb[0:1, :] + b * gb[2:3, :]).astype(BF)
            ln[0:1, :] += jnp.sum(a * xh, axis=0, keepdims=True)
            ln[1:2, :] += jnp.sum(a, axis=0, keepdims=True)
            ln[2:3, :] += jnp.sum(b * xh, axis=0, keepdims=True)
            ln[3:4, :] += jnp.sum(b, axis=0, keepdims=True)


def own_rows(x, act, dpre, wu, wd, dl, ctx, wqkv, wo, gb):
    N, D = x.shape
    FL = wu.shape[1]
    CW = wo.shape[0]
    fb = min(512, FL)
    full = lambda s: pl.BlockSpec(s, lambda f: (0,) * len(s), pipeline_mode=pl.Buffered(1))
    keep = lambda s: pl.BlockSpec(s, lambda f: (0,) * len(s))
    rows = pl.BlockSpec((N, fb), lambda f: (0, f))
    return pl.pallas_call(
        own_kernel,
        grid=(FL // fb,),
        in_specs=[rows, rows, pl.BlockSpec((D, fb), lambda f: (0, f)), pl.BlockSpec((fb, D), lambda f: (f, 0))]
        + [full((3, N, CW)), full((N, CW)), full((D, 3 * CW)), full((CW, D)), full((N, D)), full((4, D))],
        out_specs=[keep((N, D)), keep((N, D)), keep((4, D))],
        out_shape=[SD((N, D), BF), SD((N, D), BF), SD((4, D), F32)],
        scratch_shapes=[pltpu.VMEM((N, D), F32)] * 3,
        compiler_params=pltpu.CompilerParams(vmem_limit_bytes=60 * MIB),
        cost_estimate=pl.CostEstimate(
            flops=4 * N * D * FL + 8 * N * D * CW, bytes_accessed=4 * (N + D) * FL + 8 * (N + D) * CW + 6 * N * D, transcendentals=0
        ),
    )(act, dpre, wu, wd, dl, ctx, wqkv, wo, x, gb)


def final_kernel(S, first, PT, *refs):
    it = iter(refs)
    take = lambda n: [next(it) for _ in range(n)]
    x, dy = take(2)
    ys = take(S)
    gs = take(S)
    (vb,) = take(1)
    if not first:
        take(4)
    po, co, pg, cg = take(4)
    i = pl.program_id(0)
    xv = x[...].astype(F32)
    xh, inv = normed(xv)
    y = xv + vb[0:1, :] + sum(r[...].astype(F32) for r in ys) + vb[1:2, :]
    gsum = sum(r[...].astype(F32) for r in gs)
    dx = (gsum - jnp.mean(gsum, axis=-1, keepdims=True) - xh * jnp.mean(gsum * xh, axis=-1, keepdims=True)) * inv
    out = y.astype(BF)
    grad = dy[...].astype(F32) + dx

    @pl.when(i < PT)
    def _():
        po[0] = out
        pg[0] = grad

    @pl.when(i >= PT)
    def _():
        co[0] = out
        cg[0] = grad


def final_rows(m, MB, PD, x, dy, ys, gs, vb, prior):
    S = len(ys)
    N, D = x.shape
    CR = N - PD
    RT = 128
    PT = PD // RT
    first = prior is None
    row = pl.BlockSpec((RT, D), lambda i: (i, 0))
    pspec = pl.BlockSpec((1, RT, D), lambda i: (m, jnp.minimum(i, PT - 1), 0))
    cspec = pl.BlockSpec((1, RT, D), lambda i: (m, jnp.maximum(i - PT, 0), 0))
    hbm = pl.BlockSpec(memory_space=pl.ANY)
    n_in = 2 * S + 3
    return pl.pallas_call(
        functools.partial(final_kernel, S, first, PT),
        grid=(N // RT,),
        in_specs=[row] * (2 * S + 2) + [pl.BlockSpec((2, D), lambda i: (0, 0))] + ([] if first else [hbm] * 4),
        out_specs=[pspec, cspec, pspec, cspec],
        out_shape=[SD((MB, PD, D), BF), SD((MB, CR, D), BF), SD((MB, PD, D), F32), SD((MB, CR, D), F32)],
        input_output_aliases={} if first else {n_in + k: k for k in range(4)},
        compiler_params=pltpu.CompilerParams(vmem_limit_bytes=32 * MIB),
        cost_estimate=pl.CostEstimate(flops=20 * N * D, bytes_accessed=(4 * S + 10) * N * D, transcendentals=0),
    )(x, dy, *ys, *gs, vb, *(() if first else prior))


def shifted(value, S, j):
    return lax.ppermute(value, "shard", [(i, (i + j) % S) for i in range(S)])


def canonical(slots, me, S, back):
    if S == 1:
        return slots
    if S == 2:
        a, b = slots
        return [jnp.where(me == 0, a, b), jnp.where(me == 0, b, a)]
    stacked = jnp.stack(slots, axis=0)
    return [
        lax.dynamic_index_in_dim(stacked, lax.rem((me - s if back else s - me) + S, S), 0, keepdims=False) for s in range(S)
    ]


def exchanged(value, R, bit):
    return lax.ppermute(value, "rep", [(i, i ^ bit) for i in range(R)])


def columns_for(weight, me, S, j, parts, row=0, rows=None):
    cols = weight.shape[1] // parts
    rows = weight.shape[0] if rows is None else rows
    w = cols // S
    at = lax.rem(me + j, S) * w
    got = [lax.dynamic_slice(weight, (row, p * cols + at), (rows, w)) for p in range(parts)]
    return got[0] if parts == 1 else jnp.concatenate(got, axis=1)


def my_columns_halves(weight, me, S, R):
    rows = weight.shape[0]
    rep = lax.axis_index("rep")
    core = rep % 2
    y = (rep // 2) % 2
    n = rows // 4
    cut = [columns_for(weight, me, S, j, 1, (2 * core + y) * n, n) for j in range(1, S)]
    slots = [columns_for(weight, me, S, 0, 1)]

    def both(piece, other, first):
        return jnp.concatenate([jnp.where(first, piece, other), jnp.where(first, other, piece)], axis=0)

    for j in range(1, S):
        piece = shifted(cut[j - 1], S, j)
        pair = both(piece, exchanged(piece, R, 2), y == 0)
        slots.append(both(pair, exchanged(pair, R, 1), core == 0))
    return jnp.concatenate(canonical(slots, me, S, True), axis=0), piece, cut[0]


def my_columns(weight, me, S, R, parts):
    rows = weight.shape[0]
    own = columns_for(weight, me, S, 0, parts)
    if S == 1:
        return own
    rep = lax.axis_index("rep")
    chunk = rows // R
    got = []
    for j in range(1, S):
        got.append(shifted(columns_for(weight, me, S, j, parts, rep * chunk, chunk), S, j))
    others = lax.all_gather(jnp.stack(got, axis=0), "rep", axis=1, tiled=True)
    return jnp.concatenate(canonical([own] + [others[j] for j in range(S - 1)], me, S, True), axis=0)


def add_low(a, b):
    return (a.astype(F32) + b.astype(F32)).astype(BF)


def orders(R):
    bits = [1 << i for i in range(R.bit_length() - 1)]
    return bits, bits[:1] + bits[2:] + bits[1:2]


def place(rep, order):
    q = jnp.zeros((), jnp.int32)
    for bit in order:
        q = 2 * q + (rep & bit) // bit
    return q


def beside_it(got, key, beside):
    if key in beside:
        got, beside[key] = lax.optimization_barrier((got, beside[key]))
    return got


def halving(pair, R, beside):
    pair = list(pair)
    for i, bits in enumerate(zip(*orders(R))):
        h = pair[0].shape[0] // 2
        got = beside_it([exchanged(g[h:], R, bit) for g, bit in zip(pair, bits)], i, beside)
        pair = [add_low(g[:h], t) for g, t in zip(pair, got)]
    return [g[0] for g in pair]


def doubling(parts, R, beside):
    pair = [p[None] for p in parts]
    for i, bits in reversed(list(enumerate(zip(*orders(R))))):
        got = [exchanged(g, R, bit) for g, bit in zip(pair, bits)]
        got = beside_it(got, i, beside)
        pair = [jnp.concatenate([g, t], axis=0) for g, t in zip(pair, got)]
    return pair


def sum_all(v, S, R):
    bit = 1
    while bit < R:
        v = v + exchanged(v, R, bit)
        bit *= 2
    return v


def swap_shards(part, me, S, head):
    n = (part.shape[0] - head) // S
    slots = []
    for j in range(S):
        b = lax.dynamic_slice_in_dim(part, head + lax.rem(me + j, S) * n, n, 0)
        slots.append(shifted(b, S, j) if j else b)
    return jnp.concatenate(([part[:head]] if head else []) + canonical(slots, me, S, True), axis=0)


def reduce_rows(grad):
    part = lax.psum_scatter(grad, "rep", scatter_dimension=0, tiled=True)
    return lax.all_gather(part, "rep", axis=0, tiled=True).astype(F32)


def reduce_columns(grad, me, S, parts):
    rows, cols = grad.shape
    part = lax.psum_scatter(grad.reshape(S, rows // S, cols), "rep", scatter_dimension=1, tiled=True)
    slots = [lax.dynamic_index_in_dim(part, me, 0, keepdims=False)]
    for j in range(1, S):
        slots.append(shifted(lax.dynamic_index_in_dim(part, lax.rem(me + j, S), 0, keepdims=False), S, j))
    slots = [s.reshape(s.shape[0], parts, cols // parts) for s in slots]
    whole = jnp.stack(canonical(slots, me, S, True), axis=2).reshape(-1, S * cols)
    return lax.all_gather(whole, "rep", axis=0, tiled=True).astype(F32)


def rotary_tables(PR, CR, CL):
    pos = np.concatenate([np.arange(PR), PR + np.arange(CR) % CL]).astype(np.float32)
    half = ROT // 2
    freq = np.exp(np.arange(half, dtype=np.float32) * np.float32(-2.0 * math.log(10000.0) / ROT)).astype(np.float32)
    ang = (pos[:, None] * freq[None, :]).astype(np.float32)
    c = np.cos(ang)
    s = np.sin(ang)
    n = pos.shape[0]
    one = np.ones((n, HD - ROT), np.float32)
    zero = np.zeros((n, HD - ROT), np.float32)
    z8 = np.zeros((n, half), np.float32)
    tabs = ([c, c, one], [-s, z8, zero], [z8, s, zero])
    return [jnp.asarray(np.tile(np.concatenate(t, axis=1), (1, 128 // HD)), F32) for t in tabs]


def per_device(
    prompt_in,
    cont_in,
    prompt_cot,
    cont_cot,
    ln1_gain,
    ln1_bias,
    ln2_gain,
    ln2_bias,
    qkv_weight,
    qkv_bias,
    out_weight,
    out_bias,
    up_weight,
    up_bias,
    down_weight,
    down_bias,
):
    S = lax.axis_size("shard")
    R = lax.axis_size("rep")
    me = lax.axis_index("shard")
    MB, _, PD, D = prompt_in.shape
    CD, CL = cont_in.shape[2:4]
    CR = CD * CL
    N = PD + CR
    CW = D // S
    FL = up_weight.shape[1] // S
    me_arr = jnp.reshape(me, (1,)).astype(jnp.int32)

    one = lambda v: v.astype(F32).reshape(-1, CW)
    small = jnp.concatenate([one(v) for v in (ln1_gain, ln1_bias, ln2_gain, ln2_bias, out_bias, down_bias, qkv_bias)], axis=0)
    w_up, brought, cut = my_columns_halves(up_weight, me, S, R)
    (small, qkv_weight), cut = lax.optimization_barrier(((small, qkv_weight), cut))
    slots = [small] + [shifted(small, S, j) for j in range(1, S)]
    whole = jnp.stack(canonical(slots, me, S, True), axis=0)
    vec = whole[:, :6].transpose(1, 0, 2).reshape(6, D)
    gb = vec[0:4]
    gb1 = vec[0:2]
    gb2 = vec[2:4]
    vb = vec[4:6]
    bqkv = whole[:, 6:].reshape(3, S, CW)
    bqkv = lax.dynamic_index_in_dim(bqkv, me, 1, keepdims=False).reshape(1, 3 * CW)
    bup = up_bias.astype(F32).reshape(1, FL)

    w_qkv = my_columns(qkv_weight, me, S, R, 3)

    X = [[jnp.concatenate([prompt_in[m, 0], cont_in[m, 0].reshape(CR, D)], axis=0)] for m in range(MB)]
    DY = [[jnp.concatenate([prompt_cot[m, 0], cont_cot[m, 0].reshape(CR, D)], axis=0)] for m in range(MB)]
    tabs = rotary_tables(PD * S, CR * S, CL)
    src = [(X[m][0], DY[m][0]) for m in range(MB)]
    src[1:], brought = lax.optimization_barrier((src[1:], brought))
    for m in range(MB):
        for j in range(1, S):
            X[m].append(shifted(src[m][0], S, S - j))
            DY[m].append(shifted(src[m][1], S, S - j))

    ff = [[None] * S for _ in range(MB)]

    def mlp(m, j):
        ff[m][j] = mlp_rows(X[m][j], DY[m][j], w_up, bup, down_weight, gb2, int(j > 0))

    for m in range(MB):
        mlp(m, 0)
    rest = []
    y_got, g_got = [], []

    def attend(m):
        ys, gs, more = attn_group(
            S, PD, CL, me_arr, X[m], DY[m], [f[4] for f in ff[m][1:]], [f[5] for f in ff[m][1:]], w_qkv, bqkv, out_weight, gb1, tabs
        )
        rest.append(list(more))
        y_got.append([shifted(ys[j - 1], S, j) for j in range(1, S)])
        g_got.append([shifted(gs[j - 1], S, j) for j in range(1, S)])

    def own(m):
        f = ff[m][0]
        return own_rows(X[m][0], f[0], f[1], w_up, down_weight, rest[m][0], rest[m][1], w_qkv, out_weight, gb)

    chunked = (D // S // R) % 16 == 0 and R & (R - 1) == 0
    rep = lax.axis_index("rep")
    late = [(MB - 1, j) for j in range(1, S)]
    early = [(m, j) for m in range(MB) for j in range(S) if (m, j) not in late]
    of = lambda set_, k: [ff[m][j][k] for m, j in set_]
    for m, j in early:
        if j:
            mlp(m, j)
    if chunked:
        gmlp = mlp_grads(S, R, of(early, 0), [DY[m][j] for m, j in early], of(early, 2), of(early, 1))
        w_up, gmlp = lax.optimization_barrier((w_up, gmlp))
    for m, j in late:
        mlp(m, j)
    if chunked:
        if late:
            gmlp = mlp_grads(S, R, of(late, 0), [DY[m][j] for m, j in late], of(late, 2), of(late, 1), gmlp)
        part = lax.psum_scatter(gmlp, "rep", scatter_dimension=0, tiled=True)[0]
        w_qkv, gmlp = lax.optimization_barrier((w_qkv, gmlp))
    for m in range(MB):
        attend(m)
        if m + 1 < MB:
            w_qkv, rest[m][3] = lax.optimization_barrier((w_qkv, rest[m][3]))
    every = early + late
    def vectors(mine_):
        ln1 = sum(r[3] for r in rest) + sum(o[2][0:2] for o in mine_)
        ln2 = sum(f[6] for f in (ff[m][j] for m, j in every if j)) + sum(o[2][2:4] for o in mine_)
        db_out = sum(jnp.sum(DY[m][0].astype(F32), axis=0) for m in range(MB)).reshape(-1, CW)
        mine = (jnp.arange(S) == me).astype(F32)
        db_qkv = (sum(r[4] for r in rest)[:, None, :] * mine[None, :, None]).reshape(-1, CW)
        db_up = (sum(of(every, 3)) * mine[:, None]).reshape(-1, CW)
        return jnp.concatenate([ln1.reshape(-1, CW), ln2.reshape(-1, CW), db_out, db_qkv, db_up], axis=0)

    finals = lambda m, o, prior: final_rows(m, MB, PD, X[m][0], DY[m][0], [o[0]] + y_got[m], [o[1]] + g_got[m], vb, prior)
    hs, dls, ctxs = [[r[k] for r in rest] for k in (2, 0, 1)]
    if chunked:
        q = jnp.stack([place(rep, order) for order in orders(R)]).astype(jnp.int32)
        part = swap_shards(part, me, S, FL // R)
        hs, y_got[:-1], g_got[:-1], part = lax.optimization_barrier((hs, y_got[:-1], g_got[:-1], part))
        gmlp_all = lax.all_gather(part, "rep", axis=0, tiled=False)
        gatt = attn_grads(S, R, q, hs, dls, ctxs, [DY[m][j] for m in range(MB) for j in range(S)])
        dls_own, _ = lax.optimization_barrier(([r[0] for r in rest], gatt))
        for m in range(MB):
            rest[m][0] = dls_own[m]
        mine = [own(m) for m in range(MB)]
        beside = {1: mine[:1], 2: (mine[1:], y_got[-1], g_got[-1])}
        half = halving(gatt, R, beside)
        mine[:1] = beside[1]
        mine[1:], y_got[-1], g_got[-1] = beside[2]
        outs = None
        for m in range(MB - 1):
            outs = finals(m, mine[m], outs)
        vecs = sum_all(vectors(mine), S, R)
        k = D // CW * (D // S // R)
        outs = finals(MB - 1, mine[-1], outs)
        beside = {3: outs, 2: vecs, 1: mlp_finish(S, gmlp_all, FL)}
        g1, g2 = doubling([swap_shards(half[0], me, S, 0), swap_shards(half[1], me, S, k)], R, beside)
        outs = beside[3]
        vecs = beside[2]
        g_down, g_up = beside[1]
        g_out, g_qkv = attn_finish(S, q, g1, g2)
    else:
        dls, ctxs, hs = [[r[k] for r in rest] for k in (0, 1, 2)]
        mine = [own(m) for m in range(MB)]
        g_down = reduce_rows(tn_sum(of(every, 0), [DY[m][j] for m, j in every], 256))
        g_up = reduce_columns(tn_sum(of(every, 2), of(every, 1), 256), me, S, 1)
        dycs = [jnp.concatenate(DY[m], axis=0) for m in range(MB)]
        g_out = reduce_rows(tn_sum(ctxs, dycs, 256))
        g_qkv = reduce_columns(tn_sum(hs, dls, 256), me, S, 3)
        vecs = sum_all(vectors(mine), S, R)
        outs = None
        for m in range(MB):
            outs = finals(m, mine[m], outs)
    tot = vecs + sum(shifted(vecs, S, j) for j in range(1, S))
    held = lambda a, n: lax.dynamic_slice_in_dim(tot, a + me * n, n, 0).reshape(-1)
    v_ln1g, v_ln1b, v_ln2g, v_ln2b, v_out = [held(k * S, 1) for k in range(5)]
    v_qkv = held(5 * S, 3)
    v_up = held(8 * S, FL // CW)

    po, co, pg, cg = outs
    return (
        po.reshape(MB, 1, PD, D),
        co.reshape(MB, 1, CD, CL, D),
        pg.reshape(MB, 1, PD, D),
        cg.reshape(MB, 1, CD, CL, D),
        v_ln1g,
        v_ln1b,
        v_ln2g,
        v_ln2b,
        g_qkv,
        v_qkv,
        g_out,
        v_out,
        g_up,
        v_up,
        g_down,
        v_out,
    )


def solution(mesh):
    tokens = (
        P(None, "rep", "shard", None),
        P(None, "rep", "shard", None, None),
        P(None, "rep", "shard", None),
        P(None, "rep", "shard", None, None),
    )
    vec = P("shard")
    mat = P("shard", None)
    params = (vec, vec, vec, vec, mat, vec, mat, vec, mat, vec, mat, vec)
    return jax.shard_map(
        per_device, mesh=mesh, in_specs=tokens + params, out_specs=tokens + params, check_vma=False
    )
```

```python
import functools
import math

import jax
import jax.numpy as jnp
import numpy as np
from jax import lax
from jax.experimental import pallas as pl
from jax.experimental.pallas import tpu as pltpu
from jax.sharding import PartitionSpec as P

H = 16
HD = 64
ROT = 16
EPS = 1e-05
F32 = jnp.float32
BF = jnp.bfloat16
MIB = 1024 * 1024
SD = jax.ShapeDtypeStruct


def dnn(a, b):
    return lax.dot_general(a, b, (((1,), (0,)), ((), ())), preferred_element_type=F32)


def dnt(a, b):
    return lax.dot_general(a, b, (((1,), (1,)), ((), ())), preferred_element_type=F32)


def dtn(a, b):
    return lax.dot_general(a, b, (((0,), (0,)), ((), ())), preferred_element_type=F32)


def normed(rows):
    x = rows.astype(F32)
    c = x - jnp.mean(x, axis=-1, keepdims=True)
    inv = lax.rsqrt(jnp.mean(c * c, axis=-1, keepdims=True) + EPS)
    return c * inv, inv


def tile(i, n):
    return pl.ds(pl.multiple_of(i * n, n), n)


def rows_tile(n, most):
    t = most
    while n % t:
        t -= 8
    return t


def mlp_kernel(rt, x_ref, dy_ref, wu_ref, bu_ref, wd_ref, gb_ref, act_ref, dpre_ref, h_ref, bu_out):
    rows = x_ref.shape[0]

    @pl.when(pl.program_id(0) == 0)
    def _():
        @pl.loop(0, rows // 128)
        def _(i):
            r = tile(i, 128)
            xh, _ = normed(x_ref[r, :])
            h_ref[r, :] = (xh * gb_ref[0:1, :] + gb_ref[1:2, :]).astype(BF)

    def step(i, bsum):
        r = tile(i, rt)
        pre = dnn(h_ref[r, :], wu_ref[...]) + bu_ref[...]
        da = dnt(dy_ref[r, :], wd_ref[...])
        cdf = 0.5 * (1.0 + lax.erf(pre * 0.7071067811865476))
        act_ref[r, :] = (pre * cdf).astype(BF)
        dpre = (da * (cdf + pre * jnp.exp(-0.5 * pre * pre) * 0.3989422804014327)).astype(BF)
        dpre_ref[r, :] = dpre
        return bsum + jnp.sum(dpre.astype(F32), axis=0, keepdims=True)

    bu_out[...] = lax.fori_loop(0, rows // rt, step, jnp.zeros(bu_out.shape, F32))


def mlp_rows(x, dy, wu, bu, wd, gb):
    rows, width = x.shape
    hidden = wu.shape[1]
    fb = min(512, hidden)
    full = lambda s: pl.BlockSpec(s, lambda f: (0,) * len(s))
    return pl.pallas_call(
        functools.partial(mlp_kernel, rows_tile(rows, 640)),
        grid=(hidden // fb,),
        in_specs=[
            full((rows, width)),
            full((rows, width)),
            pl.BlockSpec((width, fb), lambda f: (0, f)),
            pl.BlockSpec((1, fb), lambda f: (0, f)),
            pl.BlockSpec((fb, width), lambda f: (f, 0)),
            full((2, width)),
        ],
        out_specs=[
            pl.BlockSpec((rows, fb), lambda f: (0, f)),
            pl.BlockSpec((rows, fb), lambda f: (0, f)),
            full((rows, width)),
            pl.BlockSpec((1, fb), lambda f: (0, f)),
        ],
        out_shape=[SD((rows, hidden), BF), SD((rows, hidden), BF), SD((rows, width), BF), SD((1, hidden), F32)],
        compiler_params=pltpu.CompilerParams(vmem_limit_bytes=60 * MIB),
        cost_estimate=pl.CostEstimate(
            flops=4 * rows * width * hidden, bytes_accessed=4 * (width * hidden + rows * hidden) + 6 * rows * width, transcendentals=2 * rows * hidden
        ),
    )(x, dy, wu, bu, wd, gb)


def roll8(x, left):
    w = x.shape[-1]
    return pltpu.roll(x, (w - 8) if left else 8, 1)


def attn_kernel(S, PD, CL, QB, HG, me_ref, *refs):
    it = iter(refs)
    take = lambda n: [next(it) for _ in range(n)]
    stacked = S > 2
    per = 1 if stacked else S
    xs = take(per)
    dys = take(per)
    wq, wk, wv = take(3)
    bq, bk, bv = take(3)
    wo, gb = take(2)
    cr, s1r, s2r = take(3)
    dl, ctx, h1, db = take(4)
    q_s, k_s, v_s, dc_s, kT, vT, dk_s, dv_s = take(8)
    g = pl.program_id(0)
    me = me_ref[0]
    N = xs[0].shape[-2]
    T = N * S
    PR = PD * S
    CR = N - PD
    W = HG * HD

    def every_slot(fn):
        if stacked:

            @pl.loop(0, S)
            def _(j):
                fn(j, lambda refs: refs[0].at[j])

        else:
            for j in range(S):
                fn(j, lambda refs: refs[j])

    def slot_rows(start, n):
        if start < PR:
            s, off = start // PD, start % PD
        else:
            s, off = (start - PR) // CR, PD + (start - PR) % CR
        return pl.ds(pl.multiple_of(lax.rem(s - me + S, S) * N + off, 128), n)

    def pieces(start, n):
        step = min(n, PD if start < PR else CR)
        return [(i, step) for i in range(0, n, step)]

    @pl.when(g == 0)
    def _():
        def load(j, of):
            x = of(xs)

            @pl.loop(0, N // 128)
            def _(i):
                xh, _ = normed(x[tile(i, 128), :])
                h1[pl.ds(pl.multiple_of(j * N + i * 128, 128), 128), :] = (xh * gb[0:1, :] + gb[1:2, :]).astype(BF)

        every_slot(load)

    def rot(y, r, scale):
        c = cr[r, :]
        s1 = s1r[r, :]
        s2 = s2r[r, :]
        out = []
        for p in range(W // 128):
            z = y[:, p * 128 : (p + 1) * 128]
            z = (z * c + roll8(z, True) * s1 + roll8(z, False) * s2).astype(BF)
            out.append(z * jnp.asarray(scale, BF) if scale != 1.0 else z)
        return jnp.concatenate(out, axis=1) if len(out) > 1 else out[0]

    def proj(j, of):
        s = lax.rem(me + j, S)
        rp = pl.ds(pl.multiple_of(s * PD, 128), PD)
        rc = pl.ds(pl.multiple_of(PR + s * CR, 128), CR)
        hh = h1[pl.ds(pl.multiple_of(j * N, 128), N), :]
        y = dnn(hh, wq[...]) + bq[...]
        q_s[rp, :] = rot(y[:PD], rp, HD**-0.5)
        q_s[rc, :] = rot(y[PD:], rc, HD**-0.5)
        y = dnn(hh, wk[...]) + bk[...]
        k_s[rp, :] = rot(y[:PD], rp, 1.0)
        k_s[rc, :] = rot(y[PD:], rc, 1.0)
        y = (dnn(hh, wv[...]) + bv[...]).astype(BF)
        v_s[rp, :] = y[:PD]
        v_s[rc, :] = y[PD:]
        y = dnt(of(dys)[...], wo[...]).astype(BF)
        dc_s[rp, :] = y[:PD]
        dc_s[rc, :] = y[PD:]

    every_slot(proj)
    lane = lax.broadcasted_iota(jnp.int32, (1, 128), 1)
    row_i = lax.broadcasted_iota(jnp.int32, (QB, QB), 0)
    col_i = lax.broadcasted_iota(jnp.int32, (QB, QB), 1)
    causal = row_i <= col_i
    cmask = causal & ((row_i // CL) == (col_i // CL))
    blocks = []
    for i in range(PR // QB):
        blocks.append((i * QB, [(0, i * QB, None)] * (i > 0) + [(i * QB, QB, causal)]))
    for c in range((T - PR) // QB):
        blocks.append((PR + c * QB, [(0, PR, None), (PR + c * QB, QB, cmask)]))

    @pl.loop(0, W // 128)
    def _(p):
        lanes = tile(p, 128)
        kT[...] = k_s[:, lanes].T
        vT[...] = v_s[:, lanes].T
        dk_s[...] = jnp.zeros_like(dk_s)
        dv_s[...] = jnp.zeros_like(dv_s)
        def begin(q0, parts):
            qb = q_s[pl.ds(q0, QB), lanes]
            dcb = dc_s[pl.ds(q0, QB), lanes]
            out = []
            for h in range(2):
                sel = (lane >= HD * h) & (lane < HD * h + HD)
                qm = jnp.where(sel, qb, jnp.zeros_like(qb))
                dm = jnp.where(sel, dcb, jnp.zeros_like(dcb))
                ss = []
                for k0, n, mask in parts:
                    s = dnt(k_s[k0 : k0 + n, lanes], qm)
                    ss.append(s if mask is None else jnp.where(mask, s, -1e30))
                out.append((qm, dm, ss, [dnt(v_s[k0 : k0 + n, lanes], dm) for k0, n, _ in parts]))
            return out

        ahead = begin(*blocks[0])
        for b, (q0, parts) in enumerate(blocks):
            now = ahead
            if b + 1 < len(blocks):
                ahead = begin(*blocks[b + 1])
            rq = pl.ds(q0, QB)
            P_, DS, cT, dqT = [], [], [], []
            qh = [t[0] for t in now]
            dch = [t[1] for t in now]
            for h in range(2):
                _, _, ss, dps = now[h]
                m = functools.reduce(jnp.maximum, [jnp.max(s, axis=0, keepdims=True) for s in ss])
                es = [jnp.exp(s - m) for s in ss]
                rl = 1.0 / sum(jnp.sum(e, axis=0, keepdims=True) for e in es)
                ps = [e * rl for e in es]
                delta = sum(jnp.sum(a * b, axis=0, keepdims=True) for a, b in zip(ps, dps))
                P_.append([a.astype(BF) for a in ps])
                DS.append([(a * (b - delta)).astype(BF) for a, b in zip(ps, dps)])
                hr = slice(HD * h, HD * h + HD)
                cT.append(sum(dnn(vT[hr, k0 : k0 + n], a) for (k0, n, _), a in zip(parts, P_[h])))
                dqT.append(sum(dnn(kT[hr, k0 : k0 + n], a) for (k0, n, _), a in zip(parts, DS[h])))
            q2 = jnp.concatenate(qh, axis=0)
            dc2 = jnp.concatenate(dch, axis=0)
            for i, (k0, n, _) in enumerate(parts):
                dv_s[k0 : k0 + n, :] += dnn(jnp.concatenate([P_[0][i], P_[1][i]], axis=1), dc2)
                dk_s[k0 : k0 + n, :] += dnn(jnp.concatenate([DS[0][i], DS[1][i]], axis=1), q2)
            co = jnp.concatenate(cT, axis=0).T.astype(BF)
            z = jnp.concatenate(dqT, axis=0).T * (HD**-0.5)
            z = (z * cr[rq, :] - roll8(z, True) * s1r[rq, :] - roll8(z, False) * s2r[rq, :]).astype(BF)
            for o, n in pieces(q0, QB):
                ctx[slot_rows(q0 + o, n), lanes] = co[o : o + n]
                dl[0, slot_rows(q0 + o, n), lanes] = z[o : o + n]

        @pl.loop(0, S)
        def _(s):
            to = lax.rem(s - me + S, S) * N
            for src, off, n in ((s * PD, 0, PD), (PR + s * CR, PD, CR)):
                r = pl.ds(pl.multiple_of(src, 128), n)
                w = pl.ds(pl.multiple_of(to + off, 128), n)
                z = dk_s[r, :]
                z = z * cr[r, :] - roll8(z, True) * s1r[r, :] - roll8(z, False) * s2r[r, :]
                dl[1, w, lanes] = z.astype(BF)
                dl[2, w, lanes] = dv_s[r, :].astype(BF)

    for c in range(3):
        db[c : c + 1, :] = jnp.sum(dl[c].astype(F32), axis=0, keepdims=True)


def attn_group(S, PD, CL, me, xs, dys, wqkv, bqkv, wo, gb, tabs):
    N, D = xs[0].shape
    CW = wo.shape[0]
    T = N * S
    HG = 4 if CW % 256 == 0 else 2
    QB = 256
    W = HG * HD
    G = CW // W
    full = lambda s: pl.BlockSpec(s, lambda g, m: (0,) * len(s), pipeline_mode=pl.Buffered(1))
    tok = full((N, D))
    if S > 2:
        xs, dys = [[jnp.stack(v, axis=0)] for v in (xs, dys)]
        tok = full((S, N, D))
    wspec = lambda c: pl.BlockSpec((D, W), lambda g, m: (0, c * G + g))
    bspec = lambda c: pl.BlockSpec((1, W), lambda g, m: (0, c * G + g))
    return pl.pallas_call(
        functools.partial(attn_kernel, S, PD, CL, QB, HG),
        grid_spec=pltpu.PrefetchScalarGridSpec(
            num_scalar_prefetch=1,
            grid=(G,),
            in_specs=[tok] * (len(xs) + len(dys))
            + [wspec(0), wspec(1), wspec(2), bspec(0), bspec(1), bspec(2)]
            + [pl.BlockSpec((W, D), lambda g, m: (g, 0)), full((2, D))]
            + [full((T, 128))] * 3,
            out_specs=[
                pl.BlockSpec((3, T, W), lambda g, m: (0, 0, g)),
                pl.BlockSpec((T, W), lambda g, m: (0, g)),
                pl.BlockSpec((T, D), lambda g, m: (0, 0)),
                pl.BlockSpec((3, W), lambda g, m: (0, g)),
            ],
            scratch_shapes=[pltpu.VMEM((T, W), BF)] * 4 + [pltpu.VMEM((128, T), BF)] * 2 + [pltpu.VMEM((T, 128), F32)] * 2,
        ),
        out_shape=[SD((3, T, CW), BF), SD((T, CW), BF), SD((T, D), BF), SD((3, CW), F32)],
        compiler_params=pltpu.CompilerParams(vmem_limit_bytes=62 * MIB),
        cost_estimate=pl.CostEstimate(
            flops=8 * T * D * CW + 40 * T * T * CW, bytes_accessed=6 * T * D + 8 * T * CW + 8 * D * CW, transcendentals=T * T * CW // HD
        ),
    )(me, *xs, *dys, wqkv, wqkv, wqkv, bqkv, bqkv, bqkv, wo, gb, *tabs)


def tn_kernel(n, wide, *refs):
    a = refs[:n]
    b = refs[n : 2 * n]
    o = refs[2 * n]
    if wide == 0:
        o[...] = sum(dtn(x[...], y[...]) for x, y in zip(a, b)).astype(BF)
    else:
        w = b[0].shape[2]
        for c in range(wide):
            o[:, c * w : (c + 1) * w] = sum(dtn(x[...], y[c]) for x, y in zip(a, b)).astype(BF)


def tn_sum(a, b, block):
    n = len(a)
    rows, da = a[0].shape
    block = min(block, da)
    wide = b[0].shape[0] if b[0].ndim == 3 else 0
    db = b[0].shape[-1] * max(wide, 1)
    keep = lambda s: pl.BlockSpec(s, lambda i: (0,) * len(s), pipeline_mode=pl.Buffered(1))
    return pl.pallas_call(
        functools.partial(tn_kernel, n, wide),
        grid=(da // block,),
        in_specs=[pl.BlockSpec((rows, block), lambda i: (0, i))] * n + [keep(b[0].shape)] * n,
        out_specs=pl.BlockSpec((block, db), lambda i: (i, 0)),
        out_shape=SD((da, db), BF),
        compiler_params=pltpu.CompilerParams(vmem_limit_bytes=60 * MIB),
        cost_estimate=pl.CostEstimate(flops=2 * n * rows * da * db, bytes_accessed=2 * (n * rows * (da + db) + da * db), transcendentals=0),
    )(*a, *b)


def joined(refs):
    return jnp.concatenate([r[...] for r in refs], axis=0)


def down_kernel(n, more, *refs):
    o = refs[-1]
    t = dtn(joined(refs[:n]), joined(refs[n : 2 * n])).reshape(o.shape)
    o[...] = (t + refs[2 * n][...].astype(F32) if more else t).astype(BF)


def up_kernel(n, more, *refs):
    o = refs[-1]
    c, rows, w = o.shape
    t = dtn(joined(refs[:n]), joined(refs[n : 2 * n]))
    k = t.shape[1] // w
    for i in range(k):
        r = slice(i * (rows // k), (i + 1) * (rows // k))
        p = t[:, i * w : (i + 1) * w].reshape(c, rows // k, w)
        o[:, r, :] = (p + refs[2 * n][:, r, :].astype(F32) if more else p).astype(BF)


def mlp_grads(S, R, acts, dys, hs, dpres, g=None):
    n = len(acts)
    rows, FL = acts[0].shape
    D = dys[0].shape[1]
    DR = D // S
    blk = 256
    rd = FL // R
    ru = DR // R
    k = FL // D
    per = rd + S * ru * k
    keep = lambda s: pl.BlockSpec(s, lambda i: (0,) * len(s), pipeline_mode=pl.Buffered(1))
    steps = DR // blk
    more = g is not None
    hbm = pl.BlockSpec(memory_space=pl.ANY)

    def call(kernel, a, b, spec, g):
        width = b[0].shape[1]
        prior = [] if g is None else [g]
        return pl.pallas_call(
            functools.partial(kernel, n, more),
            grid=(a[0].shape[1] // blk,),
            in_specs=[pl.BlockSpec((rows, blk), lambda i: (0, i))] * n
            + [keep((rows, width))] * n
            + ([spec if more else hbm] if prior else []),
            out_specs=spec,
            out_shape=SD((R, per, D), BF),
            input_output_aliases={2 * n: 0} if prior else {},
            compiler_params=pltpu.CompilerParams(vmem_limit_bytes=60 * MIB),
            cost_estimate=pl.CostEstimate(
                flops=2 * n * rows * D * FL, bytes_accessed=2 * (n * rows * (D + FL) + (1 + more) * D * FL), transcendentals=0
            ),
        )(*a, *b, *prior)

    g = call(down_kernel, acts, dys, pl.BlockSpec((blk // rd, rd, D), lambda i: (i, 0, 0)), g)
    spec = pl.BlockSpec((blk // ru, ru * k, D), lambda i: (i % steps, rd // (ru * k) + i // steps, 0))
    return call(up_kernel, hs, dpres, spec, g)


def mlp_finish_kernel(S, rd, ru, g, down, up):
    n, per, D = g.shape
    k = (per - rd) // (S * ru)
    for c in range(n):
        down[c * rd : (c + 1) * rd, :] = g[c, :rd, :].astype(F32)
        for t in range(S * k):
            a = rd + t * ru
            up[c * ru : (c + 1) * ru, t * D : (t + 1) * D] = g[c, a : a + ru, :].astype(F32)


def mlp_finish(S, g, FL):
    R, per, D = g.shape
    rd = FL // R
    ru = D // S // R
    n = 4
    return pl.pallas_call(
        functools.partial(mlp_finish_kernel, S, rd, ru),
        grid=(R // n,),
        in_specs=[pl.BlockSpec((n, per, D), lambda c: (c, 0, 0))],
        out_specs=[pl.BlockSpec((n * rd, D), lambda c: (c, 0)), pl.BlockSpec((n * ru, S * FL), lambda c: (c, 0))],
        out_shape=[SD((FL, D), F32), SD((D // S, S * FL), F32)],
        compiler_params=pltpu.CompilerParams(vmem_limit_bytes=40 * MIB),
        cost_estimate=pl.CostEstimate(flops=0, bytes_accessed=6 * R * per * D, transcendentals=0),
    )(g)


def attn_grads_kernel(n, S, R, q_ref, *refs):
    h = refs[:n]
    dl = refs[n : 2 * n]
    ctx = refs[2 * n : 3 * n]
    dy = refs[3 * n : -2]
    first, second = refs[-2:]
    i = pl.program_id(0)
    q1 = q_ref[0]
    q2 = q_ref[1]
    blk = h[0].shape[1]
    D = dy[0].shape[1]
    DR = D // S
    CW = dl[0].shape[2]
    ru = DR // R
    k = D // CW
    steps = DR // blk
    s = i // steps
    base = (i % steps) * (blk // ru)
    for p in range(3):
        t = dtn(joined(h), jnp.concatenate([y[p] for y in dl], axis=0)).astype(BF)
        for c in range(blk // ru):
            v = t[c * ru : (c + 1) * ru, :]
            if p < 2:
                first[(base + c) ^ q1, pl.ds(s * 2 * ru + p * ru, ru), :] = v
            else:
                second[(base + c) ^ q2, pl.ds(k * ru + s * ru, ru), :] = v
    t = dtn(joined(ctx), joined(dy)).astype(BF)
    m = ctx[0].shape[1] // ru
    for c in range(m):
        for j in range(k):
            second[(i * m + c) ^ q2, j * ru : (j + 1) * ru, :] = t[c * ru : (c + 1) * ru, j * CW : (j + 1) * CW]


def attn_grads(S, R, q, hs, dls, ctxs, dys):
    n = len(hs)
    T, D = hs[0].shape
    CW = ctxs[0].shape[1]
    DR = D // S
    ru = DR // R
    blk = 256
    G = D // blk
    keep = lambda s: pl.BlockSpec(s, lambda i, q: (0,) * len(s), pipeline_mode=pl.Buffered(1))
    shapes = [(R, S * 2 * ru, CW), (R, (D // CW + S) * ru, CW)]
    return pl.pallas_call(
        functools.partial(attn_grads_kernel, n, S, R),
        grid_spec=pltpu.PrefetchScalarGridSpec(
            num_scalar_prefetch=1,
            grid=(G,),
            in_specs=[pl.BlockSpec((T, blk), lambda i, q: (0, i))] * n
            + [keep((3, T, CW))] * n
            + [pl.BlockSpec((T, CW // G), lambda i, q: (0, i))] * n
            + [keep(dys[0].shape)] * len(dys),
            out_specs=[pl.BlockSpec(s, lambda i, q: (0, 0, 0)) for s in shapes],
        ),
        out_shape=[SD(s, BF) for s in shapes],
        compiler_params=pltpu.CompilerParams(vmem_limit_bytes=60 * MIB),
        cost_estimate=pl.CostEstimate(flops=8 * n * T * D * CW, bytes_accessed=2 * n * T * (2 * D + 4 * CW) + 8 * D * CW, transcendentals=0),
    )(q, *hs, *dls, *ctxs, *dys)


def attn_finish_kernel(S, ru, k, n, q_ref, *refs):
    firsts, seconds = refs[:n], refs[n : 2 * n]
    out, qkv = refs[2 * n :]
    CW = seconds[0].shape[2]
    D = out.shape[1]
    for c in range(n):
        r = slice(c * ru, (c + 1) * ru)
        for j in range(k):
            out[r, j * CW : (j + 1) * CW] = seconds[c][0, j * ru : (j + 1) * ru, :].astype(F32)
        for t in range(S):
            for p in range(3):
                a = (t * 2 + p) * ru if p < 2 else (k + t) * ru
                v = (firsts if p < 2 else seconds)[c][0, a : a + ru, :]
                qkv[r, p * D + t * CW : p * D + (t + 1) * CW] = v.astype(F32)


def attn_finish(S, q, g1, g2):
    R, per1, CW = g1.shape
    per2 = g2.shape[1]
    D = CW * S
    ru = D // S // R
    n = 4
    block = lambda per, k, c: pl.BlockSpec((1, per, CW), lambda i, q: ((i * n + c) ^ q[k], 0, 0))
    return pl.pallas_call(
        functools.partial(attn_finish_kernel, S, ru, S, n),
        grid_spec=pltpu.PrefetchScalarGridSpec(
            num_scalar_prefetch=1,
            grid=(R // n,),
            in_specs=[block(per1, 0, c) for c in range(n)] + [block(per2, 1, c) for c in range(n)],
            out_specs=[pl.BlockSpec((n * ru, D), lambda c, q: (c, 0)), pl.BlockSpec((n * ru, 3 * D), lambda c, q: (c, 0))],
        ),
        out_shape=[SD((CW, D), F32), SD((D // S, 3 * D), F32)],
        compiler_params=pltpu.CompilerParams(vmem_limit_bytes=40 * MIB),
        cost_estimate=pl.CostEstimate(flops=0, bytes_accessed=6 * R * (per1 + per2) * CW, transcendentals=0),
    )(q, *[g1] * n, *[g2] * n)


def rows_kernel(act, dpre, wu, wd, dl, ctx, wqkv, wo, x, gb, y, g, ln, yacc, d1, d2):
    f = pl.program_id(0)
    last = pl.num_programs(0) - 1
    N = x.shape[0]
    CW = ctx.shape[1]

    @pl.when(f == 0)
    def _():
        yacc[...] = dnn(ctx[...], wo[...])
        d1[...] = sum(dnt(dl[p], wqkv[:, p * CW : (p + 1) * CW]) for p in range(3))
        d2[...] = jnp.zeros_like(d2)

    yacc[...] += dnn(act[...], wd[...])
    d2[...] += dnt(dpre[...], wu[...])

    @pl.when(f == last)
    def _():
        ln[...] = jnp.zeros_like(ln)

        @pl.loop(0, N // 128)
        def _(i):
            r = tile(i, 128)
            xh, _ = normed(x[r, :])
            a = d1[r, :]
            b = d2[r, :]
            y[r, :] = yacc[r, :].astype(BF)
            g[r, :] = (a * gb[0:1, :] + b * gb[2:3, :]).astype(BF)
            ln[0:1, :] += jnp.sum(a * xh, axis=0, keepdims=True)
            ln[1:2, :] += jnp.sum(a, axis=0, keepdims=True)
            ln[2:3, :] += jnp.sum(b * xh, axis=0, keepdims=True)
            ln[3:4, :] += jnp.sum(b, axis=0, keepdims=True)


def branch_rows(j, x, act, dpre, wu, wd, dl, ctx, wqkv, wo, gb):
    N, D = x.shape
    FL = wu.shape[1]
    CW = wo.shape[0]
    fb = min(512, FL)
    full = lambda s: pl.BlockSpec(s, lambda f: (0,) * len(s), pipeline_mode=pl.Buffered(1))
    keep = lambda s: pl.BlockSpec(s, lambda f: (0,) * len(s))
    rows = pl.BlockSpec((N, fb), lambda f: (0, f))
    return pl.pallas_call(
        rows_kernel,
        grid=(FL // fb,),
        in_specs=[rows, rows, pl.BlockSpec((D, fb), lambda f: (0, f)), pl.BlockSpec((fb, D), lambda f: (f, 0))]
        + [
            pl.BlockSpec((3, N, CW), lambda f: (0, j, 0), pipeline_mode=pl.Buffered(1)),
            pl.BlockSpec((N, CW), lambda f: (j, 0), pipeline_mode=pl.Buffered(1)),
        ]
        + [full((D, 3 * CW)), full((CW, D)), full((N, D)), full((4, D))],
        out_specs=[keep((N, D)), keep((N, D)), keep((4, D))],
        out_shape=[SD((N, D), BF), SD((N, D), BF), SD((4, D), F32)],
        scratch_shapes=[pltpu.VMEM((N, D), F32)] * 3,
        compiler_params=pltpu.CompilerParams(vmem_limit_bytes=60 * MIB),
        cost_estimate=pl.CostEstimate(
            flops=4 * N * D * FL + 8 * N * D * CW, bytes_accessed=4 * (N + D) * FL + 8 * (N + D) * CW + 6 * N * D, transcendentals=0
        ),
    )(act, dpre, wu, wd, dl, ctx, wqkv, wo, x, gb)


def final_kernel(S, first, PT, *refs):
    it = iter(refs)
    take = lambda n: [next(it) for _ in range(n)]
    x, dy = take(2)
    ys = take(S)
    gs = take(S)
    (vb,) = take(1)
    if not first:
        take(4)
    po, co, pg, cg = take(4)
    i = pl.program_id(0)
    xv = x[...].astype(F32)
    xh, inv = normed(xv)
    y = xv + vb[0:1, :] + sum(r[...].astype(F32) for r in ys) + vb[1:2, :]
    gsum = sum(r[...].astype(F32) for r in gs)
    dx = (gsum - jnp.mean(gsum, axis=-1, keepdims=True) - xh * jnp.mean(gsum * xh, axis=-1, keepdims=True)) * inv
    out = y.astype(BF)
    grad = dy[...].astype(F32) + dx

    @pl.when(i < PT)
    def _():
        po[0] = out
        pg[0] = grad

    @pl.when(i >= PT)
    def _():
        co[0] = out
        cg[0] = grad


def final_rows(m, MB, PD, x, dy, ys, gs, vb, prior):
    S = len(ys)
    N, D = x.shape
    CR = N - PD
    RT = 128
    PT = PD // RT
    first = prior is None
    row = pl.BlockSpec((RT, D), lambda i: (i, 0))
    pspec = pl.BlockSpec((1, RT, D), lambda i: (m, jnp.minimum(i, PT - 1), 0))
    cspec = pl.BlockSpec((1, RT, D), lambda i: (m, jnp.maximum(i - PT, 0), 0))
    hbm = pl.BlockSpec(memory_space=pl.ANY)
    n_in = 2 * S + 3
    return pl.pallas_call(
        functools.partial(final_kernel, S, first, PT),
        grid=(N // RT,),
        in_specs=[row] * (2 * S + 2) + [pl.BlockSpec((2, D), lambda i: (0, 0))] + ([] if first else [hbm] * 4),
        out_specs=[pspec, cspec, pspec, cspec],
        out_shape=[SD((MB, PD, D), BF), SD((MB, CR, D), BF), SD((MB, PD, D), F32), SD((MB, CR, D), F32)],
        input_output_aliases={} if first else {n_in + k: k for k in range(4)},
        compiler_params=pltpu.CompilerParams(vmem_limit_bytes=32 * MIB),
        cost_estimate=pl.CostEstimate(flops=20 * N * D, bytes_accessed=(4 * S + 10) * N * D, transcendentals=0),
    )(x, dy, *ys, *gs, vb, *(() if first else prior))


def shifted(value, S, j):
    return lax.ppermute(value, "shard", [(i, (i + j) % S) for i in range(S)])


def canonical(slots, me, S, back):
    if S == 1:
        return slots
    if S == 2:
        a, b = slots
        return [jnp.where(me == 0, a, b), jnp.where(me == 0, b, a)]
    stacked = jnp.stack(slots, axis=0)
    return [
        lax.dynamic_index_in_dim(stacked, lax.rem((me - s if back else s - me) + S, S), 0, keepdims=False) for s in range(S)
    ]


def exchanged(value, R, bit):
    return lax.ppermute(value, "rep", [(i, i ^ bit) for i in range(R)])


def columns_for(weight, me, S, j, parts, row=0, rows=None):
    cols = weight.shape[1] // parts
    rows = weight.shape[0] if rows is None else rows
    w = cols // S
    at = lax.rem(me + j, S) * w
    got = [lax.dynamic_slice(weight, (row, p * cols + at), (rows, w)) for p in range(parts)]
    return got[0] if parts == 1 else jnp.concatenate(got, axis=1)


def my_columns_halves(weight, me, S, R, ahead):
    rows = weight.shape[0]
    rep = lax.axis_index("rep")
    core = rep % 2
    y = (rep // 2) % 2
    n = rows // 4
    cut = [columns_for(weight, me, S, j, 1, (2 * core + y) * n, n) for j in range(1, S)]
    slots = [columns_for(weight, me, S, 0, 1)]

    def both(piece, other, first):
        return jnp.concatenate([jnp.where(first, piece, other), jnp.where(first, other, piece)], axis=0)

    for j in range(1, S):
        piece = shifted(cut[j - 1], S, j)
        piece, _ = lax.optimization_barrier((piece, ahead))
        pair = both(piece, exchanged(piece, R, 2), y == 0)
        slots.append(both(pair, exchanged(pair, R, 1), core == 0))
    return jnp.concatenate(canonical(slots, me, S, True), axis=0), piece


def my_columns(weight, me, S, R, parts):
    rows = weight.shape[0]
    own = columns_for(weight, me, S, 0, parts)
    if S == 1:
        return own
    rep = lax.axis_index("rep")
    chunk = rows // R
    got = []
    for j in range(1, S):
        got.append(shifted(columns_for(weight, me, S, j, parts, rep * chunk, chunk), S, j))
    others = lax.all_gather(jnp.stack(got, axis=0), "rep", axis=1, tiled=True)
    return jnp.concatenate(canonical([own] + [others[j] for j in range(S - 1)], me, S, True), axis=0)


def add_low(a, b):
    return (a.astype(F32) + b.astype(F32)).astype(BF)


def orders(R):
    bits = [1 << i for i in range(R.bit_length() - 1)]
    return bits, bits[:1] + bits[2:] + bits[1:2]


def place(rep, order):
    q = jnp.zeros((), jnp.int32)
    for bit in order:
        q = 2 * q + (rep & bit) // bit
    return q


def beside_it(got, key, beside):
    if key in beside:
        got, beside[key] = lax.optimization_barrier((got, beside[key]))
    return got


def halving(pair, R, beside):
    pair = list(pair)
    for i, bits in enumerate(zip(*orders(R))):
        h = pair[0].shape[0] // 2
        got = beside_it([exchanged(g[h:], R, bit) for g, bit in zip(pair, bits)], i, beside)
        pair = [add_low(g[:h], t) for g, t in zip(pair, got)]
    return [g[0] for g in pair]


def doubling(parts, R, beside):
    pair = [p[None] for p in parts]
    for i, bits in reversed(list(enumerate(zip(*orders(R))))):
        got = [exchanged(g, R, bit) for g, bit in zip(pair, bits)]
        got = beside_it(got, i, beside)
        pair = [jnp.concatenate([g, t], axis=0) for g, t in zip(pair, got)]
    return pair


def sum_all(v, S, R):
    bit = 1
    while bit < R:
        v = v + exchanged(v, R, bit)
        bit *= 2
    return v


def swap_shards(part, me, S, head):
    n = (part.shape[0] - head) // S
    slots = []
    for j in range(S):
        b = lax.dynamic_slice_in_dim(part, head + lax.rem(me + j, S) * n, n, 0)
        slots.append(shifted(b, S, j) if j else b)
    return jnp.concatenate(([part[:head]] if head else []) + canonical(slots, me, S, True), axis=0)


def reduce_rows(grad):
    part = lax.psum_scatter(grad, "rep", scatter_dimension=0, tiled=True)
    return lax.all_gather(part, "rep", axis=0, tiled=True).astype(F32)


def reduce_columns(grad, me, S, parts):
    rows, cols = grad.shape
    part = lax.psum_scatter(grad.reshape(S, rows // S, cols), "rep", scatter_dimension=1, tiled=True)
    slots = [lax.dynamic_index_in_dim(part, me, 0, keepdims=False)]
    for j in range(1, S):
        slots.append(shifted(lax.dynamic_index_in_dim(part, lax.rem(me + j, S), 0, keepdims=False), S, j))
    slots = [s.reshape(s.shape[0], parts, cols // parts) for s in slots]
    whole = jnp.stack(canonical(slots, me, S, True), axis=2).reshape(-1, S * cols)
    return lax.all_gather(whole, "rep", axis=0, tiled=True).astype(F32)


def rotary_tables(PR, CR, CL):
    pos = np.concatenate([np.arange(PR), PR + np.arange(CR) % CL]).astype(np.float32)
    half = ROT // 2
    freq = np.exp(np.arange(half, dtype=np.float32) * np.float32(-2.0 * math.log(10000.0) / ROT)).astype(np.float32)
    ang = (pos[:, None] * freq[None, :]).astype(np.float32)
    c = np.cos(ang)
    s = np.sin(ang)
    n = pos.shape[0]
    one = np.ones((n, HD - ROT), np.float32)
    zero = np.zeros((n, HD - ROT), np.float32)
    z8 = np.zeros((n, half), np.float32)
    tabs = ([c, c, one], [-s, z8, zero], [z8, s, zero])
    return [jnp.asarray(np.tile(np.concatenate(t, axis=1), (1, 128 // HD)), F32) for t in tabs]


def per_device(
    prompt_in,
    cont_in,
    prompt_cot,
    cont_cot,
    ln1_gain,
    ln1_bias,
    ln2_gain,
    ln2_bias,
    qkv_weight,
    qkv_bias,
    out_weight,
    out_bias,
    up_weight,
    up_bias,
    down_weight,
    down_bias,
):
    S = lax.axis_size("shard")
    R = lax.axis_size("rep")
    me = lax.axis_index("shard")
    MB, _, PD, D = prompt_in.shape
    CD, CL = cont_in.shape[2:4]
    CR = CD * CL
    N = PD + CR
    CW = D // S
    FL = up_weight.shape[1] // S
    me_arr = jnp.reshape(me, (1,)).astype(jnp.int32)

    X = [[jnp.concatenate([prompt_in[m, 0], cont_in[m, 0].reshape(CR, D)], axis=0)] for m in range(MB)]
    DY = [[jnp.concatenate([prompt_cot[m, 0], cont_cot[m, 0].reshape(CR, D)], axis=0)] for m in range(MB)]

    w_up, brought = my_columns_halves(up_weight, me, S, R, (X[0], DY[0]))
    vecs_in = (ln1_gain, ln1_bias, ln2_gain, ln2_bias, out_bias, down_bias, qkv_bias)
    (vecs_in, qkv_weight), brought = lax.optimization_barrier(((vecs_in, qkv_weight), brought))

    one = lambda v: v.astype(F32).reshape(-1, CW)
    small = jnp.concatenate([one(v) for v in vecs_in], axis=0)
    slots = [small] + [shifted(small, S, j) for j in range(1, S)]
    whole = jnp.stack(canonical(slots, me, S, True), axis=0)
    vec = whole[:, :6].transpose(1, 0, 2).reshape(6, D)
    gb = vec[0:4]
    gb1 = vec[0:2]
    gb2 = vec[2:4]
    vb = vec[4:6]
    bqkv = whole[:, 6:].reshape(3, S, CW)
    bqkv = lax.dynamic_index_in_dim(bqkv, me, 1, keepdims=False).reshape(1, 3 * CW)
    bup = up_bias.astype(F32).reshape(1, FL)

    w_qkv = my_columns(qkv_weight, me, S, R, 3)

    tabs = rotary_tables(PD * S, CR * S, CL)
    src = [(X[m][0], DY[m][0]) for m in range(MB)]
    src[1:], w_up = lax.optimization_barrier((src[1:], w_up))
    for m in range(MB):
        for j in range(1, S):
            X[m].append(shifted(src[m][0], S, S - j))
            DY[m].append(shifted(src[m][1], S, S - j))

    ff = [[None] * S for _ in range(MB)]

    def mlp(m, j):
        ff[m][j] = mlp_rows(X[m][j], DY[m][j], w_up, bup, down_weight, gb2)

    for m in range(MB):
        mlp(m, 0)
    rest = []

    def attend(m):
        rest.append(list(attn_group(S, PD, CL, me_arr, X[m], DY[m], w_qkv, bqkv, out_weight, gb1, tabs)))

    def rows(m, j):
        f = ff[m][j]
        return branch_rows(j, X[m][j], f[0], f[1], w_up, down_weight, rest[m][0], rest[m][1], w_qkv, out_weight, gb)

    def far_rows(m):
        r = [rows(m, j) for j in range(1, S)]
        got = [[shifted(r[j - 1][i], S, j) for j in range(1, S)] for i in range(2)]
        return got, [v[2] for v in r]

    chunked = (D // S // R) % 16 == 0 and R & (R - 1) == 0
    rep = lax.axis_index("rep")
    late = [(MB - 1, j) for j in range(1, S)]
    early = [(m, j) for m in range(MB) for j in range(S) if (m, j) not in late]
    of = lambda set_, k: [ff[m][j][k] for m, j in set_]
    for m, j in early:
        if j:
            mlp(m, j)
    if chunked:
        gmlp = mlp_grads(S, R, of(early, 0), [DY[m][j] for m, j in early], of(early, 2), of(early, 1))
        w_up, gmlp = lax.optimization_barrier((w_up, gmlp))
    for m, j in late:
        mlp(m, j)
    if chunked:
        if late:
            gmlp = mlp_grads(S, R, of(late, 0), [DY[m][j] for m, j in late], of(late, 2), of(late, 1), gmlp)
        part = lax.psum_scatter(gmlp, "rep", scatter_dimension=0, tiled=True)[0]
        w_qkv, gmlp = lax.optimization_barrier((w_qkv, gmlp))
    for m in range(MB):
        attend(m)
        if m + 1 < MB:
            w_qkv, rest[m][3] = lax.optimization_barrier((w_qkv, rest[m][3]))
    every = early + late
    def vectors(sums):
        ln1 = sum(o[0:2] for o in sums)
        ln2 = sum(o[2:4] for o in sums)
        db_out = sum(jnp.sum(DY[m][0].astype(F32), axis=0) for m in range(MB)).reshape(-1, CW)
        mine = (jnp.arange(S) == me).astype(F32)
        db_qkv = (sum(r[3] for r in rest)[:, None, :] * mine[None, :, None]).reshape(-1, CW)
        db_up = (sum(of(every, 3)) * mine[:, None]).reshape(-1, CW)
        return jnp.concatenate([ln1.reshape(-1, CW), ln2.reshape(-1, CW), db_out, db_qkv, db_up], axis=0)

    def finals(m, o, got, prior):
        return final_rows(m, MB, PD, X[m][0], DY[m][0], [o[0]] + got[0], [o[1]] + got[1], vb, prior)

    hs, dls, ctxs = [[r[k] for r in rest] for k in (2, 0, 1)]
    if chunked:
        q = jnp.stack([place(rep, order) for order in orders(R)]).astype(jnp.int32)
        gatt = attn_grads(S, R, q, hs, dls, ctxs, [DY[m][j] for m in range(MB) for j in range(S)])
        part, gatt = lax.optimization_barrier((part, gatt))
        part = swap_shards(part, me, S, FL // R)
        gmlp_all = lax.all_gather(part, "rep", axis=0, tiled=False)
        dls, _ = lax.optimization_barrier(([r[0] for r in rest], part))
        for m in range(MB):
            rest[m][0] = dls[m]
        levels = R.bit_length() - 1
        beside = {}
        far, mine = [], []
        for m in range(MB):
            far.append(far_rows(m))
            beside.setdefault(min(m, levels - 1), {})["far", m] = far[m][1]
            dls, beside[min(m, levels - 1)] = lax.optimization_barrier(([r[0] for r in rest], beside[min(m, levels - 1)]))
            for k in range(MB):
                rest[k][0] = dls[k]
        for m in range(MB):
            mine.append(rows(m, 0))
            beside.setdefault(min(MB + m, levels - 1), {})["own", m] = mine[m]
        beside.setdefault(levels - 1, {})["got", 0] = far[0][0]
        half = halving(gatt, R, beside)
        done = {k: v for d in beside.values() for k, v in d.items()}
        sums = [v for m in range(MB) for v in done["far", m]]
        mine = [done["own", m] for m in range(MB)]
        vecs = sum_all(vectors(sums + [o[2] for o in mine]), S, R)
        got = [f[0] for f in far]
        got[0] = done["got", 0]
        beside = {1: (got[1:], mlp_finish(S, gmlp_all, FL), vecs)}
        k = D // CW * (D // S // R)
        g1, g2 = doubling([swap_shards(half[0], me, S, 0), swap_shards(half[1], me, S, k)], R, beside)
        got[1:], (g_down, g_up), vecs = beside[1]
        outs = None
        for m in range(MB):
            outs = finals(m, mine[m], got[m], outs)
        g_out, g_qkv = attn_finish(S, q, g1, g2)
    else:
        dls, ctxs, hs = [[r[k] for r in rest] for k in (0, 1, 2)]
        far = [far_rows(m) for m in range(MB)]
        mine = [rows(m, 0) for m in range(MB)]
        g_down = reduce_rows(tn_sum(of(every, 0), [DY[m][j] for m, j in every], 256))
        g_up = reduce_columns(tn_sum(of(every, 2), of(every, 1), 256), me, S, 1)
        dycs = [jnp.concatenate(DY[m], axis=0) for m in range(MB)]
        g_out = reduce_rows(tn_sum(ctxs, dycs, 256))
        g_qkv = reduce_columns(tn_sum(hs, dls, 256), me, S, 3)
        vecs = sum_all(vectors([v for f in far for v in f[1]] + [o[2] for o in mine]), S, R)
        outs = None
        for m in range(MB):
            outs = finals(m, mine[m], far[m][0], outs)
    tot = vecs + sum(shifted(vecs, S, j) for j in range(1, S))
    held = lambda a, n: lax.dynamic_slice_in_dim(tot, a + me * n, n, 0).reshape(-1)
    v_ln1g, v_ln1b, v_ln2g, v_ln2b, v_out = [held(k * S, 1) for k in range(5)]
    v_qkv = held(5 * S, 3)
    v_up = held(8 * S, FL // CW)

    po, co, pg, cg = outs
    return (
        po.reshape(MB, 1, PD, D),
        co.reshape(MB, 1, CD, CL, D),
        pg.reshape(MB, 1, PD, D),
        cg.reshape(MB, 1, CD, CL, D),
        v_ln1g,
        v_ln1b,
        v_ln2g,
        v_ln2b,
        g_qkv,
        v_qkv,
        g_out,
        v_out,
        g_up,
        v_up,
        g_down,
        v_out,
    )


def solution(mesh):
    tokens = (
        P(None, "rep", "shard", None),
        P(None, "rep", "shard", None, None),
        P(None, "rep", "shard", None),
        P(None, "rep", "shard", None, None),
    )
    vec = P("shard")
    mat = P("shard", None)
    params = (vec, vec, vec, vec, mat, vec, mat, vec, mat, vec, mat, vec)
    return jax.shard_map(
        per_device, mesh=mesh, in_specs=tokens + params, out_specs=tokens + params, check_vma=False
    )
```

```python
import functools
import math

import jax
import jax.numpy as jnp
import numpy as np
from jax import lax
from jax.experimental import pallas as pl
from jax.experimental.pallas import tpu as pltpu
from jax.sharding import PartitionSpec as P

H = 16
HD = 64
ROT = 16
EPS = 1e-05
F32 = jnp.float32
BF = jnp.bfloat16
MIB = 1024 * 1024
SD = jax.ShapeDtypeStruct


def dnn(a, b):
    return lax.dot_general(a, b, (((1,), (0,)), ((), ())), preferred_element_type=F32)


def dnt(a, b):
    return lax.dot_general(a, b, (((1,), (1,)), ((), ())), preferred_element_type=F32)


def dtn(a, b):
    return lax.dot_general(a, b, (((0,), (0,)), ((), ())), preferred_element_type=F32)


def normed(rows):
    x = rows.astype(F32)
    c = x - jnp.mean(x, axis=-1, keepdims=True)
    inv = lax.rsqrt(jnp.mean(c * c, axis=-1, keepdims=True) + EPS)
    return c * inv, inv


def tile(i, n):
    return pl.ds(pl.multiple_of(i * n, n), n)


def rows_tile(n, most):
    t = most
    while n % t:
        t -= 8
    return t


def mlp_kernel(rt, x_ref, dy_ref, wu_ref, bu_ref, wd_ref, gb_ref, act_ref, dpre_ref, h_ref, bu_out):
    rows = x_ref.shape[0]

    @pl.when(pl.program_id(0) == 0)
    def _():
        @pl.loop(0, rows // 128)
        def _(i):
            r = tile(i, 128)
            xh, _ = normed(x_ref[r, :])
            h_ref[r, :] = (xh * gb_ref[0:1, :] + gb_ref[1:2, :]).astype(BF)

    def step(i, bsum):
        r = tile(i, rt)
        pre = dnn(h_ref[r, :], wu_ref[...]) + bu_ref[...]
        da = dnt(dy_ref[r, :], wd_ref[...])
        cdf = 0.5 * (1.0 + lax.erf(pre * 0.7071067811865476))
        act_ref[r, :] = (pre * cdf).astype(BF)
        dpre = (da * (cdf + pre * jnp.exp(-0.5 * pre * pre) * 0.3989422804014327)).astype(BF)
        dpre_ref[r, :] = dpre
        return bsum + jnp.sum(dpre.astype(F32), axis=0, keepdims=True)

    bu_out[...] = lax.fori_loop(0, rows // rt, step, jnp.zeros(bu_out.shape, F32))


def mlp_rows(x, dy, wu, bu, wd, gb):
    rows, width = x.shape
    hidden = wu.shape[1]
    fb = min(512, hidden)
    full = lambda s: pl.BlockSpec(s, lambda f: (0,) * len(s))
    return pl.pallas_call(
        functools.partial(mlp_kernel, rows_tile(rows, 640)),
        grid=(hidden // fb,),
        in_specs=[
            full((rows, width)),
            full((rows, width)),
            pl.BlockSpec((width, fb), lambda f: (0, f)),
            pl.BlockSpec((1, fb), lambda f: (0, f)),
            pl.BlockSpec((fb, width), lambda f: (f, 0)),
            full((2, width)),
        ],
        out_specs=[
            pl.BlockSpec((rows, fb), lambda f: (0, f)),
            pl.BlockSpec((rows, fb), lambda f: (0, f)),
            full((rows, width)),
            pl.BlockSpec((1, fb), lambda f: (0, f)),
        ],
        out_shape=[SD((rows, hidden), BF), SD((rows, hidden), BF), SD((rows, width), BF), SD((1, hidden), F32)],
        compiler_params=pltpu.CompilerParams(vmem_limit_bytes=60 * MIB),
        cost_estimate=pl.CostEstimate(
            flops=4 * rows * width * hidden, bytes_accessed=4 * (width * hidden + rows * hidden) + 6 * rows * width, transcendentals=2 * rows * hidden
        ),
    )(x, dy, wu, bu, wd, gb)


def roll8(x, left):
    w = x.shape[-1]
    return pltpu.roll(x, (w - 8) if left else 8, 1)


def attn_kernel(S, PD, CL, QB, HG, me_ref, *refs):
    it = iter(refs)
    take = lambda n: [next(it) for _ in range(n)]
    stacked = S > 2
    per = 1 if stacked else S
    xs = take(per)
    dys = take(per)
    wq, wk, wv = take(3)
    bq, bk, bv = take(3)
    wo, gb = take(2)
    cr, s1r, s2r = take(3)
    dl, ctx, h1, db = take(4)
    q_s, k_s, v_s, dc_s, kT, vT, dk_s, dv_s = take(8)
    g = pl.program_id(0)
    me = me_ref[0]
    N = xs[0].shape[-2]
    T = N * S
    PR = PD * S
    CR = N - PD
    W = HG * HD

    def every_slot(fn):
        if stacked:

            @pl.loop(0, S)
            def _(j):
                fn(j, lambda refs: refs[0].at[j])

        else:
            for j in range(S):
                fn(j, lambda refs: refs[j])

    def slot_rows(start, n):
        if start < PR:
            s, off = start // PD, start % PD
        else:
            s, off = (start - PR) // CR, PD + (start - PR) % CR
        return pl.ds(pl.multiple_of(lax.rem(s - me + S, S) * N + off, 128), n)

    def pieces(start, n):
        step = min(n, PD if start < PR else CR)
        return [(i, step) for i in range(0, n, step)]

    @pl.when(g == 0)
    def _():
        def load(j, of):
            x = of(xs)

            @pl.loop(0, N // 128)
            def _(i):
                xh, _ = normed(x[tile(i, 128), :])
                h1[pl.ds(pl.multiple_of(j * N + i * 128, 128), 128), :] = (xh * gb[0:1, :] + gb[1:2, :]).astype(BF)

        every_slot(load)

    def rot(y, r, scale):
        c = cr[r, :]
        s1 = s1r[r, :]
        s2 = s2r[r, :]
        out = []
        for p in range(W // 128):
            z = y[:, p * 128 : (p + 1) * 128]
            z = (z * c + roll8(z, True) * s1 + roll8(z, False) * s2).astype(BF)
            out.append(z * jnp.asarray(scale, BF) if scale != 1.0 else z)
        return jnp.concatenate(out, axis=1) if len(out) > 1 else out[0]

    def proj(j, of):
        s = lax.rem(me + j, S)
        rp = pl.ds(pl.multiple_of(s * PD, 128), PD)
        rc = pl.ds(pl.multiple_of(PR + s * CR, 128), CR)
        hh = h1[pl.ds(pl.multiple_of(j * N, 128), N), :]
        y = dnn(hh, wq[...]) + bq[...]
        q_s[rp, :] = rot(y[:PD], rp, HD**-0.5)
        q_s[rc, :] = rot(y[PD:], rc, HD**-0.5)
        y = dnn(hh, wk[...]) + bk[...]
        k_s[rp, :] = rot(y[:PD], rp, 1.0)
        k_s[rc, :] = rot(y[PD:], rc, 1.0)
        y = (dnn(hh, wv[...]) + bv[...]).astype(BF)
        v_s[rp, :] = y[:PD]
        v_s[rc, :] = y[PD:]
        y = dnt(of(dys)[...], wo[...]).astype(BF)
        dc_s[rp, :] = y[:PD]
        dc_s[rc, :] = y[PD:]

    every_slot(proj)
    lane = lax.broadcasted_iota(jnp.int32, (1, 128), 1)
    row_i = lax.broadcasted_iota(jnp.int32, (QB, QB), 0)
    col_i = lax.broadcasted_iota(jnp.int32, (QB, QB), 1)
    causal = row_i <= col_i
    cmask = causal & ((row_i // CL) == (col_i // CL))
    blocks = []
    for i in range(PR // QB):
        blocks.append((i * QB, [(0, i * QB, None)] * (i > 0) + [(i * QB, QB, causal)]))
    for c in range((T - PR) // QB):
        blocks.append((PR + c * QB, [(0, PR, None), (PR + c * QB, QB, cmask)]))

    @pl.loop(0, W // 128)
    def _(p):
        lanes = tile(p, 128)
        kT[...] = k_s[:, lanes].T
        vT[...] = v_s[:, lanes].T
        dk_s[...] = jnp.zeros_like(dk_s)
        dv_s[...] = jnp.zeros_like(dv_s)
        def begin(q0, parts):
            qb = q_s[pl.ds(q0, QB), lanes]
            dcb = dc_s[pl.ds(q0, QB), lanes]
            out = []
            for h in range(2):
                sel = (lane >= HD * h) & (lane < HD * h + HD)
                qm = jnp.where(sel, qb, jnp.zeros_like(qb))
                dm = jnp.where(sel, dcb, jnp.zeros_like(dcb))
                ss = []
                for k0, n, mask in parts:
                    s = dnt(k_s[k0 : k0 + n, lanes], qm)
                    ss.append(s if mask is None else jnp.where(mask, s, -1e30))
                out.append((qm, dm, ss, [dnt(v_s[k0 : k0 + n, lanes], dm) for k0, n, _ in parts]))
            return out

        ahead = begin(*blocks[0])
        for b, (q0, parts) in enumerate(blocks):
            now = ahead
            if b + 1 < len(blocks):
                ahead = begin(*blocks[b + 1])
            rq = pl.ds(q0, QB)
            P_, DS, cT, dqT = [], [], [], []
            qh = [t[0] for t in now]
            dch = [t[1] for t in now]
            for h in range(2):
                _, _, ss, dps = now[h]
                m = functools.reduce(jnp.maximum, [jnp.max(s, axis=0, keepdims=True) for s in ss])
                es = [jnp.exp(s - m) for s in ss]
                rl = 1.0 / sum(jnp.sum(e, axis=0, keepdims=True) for e in es)
                ps = [e * rl for e in es]
                delta = sum(jnp.sum(a * b, axis=0, keepdims=True) for a, b in zip(ps, dps))
                P_.append([a.astype(BF) for a in ps])
                DS.append([(a * (b - delta)).astype(BF) for a, b in zip(ps, dps)])
                hr = slice(HD * h, HD * h + HD)
                cT.append(sum(dnn(vT[hr, k0 : k0 + n], a) for (k0, n, _), a in zip(parts, P_[h])))
                dqT.append(sum(dnn(kT[hr, k0 : k0 + n], a) for (k0, n, _), a in zip(parts, DS[h])))
            q2 = jnp.concatenate(qh, axis=0)
            dc2 = jnp.concatenate(dch, axis=0)
            for i, (k0, n, _) in enumerate(parts):
                dv_s[k0 : k0 + n, :] += dnn(jnp.concatenate([P_[0][i], P_[1][i]], axis=1), dc2)
                dk_s[k0 : k0 + n, :] += dnn(jnp.concatenate([DS[0][i], DS[1][i]], axis=1), q2)
            co = jnp.concatenate(cT, axis=0).T.astype(BF)
            z = jnp.concatenate(dqT, axis=0).T * (HD**-0.5)
            z = (z * cr[rq, :] - roll8(z, True) * s1r[rq, :] - roll8(z, False) * s2r[rq, :]).astype(BF)
            for o, n in pieces(q0, QB):
                ctx[slot_rows(q0 + o, n), lanes] = co[o : o + n]
                dl[0, slot_rows(q0 + o, n), lanes] = z[o : o + n]

        @pl.loop(0, S)
        def _(s):
            to = lax.rem(s - me + S, S) * N
            for src, off, n in ((s * PD, 0, PD), (PR + s * CR, PD, CR)):
                r = pl.ds(pl.multiple_of(src, 128), n)
                w = pl.ds(pl.multiple_of(to + off, 128), n)
                z = dk_s[r, :]
                z = z * cr[r, :] - roll8(z, True) * s1r[r, :] - roll8(z, False) * s2r[r, :]
                dl[1, w, lanes] = z.astype(BF)
                dl[2, w, lanes] = dv_s[r, :].astype(BF)

    for c in range(3):
        db[c : c + 1, :] = jnp.sum(dl[c].astype(F32), axis=0, keepdims=True)


def attn_group(S, PD, CL, me, xs, dys, wqkv, bqkv, wo, gb, tabs):
    N, D = xs[0].shape
    CW = wo.shape[0]
    T = N * S
    HG = 4 if CW % 256 == 0 else 2
    QB = 256
    W = HG * HD
    G = CW // W
    full = lambda s: pl.BlockSpec(s, lambda g, m: (0,) * len(s), pipeline_mode=pl.Buffered(1))
    tok = full((N, D))
    if S > 2:
        xs, dys = [[jnp.stack(v, axis=0)] for v in (xs, dys)]
        tok = full((S, N, D))
    wspec = lambda c: pl.BlockSpec((D, W), lambda g, m: (0, c * G + g))
    bspec = lambda c: pl.BlockSpec((1, W), lambda g, m: (0, c * G + g))
    return pl.pallas_call(
        functools.partial(attn_kernel, S, PD, CL, QB, HG),
        grid_spec=pltpu.PrefetchScalarGridSpec(
            num_scalar_prefetch=1,
            grid=(G,),
            in_specs=[tok] * (len(xs) + len(dys))
            + [wspec(0), wspec(1), wspec(2), bspec(0), bspec(1), bspec(2)]
            + [pl.BlockSpec((W, D), lambda g, m: (g, 0)), full((2, D))]
            + [full((T, 128))] * 3,
            out_specs=[
                pl.BlockSpec((3, T, W), lambda g, m: (0, 0, g)),
                pl.BlockSpec((T, W), lambda g, m: (0, g)),
                pl.BlockSpec((T, D), lambda g, m: (0, 0)),
                pl.BlockSpec((3, W), lambda g, m: (0, g)),
            ],
            scratch_shapes=[pltpu.VMEM((T, W), BF)] * 4 + [pltpu.VMEM((128, T), BF)] * 2 + [pltpu.VMEM((T, 128), F32)] * 2,
        ),
        out_shape=[SD((3, T, CW), BF), SD((T, CW), BF), SD((T, D), BF), SD((3, CW), F32)],
        compiler_params=pltpu.CompilerParams(vmem_limit_bytes=62 * MIB),
        cost_estimate=pl.CostEstimate(
            flops=8 * T * D * CW + 40 * T * T * CW, bytes_accessed=6 * T * D + 8 * T * CW + 8 * D * CW, transcendentals=T * T * CW // HD
        ),
    )(me, *xs, *dys, wqkv, wqkv, wqkv, bqkv, bqkv, bqkv, wo, gb, *tabs)


def tn_kernel(n, wide, *refs):
    a = refs[:n]
    b = refs[n : 2 * n]
    o = refs[2 * n]
    if wide == 0:
        o[...] = sum(dtn(x[...], y[...]) for x, y in zip(a, b)).astype(BF)
    else:
        w = b[0].shape[2]
        for c in range(wide):
            o[:, c * w : (c + 1) * w] = sum(dtn(x[...], y[c]) for x, y in zip(a, b)).astype(BF)


def tn_sum(a, b, block):
    n = len(a)
    rows, da = a[0].shape
    block = min(block, da)
    wide = b[0].shape[0] if b[0].ndim == 3 else 0
    db = b[0].shape[-1] * max(wide, 1)
    keep = lambda s: pl.BlockSpec(s, lambda i: (0,) * len(s), pipeline_mode=pl.Buffered(1))
    return pl.pallas_call(
        functools.partial(tn_kernel, n, wide),
        grid=(da // block,),
        in_specs=[pl.BlockSpec((rows, block), lambda i: (0, i))] * n + [keep(b[0].shape)] * n,
        out_specs=pl.BlockSpec((block, db), lambda i: (i, 0)),
        out_shape=SD((da, db), BF),
        compiler_params=pltpu.CompilerParams(vmem_limit_bytes=60 * MIB),
        cost_estimate=pl.CostEstimate(flops=2 * n * rows * da * db, bytes_accessed=2 * (n * rows * (da + db) + da * db), transcendentals=0),
    )(*a, *b)


def joined(refs):
    return jnp.concatenate([r[...] for r in refs], axis=0)


def down_kernel(n, more, *refs):
    o = refs[-1]
    t = dtn(joined(refs[:n]), joined(refs[n : 2 * n])).reshape(o.shape)
    o[...] = (t + refs[2 * n][...].astype(F32) if more else t).astype(BF)


def up_kernel(n, more, *refs):
    o = refs[-1]
    c, rows, w = o.shape
    t = dtn(joined(refs[:n]), joined(refs[n : 2 * n]))
    k = t.shape[1] // w
    for i in range(k):
        r = slice(i * (rows // k), (i + 1) * (rows // k))
        p = t[:, i * w : (i + 1) * w].reshape(c, rows // k, w)
        o[:, r, :] = (p + refs[2 * n][:, r, :].astype(F32) if more else p).astype(BF)


def mlp_grads(S, R, acts, dys, hs, dpres, g=None):
    n = len(acts)
    rows, FL = acts[0].shape
    D = dys[0].shape[1]
    DR = D // S
    blk = 256
    rd = FL // R
    ru = DR // R
    k = FL // D
    per = rd + S * ru * k
    keep = lambda s: pl.BlockSpec(s, lambda i: (0,) * len(s), pipeline_mode=pl.Buffered(1))
    steps = DR // blk
    more = g is not None
    hbm = pl.BlockSpec(memory_space=pl.ANY)

    def call(kernel, a, b, spec, g):
        width = b[0].shape[1]
        prior = [] if g is None else [g]
        return pl.pallas_call(
            functools.partial(kernel, n, more),
            grid=(a[0].shape[1] // blk,),
            in_specs=[pl.BlockSpec((rows, blk), lambda i: (0, i))] * n
            + [keep((rows, width))] * n
            + ([spec if more else hbm] if prior else []),
            out_specs=spec,
            out_shape=SD((R, per, D), BF),
            input_output_aliases={2 * n: 0} if prior else {},
            compiler_params=pltpu.CompilerParams(vmem_limit_bytes=60 * MIB),
            cost_estimate=pl.CostEstimate(
                flops=2 * n * rows * D * FL, bytes_accessed=2 * (n * rows * (D + FL) + (1 + more) * D * FL), transcendentals=0
            ),
        )(*a, *b, *prior)

    g = call(down_kernel, acts, dys, pl.BlockSpec((blk // rd, rd, D), lambda i: (i, 0, 0)), g)
    spec = pl.BlockSpec((blk // ru, ru * k, D), lambda i: (i % steps, rd // (ru * k) + i // steps, 0))
    return call(up_kernel, hs, dpres, spec, g)


def mlp_finish_kernel(S, rd, ru, g, down, up):
    n, per, D = g.shape
    k = (per - rd) // (S * ru)
    for c in range(n):
        down[c * rd : (c + 1) * rd, :] = g[c, :rd, :].astype(F32)
        for t in range(S * k):
            a = rd + t * ru
            up[c * ru : (c + 1) * ru, t * D : (t + 1) * D] = g[c, a : a + ru, :].astype(F32)


def mlp_finish(S, g, FL):
    R, per, D = g.shape
    rd = FL // R
    ru = D // S // R
    n = 4
    return pl.pallas_call(
        functools.partial(mlp_finish_kernel, S, rd, ru),
        grid=(R // n,),
        in_specs=[pl.BlockSpec((n, per, D), lambda c: (c, 0, 0))],
        out_specs=[pl.BlockSpec((n * rd, D), lambda c: (c, 0)), pl.BlockSpec((n * ru, S * FL), lambda c: (c, 0))],
        out_shape=[SD((FL, D), F32), SD((D // S, S * FL), F32)],
        compiler_params=pltpu.CompilerParams(vmem_limit_bytes=40 * MIB),
        cost_estimate=pl.CostEstimate(flops=0, bytes_accessed=6 * R * per * D, transcendentals=0),
    )(g)


def attn_grads_kernel(n, S, R, q_ref, *refs):
    h = refs[:n]
    dl = refs[n : 2 * n]
    ctx = refs[2 * n : 3 * n]
    dy = refs[3 * n : -2]
    first, second = refs[-2:]
    i = pl.program_id(0)
    q1 = q_ref[0]
    q2 = q_ref[1]
    blk = h[0].shape[1]
    D = dy[0].shape[1]
    DR = D // S
    CW = dl[0].shape[2]
    ru = DR // R
    k = D // CW
    steps = DR // blk
    s = i // steps
    base = (i % steps) * (blk // ru)
    for p in range(3):
        t = dtn(joined(h), jnp.concatenate([y[p] for y in dl], axis=0)).astype(BF)
        for c in range(blk // ru):
            v = t[c * ru : (c + 1) * ru, :]
            if p < 2:
                first[(base + c) ^ q1, pl.ds(s * 2 * ru + p * ru, ru), :] = v
            else:
                second[(base + c) ^ q2, pl.ds(k * ru + s * ru, ru), :] = v
    t = dtn(joined(ctx), joined(dy)).astype(BF)
    m = ctx[0].shape[1] // ru
    for c in range(m):
        for j in range(k):
            second[(i * m + c) ^ q2, j * ru : (j + 1) * ru, :] = t[c * ru : (c + 1) * ru, j * CW : (j + 1) * CW]


def attn_grads(S, R, q, hs, dls, ctxs, dys):
    n = len(hs)
    T, D = hs[0].shape
    CW = ctxs[0].shape[1]
    DR = D // S
    ru = DR // R
    blk = 256
    G = D // blk
    keep = lambda s: pl.BlockSpec(s, lambda i, q: (0,) * len(s), pipeline_mode=pl.Buffered(1))
    shapes = [(R, S * 2 * ru, CW), (R, (D // CW + S) * ru, CW)]
    return pl.pallas_call(
        functools.partial(attn_grads_kernel, n, S, R),
        grid_spec=pltpu.PrefetchScalarGridSpec(
            num_scalar_prefetch=1,
            grid=(G,),
            in_specs=[pl.BlockSpec((T, blk), lambda i, q: (0, i))] * n
            + [keep((3, T, CW))] * n
            + [pl.BlockSpec((T, CW // G), lambda i, q: (0, i))] * n
            + [keep(dys[0].shape)] * len(dys),
            out_specs=[pl.BlockSpec(s, lambda i, q: (0, 0, 0)) for s in shapes],
        ),
        out_shape=[SD(s, BF) for s in shapes],
        compiler_params=pltpu.CompilerParams(vmem_limit_bytes=60 * MIB),
        cost_estimate=pl.CostEstimate(flops=8 * n * T * D * CW, bytes_accessed=2 * n * T * (2 * D + 4 * CW) + 8 * D * CW, transcendentals=0),
    )(q, *hs, *dls, *ctxs, *dys)


def attn_finish_kernel(S, ru, k, n, q_ref, *refs):
    firsts, seconds = refs[:n], refs[n : 2 * n]
    out, qkv = refs[2 * n :]
    CW = seconds[0].shape[2]
    D = out.shape[1]
    for c in range(n):
        r = slice(c * ru, (c + 1) * ru)
        for j in range(k):
            out[r, j * CW : (j + 1) * CW] = seconds[c][0, j * ru : (j + 1) * ru, :].astype(F32)
        for t in range(S):
            for p in range(3):
                a = (t * 2 + p) * ru if p < 2 else (k + t) * ru
                v = (firsts if p < 2 else seconds)[c][0, a : a + ru, :]
                qkv[r, p * D + t * CW : p * D + (t + 1) * CW] = v.astype(F32)


def attn_finish(S, q, g1, g2):
    R, per1, CW = g1.shape
    per2 = g2.shape[1]
    D = CW * S
    ru = D // S // R
    n = 4
    block = lambda per, k, c: pl.BlockSpec((1, per, CW), lambda i, q: ((i * n + c) ^ q[k], 0, 0))
    return pl.pallas_call(
        functools.partial(attn_finish_kernel, S, ru, S, n),
        grid_spec=pltpu.PrefetchScalarGridSpec(
            num_scalar_prefetch=1,
            grid=(R // n,),
            in_specs=[block(per1, 0, c) for c in range(n)] + [block(per2, 1, c) for c in range(n)],
            out_specs=[pl.BlockSpec((n * ru, D), lambda c, q: (c, 0)), pl.BlockSpec((n * ru, 3 * D), lambda c, q: (c, 0))],
        ),
        out_shape=[SD((CW, D), F32), SD((D // S, 3 * D), F32)],
        compiler_params=pltpu.CompilerParams(vmem_limit_bytes=40 * MIB),
        cost_estimate=pl.CostEstimate(flops=0, bytes_accessed=6 * R * (per1 + per2) * CW, transcendentals=0),
    )(q, *[g1] * n, *[g2] * n)


def rows_kernel(act, dpre, wu, wd, dl, ctx, wqkv, wo, x, gb, y, g, ln, yacc, d1, d2):
    f = pl.program_id(0)
    last = pl.num_programs(0) - 1
    N = x.shape[0]
    CW = ctx.shape[1]

    @pl.when(f == 0)
    def _():
        yacc[...] = dnn(ctx[...], wo[...])
        d1[...] = sum(dnt(dl[p], wqkv[:, p * CW : (p + 1) * CW]) for p in range(3))
        d2[...] = jnp.zeros_like(d2)

    yacc[...] += dnn(act[...], wd[...])
    d2[...] += dnt(dpre[...], wu[...])

    @pl.when(f == last)
    def _():
        ln[...] = jnp.zeros_like(ln)

        @pl.loop(0, N // 128)
        def _(i):
            r = tile(i, 128)
            xh, _ = normed(x[r, :])
            a = d1[r, :]
            b = d2[r, :]
            y[r, :] = yacc[r, :].astype(BF)
            g[r, :] = (a * gb[0:1, :] + b * gb[2:3, :]).astype(BF)
            ln[0:1, :] += jnp.sum(a * xh, axis=0, keepdims=True)
            ln[1:2, :] += jnp.sum(a, axis=0, keepdims=True)
            ln[2:3, :] += jnp.sum(b * xh, axis=0, keepdims=True)
            ln[3:4, :] += jnp.sum(b, axis=0, keepdims=True)


def branch_rows(j, x, act, dpre, wu, wd, dl, ctx, wqkv, wo, gb):
    N, D = x.shape
    FL = wu.shape[1]
    CW = wo.shape[0]
    fb = min(512, FL)
    full = lambda s: pl.BlockSpec(s, lambda f: (0,) * len(s), pipeline_mode=pl.Buffered(1))
    keep = lambda s: pl.BlockSpec(s, lambda f: (0,) * len(s))
    rows = pl.BlockSpec((N, fb), lambda f: (0, f))
    return pl.pallas_call(
        rows_kernel,
        grid=(FL // fb,),
        in_specs=[rows, rows, pl.BlockSpec((D, fb), lambda f: (0, f)), pl.BlockSpec((fb, D), lambda f: (f, 0))]
        + [
            pl.BlockSpec((3, N, CW), lambda f: (0, j, 0), pipeline_mode=pl.Buffered(1)),
            pl.BlockSpec((N, CW), lambda f: (j, 0), pipeline_mode=pl.Buffered(1)),
        ]
        + [full((D, 3 * CW)), full((CW, D)), full((N, D)), full((4, D))],
        out_specs=[keep((N, D)), keep((N, D)), keep((4, D))],
        out_shape=[SD((N, D), BF), SD((N, D), BF), SD((4, D), F32)],
        scratch_shapes=[pltpu.VMEM((N, D), F32)] * 3,
        compiler_params=pltpu.CompilerParams(vmem_limit_bytes=60 * MIB),
        cost_estimate=pl.CostEstimate(
            flops=N * D * FL // 8, bytes_accessed=N * D, transcendentals=0
        ),
    )(act, dpre, wu, wd, dl, ctx, wqkv, wo, x, gb)


def final_kernel(S, first, PT, *refs):
    it = iter(refs)
    take = lambda n: [next(it) for _ in range(n)]
    x, dy = take(2)
    ys = take(S)
    gs = take(S)
    (vb,) = take(1)
    if not first:
        take(4)
    po, co, pg, cg = take(4)
    i = pl.program_id(0)
    xv = x[...].astype(F32)
    xh, inv = normed(xv)
    y = xv + vb[0:1, :] + sum(r[...].astype(F32) for r in ys) + vb[1:2, :]
    gsum = sum(r[...].astype(F32) for r in gs)
    dx = (gsum - jnp.mean(gsum, axis=-1, keepdims=True) - xh * jnp.mean(gsum * xh, axis=-1, keepdims=True)) * inv
    out = y.astype(BF)
    grad = dy[...].astype(F32) + dx

    @pl.when(i < PT)
    def _():
        po[0] = out
        pg[0] = grad

    @pl.when(i >= PT)
    def _():
        co[0] = out
        cg[0] = grad


def final_rows(m, MB, PD, x, dy, ys, gs, vb, prior):
    S = len(ys)
    N, D = x.shape
    CR = N - PD
    RT = 128
    PT = PD // RT
    first = prior is None
    row = pl.BlockSpec((RT, D), lambda i: (i, 0))
    pspec = pl.BlockSpec((1, RT, D), lambda i: (m, jnp.minimum(i, PT - 1), 0))
    cspec = pl.BlockSpec((1, RT, D), lambda i: (m, jnp.maximum(i - PT, 0), 0))
    hbm = pl.BlockSpec(memory_space=pl.ANY)
    n_in = 2 * S + 3
    return pl.pallas_call(
        functools.partial(final_kernel, S, first, PT),
        grid=(N // RT,),
        in_specs=[row] * (2 * S + 2) + [pl.BlockSpec((2, D), lambda i: (0, 0))] + ([] if first else [hbm] * 4),
        out_specs=[pspec, cspec, pspec, cspec],
        out_shape=[SD((MB, PD, D), BF), SD((MB, CR, D), BF), SD((MB, PD, D), F32), SD((MB, CR, D), F32)],
        input_output_aliases={} if first else {n_in + k: k for k in range(4)},
        compiler_params=pltpu.CompilerParams(vmem_limit_bytes=32 * MIB),
        cost_estimate=pl.CostEstimate(flops=20 * N * D, bytes_accessed=(4 * S + 10) * N * D, transcendentals=0),
    )(x, dy, *ys, *gs, vb, *(() if first else prior))


def shifted(value, S, j):
    return lax.ppermute(value, "shard", [(i, (i + j) % S) for i in range(S)])


def canonical(slots, me, S, back):
    if S == 1:
        return slots
    if S == 2:
        a, b = slots
        return [jnp.where(me == 0, a, b), jnp.where(me == 0, b, a)]
    stacked = jnp.stack(slots, axis=0)
    return [
        lax.dynamic_index_in_dim(stacked, lax.rem((me - s if back else s - me) + S, S), 0, keepdims=False) for s in range(S)
    ]


def exchanged(value, R, bit):
    return lax.ppermute(value, "rep", [(i, i ^ bit) for i in range(R)])


def columns_for(weight, me, S, j, parts, row=0, rows=None):
    cols = weight.shape[1] // parts
    rows = weight.shape[0] if rows is None else rows
    w = cols // S
    at = lax.rem(me + j, S) * w
    got = [lax.dynamic_slice(weight, (row, p * cols + at), (rows, w)) for p in range(parts)]
    return got[0] if parts == 1 else jnp.concatenate(got, axis=1)


def my_columns_halves(weight, me, S, R, ahead):
    rows = weight.shape[0]
    rep = lax.axis_index("rep")
    core = rep % 2
    y = (rep // 2) % 2
    n = rows // 4
    cut = [columns_for(weight, me, S, j, 1, (2 * core + y) * n, n) for j in range(1, S)]
    slots = [columns_for(weight, me, S, 0, 1)]

    def both(piece, other, first):
        return jnp.concatenate([jnp.where(first, piece, other), jnp.where(first, other, piece)], axis=0)

    for j in range(1, S):
        piece = shifted(cut[j - 1], S, j)
        piece, _ = lax.optimization_barrier((piece, ahead))
        pair = both(piece, exchanged(piece, R, 2), y == 0)
        slots.append(both(pair, exchanged(pair, R, 1), core == 0))
    return jnp.concatenate(canonical(slots, me, S, True), axis=0), cut[0]


def my_columns(weight, me, S, R, parts):
    rows = weight.shape[0]
    own = columns_for(weight, me, S, 0, parts)
    if S == 1:
        return own
    rep = lax.axis_index("rep")
    chunk = rows // R
    got = []
    for j in range(1, S):
        got.append(shifted(columns_for(weight, me, S, j, parts, rep * chunk, chunk), S, j))
    others = lax.all_gather(jnp.stack(got, axis=0), "rep", axis=1, tiled=True)
    return jnp.concatenate(canonical([own] + [others[j] for j in range(S - 1)], me, S, True), axis=0)


def add_low(a, b):
    return (a.astype(F32) + b.astype(F32)).astype(BF)


def orders(R):
    bits = [1 << i for i in range(R.bit_length() - 1)]
    return bits, bits[:1] + bits[2:] + bits[1:2]


def place(rep, order):
    q = jnp.zeros((), jnp.int32)
    for bit in order:
        q = 2 * q + (rep & bit) // bit
    return q


def beside_it(got, key, beside):
    if key in beside:
        got, beside[key] = lax.optimization_barrier((got, beside[key]))
    return got


def halving(pair, R, beside):
    pair = list(pair)
    for i, bits in enumerate(zip(*orders(R))):
        h = pair[0].shape[0] // 2
        got = beside_it([exchanged(g[h:], R, bit) for g, bit in zip(pair, bits)], i, beside)
        pair = [add_low(g[:h], t) for g, t in zip(pair, got)]
    return [g[0] for g in pair]


def doubling(parts, R, beside):
    pair = [p[None] for p in parts]
    for i, bits in reversed(list(enumerate(zip(*orders(R))))):
        got = [exchanged(g, R, bit) for g, bit in zip(pair, bits)]
        got = beside_it(got, i, beside)
        pair = [jnp.concatenate([g, t], axis=0) for g, t in zip(pair, got)]
    return pair


def sum_all(v, S, R):
    bit = 1
    while bit < R:
        v = v + exchanged(v, R, bit)
        bit *= 2
    return v


def swap_shards(part, me, S, head):
    n = (part.shape[0] - head) // S
    slots = []
    for j in range(S):
        b = lax.dynamic_slice_in_dim(part, head + lax.rem(me + j, S) * n, n, 0)
        slots.append(shifted(b, S, j) if j else b)
    return jnp.concatenate(([part[:head]] if head else []) + canonical(slots, me, S, True), axis=0)


def reduce_rows(grad):
    part = lax.psum_scatter(grad, "rep", scatter_dimension=0, tiled=True)
    return lax.all_gather(part, "rep", axis=0, tiled=True).astype(F32)


def reduce_columns(grad, me, S, parts):
    rows, cols = grad.shape
    part = lax.psum_scatter(grad.reshape(S, rows // S, cols), "rep", scatter_dimension=1, tiled=True)
    slots = [lax.dynamic_index_in_dim(part, me, 0, keepdims=False)]
    for j in range(1, S):
        slots.append(shifted(lax.dynamic_index_in_dim(part, lax.rem(me + j, S), 0, keepdims=False), S, j))
    slots = [s.reshape(s.shape[0], parts, cols // parts) for s in slots]
    whole = jnp.stack(canonical(slots, me, S, True), axis=2).reshape(-1, S * cols)
    return lax.all_gather(whole, "rep", axis=0, tiled=True).astype(F32)


def rotary_tables(PR, CR, CL):
    pos = np.concatenate([np.arange(PR), PR + np.arange(CR) % CL]).astype(np.float32)
    half = ROT // 2
    freq = np.exp(np.arange(half, dtype=np.float32) * np.float32(-2.0 * math.log(10000.0) / ROT)).astype(np.float32)
    ang = (pos[:, None] * freq[None, :]).astype(np.float32)
    c = np.cos(ang)
    s = np.sin(ang)
    n = pos.shape[0]
    one = np.ones((n, HD - ROT), np.float32)
    zero = np.zeros((n, HD - ROT), np.float32)
    z8 = np.zeros((n, half), np.float32)
    tabs = ([c, c, one], [-s, z8, zero], [z8, s, zero])
    return [jnp.asarray(np.tile(np.concatenate(t, axis=1), (1, 128 // HD)), F32) for t in tabs]


def per_device(
    prompt_in,
    cont_in,
    prompt_cot,
    cont_cot,
    ln1_gain,
    ln1_bias,
    ln2_gain,
    ln2_bias,
    qkv_weight,
    qkv_bias,
    out_weight,
    out_bias,
    up_weight,
    up_bias,
    down_weight,
    down_bias,
):
    S = lax.axis_size("shard")
    R = lax.axis_size("rep")
    me = lax.axis_index("shard")
    MB, _, PD, D = prompt_in.shape
    CD, CL = cont_in.shape[2:4]
    CR = CD * CL
    N = PD + CR
    CW = D // S
    FL = up_weight.shape[1] // S
    me_arr = jnp.reshape(me, (1,)).astype(jnp.int32)

    X = [[jnp.concatenate([prompt_in[m, 0], cont_in[m, 0].reshape(CR, D)], axis=0)] for m in range(MB)]
    DY = [[jnp.concatenate([prompt_cot[m, 0], cont_cot[m, 0].reshape(CR, D)], axis=0)] for m in range(MB)]

    w_up, brought = my_columns_halves(up_weight, me, S, R, (X[0], DY[0]))
    vecs_in = (ln1_gain, ln1_bias, ln2_gain, ln2_bias, out_bias, down_bias, qkv_bias)
    (vecs_in, qkv_weight), brought = lax.optimization_barrier(((vecs_in, qkv_weight), brought))

    one = lambda v: v.astype(F32).reshape(-1, CW)
    small = jnp.concatenate([one(v) for v in vecs_in], axis=0)
    slots = [small] + [shifted(small, S, j) for j in range(1, S)]
    whole = jnp.stack(canonical(slots, me, S, True), axis=0)
    vec = whole[:, :6].transpose(1, 0, 2).reshape(6, D)
    gb = vec[0:4]
    gb1 = vec[0:2]
    gb2 = vec[2:4]
    vb = vec[4:6]
    bqkv = whole[:, 6:].reshape(3, S, CW)
    bqkv = lax.dynamic_index_in_dim(bqkv, me, 1, keepdims=False).reshape(1, 3 * CW)
    bup = up_bias.astype(F32).reshape(1, FL)

    w_qkv = my_columns(qkv_weight, me, S, R, 3)

    tabs = rotary_tables(PD * S, CR * S, CL)
    src = [(X[m][0], DY[m][0]) for m in range(MB)]
    src[0], small = lax.optimization_barrier((src[0], small))
    src[1:], w_up = lax.optimization_barrier((src[1:], w_up))
    for m in range(MB):
        for j in range(1, S):
            X[m].append(shifted(src[m][0], S, S - j))
            DY[m].append(shifted(src[m][1], S, S - j))

    ff = [[None] * S for _ in range(MB)]

    def mlp(m, j):
        ff[m][j] = mlp_rows(X[m][j], DY[m][j], w_up, bup, down_weight, gb2)

    for m in range(MB):
        mlp(m, 0)
    rest = []

    def attend(m):
        rest.append(list(attn_group(S, PD, CL, me_arr, X[m], DY[m], w_qkv, bqkv, out_weight, gb1, tabs)))

    def rows(m, j):
        f = ff[m][j]
        return branch_rows(j, X[m][j], f[0], f[1], w_up, down_weight, rest[m][0], rest[m][1], w_qkv, out_weight, gb)

    def far_rows(m):
        r = [rows(m, j) for j in range(1, S)]
        got = [[shifted(r[j - 1][i], S, j) for j in range(1, S)] for i in range(2)]
        return got, [v[2] for v in r]

    chunked = (D // S // R) % 16 == 0 and R & (R - 1) == 0
    rep = lax.axis_index("rep")
    late = [(MB - 1, j) for j in range(1, S)]
    early = [(m, j) for m in range(MB) for j in range(S) if (m, j) not in late]
    of = lambda set_, k: [ff[m][j][k] for m, j in set_]
    for m, j in early:
        if j:
            mlp(m, j)
    if chunked:
        gmlp = mlp_grads(S, R, of(early, 0), [DY[m][j] for m, j in early], of(early, 2), of(early, 1))
        w_up, gmlp = lax.optimization_barrier((w_up, gmlp))
    for m, j in late:
        mlp(m, j)
    if chunked:
        if late:
            gmlp = mlp_grads(S, R, of(late, 0), [DY[m][j] for m, j in late], of(late, 2), of(late, 1), gmlp)
        part = lax.psum_scatter(gmlp, "rep", scatter_dimension=0, tiled=True)[0]
        w_qkv, gmlp = lax.optimization_barrier((w_qkv, gmlp))
    for m in range(MB):
        attend(m)
        if m + 1 < MB:
            w_qkv, rest[m][3] = lax.optimization_barrier((w_qkv, rest[m][3]))
    every = early + late
    def vectors(sums):
        ln1 = sum(o[0:2] for o in sums)
        ln2 = sum(o[2:4] for o in sums)
        db_out = sum(jnp.sum(DY[m][0].astype(F32), axis=0) for m in range(MB)).reshape(-1, CW)
        mine = (jnp.arange(S) == me).astype(F32)
        db_qkv = (sum(r[3] for r in rest)[:, None, :] * mine[None, :, None]).reshape(-1, CW)
        db_up = (sum(of(every, 3)) * mine[:, None]).reshape(-1, CW)
        return jnp.concatenate([ln1.reshape(-1, CW), ln2.reshape(-1, CW), db_out, db_qkv, db_up], axis=0)

    def finals(m, o, got, prior):
        return final_rows(m, MB, PD, X[m][0], DY[m][0], [o[0]] + got[0], [o[1]] + got[1], vb, prior)

    hs, dls, ctxs = [[r[k] for r in rest] for k in (2, 0, 1)]
    if chunked:
        q = jnp.stack([place(rep, order) for order in orders(R)]).astype(jnp.int32)
        part = swap_shards(part, me, S, FL // R)
        hs, part = lax.optimization_barrier((hs, part))
        gmlp_all = lax.all_gather(part, "rep", axis=0, tiled=False)
        gatt = attn_grads(S, R, q, hs, dls, ctxs, [DY[m][j] for m in range(MB) for j in range(S)])
        levels = R.bit_length() - 1
        beside, after = {}, {}
        far, mine = [], []

        def behind(value):
            dls, value = lax.optimization_barrier(([r[0] for r in rest], value))
            for k in range(MB):
                rest[k][0] = dls[k]
            return value

        behind(gatt)
        for m in range(MB):
            far.append(far_rows(m))
            at = min(m + 1, levels - 1)
            beside.setdefault(at, {})["far", m] = behind(far[m][1])
        for m in range(MB):
            mine.append(rows(m, 0))
            if m == 0:
                beside.setdefault(levels - 1, {})["own", m] = behind(mine[m])
            else:
                after.setdefault(levels - 2, {})["own", m] = mine[m]
        beside.setdefault(levels - 1, {})["got", 0] = far[0][0]
        half = halving(gatt, R, beside)
        for d in beside.values():
            for (kind, m), v in d.items():
                if kind == "far":
                    far[m] = (far[m][0], v)
                elif kind == "got":
                    far[m] = (v, far[m][1])
                else:
                    mine[m] = v
        sums = [v for f in far for v in f[1]] + [o[2] for o in mine]
        after[1] = {("vec", 0): sum_all(vectors(sums), S, R), ("mlp", 0): mlp_finish(S, gmlp_all, FL)}
        after[1].update({("got", m): far[m][0] for m in range(1, MB)})
        k = D // CW * (D // S // R)
        g1, g2 = doubling([swap_shards(half[0], me, S, 0), swap_shards(half[1], me, S, k)], R, after)
        done = {k_: v for d in after.values() for k_, v in d.items()}
        got = [done.get(("got", m), far[m][0]) for m in range(MB)]
        mine = [done.get(("own", m), mine[m]) for m in range(MB)]
        vecs = done["vec", 0]
        g_down, g_up = done["mlp", 0]
        outs = None
        for m in range(MB):
            outs = finals(m, mine[m], got[m], outs)
        g_out, g_qkv = attn_finish(S, q, g1, g2)
    else:
        dls, ctxs, hs = [[r[k] for r in rest] for k in (0, 1, 2)]
        far = [far_rows(m) for m in range(MB)]
        mine = [rows(m, 0) for m in range(MB)]
        g_down = reduce_rows(tn_sum(of(every, 0), [DY[m][j] for m, j in every], 256))
        g_up = reduce_columns(tn_sum(of(every, 2), of(every, 1), 256), me, S, 1)
        dycs = [jnp.concatenate(DY[m], axis=0) for m in range(MB)]
        g_out = reduce_rows(tn_sum(ctxs, dycs, 256))
        g_qkv = reduce_columns(tn_sum(hs, dls, 256), me, S, 3)
        vecs = sum_all(vectors([v for f in far for v in f[1]] + [o[2] for o in mine]), S, R)
        outs = None
        for m in range(MB):
            outs = finals(m, mine[m], far[m][0], outs)
    tot = vecs + sum(shifted(vecs, S, j) for j in range(1, S))
    held = lambda a, n: lax.dynamic_slice_in_dim(tot, a + me * n, n, 0).reshape(-1)
    v_ln1g, v_ln1b, v_ln2g, v_ln2b, v_out = [held(k * S, 1) for k in range(5)]
    v_qkv = held(5 * S, 3)
    v_up = held(8 * S, FL // CW)

    po, co, pg, cg = outs
    return (
        po.reshape(MB, 1, PD, D),
        co.reshape(MB, 1, CD, CL, D),
        pg.reshape(MB, 1, PD, D),
        cg.reshape(MB, 1, CD, CL, D),
        v_ln1g,
        v_ln1b,
        v_ln2g,
        v_ln2b,
        g_qkv,
        v_qkv,
        g_out,
        v_out,
        g_up,
        v_up,
        g_down,
        v_out,
    )


def solution(mesh):
    tokens = (
        P(None, "rep", "shard", None),
        P(None, "rep", "shard", None, None),
        P(None, "rep", "shard", None),
        P(None, "rep", "shard", None, None),
    )
    vec = P("shard")
    mat = P("shard", None)
    params = (vec, vec, vec, vec, mat, vec, mat, vec, mat, vec, mat, vec)
    return jax.shard_map(
        per_device, mesh=mesh, in_specs=tokens + params, out_specs=tokens + params, check_vma=False
    )
```

```python
import functools
import math

import jax
import jax.numpy as jnp
import numpy as np
from jax import lax
from jax.experimental import pallas as pl
from jax.experimental.pallas import tpu as pltpu
from jax.sharding import PartitionSpec as P

H = 16
HD = 64
ROT = 16
EPS = 1e-05
F32 = jnp.float32
BF = jnp.bfloat16
MIB = 1024 * 1024
SD = jax.ShapeDtypeStruct


def dnn(a, b):
    return lax.dot_general(a, b, (((1,), (0,)), ((), ())), preferred_element_type=F32)


def dnt(a, b):
    return lax.dot_general(a, b, (((1,), (1,)), ((), ())), preferred_element_type=F32)


def dtn(a, b):
    return lax.dot_general(a, b, (((0,), (0,)), ((), ())), preferred_element_type=F32)


def normed(rows):
    x = rows.astype(F32)
    c = x - jnp.mean(x, axis=-1, keepdims=True)
    inv = lax.rsqrt(jnp.mean(c * c, axis=-1, keepdims=True) + EPS)
    return c * inv, inv


def tile(i, n):
    return pl.ds(pl.multiple_of(i * n, n), n)


def rows_tile(n, most):
    t = most
    while n % t:
        t -= 8
    return t


def mlp_kernel(rt, x_ref, dy_ref, wu_ref, bu_ref, wd_ref, gb_ref, act_ref, dpre_ref, h_ref, bu_out, *back):
    f = pl.program_id(0)
    if back:
        yp_ref, g2_ref, ln_ref, yacc, dacc = back
    last = pl.num_programs(0) - 1
    rows = x_ref.shape[0]

    @pl.when(f == 0)
    def _():
        @pl.loop(0, rows // 128)
        def _(i):
            r = tile(i, 128)
            xh, _ = normed(x_ref[r, :])
            h_ref[r, :] = (xh * gb_ref[0:1, :] + gb_ref[1:2, :]).astype(BF)
            if back:
                yacc[r, :] = jnp.zeros((128, yacc.shape[1]), F32)
                dacc[r, :] = jnp.zeros((128, dacc.shape[1]), F32)

    def step(i, bsum):
        r = tile(i, rt)
        pre = dnn(h_ref[r, :], wu_ref[...]) + bu_ref[...]
        da = dnt(dy_ref[r, :], wd_ref[...])
        cdf = 0.5 * (1.0 + lax.erf(pre * 0.7071067811865476))
        act = (pre * cdf).astype(BF)
        dpre = (da * (cdf + pre * jnp.exp(-0.5 * pre * pre) * 0.3989422804014327)).astype(BF)
        act_ref[r, :] = act
        dpre_ref[r, :] = dpre
        if back:
            yacc[r, :] += dnn(act, wd_ref[...])
            dacc[r, :] += dnt(dpre, wu_ref[...])
        return bsum + jnp.sum(dpre.astype(F32), axis=0, keepdims=True)

    bu_out[...] = lax.fori_loop(0, rows // rt, step, jnp.zeros(bu_out.shape, F32))
    if not back:
        return

    @pl.when(f == last)
    def _():
        ln_ref[...] = jnp.zeros_like(ln_ref)

        @pl.loop(0, rows // 128)
        def _(i):
            r = tile(i, 128)
            xh, _ = normed(x_ref[r, :])
            dh = dacc[r, :]
            yp_ref[r, :] = yacc[r, :].astype(BF)
            g2_ref[r, :] = (dh * gb_ref[0:1, :]).astype(BF)
            ln_ref[0:1, :] += jnp.sum(dh * xh, axis=0, keepdims=True)
            ln_ref[1:2, :] += jnp.sum(dh, axis=0, keepdims=True)


def mlp_rows(x, dy, wu, bu, wd, gb, back):
    rows, width = x.shape
    hidden = wu.shape[1]
    fb = min(512, hidden)
    full = lambda s: pl.BlockSpec(s, lambda f: (0,) * len(s))
    return pl.pallas_call(
        functools.partial(mlp_kernel, rows_tile(rows, 640)),
        grid=(hidden // fb,),
        in_specs=[
            full((rows, width)),
            full((rows, width)),
            pl.BlockSpec((width, fb), lambda f: (0, f)),
            pl.BlockSpec((1, fb), lambda f: (0, f)),
            pl.BlockSpec((fb, width), lambda f: (f, 0)),
            full((2, width)),
        ],
        out_specs=[
            pl.BlockSpec((rows, fb), lambda f: (0, f)),
            pl.BlockSpec((rows, fb), lambda f: (0, f)),
            full((rows, width)),
            pl.BlockSpec((1, fb), lambda f: (0, f)),
        ]
        + [full((rows, width)), full((rows, width)), full((2, width))] * back,
        out_shape=[SD((rows, hidden), BF), SD((rows, hidden), BF), SD((rows, width), BF), SD((1, hidden), F32)]
        + [SD((rows, width), BF), SD((rows, width), BF), SD((2, width), F32)] * back,
        scratch_shapes=[pltpu.VMEM((rows, width), F32)] * (2 * back),
        compiler_params=pltpu.CompilerParams(vmem_limit_bytes=60 * MIB),
        cost_estimate=pl.CostEstimate(
            flops=4 * (1 + back) * rows * width * hidden,
            bytes_accessed=4 * (width * hidden + rows * hidden) + (6 + 4 * back) * rows * width,
            transcendentals=2 * rows * hidden,
        ),
    )(x, dy, wu, bu, wd, gb)


def roll8(x, left):
    w = x.shape[-1]
    return pltpu.roll(x, (w - 8) if left else 8, 1)


def attn_kernel(S, PD, CL, QB, HG, adding, me_ref, *refs):
    it = iter(refs)
    take = lambda n: [next(it) for _ in range(n)]
    stacked = S > 2
    per = 1 if stacked else S
    xs = take(per)
    dys = take(per)
    far = 1 if stacked else S - 1
    yps = take(far * adding)
    g2s = take(far * adding)
    wq, wk, wv = take(3)
    bq, bk, bv = take(3)
    wo, gb = take(2)
    cr, s1r, s2r = take(3)
    ys = take(far)
    gs = take(far)
    dl, ctx, h1, ln, db = take(5)
    yacc, dacc, q_s, k_s, v_s, dc_s, kT, vT, dk_s, dv_s = take(10)
    g = pl.program_id(0)
    last = pl.num_programs(0) - 1
    me = me_ref[0]
    N = xs[0].shape[-2]
    T = N * S
    PR = PD * S
    CR = N - PD
    W = HG * HD

    def every_slot(fn, start=0):
        if stacked:

            @pl.loop(start, S)
            def _(j):
                fn(j, lambda refs: refs[0].at[j], lambda refs: refs[0].at[j - 1])

        else:
            for j in range(start, S):
                fn(j, lambda refs: refs[j], lambda refs: refs[j - 1])

    def slot_rows(start, n):
        if start < PR:
            s, off = start // PD, start % PD
        else:
            s, off = (start - PR) // CR, PD + (start - PR) % CR
        return pl.ds(pl.multiple_of(lax.rem(s - me + S, S) * N + off, 128), n)

    def pieces(start, n):
        step = min(n, PD if start < PR else CR)
        return [(i, step) for i in range(0, n, step)]

    @pl.when(g == 0)
    def _():
        def load(j, of, away):
            x = of(xs)

            @pl.loop(0, N // 128)
            def _(i):
                xh, _ = normed(x[tile(i, 128), :])
                h1[pl.ds(pl.multiple_of(j * N + i * 128, 128), 128), :] = (xh * gb[0:1, :] + gb[1:2, :]).astype(BF)

        every_slot(load)

    def rot(y, r, scale):
        c = cr[r, :]
        s1 = s1r[r, :]
        s2 = s2r[r, :]
        out = []
        for p in range(W // 128):
            z = y[:, p * 128 : (p + 1) * 128]
            z = (z * c + roll8(z, True) * s1 + roll8(z, False) * s2).astype(BF)
            out.append(z * jnp.asarray(scale, BF) if scale != 1.0 else z)
        return jnp.concatenate(out, axis=1) if len(out) > 1 else out[0]

    def proj(j, of, away):
        s = lax.rem(me + j, S)
        rp = pl.ds(pl.multiple_of(s * PD, 128), PD)
        rc = pl.ds(pl.multiple_of(PR + s * CR, 128), CR)
        hh = h1[pl.ds(pl.multiple_of(j * N, 128), N), :]
        y = dnn(hh, wq[...]) + bq[...]
        q_s[rp, :] = rot(y[:PD], rp, HD**-0.5)
        q_s[rc, :] = rot(y[PD:], rc, HD**-0.5)
        y = dnn(hh, wk[...]) + bk[...]
        k_s[rp, :] = rot(y[:PD], rp, 1.0)
        k_s[rc, :] = rot(y[PD:], rc, 1.0)
        y = (dnn(hh, wv[...]) + bv[...]).astype(BF)
        v_s[rp, :] = y[:PD]
        v_s[rc, :] = y[PD:]
        y = dnt(of(dys)[...], wo[...]).astype(BF)
        dc_s[rp, :] = y[:PD]
        dc_s[rc, :] = y[PD:]

    def bring(j, of, away):
        nb = away(yps).shape[0]
        r = pl.ds(pl.multiple_of(g * nb, 16), nb)
        away(ys)[r, :] = away(yps)[...]
        away(gs)[r, :] = away(g2s)[...]

    every_slot(proj)
    if adding:
        every_slot(bring, 1)
    lane = lax.broadcasted_iota(jnp.int32, (1, 128), 1)
    row_i = lax.broadcasted_iota(jnp.int32, (QB, QB), 0)
    col_i = lax.broadcasted_iota(jnp.int32, (QB, QB), 1)
    causal = row_i <= col_i
    cmask = causal & ((row_i // CL) == (col_i // CL))
    blocks = []
    for i in range(PR // QB):
        blocks.append((i * QB, [(0, i * QB, None)] * (i > 0) + [(i * QB, QB, causal)]))
    for c in range((T - PR) // QB):
        blocks.append((PR + c * QB, [(0, PR, None), (PR + c * QB, QB, cmask)]))

    @pl.loop(0, W // 128)
    def _(p):
        lanes = tile(p, 128)
        kT[...] = k_s[:, lanes].T
        vT[...] = v_s[:, lanes].T
        dk_s[...] = jnp.zeros_like(dk_s)
        dv_s[...] = jnp.zeros_like(dv_s)
        def begin(q0, parts):
            qb = q_s[pl.ds(q0, QB), lanes]
            dcb = dc_s[pl.ds(q0, QB), lanes]
            out = []
            for h in range(2):
                sel = (lane >= HD * h) & (lane < HD * h + HD)
                qm = jnp.where(sel, qb, jnp.zeros_like(qb))
                dm = jnp.where(sel, dcb, jnp.zeros_like(dcb))
                ss = []
                for k0, n, mask in parts:
                    s = dnt(k_s[k0 : k0 + n, lanes], qm)
                    ss.append(s if mask is None else jnp.where(mask, s, -1e30))
                out.append((qm, dm, ss, [dnt(v_s[k0 : k0 + n, lanes], dm) for k0, n, _ in parts]))
            return out

        ahead = begin(*blocks[0])
        for b, (q0, parts) in enumerate(blocks):
            now = ahead
            if b + 1 < len(blocks):
                ahead = begin(*blocks[b + 1])
            rq = pl.ds(q0, QB)
            P_, DS, cT, dqT = [], [], [], []
            qh = [t[0] for t in now]
            dch = [t[1] for t in now]
            for h in range(2):
                _, _, ss, dps = now[h]
                m = functools.reduce(jnp.maximum, [jnp.max(s, axis=0, keepdims=True) for s in ss])
                es = [jnp.exp(s - m) for s in ss]
                rl = 1.0 / sum(jnp.sum(e, axis=0, keepdims=True) for e in es)
                ps = [e * rl for e in es]
                delta = sum(jnp.sum(a * b, axis=0, keepdims=True) for a, b in zip(ps, dps))
                P_.append([a.astype(BF) for a in ps])
                DS.append([(a * (b - delta)).astype(BF) for a, b in zip(ps, dps)])
                hr = slice(HD * h, HD * h + HD)
                cT.append(sum(dnn(vT[hr, k0 : k0 + n], a) for (k0, n, _), a in zip(parts, P_[h])))
                dqT.append(sum(dnn(kT[hr, k0 : k0 + n], a) for (k0, n, _), a in zip(parts, DS[h])))
            q2 = jnp.concatenate(qh, axis=0)
            dc2 = jnp.concatenate(dch, axis=0)
            for i, (k0, n, _) in enumerate(parts):
                dv_s[k0 : k0 + n, :] += dnn(jnp.concatenate([P_[0][i], P_[1][i]], axis=1), dc2)
                dk_s[k0 : k0 + n, :] += dnn(jnp.concatenate([DS[0][i], DS[1][i]], axis=1), q2)
            co = jnp.concatenate(cT, axis=0).T.astype(BF)
            z = jnp.concatenate(dqT, axis=0).T * (HD**-0.5)
            z = (z * cr[rq, :] - roll8(z, True) * s1r[rq, :] - roll8(z, False) * s2r[rq, :]).astype(BF)
            for o, n in pieces(q0, QB):
                ctx[slot_rows(q0 + o, n), lanes] = co[o : o + n]
                dl[0, slot_rows(q0 + o, n), lanes] = z[o : o + n]

        @pl.loop(0, S)
        def _(s):
            to = lax.rem(s - me + S, S) * N
            for src, off, n in ((s * PD, 0, PD), (PR + s * CR, PD, CR)):
                r = pl.ds(pl.multiple_of(src, 128), n)
                w = pl.ds(pl.multiple_of(to + off, 128), n)
                z = dk_s[r, :]
                z = z * cr[r, :] - roll8(z, True) * s1r[r, :] - roll8(z, False) * s2r[r, :]
                dl[1, w, lanes] = z.astype(BF)
                dl[2, w, lanes] = dv_s[r, :].astype(BF)

    for c in range(3):
        db[c : c + 1, :] = jnp.sum(dl[c].astype(F32), axis=0, keepdims=True)

    @pl.loop(1, S)
    def _(j):
        r = pl.ds(pl.multiple_of(j * N, 128), N)
        w = pl.ds(pl.multiple_of((j - 1) * N, 128), N)
        y = dnn(ctx[r, :], wo[...])
        d = dnt(dl[0, r, :], wq[...]) + dnt(dl[1, r, :], wk[...]) + dnt(dl[2, r, :], wv[...])

        @pl.when(g == 0)
        def _():
            yacc[w, :] = y
            dacc[w, :] = d

        @pl.when(g > 0)
        def _():
            yacc[w, :] += y
            dacc[w, :] += d

    @pl.when(g == last)
    def _():
        ln[...] = jnp.zeros_like(ln)

        def store(j, of, away):
            x, yo, go = of(xs), away(ys), away(gs)

            @pl.loop(0, N // 128)
            def _(i):
                r = tile(i, 128)
                w = pl.ds(pl.multiple_of((j - 1) * N + i * 128, 128), 128)
                xh, _ = normed(x[r, :])
                d = dacc[w, :]
                y = yacc[w, :]
                gg = d * gb[0:1, :]
                if adding:
                    y = y + yo[r, :].astype(F32)
                    gg = gg + go[r, :].astype(F32)
                yo[r, :] = y.astype(BF)
                go[r, :] = gg.astype(BF)
                ln[0:1, :] += jnp.sum(d * xh, axis=0, keepdims=True)
                ln[1:2, :] += jnp.sum(d, axis=0, keepdims=True)

        every_slot(store, 1)


def attn_group(S, PD, CL, me, xs, dys, yps, g2s, wqkv, bqkv, wo, gb, tabs):
    N, D = xs[0].shape
    CW = wo.shape[0]
    T = N * S
    HG = 4 if CW % 256 == 0 else 2
    QB = 256
    W = HG * HD
    G = CW // W
    full = lambda s: pl.BlockSpec(s, lambda g, m: (0,) * len(s), pipeline_mode=pl.Buffered(1))
    keep = lambda s: pl.BlockSpec(s, lambda g, m: (0,) * len(s))
    tok, tok_out, per, far = full((N, D)), keep((N, D)), S, S - 1
    adding = int(T * D <= 1536 * 1024)
    others = (yps, g2s)
    if not adding:
        yps, g2s = [], []
    out_tok = SD((N, D), BF)
    part = pl.BlockSpec((N // G, D), lambda g, m: (g, 0))
    if S > 2:
        xs, dys, yps, g2s = [[jnp.stack(v, axis=0)] if v else v for v in (xs, dys, yps, g2s)]
        tok, tok_out, per, far = full((S, N, D)), keep((S - 1, N, D)), 1, 1
        out_tok = SD((S - 1, N, D), BF)
        part = pl.BlockSpec((S - 1, N // G, D), lambda g, m: (0, g, 0))
    wspec = lambda c: pl.BlockSpec((D, W), lambda g, m: (0, c * G + g))
    bspec = lambda c: pl.BlockSpec((1, W), lambda g, m: (0, c * G + g))
    outs = pl.pallas_call(
        functools.partial(attn_kernel, S, PD, CL, QB, HG, adding),
        grid_spec=pltpu.PrefetchScalarGridSpec(
            num_scalar_prefetch=1,
            grid=(G,),
            in_specs=[tok] * (2 * per)
            + [part] * (2 * adding * far)
            + [wspec(0), wspec(1), wspec(2), bspec(0), bspec(1), bspec(2)]
            + [pl.BlockSpec((W, D), lambda g, m: (g, 0)), full((2, D))]
            + [full((T, 128))] * 3,
            out_specs=[tok_out] * (2 * far)
            + [
                pl.BlockSpec((3, T, W), lambda g, m: (0, 0, g)),
                pl.BlockSpec((T, W), lambda g, m: (0, g)),
                keep((T, D)),
                keep((2, D)),
                pl.BlockSpec((3, W), lambda g, m: (0, g)),
            ],
            scratch_shapes=[pltpu.VMEM((T - N, D), F32)] * 2
            + [pltpu.VMEM((T, W), BF)] * 4
            + [pltpu.VMEM((128, T), BF)] * 2
            + [pltpu.VMEM((T, 128), F32)] * 2,
        ),
        out_shape=[out_tok] * (2 * far)
        + [SD((3, T, CW), BF), SD((T, CW), BF), SD((T, D), BF), SD((2, D), F32), SD((3, CW), F32)],
        compiler_params=pltpu.CompilerParams(vmem_limit_bytes=62 * MIB),
        cost_estimate=pl.CostEstimate(
            flops=16 * T * D * CW + 40 * T * T * CW,
            bytes_accessed=12 * T * D + 12 * T * CW + 8 * D * CW,
            transcendentals=T * T * CW // HD,
        ),
    )(me, *xs, *dys, *yps, *g2s, wqkv, wqkv, wqkv, bqkv, bqkv, bqkv, wo, gb, *tabs)
    ys, gs = outs[:far], outs[far : 2 * far]
    if S > 2:
        ys, gs = [[v[0][j] for j in range(S - 1)] for v in (ys, gs)]
    if not adding:
        ys, gs = [[a + b for a, b in zip(p, q)] for p, q in zip((ys, gs), others)]
    return ys, gs, outs[2 * far :]


def tn_kernel(n, wide, *refs):
    a = refs[:n]
    b = refs[n : 2 * n]
    o = refs[2 * n]
    if wide == 0:
        o[...] = sum(dtn(x[...], y[...]) for x, y in zip(a, b)).astype(BF)
    else:
        w = b[0].shape[2]
        for c in range(wide):
            o[:, c * w : (c + 1) * w] = sum(dtn(x[...], y[c]) for x, y in zip(a, b)).astype(BF)


def tn_sum(a, b, block):
    n = len(a)
    rows, da = a[0].shape
    block = min(block, da)
    wide = b[0].shape[0] if b[0].ndim == 3 else 0
    db = b[0].shape[-1] * max(wide, 1)
    keep = lambda s: pl.BlockSpec(s, lambda i: (0,) * len(s), pipeline_mode=pl.Buffered(1))
    return pl.pallas_call(
        functools.partial(tn_kernel, n, wide),
        grid=(da // block,),
        in_specs=[pl.BlockSpec((rows, block), lambda i: (0, i))] * n + [keep(b[0].shape)] * n,
        out_specs=pl.BlockSpec((block, db), lambda i: (i, 0)),
        out_shape=SD((da, db), BF),
        compiler_params=pltpu.CompilerParams(vmem_limit_bytes=60 * MIB),
        cost_estimate=pl.CostEstimate(flops=2 * n * rows * da * db, bytes_accessed=2 * (n * rows * (da + db) + da * db), transcendentals=0),
    )(*a, *b)


def joined(refs):
    return jnp.concatenate([r[...] for r in refs], axis=0)


def down_kernel(n, more, *refs):
    o = refs[-1]
    t = dtn(joined(refs[:n]), joined(refs[n : 2 * n])).reshape(o.shape)
    o[...] = (t + refs[2 * n][...].astype(F32) if more else t).astype(BF)


def up_kernel(n, more, *refs):
    o = refs[-1]
    c, rows, w = o.shape
    t = dtn(joined(refs[:n]), joined(refs[n : 2 * n]))
    k = t.shape[1] // w
    for i in range(k):
        r = slice(i * (rows // k), (i + 1) * (rows // k))
        p = t[:, i * w : (i + 1) * w].reshape(c, rows // k, w)
        o[:, r, :] = (p + refs[2 * n][:, r, :].astype(F32) if more else p).astype(BF)


def mlp_grads(S, R, acts, dys, hs, dpres, g=None):
    n = len(acts)
    rows, FL = acts[0].shape
    D = dys[0].shape[1]
    DR = D // S
    blk = 256
    rd = FL // R
    ru = DR // R
    k = FL // D
    per = rd + S * ru * k
    keep = lambda s: pl.BlockSpec(s, lambda i: (0,) * len(s), pipeline_mode=pl.Buffered(1))
    steps = DR // blk
    more = g is not None
    hbm = pl.BlockSpec(memory_space=pl.ANY)

    def call(kernel, a, b, spec, g):
        width = b[0].shape[1]
        prior = [] if g is None else [g]
        return pl.pallas_call(
            functools.partial(kernel, n, more),
            grid=(a[0].shape[1] // blk,),
            in_specs=[pl.BlockSpec((rows, blk), lambda i: (0, i))] * n
            + [keep((rows, width))] * n
            + ([spec if more else hbm] if prior else []),
            out_specs=spec,
            out_shape=SD((R, per, D), BF),
            input_output_aliases={2 * n: 0} if prior else {},
            compiler_params=pltpu.CompilerParams(vmem_limit_bytes=60 * MIB),
            cost_estimate=pl.CostEstimate(
                flops=2 * n * rows * D * FL, bytes_accessed=2 * (n * rows * (D + FL) + (1 + more) * D * FL), transcendentals=0
            ),
        )(*a, *b, *prior)

    g = call(down_kernel, acts, dys, pl.BlockSpec((blk // rd, rd, D), lambda i: (i, 0, 0)), g)
    spec = pl.BlockSpec((blk // ru, ru * k, D), lambda i: (i % steps, rd // (ru * k) + i // steps, 0))
    return call(up_kernel, hs, dpres, spec, g)


def mlp_finish_kernel(S, rd, ru, g, down, up):
    n, per, D = g.shape
    k = (per - rd) // (S * ru)
    for c in range(n):
        down[c * rd : (c + 1) * rd, :] = g[c, :rd, :].astype(F32)
        for t in range(S * k):
            a = rd + t * ru
            up[c * ru : (c + 1) * ru, t * D : (t + 1) * D] = g[c, a : a + ru, :].astype(F32)


def mlp_finish(S, g, FL):
    R, per, D = g.shape
    rd = FL // R
    ru = D // S // R
    n = 4
    return pl.pallas_call(
        functools.partial(mlp_finish_kernel, S, rd, ru),
        grid=(R // n,),
        in_specs=[pl.BlockSpec((n, per, D), lambda c: (c, 0, 0))],
        out_specs=[pl.BlockSpec((n * rd, D), lambda c: (c, 0)), pl.BlockSpec((n * ru, S * FL), lambda c: (c, 0))],
        out_shape=[SD((FL, D), F32), SD((D // S, S * FL), F32)],
        compiler_params=pltpu.CompilerParams(vmem_limit_bytes=40 * MIB),
        cost_estimate=pl.CostEstimate(flops=0, bytes_accessed=6 * R * per * D, transcendentals=0),
    )(g)


def attn_grads_kernel(n, S, R, q_ref, *refs):
    h = refs[:n]
    dl = refs[n : 2 * n]
    ctx = refs[2 * n : 3 * n]
    dy = refs[3 * n : -4]
    first, second = refs[-4:-2], refs[-2:]
    i = pl.program_id(0)
    q1 = q_ref[0]
    q2 = q_ref[1]
    blk = h[0].shape[1]
    D = dy[0].shape[1]
    DR = D // S
    CW = dl[0].shape[2]
    ru = DR // R
    k = D // CW
    steps = DR // blk
    s = i // steps
    base = (i % steps) * (blk // ru)

    def put(pair, pos, rows, v):
        for half in range(2):

            @pl.when(pos // (R // 2) == half)
            def _():
                pair[half][pos % (R // 2), rows, :] = v

    for p in range(3):
        t = dtn(joined(h), jnp.concatenate([y[p] for y in dl], axis=0)).astype(BF)
        for c in range(blk // ru):
            v = t[c * ru : (c + 1) * ru, :]
            if p < 2:
                put(first, (base + c) ^ q1, pl.ds(s * 2 * ru + p * ru, ru), v)
            else:
                put(second, (base + c) ^ q2, pl.ds(k * ru + s * ru, ru), v)
    t = dtn(joined(ctx), joined(dy)).astype(BF)
    m = ctx[0].shape[1] // ru
    for c in range(m):
        for j in range(k):
            put(second, (i * m + c) ^ q2, pl.ds(j * ru, ru), t[c * ru : (c + 1) * ru, j * CW : (j + 1) * CW])


def attn_grads(S, R, q, hs, dls, ctxs, dys):
    n = len(hs)
    T, D = hs[0].shape
    CW = ctxs[0].shape[1]
    DR = D // S
    ru = DR // R
    blk = 256
    G = D // blk
    keep = lambda s: pl.BlockSpec(s, lambda i, q: (0,) * len(s), pipeline_mode=pl.Buffered(1))
    shapes = [(R // 2, S * 2 * ru, CW)] * 2 + [(R // 2, (D // CW + S) * ru, CW)] * 2
    return pl.pallas_call(
        functools.partial(attn_grads_kernel, n, S, R),
        grid_spec=pltpu.PrefetchScalarGridSpec(
            num_scalar_prefetch=1,
            grid=(G,),
            in_specs=[pl.BlockSpec((T, blk), lambda i, q: (0, i))] * n
            + [keep((3, T, CW))] * n
            + [pl.BlockSpec((T, CW // G), lambda i, q: (0, i))] * n
            + [keep(dys[0].shape)] * len(dys),
            out_specs=[pl.BlockSpec(s, lambda i, q: (0, 0, 0)) for s in shapes],
        ),
        out_shape=[SD(s, BF) for s in shapes],
        compiler_params=pltpu.CompilerParams(vmem_limit_bytes=60 * MIB),
        cost_estimate=pl.CostEstimate(flops=8 * n * T * D * CW, bytes_accessed=2 * n * T * (2 * D + 4 * CW) + 8 * D * CW, transcendentals=0),
    )(q, *hs, *dls, *ctxs, *dys)


def attn_finish_kernel(S, ru, k, n, half, q_ref, *refs):
    out, qkv = refs[4 * n :]
    CW = refs[0].shape[2]
    D = out.shape[1]
    i = pl.program_id(0)

    def piece(which, c, a):
        low, high = refs[2 * which * n + c], refs[(2 * which + 1) * n + c]
        here = ((i * n + c) ^ q_ref[which]) < half
        rows = pl.ds(a, ru)
        return jnp.where(here, low[0, rows, :].astype(F32), high[0, rows, :].astype(F32))

    for c in range(n):
        r = slice(c * ru, (c + 1) * ru)
        for j in range(k):
            out[r, j * CW : (j + 1) * CW] = piece(1, c, j * ru)
        for t in range(S):
            for p in range(3):
                v = piece(0, c, (t * 2 + p) * ru) if p < 2 else piece(1, c, (k + t) * ru)
                qkv[r, p * D + t * CW : p * D + (t + 1) * CW] = v


def attn_finish(S, q, one, two):
    half, per1, CW = one[0].shape
    per2 = two[0].shape[1]
    R = 2 * half
    D = CW * S
    ru = D // S // R
    n = 4
    place_of = lambda i, q, k, c: (i * n + c) ^ q[k]
    low = lambda per, k, c: pl.BlockSpec((1, per, CW), lambda i, q: (jnp.minimum(place_of(i, q, k, c), half - 1), 0, 0))
    high = lambda per, k, c: pl.BlockSpec((1, per, CW), lambda i, q: (jnp.maximum(place_of(i, q, k, c) - half, 0), 0, 0))
    specs = [f(per, k, c) for k, per in ((0, per1), (1, per2)) for f in (low, high) for c in range(n)]
    return pl.pallas_call(
        functools.partial(attn_finish_kernel, S, ru, S, n, half),
        grid_spec=pltpu.PrefetchScalarGridSpec(
            num_scalar_prefetch=1,
            grid=(R // n,),
            in_specs=specs,
            out_specs=[pl.BlockSpec((n * ru, D), lambda c, q: (c, 0)), pl.BlockSpec((n * ru, 3 * D), lambda c, q: (c, 0))],
        ),
        out_shape=[SD((CW, D), F32), SD((D // S, 3 * D), F32)],
        compiler_params=pltpu.CompilerParams(vmem_limit_bytes=40 * MIB),
        cost_estimate=pl.CostEstimate(flops=0, bytes_accessed=6 * R * (per1 + per2) * CW, transcendentals=0),
    )(q, *[a for pair in (one, two) for arr in pair for a in [arr] * n])


def own_kernel(dl, ctx, wqkv, wo, x, yp, g2, gb, y, g, ln, d1):
    N = x.shape[0]
    CW = ctx.shape[1]
    d1[...] = sum(dnt(dl[p], wqkv[:, p * CW : (p + 1) * CW]) for p in range(3))
    y[...] = (yp[...].astype(F32) + dnn(ctx[...], wo[...])).astype(BF)
    ln[...] = jnp.zeros_like(ln)

    @pl.loop(0, N // 128)
    def _(i):
        r = tile(i, 128)
        xh, _ = normed(x[r, :])
        a = d1[r, :]
        g[r, :] = (a * gb[0:1, :] + g2[r, :].astype(F32)).astype(BF)
        ln[0:1, :] += jnp.sum(a * xh, axis=0, keepdims=True)
        ln[1:2, :] += jnp.sum(a, axis=0, keepdims=True)


def own_rows(x, yp, g2, dl, ctx, wqkv, wo, gb):
    N, D = x.shape
    CW = wo.shape[0]
    full = lambda s: pl.BlockSpec(s, lambda f: (0,) * len(s))
    return pl.pallas_call(
        own_kernel,
        grid=(1,),
        in_specs=[full((3, N, CW)), full((N, CW)), full((D, 3 * CW)), full((CW, D))] + [full((N, D))] * 3 + [full((2, D))],
        out_specs=[full((N, D)), full((N, D)), full((2, D))],
        out_shape=[SD((N, D), BF), SD((N, D), BF), SD((2, D), F32)],
        scratch_shapes=[pltpu.VMEM((N, D), F32)],
        compiler_params=pltpu.CompilerParams(vmem_limit_bytes=60 * MIB),
        cost_estimate=pl.CostEstimate(flops=8 * N * D * CW, bytes_accessed=8 * (N + D) * CW + 10 * N * D, transcendentals=0),
    )(dl, ctx, wqkv, wo, x, yp, g2, gb)


def final_kernel(S, first, PT, *refs):
    it = iter(refs)
    take = lambda n: [next(it) for _ in range(n)]
    x, dy = take(2)
    ys = take(S)
    gs = take(S)
    (vb,) = take(1)
    if not first:
        take(4)
    po, co, pg, cg = take(4)
    i = pl.program_id(0)
    xv = x[...].astype(F32)
    xh, inv = normed(xv)
    y = xv + vb[0:1, :] + sum(r[...].astype(F32) for r in ys) + vb[1:2, :]
    gsum = sum(r[...].astype(F32) for r in gs)
    dx = (gsum - jnp.mean(gsum, axis=-1, keepdims=True) - xh * jnp.mean(gsum * xh, axis=-1, keepdims=True)) * inv
    out = y.astype(BF)
    grad = dy[...].astype(F32) + dx

    @pl.when(i < PT)
    def _():
        po[0] = out
        pg[0] = grad

    @pl.when(i >= PT)
    def _():
        co[0] = out
        cg[0] = grad


def final_rows(m, MB, PD, x, dy, ys, gs, vb, prior):
    S = len(ys)
    N, D = x.shape
    CR = N - PD
    RT = 128
    PT = PD // RT
    first = prior is None
    row = pl.BlockSpec((RT, D), lambda i: (i, 0))
    pspec = pl.BlockSpec((1, RT, D), lambda i: (m, jnp.minimum(i, PT - 1), 0))
    cspec = pl.BlockSpec((1, RT, D), lambda i: (m, jnp.maximum(i - PT, 0), 0))
    hbm = pl.BlockSpec(memory_space=pl.ANY)
    n_in = 2 * S + 3
    return pl.pallas_call(
        functools.partial(final_kernel, S, first, PT),
        grid=(N // RT,),
        in_specs=[row] * (2 * S + 2) + [pl.BlockSpec((2, D), lambda i: (0, 0))] + ([] if first else [hbm] * 4),
        out_specs=[pspec, cspec, pspec, cspec],
        out_shape=[SD((MB, PD, D), BF), SD((MB, CR, D), BF), SD((MB, PD, D), F32), SD((MB, CR, D), F32)],
        input_output_aliases={} if first else {n_in + k: k for k in range(4)},
        compiler_params=pltpu.CompilerParams(vmem_limit_bytes=32 * MIB),
        cost_estimate=pl.CostEstimate(flops=20 * N * D, bytes_accessed=(4 * S + 10) * N * D, transcendentals=0),
    )(x, dy, *ys, *gs, vb, *(() if first else prior))


def shifted(value, S, j):
    return lax.ppermute(value, "shard", [(i, (i + j) % S) for i in range(S)])


def canonical(slots, me, S, back):
    if S == 1:
        return slots
    if S == 2:
        a, b = slots
        return [jnp.where(me == 0, a, b), jnp.where(me == 0, b, a)]
    stacked = jnp.stack(slots, axis=0)
    return [
        lax.dynamic_index_in_dim(stacked, lax.rem((me - s if back else s - me) + S, S), 0, keepdims=False) for s in range(S)
    ]


def exchanged(value, R, bit):
    return lax.ppermute(value, "rep", [(i, i ^ bit) for i in range(R)])


def columns_for(weight, me, S, j, parts, row=0, rows=None):
    cols = weight.shape[1] // parts
    rows = weight.shape[0] if rows is None else rows
    w = cols // S
    at = lax.rem(me + j, S) * w
    got = [lax.dynamic_slice(weight, (row, p * cols + at), (rows, w)) for p in range(parts)]
    return got[0] if parts == 1 else jnp.concatenate(got, axis=1)


def my_columns_halves(weight, me, S, R):
    rows = weight.shape[0]
    rep = lax.axis_index("rep")
    core = rep % 2
    y = (rep // 2) % 2
    n = rows // 4
    cut = [columns_for(weight, me, S, j, 1, (2 * core + y) * n, n) for j in range(1, S)]
    slots = [columns_for(weight, me, S, 0, 1)]

    def both(piece, other, first):
        return jnp.concatenate([jnp.where(first, piece, other), jnp.where(first, other, piece)], axis=0)

    for j in range(1, S):
        piece = shifted(cut[j - 1], S, j)
        pair = both(piece, exchanged(piece, R, 2), y == 0)
        slots.append(both(pair, exchanged(pair, R, 1), core == 0))
    return jnp.concatenate(canonical(slots, me, S, True), axis=0), piece, cut[0]


def my_columns(weight, me, S, R, parts):
    rows = weight.shape[0]
    own = columns_for(weight, me, S, 0, parts)
    if S == 1:
        return own
    rep = lax.axis_index("rep")
    chunk = rows // R
    got = []
    for j in range(1, S):
        got.append(shifted(columns_for(weight, me, S, j, parts, rep * chunk, chunk), S, j))
    others = lax.all_gather(jnp.stack(got, axis=0), "rep", axis=1, tiled=True)
    return jnp.concatenate(canonical([own] + [others[j] for j in range(S - 1)], me, S, True), axis=0)


def add_low(a, b):
    return (a.astype(F32) + b.astype(F32)).astype(BF)


def orders(R):
    bits = [1 << i for i in range(R.bit_length() - 1)]
    return bits, bits[:1] + bits[2:] + bits[1:2]


def place(rep, order):
    q = jnp.zeros((), jnp.int32)
    for bit in order:
        q = 2 * q + (rep & bit) // bit
    return q


def beside_it(got, key, beside):
    if key in beside:
        got, beside[key] = lax.optimization_barrier((got, beside[key]))
    return got


def halving(pairs, R, beside):
    for i, bits in enumerate(zip(*orders(R))):
        got = beside_it([exchanged(p[1], R, bit) for p, bit in zip(pairs, bits)], i, beside)
        h = got[0].shape[0] // 2
        if h:
            pairs = [(add_low(p[0][:h], t[:h]), add_low(p[0][h:], t[h:])) for p, t in zip(pairs, got)]
        else:
            pairs = [add_low(p[0], t) for p, t in zip(pairs, got)]
    return [p[0] for p in pairs]


def doubling(parts, R, beside):
    pair = [p[None] for p in parts]
    for i, bits in reversed(list(enumerate(zip(*orders(R))))):
        got = beside_it([exchanged(g, R, bit) for g, bit in zip(pair, bits)], i, beside)
        if i:
            pair = [jnp.concatenate([g, t], axis=0) for g, t in zip(pair, got)]
    return list(zip(pair, got))


def sum_all(v, S, R):
    bit = 1
    while bit < R:
        v = v + exchanged(v, R, bit)
        bit *= 2
    return v


def swap_shards(part, me, S, head):
    n = (part.shape[0] - head) // S
    slots = []
    for j in range(S):
        b = lax.dynamic_slice_in_dim(part, head + lax.rem(me + j, S) * n, n, 0)
        slots.append(shifted(b, S, j) if j else b)
    return jnp.concatenate(([part[:head]] if head else []) + canonical(slots, me, S, True), axis=0)


def reduce_rows(grad):
    part = lax.psum_scatter(grad, "rep", scatter_dimension=0, tiled=True)
    return lax.all_gather(part, "rep", axis=0, tiled=True).astype(F32)


def reduce_columns(grad, me, S, parts):
    rows, cols = grad.shape
    part = lax.psum_scatter(grad.reshape(S, rows // S, cols), "rep", scatter_dimension=1, tiled=True)
    slots = [lax.dynamic_index_in_dim(part, me, 0, keepdims=False)]
    for j in range(1, S):
        slots.append(shifted(lax.dynamic_index_in_dim(part, lax.rem(me + j, S), 0, keepdims=False), S, j))
    slots = [s.reshape(s.shape[0], parts, cols // parts) for s in slots]
    whole = jnp.stack(canonical(slots, me, S, True), axis=2).reshape(-1, S * cols)
    return lax.all_gather(whole, "rep", axis=0, tiled=True).astype(F32)


def rotary_tables(PR, CR, CL):
    pos = np.concatenate([np.arange(PR), PR + np.arange(CR) % CL]).astype(np.float32)
    half = ROT // 2
    freq = np.exp(np.arange(half, dtype=np.float32) * np.float32(-2.0 * math.log(10000.0) / ROT)).astype(np.float32)
    ang = (pos[:, None] * freq[None, :]).astype(np.float32)
    c = np.cos(ang)
    s = np.sin(ang)
    n = pos.shape[0]
    one = np.ones((n, HD - ROT), np.float32)
    zero = np.zeros((n, HD - ROT), np.float32)
    z8 = np.zeros((n, half), np.float32)
    tabs = ([c, c, one], [-s, z8, zero], [z8, s, zero])
    return [jnp.asarray(np.tile(np.concatenate(t, axis=1), (1, 128 // HD)), F32) for t in tabs]


def per_device(
    prompt_in,
    cont_in,
    prompt_cot,
    cont_cot,
    ln1_gain,
    ln1_bias,
    ln2_gain,
    ln2_bias,
    qkv_weight,
    qkv_bias,
    out_weight,
    out_bias,
    up_weight,
    up_bias,
    down_weight,
    down_bias,
):
    S = lax.axis_size("shard")
    R = lax.axis_size("rep")
    me = lax.axis_index("shard")
    MB, _, PD, D = prompt_in.shape
    CD, CL = cont_in.shape[2:4]
    CR = CD * CL
    N = PD + CR
    CW = D // S
    FL = up_weight.shape[1] // S
    me_arr = jnp.reshape(me, (1,)).astype(jnp.int32)

    one = lambda v: v.astype(F32).reshape(-1, CW)
    small = jnp.concatenate([one(v) for v in (ln1_gain, ln1_bias, ln2_gain, ln2_bias, out_bias, down_bias, qkv_bias)], axis=0)
    w_up, brought, cut = my_columns_halves(up_weight, me, S, R)
    (small, qkv_weight), cut = lax.optimization_barrier(((small, qkv_weight), cut))
    slots = [small] + [shifted(small, S, j) for j in range(1, S)]
    whole = jnp.stack(canonical(slots, me, S, True), axis=0)
    vec = whole[:, :6].transpose(1, 0, 2).reshape(6, D)
    gb1 = vec[0:2]
    gb2 = vec[2:4]
    vb = vec[4:6]
    bqkv = whole[:, 6:].reshape(3, S, CW)
    bqkv = lax.dynamic_index_in_dim(bqkv, me, 1, keepdims=False).reshape(1, 3 * CW)
    bup = up_bias.astype(F32).reshape(1, FL)

    w_qkv = my_columns(qkv_weight, me, S, R, 3)

    X = [[jnp.concatenate([prompt_in[m, 0], cont_in[m, 0].reshape(CR, D)], axis=0)] for m in range(MB)]
    DY = [[jnp.concatenate([prompt_cot[m, 0], cont_cot[m, 0].reshape(CR, D)], axis=0)] for m in range(MB)]
    tabs = rotary_tables(PD * S, CR * S, CL)
    src = [(X[m][0], DY[m][0]) for m in range(MB)]
    src[1:], brought = lax.optimization_barrier((src[1:], brought))
    for m in range(MB):
        for j in range(1, S):
            X[m].append(shifted(src[m][0], S, S - j))
            DY[m].append(shifted(src[m][1], S, S - j))

    ff = [[None] * S for _ in range(MB)]

    def mlp(m, j):
        ff[m][j] = mlp_rows(X[m][j], DY[m][j], w_up, bup, down_weight, gb2, 1)

    for m in range(MB):
        mlp(m, 0)
    rest = []
    y_got, g_got = [], []

    def attend(m):
        ys, gs, more = attn_group(
            S, PD, CL, me_arr, X[m], DY[m], [f[4] for f in ff[m][1:]], [f[5] for f in ff[m][1:]], w_qkv, bqkv, out_weight, gb1, tabs
        )
        rest.append(list(more))
        y_got.append([shifted(ys[j - 1], S, j) for j in range(1, S)])
        g_got.append([shifted(gs[j - 1], S, j) for j in range(1, S)])

    def own(m):
        f = ff[m][0]
        return own_rows(X[m][0], f[4], f[5], rest[m][0], rest[m][1], w_qkv, out_weight, gb1)

    chunked = (D // S // R) % 16 == 0 and R & (R - 1) == 0
    rep = lax.axis_index("rep")
    late = [(MB - 1, j) for j in range(1, S)]
    early = [(m, j) for m in range(MB) for j in range(S) if (m, j) not in late]
    of = lambda set_, k: [ff[m][j][k] for m, j in set_]
    for m, j in early:
        if j:
            mlp(m, j)
    if chunked:
        gmlp = mlp_grads(S, R, of(early, 0), [DY[m][j] for m, j in early], of(early, 2), of(early, 1))
        w_up, gmlp = lax.optimization_barrier((w_up, gmlp))
    for m, j in late:
        mlp(m, j)
    if chunked:
        if late:
            gmlp = mlp_grads(S, R, of(late, 0), [DY[m][j] for m, j in late], of(late, 2), of(late, 1), gmlp)
        part = lax.psum_scatter(gmlp, "rep", scatter_dimension=0, tiled=True)[0]
        w_qkv, gmlp = lax.optimization_barrier((w_qkv, gmlp))
    for m in range(MB):
        attend(m)
        if m + 1 < MB:
            w_qkv, rest[m][3] = lax.optimization_barrier((w_qkv, rest[m][3]))
    every = early + late
    def vectors(mine_):
        ln1 = sum(r[3] for r in rest) + sum(o[2] for o in mine_)
        ln2 = sum(of(every, 6))
        db_out = sum(jnp.sum(DY[m][0].astype(F32), axis=0) for m in range(MB)).reshape(-1, CW)
        mine = (jnp.arange(S) == me).astype(F32)
        db_qkv = (sum(r[4] for r in rest)[:, None, :] * mine[None, :, None]).reshape(-1, CW)
        db_up = (sum(of(every, 3)) * mine[:, None]).reshape(-1, CW)
        return jnp.concatenate([ln1.reshape(-1, CW), ln2.reshape(-1, CW), db_out, db_qkv, db_up], axis=0)

    finals = lambda m, o, prior: final_rows(m, MB, PD, X[m][0], DY[m][0], [o[0]] + y_got[m], [o[1]] + g_got[m], vb, prior)
    hs, dls, ctxs = [[r[k] for r in rest] for k in (2, 0, 1)]
    if chunked:
        q = jnp.stack([place(rep, order) for order in orders(R)]).astype(jnp.int32)
        part = swap_shards(part, me, S, FL // R)
        hs, y_got[:-1], g_got[:-1], part = lax.optimization_barrier((hs, y_got[:-1], g_got[:-1], part))
        gmlp_all = lax.all_gather(part, "rep", axis=0, tiled=False)
        gatt = attn_grads(S, R, q, hs, dls, ctxs, [DY[m][j] for m in range(MB) for j in range(S)])
        dls_own, _ = lax.optimization_barrier(([r[0] for r in rest], gatt))
        for m in range(MB):
            rest[m][0] = dls_own[m]
        mine = [own(m) for m in range(MB)]
        beside = {1: mine, 2: (y_got[-1], g_got[-1])}
        half = halving([gatt[:2], gatt[2:]], R, beside)
        mine = beside[1]
        y_got[-1], g_got[-1] = beside[2]
        outs = None
        for m in range(MB - 1):
            outs = finals(m, mine[m], outs)
        vecs = sum_all(vectors(mine), S, R)
        k = D // CW * (D // S // R)
        beside = {3: outs, 1: (finals(MB - 1, mine[-1], outs), vecs, mlp_finish(S, gmlp_all, FL))}
        g1, g2 = doubling([swap_shards(half[0], me, S, 0), swap_shards(half[1], me, S, k)], R, beside)
        outs, vecs, (g_down, g_up) = beside[1]
        g_out, g_qkv = attn_finish(S, q, g1, g2)
    else:
        dls, ctxs, hs = [[r[k] for r in rest] for k in (0, 1, 2)]
        mine = [own(m) for m in range(MB)]
        g_down = reduce_rows(tn_sum(of(every, 0), [DY[m][j] for m, j in every], 256))
        g_up = reduce_columns(tn_sum(of(every, 2), of(every, 1), 256), me, S, 1)
        dycs = [jnp.concatenate(DY[m], axis=0) for m in range(MB)]
        g_out = reduce_rows(tn_sum(ctxs, dycs, 256))
        g_qkv = reduce_columns(tn_sum(hs, dls, 256), me, S, 3)
        vecs = sum_all(vectors(mine), S, R)
        outs = None
        for m in range(MB):
            outs = finals(m, mine[m], outs)
    tot = vecs + sum(shifted(vecs, S, j) for j in range(1, S))
    held = lambda a, n: lax.dynamic_slice_in_dim(tot, a + me * n, n, 0).reshape(-1)
    v_ln1g, v_ln1b, v_ln2g, v_ln2b, v_out = [held(k * S, 1) for k in range(5)]
    v_qkv = held(5 * S, 3)
    v_up = held(8 * S, FL // CW)

    po, co, pg, cg = outs
    return (
        po.reshape(MB, 1, PD, D),
        co.reshape(MB, 1, CD, CL, D),
        pg.reshape(MB, 1, PD, D),
        cg.reshape(MB, 1, CD, CL, D),
        v_ln1g,
        v_ln1b,
        v_ln2g,
        v_ln2b,
        g_qkv,
        v_qkv,
        g_out,
        v_out,
        g_up,
        v_up,
        g_down,
        v_out,
    )


def solution(mesh):
    tokens = (
        P(None, "rep", "shard", None),
        P(None, "rep", "shard", None, None),
        P(None, "rep", "shard", None),
        P(None, "rep", "shard", None, None),
    )
    vec = P("shard")
    mat = P("shard", None)
    params = (vec, vec, vec, vec, mat, vec, mat, vec, mat, vec, mat, vec)
    return jax.shard_map(
        per_device, mesh=mesh, in_specs=tokens + params, out_specs=tokens + params, check_vma=False
    )
```

```python
import functools
import math

import jax
import jax.numpy as jnp
import numpy as np
from jax import lax
from jax.experimental import pallas as pl
from jax.experimental.pallas import tpu as pltpu
from jax.sharding import PartitionSpec as P

H = 16
HD = 64
ROT = 16
EPS = 1e-05
F32 = jnp.float32
BF = jnp.bfloat16
MIB = 1024 * 1024
SD = jax.ShapeDtypeStruct
SMALL = pl.CostEstimate(flops=1000000, bytes_accessed=100000, transcendentals=0)


def dnn(a, b):
    return lax.dot_general(a, b, (((1,), (0,)), ((), ())), preferred_element_type=F32)


def dnt(a, b):
    return lax.dot_general(a, b, (((1,), (1,)), ((), ())), preferred_element_type=F32)


def dtn(a, b):
    return lax.dot_general(a, b, (((0,), (0,)), ((), ())), preferred_element_type=F32)


def normed(rows):
    x = rows.astype(F32)
    c = x - jnp.mean(x, axis=-1, keepdims=True)
    inv = lax.rsqrt(jnp.mean(c * c, axis=-1, keepdims=True) + EPS)
    return c * inv, inv


def tile(i, n):
    return pl.ds(pl.multiple_of(i * n, n), n)


def rows_tile(n, most):
    t = most
    while n % t:
        t -= 8
    return t


def mlp_kernel(rt, x_ref, dy_ref, wu_ref, bu_ref, wd_ref, gb_ref, act_ref, dpre_ref, h_ref, bu_out, *back):
    f = pl.program_id(0)
    if back:
        yp_ref, g2_ref, ln_ref, yacc, dacc = back
    last = pl.num_programs(0) - 1
    rows = x_ref.shape[0]

    @pl.when(f == 0)
    def _():
        @pl.loop(0, rows // 128)
        def _(i):
            r = tile(i, 128)
            xh, _ = normed(x_ref[r, :])
            h_ref[r, :] = (xh * gb_ref[0:1, :] + gb_ref[1:2, :]).astype(BF)
            if back:
                yacc[r, :] = jnp.zeros((128, yacc.shape[1]), F32)
                dacc[r, :] = jnp.zeros((128, dacc.shape[1]), F32)

    def step(i, bsum):
        r = tile(i, rt)
        pre = dnn(h_ref[r, :], wu_ref[...]) + bu_ref[...]
        da = dnt(dy_ref[r, :], wd_ref[...])
        cdf = 0.5 * (1.0 + lax.erf(pre * 0.7071067811865476))
        act = (pre * cdf).astype(BF)
        dpre = (da * (cdf + pre * jnp.exp(-0.5 * pre * pre) * 0.3989422804014327)).astype(BF)
        act_ref[r, :] = act
        dpre_ref[r, :] = dpre
        if back:
            yacc[r, :] += dnn(act, wd_ref[...])
            dacc[r, :] += dnt(dpre, wu_ref[...])
        return bsum + jnp.sum(dpre.astype(F32), axis=0, keepdims=True)

    bu_out[...] = lax.fori_loop(0, rows // rt, step, jnp.zeros(bu_out.shape, F32))
    if not back:
        return

    @pl.when(f == last)
    def _():
        ln_ref[...] = jnp.zeros_like(ln_ref)

        @pl.loop(0, rows // 128)
        def _(i):
            r = tile(i, 128)
            xh, _ = normed(x_ref[r, :])
            dh = dacc[r, :]
            yp_ref[r, :] = yacc[r, :].astype(BF)
            g2_ref[r, :] = (dh * gb_ref[0:1, :]).astype(BF)
            ln_ref[0:1, :] += jnp.sum(dh * xh, axis=0, keepdims=True)
            ln_ref[1:2, :] += jnp.sum(dh, axis=0, keepdims=True)


def mlp_rows(x, dy, wu, bu, wd, gb, back):
    rows, width = x.shape
    hidden = wu.shape[1]
    fb = min(512, hidden)
    full = lambda s: pl.BlockSpec(s, lambda f: (0,) * len(s))
    return pl.pallas_call(
        functools.partial(mlp_kernel, rows_tile(rows, 640)),
        grid=(hidden // fb,),
        in_specs=[
            full((rows, width)),
            full((rows, width)),
            pl.BlockSpec((width, fb), lambda f: (0, f)),
            pl.BlockSpec((1, fb), lambda f: (0, f)),
            pl.BlockSpec((fb, width), lambda f: (f, 0)),
            full((2, width)),
        ],
        out_specs=[
            pl.BlockSpec((rows, fb), lambda f: (0, f)),
            pl.BlockSpec((rows, fb), lambda f: (0, f)),
            full((rows, width)),
            pl.BlockSpec((1, fb), lambda f: (0, f)),
        ]
        + [full((rows, width)), full((rows, width)), full((2, width))] * back,
        out_shape=[SD((rows, hidden), BF), SD((rows, hidden), BF), SD((rows, width), BF), SD((1, hidden), F32)]
        + [SD((rows, width), BF), SD((rows, width), BF), SD((2, width), F32)] * back,
        scratch_shapes=[pltpu.VMEM((rows, width), F32)] * (2 * back),
        compiler_params=pltpu.CompilerParams(vmem_limit_bytes=60 * MIB),
        cost_estimate=SMALL,
    )(x, dy, wu, bu, wd, gb)


def roll8(x, left):
    w = x.shape[-1]
    return pltpu.roll(x, (w - 8) if left else 8, 1)


def attn_kernel(S, PD, CL, QB, HG, adding, me_ref, *refs):
    it = iter(refs)
    take = lambda n: [next(it) for _ in range(n)]
    stacked = S > 2
    per = 1 if stacked else S
    xs = take(per)
    dys = take(per)
    far = 1 if stacked else S - 1
    yps = take(far * adding)
    g2s = take(far * adding)
    wq, wk, wv = take(3)
    bq, bk, bv = take(3)
    wo, gb = take(2)
    cr, s1r, s2r = take(3)
    ys = take(far)
    gs = take(far)
    dl, ctx, h1, ln, db = take(5)
    yacc, dacc, q_s, k_s, v_s, dc_s, kT, vT, dk_s, dv_s = take(10)
    g = pl.program_id(0)
    last = pl.num_programs(0) - 1
    me = me_ref[0]
    N = xs[0].shape[-2]
    T = N * S
    PR = PD * S
    CR = N - PD
    W = HG * HD

    def every_slot(fn, start=0):
        if stacked:

            @pl.loop(start, S)
            def _(j):
                fn(j, lambda refs: refs[0].at[j], lambda refs: refs[0].at[j - 1])

        else:
            for j in range(start, S):
                fn(j, lambda refs: refs[j], lambda refs: refs[j - 1])

    def slot_rows(start, n):
        if start < PR:
            s, off = start // PD, start % PD
        else:
            s, off = (start - PR) // CR, PD + (start - PR) % CR
        return pl.ds(pl.multiple_of(lax.rem(s - me + S, S) * N + off, 128), n)

    def pieces(start, n):
        step = min(n, PD if start < PR else CR)
        return [(i, step) for i in range(0, n, step)]

    @pl.when(g == 0)
    def _():
        def load(j, of, away):
            x = of(xs)

            @pl.loop(0, N // 128)
            def _(i):
                xh, _ = normed(x[tile(i, 128), :])
                h1[pl.ds(pl.multiple_of(j * N + i * 128, 128), 128), :] = (xh * gb[0:1, :] + gb[1:2, :]).astype(BF)

        every_slot(load)

    def rot(y, r, scale):
        c = cr[r, :]
        s1 = s1r[r, :]
        s2 = s2r[r, :]
        out = []
        for p in range(W // 128):
            z = y[:, p * 128 : (p + 1) * 128]
            z = (z * c + roll8(z, True) * s1 + roll8(z, False) * s2).astype(BF)
            out.append(z * jnp.asarray(scale, BF) if scale != 1.0 else z)
        return jnp.concatenate(out, axis=1) if len(out) > 1 else out[0]

    def proj(j, of, away):
        s = lax.rem(me + j, S)
        rp = pl.ds(pl.multiple_of(s * PD, 128), PD)
        rc = pl.ds(pl.multiple_of(PR + s * CR, 128), CR)
        hh = h1[pl.ds(pl.multiple_of(j * N, 128), N), :]
        y = dnn(hh, wq[...]) + bq[...]
        q_s[rp, :] = rot(y[:PD], rp, HD**-0.5)
        q_s[rc, :] = rot(y[PD:], rc, HD**-0.5)
        y = dnn(hh, wk[...]) + bk[...]
        k_s[rp, :] = rot(y[:PD], rp, 1.0)
        k_s[rc, :] = rot(y[PD:], rc, 1.0)
        y = (dnn(hh, wv[...]) + bv[...]).astype(BF)
        v_s[rp, :] = y[:PD]
        v_s[rc, :] = y[PD:]
        y = dnt(of(dys)[...], wo[...]).astype(BF)
        dc_s[rp, :] = y[:PD]
        dc_s[rc, :] = y[PD:]

    def bring(j, of, away):
        nb = away(yps).shape[0]
        r = pl.ds(pl.multiple_of(g * nb, 16), nb)
        away(ys)[r, :] = away(yps)[...]
        away(gs)[r, :] = away(g2s)[...]

    every_slot(proj)
    if adding:
        every_slot(bring, 1)
    lane = lax.broadcasted_iota(jnp.int32, (1, 128), 1)
    row_i = lax.broadcasted_iota(jnp.int32, (QB, QB), 0)
    col_i = lax.broadcasted_iota(jnp.int32, (QB, QB), 1)
    causal = row_i <= col_i
    cmask = causal & ((row_i // CL) == (col_i // CL))
    blocks = []
    for i in range(PR // QB):
        blocks.append((i * QB, [(0, i * QB, None)] * (i > 0) + [(i * QB, QB, causal)]))
    for c in range((T - PR) // QB):
        blocks.append((PR + c * QB, [(0, PR, None), (PR + c * QB, QB, cmask)]))

    @pl.loop(0, W // 128)
    def _(p):
        lanes = tile(p, 128)
        kT[...] = k_s[:, lanes].T
        vT[...] = v_s[:, lanes].T
        dk_s[...] = jnp.zeros_like(dk_s)
        dv_s[...] = jnp.zeros_like(dv_s)
        def begin(q0, parts):
            qb = q_s[pl.ds(q0, QB), lanes]
            dcb = dc_s[pl.ds(q0, QB), lanes]
            out = []
            for h in range(2):
                sel = (lane >= HD * h) & (lane < HD * h + HD)
                qm = jnp.where(sel, qb, jnp.zeros_like(qb))
                dm = jnp.where(sel, dcb, jnp.zeros_like(dcb))
                ss = []
                for k0, n, mask in parts:
                    s = dnt(k_s[k0 : k0 + n, lanes], qm)
                    ss.append(s if mask is None else jnp.where(mask, s, -1e30))
                out.append((qm, dm, ss, [dnt(v_s[k0 : k0 + n, lanes], dm) for k0, n, _ in parts]))
            return out

        ahead = begin(*blocks[0])
        for b, (q0, parts) in enumerate(blocks):
            now = ahead
            if b + 1 < len(blocks):
                ahead = begin(*blocks[b + 1])
            rq = pl.ds(q0, QB)
            P_, DS, cT, dqT = [], [], [], []
            qh = [t[0] for t in now]
            dch = [t[1] for t in now]
            for h in range(2):
                _, _, ss, dps = now[h]
                m = functools.reduce(jnp.maximum, [jnp.max(s, axis=0, keepdims=True) for s in ss])
                es = [jnp.exp(s - m) for s in ss]
                rl = 1.0 / sum(jnp.sum(e, axis=0, keepdims=True) for e in es)
                ps = [e * rl for e in es]
                delta = sum(jnp.sum(a * b, axis=0, keepdims=True) for a, b in zip(ps, dps))
                P_.append([a.astype(BF) for a in ps])
                DS.append([(a * (b - delta)).astype(BF) for a, b in zip(ps, dps)])
                hr = slice(HD * h, HD * h + HD)
                cT.append(sum(dnn(vT[hr, k0 : k0 + n], a) for (k0, n, _), a in zip(parts, P_[h])))
                dqT.append(sum(dnn(kT[hr, k0 : k0 + n], a) for (k0, n, _), a in zip(parts, DS[h])))
            q2 = jnp.concatenate(qh, axis=0)
            dc2 = jnp.concatenate(dch, axis=0)
            for i, (k0, n, _) in enumerate(parts):
                dv_s[k0 : k0 + n, :] += dnn(jnp.concatenate([P_[0][i], P_[1][i]], axis=1), dc2)
                dk_s[k0 : k0 + n, :] += dnn(jnp.concatenate([DS[0][i], DS[1][i]], axis=1), q2)
            co = jnp.concatenate(cT, axis=0).T.astype(BF)
            z = jnp.concatenate(dqT, axis=0).T * (HD**-0.5)
            z = (z * cr[rq, :] - roll8(z, True) * s1r[rq, :] - roll8(z, False) * s2r[rq, :]).astype(BF)
            for o, n in pieces(q0, QB):
                ctx[slot_rows(q0 + o, n), lanes] = co[o : o + n]
                dl[0, slot_rows(q0 + o, n), lanes] = z[o : o + n]

        @pl.loop(0, S)
        def _(s):
            to = lax.rem(s - me + S, S) * N
            for src, off, n in ((s * PD, 0, PD), (PR + s * CR, PD, CR)):
                r = pl.ds(pl.multiple_of(src, 128), n)
                w = pl.ds(pl.multiple_of(to + off, 128), n)
                z = dk_s[r, :]
                z = z * cr[r, :] - roll8(z, True) * s1r[r, :] - roll8(z, False) * s2r[r, :]
                dl[1, w, lanes] = z.astype(BF)
                dl[2, w, lanes] = dv_s[r, :].astype(BF)

    for c in range(3):
        db[c : c + 1, :] = jnp.sum(dl[c].astype(F32), axis=0, keepdims=True)

    @pl.loop(1, S)
    def _(j):
        r = pl.ds(pl.multiple_of(j * N, 128), N)
        w = pl.ds(pl.multiple_of((j - 1) * N, 128), N)
        y = dnn(ctx[r, :], wo[...])
        d = dnt(dl[0, r, :], wq[...]) + dnt(dl[1, r, :], wk[...]) + dnt(dl[2, r, :], wv[...])

        @pl.when(g == 0)
        def _():
            yacc[w, :] = y
            dacc[w, :] = d

        @pl.when(g > 0)
        def _():
            yacc[w, :] += y
            dacc[w, :] += d

    @pl.when(g == last)
    def _():
        ln[...] = jnp.zeros_like(ln)

        def store(j, of, away):
            x, yo, go = of(xs), away(ys), away(gs)

            @pl.loop(0, N // 128)
            def _(i):
                r = tile(i, 128)
                w = pl.ds(pl.multiple_of((j - 1) * N + i * 128, 128), 128)
                xh, _ = normed(x[r, :])
                d = dacc[w, :]
                y = yacc[w, :]
                gg = d * gb[0:1, :]
                if adding:
                    y = y + yo[r, :].astype(F32)
                    gg = gg + go[r, :].astype(F32)
                yo[r, :] = y.astype(BF)
                go[r, :] = gg.astype(BF)
                ln[0:1, :] += jnp.sum(d * xh, axis=0, keepdims=True)
                ln[1:2, :] += jnp.sum(d, axis=0, keepdims=True)

        every_slot(store, 1)


def attn_group(S, PD, CL, me, xs, dys, yps, g2s, wqkv, bqkv, wo, gb, tabs):
    N, D = xs[0].shape
    CW = wo.shape[0]
    T = N * S
    HG = 4 if CW % 256 == 0 else 2
    QB = 256
    W = HG * HD
    G = CW // W
    full = lambda s: pl.BlockSpec(s, lambda g, m: (0,) * len(s), pipeline_mode=pl.Buffered(1))
    keep = lambda s: pl.BlockSpec(s, lambda g, m: (0,) * len(s))
    tok, tok_out, per, far = full((N, D)), keep((N, D)), S, S - 1
    adding = int(T * D <= 1536 * 1024)
    others = (yps, g2s)
    if not adding:
        yps, g2s = [], []
    out_tok = SD((N, D), BF)
    part = pl.BlockSpec((N // G, D), lambda g, m: (g, 0))
    if S > 2:
        xs, dys, yps, g2s = [[jnp.stack(v, axis=0)] if v else v for v in (xs, dys, yps, g2s)]
        tok, tok_out, per, far = full((S, N, D)), keep((S - 1, N, D)), 1, 1
        out_tok = SD((S - 1, N, D), BF)
        part = pl.BlockSpec((S - 1, N // G, D), lambda g, m: (0, g, 0))
    wspec = lambda c: pl.BlockSpec((D, W), lambda g, m: (0, c * G + g))
    bspec = lambda c: pl.BlockSpec((1, W), lambda g, m: (0, c * G + g))
    outs = pl.pallas_call(
        functools.partial(attn_kernel, S, PD, CL, QB, HG, adding),
        grid_spec=pltpu.PrefetchScalarGridSpec(
            num_scalar_prefetch=1,
            grid=(G,),
            in_specs=[tok] * (2 * per)
            + [part] * (2 * adding * far)
            + [wspec(0), wspec(1), wspec(2), bspec(0), bspec(1), bspec(2)]
            + [pl.BlockSpec((W, D), lambda g, m: (g, 0)), full((2, D))]
            + [full((T, 128))] * 3,
            out_specs=[tok_out] * (2 * far)
            + [
                pl.BlockSpec((3, T, W), lambda g, m: (0, 0, g)),
                pl.BlockSpec((T, W), lambda g, m: (0, g)),
                keep((T, D)),
                keep((2, D)),
                pl.BlockSpec((3, W), lambda g, m: (0, g)),
            ],
            scratch_shapes=[pltpu.VMEM((T - N, D), F32)] * 2
            + [pltpu.VMEM((T, W), BF)] * 4
            + [pltpu.VMEM((128, T), BF)] * 2
            + [pltpu.VMEM((T, 128), F32)] * 2,
        ),
        out_shape=[out_tok] * (2 * far)
        + [SD((3, T, CW), BF), SD((T, CW), BF), SD((T, D), BF), SD((2, D), F32), SD((3, CW), F32)],
        compiler_params=pltpu.CompilerParams(vmem_limit_bytes=62 * MIB),
        cost_estimate=SMALL,
    )(me, *xs, *dys, *yps, *g2s, wqkv, wqkv, wqkv, bqkv, bqkv, bqkv, wo, gb, *tabs)
    ys, gs = outs[:far], outs[far : 2 * far]
    if S > 2:
        ys, gs = [[v[0][j] for j in range(S - 1)] for v in (ys, gs)]
    if not adding:
        ys, gs = [[a + b for a, b in zip(p, q)] for p, q in zip((ys, gs), others)]
    return ys, gs, outs[2 * far :]


def tn_kernel(n, wide, *refs):
    a = refs[:n]
    b = refs[n : 2 * n]
    o = refs[2 * n]
    if wide == 0:
        o[...] = sum(dtn(x[...], y[...]) for x, y in zip(a, b)).astype(BF)
    else:
        w = b[0].shape[2]
        for c in range(wide):
            o[:, c * w : (c + 1) * w] = sum(dtn(x[...], y[c]) for x, y in zip(a, b)).astype(BF)


def tn_sum(a, b, block):
    n = len(a)
    rows, da = a[0].shape
    block = min(block, da)
    wide = b[0].shape[0] if b[0].ndim == 3 else 0
    db = b[0].shape[-1] * max(wide, 1)
    keep = lambda s: pl.BlockSpec(s, lambda i: (0,) * len(s), pipeline_mode=pl.Buffered(1))
    return pl.pallas_call(
        functools.partial(tn_kernel, n, wide),
        grid=(da // block,),
        in_specs=[pl.BlockSpec((rows, block), lambda i: (0, i))] * n + [keep(b[0].shape)] * n,
        out_specs=pl.BlockSpec((block, db), lambda i: (i, 0)),
        out_shape=SD((da, db), BF),
        compiler_params=pltpu.CompilerParams(vmem_limit_bytes=60 * MIB),
        cost_estimate=SMALL,
    )(*a, *b)


def joined(refs):
    return jnp.concatenate([r[...] for r in refs], axis=0)


def down_kernel(n, more, *refs):
    o = refs[-1]
    t = dtn(joined(refs[:n]), joined(refs[n : 2 * n])).reshape(o.shape)
    o[...] = (t + refs[2 * n][...].astype(F32) if more else t).astype(BF)


def up_kernel(n, more, *refs):
    o = refs[-1]
    c, rows, w = o.shape
    t = dtn(joined(refs[:n]), joined(refs[n : 2 * n]))
    k = t.shape[1] // w
    for i in range(k):
        r = slice(i * (rows // k), (i + 1) * (rows // k))
        p = t[:, i * w : (i + 1) * w].reshape(c, rows // k, w)
        o[:, r, :] = (p + refs[2 * n][:, r, :].astype(F32) if more else p).astype(BF)


def mlp_grads(S, R, acts, dys, hs, dpres, g=None):
    n = len(acts)
    rows, FL = acts[0].shape
    D = dys[0].shape[1]
    DR = D // S
    blk = 256
    rd = FL // R
    ru = DR // R
    k = FL // D
    per = rd + S * ru * k
    keep = lambda s: pl.BlockSpec(s, lambda i: (0,) * len(s), pipeline_mode=pl.Buffered(1))
    steps = DR // blk
    more = g is not None
    hbm = pl.BlockSpec(memory_space=pl.ANY)

    def call(kernel, a, b, spec, g):
        width = b[0].shape[1]
        prior = [] if g is None else [g]
        return pl.pallas_call(
            functools.partial(kernel, n, more),
            grid=(a[0].shape[1] // blk,),
            in_specs=[pl.BlockSpec((rows, blk), lambda i: (0, i))] * n
            + [keep((rows, width))] * n
            + ([spec if more else hbm] if prior else []),
            out_specs=spec,
            out_shape=SD((R, per, D), BF),
            input_output_aliases={2 * n: 0} if prior else {},
            compiler_params=pltpu.CompilerParams(vmem_limit_bytes=60 * MIB),
            cost_estimate=SMALL,
        )(*a, *b, *prior)

    g = call(down_kernel, acts, dys, pl.BlockSpec((blk // rd, rd, D), lambda i: (i, 0, 0)), g)
    spec = pl.BlockSpec((blk // ru, ru * k, D), lambda i: (i % steps, rd // (ru * k) + i // steps, 0))
    return call(up_kernel, hs, dpres, spec, g)


def mlp_finish_kernel(S, rd, ru, g, down, up):
    n, per, D = g.shape
    k = (per - rd) // (S * ru)
    for c in range(n):
        down[c * rd : (c + 1) * rd, :] = g[c, :rd, :].astype(F32)
        for t in range(S * k):
            a = rd + t * ru
            up[c * ru : (c + 1) * ru, t * D : (t + 1) * D] = g[c, a : a + ru, :].astype(F32)


def mlp_finish(S, g, FL):
    R, per, D = g.shape
    rd = FL // R
    ru = D // S // R
    n = 4
    return pl.pallas_call(
        functools.partial(mlp_finish_kernel, S, rd, ru),
        grid=(R // n,),
        in_specs=[pl.BlockSpec((n, per, D), lambda c: (c, 0, 0))],
        out_specs=[pl.BlockSpec((n * rd, D), lambda c: (c, 0)), pl.BlockSpec((n * ru, S * FL), lambda c: (c, 0))],
        out_shape=[SD((FL, D), F32), SD((D // S, S * FL), F32)],
        compiler_params=pltpu.CompilerParams(vmem_limit_bytes=40 * MIB),
        cost_estimate=SMALL,
    )(g)


def attn_grads_kernel(n, S, R, q_ref, *refs):
    h = refs[:n]
    dl = refs[n : 2 * n]
    ctx = refs[2 * n : 3 * n]
    dy = refs[3 * n : -4]
    first, second = refs[-4:-2], refs[-2:]
    i = pl.program_id(0)
    q1 = q_ref[0]
    q2 = q_ref[1]
    blk = h[0].shape[1]
    D = dy[0].shape[1]
    DR = D // S
    CW = dl[0].shape[2]
    ru = DR // R
    k = D // CW
    steps = DR // blk
    s = i // steps
    base = (i % steps) * (blk // ru)

    def put(pair, pos, rows, v):
        for half in range(2):

            @pl.when(pos // (R // 2) == half)
            def _():
                pair[half][pos % (R // 2), rows, :] = v

    for p in range(3):
        t = dtn(joined(h), jnp.concatenate([y[p] for y in dl], axis=0)).astype(BF)
        for c in range(blk // ru):
            v = t[c * ru : (c + 1) * ru, :]
            if p < 2:
                put(first, (base + c) ^ q1, pl.ds(s * 2 * ru + p * ru, ru), v)
            else:
                put(second, (base + c) ^ q2, pl.ds(k * ru + s * ru, ru), v)
    t = dtn(joined(ctx), joined(dy)).astype(BF)
    m = ctx[0].shape[1] // ru
    for c in range(m):
        for j in range(k):
            put(second, (i * m + c) ^ q2, pl.ds(j * ru, ru), t[c * ru : (c + 1) * ru, j * CW : (j + 1) * CW])


def attn_grads(S, R, q, hs, dls, ctxs, dys):
    n = len(hs)
    T, D = hs[0].shape
    CW = ctxs[0].shape[1]
    DR = D // S
    ru = DR // R
    blk = 256
    G = D // blk
    keep = lambda s: pl.BlockSpec(s, lambda i, q: (0,) * len(s), pipeline_mode=pl.Buffered(1))
    shapes = [(R // 2, S * 2 * ru, CW)] * 2 + [(R // 2, (D // CW + S) * ru, CW)] * 2
    return pl.pallas_call(
        functools.partial(attn_grads_kernel, n, S, R),
        grid_spec=pltpu.PrefetchScalarGridSpec(
            num_scalar_prefetch=1,
            grid=(G,),
            in_specs=[pl.BlockSpec((T, blk), lambda i, q: (0, i))] * n
            + [keep((3, T, CW))] * n
            + [pl.BlockSpec((T, CW // G), lambda i, q: (0, i))] * n
            + [keep(dys[0].shape)] * len(dys),
            out_specs=[pl.BlockSpec(s, lambda i, q: (0, 0, 0)) for s in shapes],
        ),
        out_shape=[SD(s, BF) for s in shapes],
        compiler_params=pltpu.CompilerParams(vmem_limit_bytes=60 * MIB),
        cost_estimate=SMALL,
    )(q, *hs, *dls, *ctxs, *dys)


def attn_finish_kernel(S, ru, k, n, half, q_ref, *refs):
    out, qkv = refs[4 * n :]
    CW = refs[0].shape[2]
    D = out.shape[1]
    i = pl.program_id(0)

    def piece(which, c, a):
        low, high = refs[2 * which * n + c], refs[(2 * which + 1) * n + c]
        here = ((i * n + c) ^ q_ref[which]) < half
        rows = pl.ds(a, ru)
        return jnp.where(here, low[0, rows, :].astype(F32), high[0, rows, :].astype(F32))

    for c in range(n):
        r = slice(c * ru, (c + 1) * ru)
        for j in range(k):
            out[r, j * CW : (j + 1) * CW] = piece(1, c, j * ru)
        for t in range(S):
            for p in range(3):
                v = piece(0, c, (t * 2 + p) * ru) if p < 2 else piece(1, c, (k + t) * ru)
                qkv[r, p * D + t * CW : p * D + (t + 1) * CW] = v


def attn_finish(S, q, one, two):
    half, per1, CW = one[0].shape
    per2 = two[0].shape[1]
    R = 2 * half
    D = CW * S
    ru = D // S // R
    n = 4
    place_of = lambda i, q, k, c: (i * n + c) ^ q[k]
    low = lambda per, k, c: pl.BlockSpec((1, per, CW), lambda i, q: (jnp.minimum(place_of(i, q, k, c), half - 1), 0, 0))
    high = lambda per, k, c: pl.BlockSpec((1, per, CW), lambda i, q: (jnp.maximum(place_of(i, q, k, c) - half, 0), 0, 0))
    specs = [f(per, k, c) for k, per in ((0, per1), (1, per2)) for f in (low, high) for c in range(n)]
    return pl.pallas_call(
        functools.partial(attn_finish_kernel, S, ru, S, n, half),
        grid_spec=pltpu.PrefetchScalarGridSpec(
            num_scalar_prefetch=1,
            grid=(R // n,),
            in_specs=specs,
            out_specs=[pl.BlockSpec((n * ru, D), lambda c, q: (c, 0)), pl.BlockSpec((n * ru, 3 * D), lambda c, q: (c, 0))],
        ),
        out_shape=[SD((CW, D), F32), SD((D // S, 3 * D), F32)],
        compiler_params=pltpu.CompilerParams(vmem_limit_bytes=40 * MIB),
        cost_estimate=SMALL,
    )(q, *[a for pair in (one, two) for arr in pair for a in [arr] * n])


def own_kernel(dl, ctx, wqkv, wo, x, yp, g2, gb, y, g, ln, d1):
    N = x.shape[0]
    CW = ctx.shape[1]
    d1[...] = sum(dnt(dl[p], wqkv[:, p * CW : (p + 1) * CW]) for p in range(3))
    y[...] = (yp[...].astype(F32) + dnn(ctx[...], wo[...])).astype(BF)
    ln[...] = jnp.zeros_like(ln)

    @pl.loop(0, N // 128)
    def _(i):
        r = tile(i, 128)
        xh, _ = normed(x[r, :])
        a = d1[r, :]
        g[r, :] = (a * gb[0:1, :] + g2[r, :].astype(F32)).astype(BF)
        ln[0:1, :] += jnp.sum(a * xh, axis=0, keepdims=True)
        ln[1:2, :] += jnp.sum(a, axis=0, keepdims=True)


def own_rows(x, yp, g2, dl, ctx, wqkv, wo, gb):
    N, D = x.shape
    CW = wo.shape[0]
    full = lambda s: pl.BlockSpec(s, lambda f: (0,) * len(s))
    return pl.pallas_call(
        own_kernel,
        grid=(1,),
        in_specs=[full((3, N, CW)), full((N, CW)), full((D, 3 * CW)), full((CW, D))] + [full((N, D))] * 3 + [full((2, D))],
        out_specs=[full((N, D)), full((N, D)), full((2, D))],
        out_shape=[SD((N, D), BF), SD((N, D), BF), SD((2, D), F32)],
        scratch_shapes=[pltpu.VMEM((N, D), F32)],
        compiler_params=pltpu.CompilerParams(vmem_limit_bytes=60 * MIB),
        cost_estimate=SMALL,
    )(dl, ctx, wqkv, wo, x, yp, g2, gb)


def final_kernel(S, first, PT, *refs):
    it = iter(refs)
    take = lambda n: [next(it) for _ in range(n)]
    x, dy = take(2)
    ys = take(S)
    gs = take(S)
    (vb,) = take(1)
    if not first:
        take(4)
    po, co, pg, cg = take(4)
    i = pl.program_id(0)
    xv = x[...].astype(F32)
    xh, inv = normed(xv)
    y = xv + vb[0:1, :] + sum(r[...].astype(F32) for r in ys) + vb[1:2, :]
    gsum = sum(r[...].astype(F32) for r in gs)
    dx = (gsum - jnp.mean(gsum, axis=-1, keepdims=True) - xh * jnp.mean(gsum * xh, axis=-1, keepdims=True)) * inv
    out = y.astype(BF)
    grad = dy[...].astype(F32) + dx

    @pl.when(i < PT)
    def _():
        po[0] = out
        pg[0] = grad

    @pl.when(i >= PT)
    def _():
        co[0] = out
        cg[0] = grad


def final_rows(m, MB, PD, x, dy, ys, gs, vb, prior):
    S = len(ys)
    N, D = x.shape
    CR = N - PD
    RT = 128
    PT = PD // RT
    first = prior is None
    row = pl.BlockSpec((RT, D), lambda i: (i, 0))
    pspec = pl.BlockSpec((1, RT, D), lambda i: (m, jnp.minimum(i, PT - 1), 0))
    cspec = pl.BlockSpec((1, RT, D), lambda i: (m, jnp.maximum(i - PT, 0), 0))
    hbm = pl.BlockSpec(memory_space=pl.ANY)
    n_in = 2 * S + 3
    return pl.pallas_call(
        functools.partial(final_kernel, S, first, PT),
        grid=(N // RT,),
        in_specs=[row] * (2 * S + 2) + [pl.BlockSpec((2, D), lambda i: (0, 0))] + ([] if first else [hbm] * 4),
        out_specs=[pspec, cspec, pspec, cspec],
        out_shape=[SD((MB, PD, D), BF), SD((MB, CR, D), BF), SD((MB, PD, D), F32), SD((MB, CR, D), F32)],
        input_output_aliases={} if first else {n_in + k: k for k in range(4)},
        compiler_params=pltpu.CompilerParams(vmem_limit_bytes=32 * MIB),
        cost_estimate=SMALL,
    )(x, dy, *ys, *gs, vb, *(() if first else prior))


def shifted(value, S, j):
    return lax.ppermute(value, "shard", [(i, (i + j) % S) for i in range(S)])


def canonical(slots, me, S, back):
    if S == 1:
        return slots
    if S == 2:
        a, b = slots
        return [jnp.where(me == 0, a, b), jnp.where(me == 0, b, a)]
    stacked = jnp.stack(slots, axis=0)
    return [
        lax.dynamic_index_in_dim(stacked, lax.rem((me - s if back else s - me) + S, S), 0, keepdims=False) for s in range(S)
    ]


def exchanged(value, R, bit):
    return lax.ppermute(value, "rep", [(i, i ^ bit) for i in range(R)])


def columns_for(weight, me, S, j, parts, row=0, rows=None):
    cols = weight.shape[1] // parts
    rows = weight.shape[0] if rows is None else rows
    w = cols // S
    at = lax.rem(me + j, S) * w
    got = [lax.dynamic_slice(weight, (row, p * cols + at), (rows, w)) for p in range(parts)]
    return got[0] if parts == 1 else jnp.concatenate(got, axis=1)


def half_pieces(weight, me, S):
    n = weight.shape[0] // 2
    at = lax.axis_index("rep") % 2 * n
    return [columns_for(weight, me, S, j, 1, at, n) for j in range(1, S)]


def from_halves(weight, pieces, me, S, R):
    first = lax.axis_index("rep") % 2 == 0
    slots = [columns_for(weight, me, S, 0, 1)]
    for piece in pieces:
        other = exchanged(piece, R, 1)
        slots.append(jnp.concatenate([jnp.where(first, piece, other), jnp.where(first, other, piece)], axis=0))
    return jnp.concatenate(canonical(slots, me, S, True), axis=0)


def rep_pieces(weight, me, S, R, parts):
    n = weight.shape[0] // R
    rep = lax.axis_index("rep")
    return [columns_for(weight, me, S, j, parts, rep * n, n) for j in range(1, S)]


def from_rep(weight, pieces, me, S, parts):
    others = lax.all_gather(jnp.stack(pieces, axis=0), "rep", axis=1, tiled=True)
    slots = [columns_for(weight, me, S, 0, parts)] + [others[j] for j in range(S - 1)]
    return jnp.concatenate(canonical(slots, me, S, True), axis=0)


def add_low(a, b):
    return (a.astype(F32) + b.astype(F32)).astype(BF)


def orders(R):
    bits = [1 << i for i in range(R.bit_length() - 1)]
    return bits, bits[:1] + bits[2:] + bits[1:2]


def place(rep, order):
    q = jnp.zeros((), jnp.int32)
    for bit in order:
        q = 2 * q + (rep & bit) // bit
    return q


def beside_it(got, key, beside):
    if key in beside:
        got, beside[key] = lax.optimization_barrier((got, beside[key]))
    return got


def halving(pairs, R, beside):
    for i, bits in enumerate(zip(*orders(R))):
        got = beside_it([exchanged(p[1], R, bit) for p, bit in zip(pairs, bits)], i, beside)
        h = got[0].shape[0] // 2
        if h:
            pairs = [(add_low(p[0][:h], t[:h]), add_low(p[0][h:], t[h:])) for p, t in zip(pairs, got)]
        else:
            pairs = [add_low(p[0], t) for p, t in zip(pairs, got)]
    return [p[0] for p in pairs]


def doubling(parts, R, beside):
    pair = [p[None] for p in parts]
    for i, bits in reversed(list(enumerate(zip(*orders(R))))):
        got = beside_it([exchanged(g, R, bit) for g, bit in zip(pair, bits)], i, beside)
        if i:
            pair = [jnp.concatenate([g, t], axis=0) for g, t in zip(pair, got)]
    return list(zip(pair, got))


def hops(v, R):
    out = []
    for b in range(R.bit_length() - 1):
        v = v + exchanged(v, R, 1 << b)
        out.append(v)
    return out


def sum_all(v, S, R):
    bit = 1
    while bit < R:
        v = v + exchanged(v, R, bit)
        bit *= 2
    return v


def swap_shards(part, me, S, head):
    n = (part.shape[0] - head) // S
    slots = []
    for j in range(S):
        b = lax.dynamic_slice_in_dim(part, head + lax.rem(me + j, S) * n, n, 0)
        slots.append(shifted(b, S, j) if j else b)
    return jnp.concatenate(([part[:head]] if head else []) + canonical(slots, me, S, True), axis=0)


def reduce_rows(grad):
    part = lax.psum_scatter(grad, "rep", scatter_dimension=0, tiled=True)
    return lax.all_gather(part, "rep", axis=0, tiled=True).astype(F32)


def reduce_columns(grad, me, S, parts):
    rows, cols = grad.shape
    part = lax.psum_scatter(grad.reshape(S, rows // S, cols), "rep", scatter_dimension=1, tiled=True)
    slots = [lax.dynamic_index_in_dim(part, me, 0, keepdims=False)]
    for j in range(1, S):
        slots.append(shifted(lax.dynamic_index_in_dim(part, lax.rem(me + j, S), 0, keepdims=False), S, j))
    slots = [s.reshape(s.shape[0], parts, cols // parts) for s in slots]
    whole = jnp.stack(canonical(slots, me, S, True), axis=2).reshape(-1, S * cols)
    return lax.all_gather(whole, "rep", axis=0, tiled=True).astype(F32)


def rotary_tables(PR, CR, CL):
    pos = np.concatenate([np.arange(PR), PR + np.arange(CR) % CL]).astype(np.float32)
    half = ROT // 2
    freq = np.exp(np.arange(half, dtype=np.float32) * np.float32(-2.0 * math.log(10000.0) / ROT)).astype(np.float32)
    ang = (pos[:, None] * freq[None, :]).astype(np.float32)
    c = np.cos(ang)
    s = np.sin(ang)
    n = pos.shape[0]
    one = np.ones((n, HD - ROT), np.float32)
    zero = np.zeros((n, HD - ROT), np.float32)
    z8 = np.zeros((n, half), np.float32)
    tabs = ([c, c, one], [-s, z8, zero], [z8, s, zero])
    return [jnp.asarray(np.tile(np.concatenate(t, axis=1), (1, 128 // HD)), F32) for t in tabs]


def per_device(
    prompt_in,
    cont_in,
    prompt_cot,
    cont_cot,
    ln1_gain,
    ln1_bias,
    ln2_gain,
    ln2_bias,
    qkv_weight,
    qkv_bias,
    out_weight,
    out_bias,
    up_weight,
    up_bias,
    down_weight,
    down_bias,
):
    S = lax.axis_size("shard")
    R = lax.axis_size("rep")
    me = lax.axis_index("shard")
    MB, _, PD, D = prompt_in.shape
    CD, CL = cont_in.shape[2:4]
    CR = CD * CL
    N = PD + CR
    CW = D // S
    FL = up_weight.shape[1] // S
    me_arr = jnp.reshape(me, (1,)).astype(jnp.int32)

    X = [[jnp.concatenate([prompt_in[m, 0], cont_in[m, 0].reshape(CR, D)], axis=0)] for m in range(MB)]
    DY = [[jnp.concatenate([prompt_cot[m, 0], cont_cot[m, 0].reshape(CR, D)], axis=0)] for m in range(MB)]
    away = lambda values: [shifted(v, S, j + 1) for j, v in enumerate(values)]
    cut = half_pieces(up_weight, me, S)
    vectors_in = (ln1_gain, ln1_bias, ln2_gain, ln2_bias, out_bias, down_bias, qkv_bias)
    (vectors_in, qkv_weight), cut = lax.optimization_barrier(((vectors_in, qkv_weight), cut))
    small = jnp.concatenate([v.astype(F32).reshape(-1, CW) for v in vectors_in], axis=0)
    slots = [small] + away([small] * (S - 1))
    pieces_qkv = away(rep_pieces(qkv_weight, me, S, R, 3))
    pieces_up = away(cut)
    src = [(X[m][0], DY[m][0]) for m in range(MB)]
    src[1:], _ = lax.optimization_barrier((src[1:], pieces_up))
    pieces_up, _ = lax.optimization_barrier((pieces_up, (X[0][0], DY[0][0])))
    src[0], _ = lax.optimization_barrier((src[0], (slots[1:])))
    w_up = from_halves(up_weight, pieces_up, me, S, R)
    w_qkv = from_rep(qkv_weight, pieces_qkv, me, S, 3)

    whole = jnp.stack(canonical(slots, me, S, True), axis=0)
    vec = whole[:, :6].transpose(1, 0, 2).reshape(6, D)
    gb1 = vec[0:2]
    gb2 = vec[2:4]
    vb = vec[4:6]
    bqkv = whole[:, 6:].reshape(3, S, CW)
    bqkv = lax.dynamic_index_in_dim(bqkv, me, 1, keepdims=False).reshape(1, 3 * CW)
    bup = up_bias.astype(F32).reshape(1, FL)

    tabs = rotary_tables(PD * S, CR * S, CL)
    for m in range(MB):
        for j in range(1, S):
            X[m].append(shifted(src[m][0], S, S - j))
            DY[m].append(shifted(src[m][1], S, S - j))

    ff = [[None] * S for _ in range(MB)]

    def mlp(m, j):
        ff[m][j] = mlp_rows(X[m][j], DY[m][j], w_up, bup, down_weight, gb2, 1)

    for m in range(MB):
        mlp(m, 0)
    rest = []
    y_got, g_got = [], []

    def attend(m):
        ys, gs, more = attn_group(
            S, PD, CL, me_arr, X[m], DY[m], [f[4] for f in ff[m][1:]], [f[5] for f in ff[m][1:]], w_qkv, bqkv, out_weight, gb1, tabs
        )
        rest.append(list(more))
        y_got.append([shifted(ys[j - 1], S, j) for j in range(1, S)])
        g_got.append([shifted(gs[j - 1], S, j) for j in range(1, S)])

    def own(m):
        f = ff[m][0]
        return own_rows(X[m][0], f[4], f[5], rest[m][0], rest[m][1], w_qkv, out_weight, gb1)

    chunked = (D // S // R) % 16 == 0 and R & (R - 1) == 0
    rep = lax.axis_index("rep")
    late = [(MB - 1, j) for j in range(1, S)]
    early = [(m, j) for m in range(MB) for j in range(S) if (m, j) not in late]
    of = lambda set_, k: [ff[m][j][k] for m, j in set_]
    for m, j in early:
        if j:
            mlp(m, j)
    if chunked:
        gmlp = mlp_grads(S, R, of(early, 0), [DY[m][j] for m, j in early], of(early, 2), of(early, 1))
        w_up, gmlp = lax.optimization_barrier((w_up, gmlp))
    for m, j in late:
        mlp(m, j)
    if chunked:
        if late:
            gmlp = mlp_grads(S, R, of(late, 0), [DY[m][j] for m, j in late], of(late, 2), of(late, 1), gmlp)
        part = lax.psum_scatter(gmlp, "rep", scatter_dimension=0, tiled=True)[0]
        w_qkv, gmlp = lax.optimization_barrier((w_qkv, gmlp))
    for m in range(MB):
        attend(m)
        if m + 1 < MB:
            w_qkv, rest[m][3] = lax.optimization_barrier((w_qkv, rest[m][3]))
    every = early + late
    def vectors(mine_):
        ln1 = sum(r[3] for r in rest) + sum(o[2] for o in mine_)
        ln2 = sum(of(every, 6))
        db_out = sum(jnp.sum(DY[m][0].astype(F32), axis=0) for m in range(MB)).reshape(-1, CW)
        mine = (jnp.arange(S) == me).astype(F32)
        db_qkv = (sum(r[4] for r in rest)[:, None, :] * mine[None, :, None]).reshape(-1, CW)
        db_up = (sum(of(every, 3)) * mine[:, None]).reshape(-1, CW)
        return jnp.concatenate([ln1.reshape(-1, CW), ln2.reshape(-1, CW), db_out, db_qkv, db_up], axis=0)

    finals = lambda m, o, prior: final_rows(m, MB, PD, X[m][0], DY[m][0], [o[0]] + y_got[m], [o[1]] + g_got[m], vb, prior)
    hs, dls, ctxs = [[r[k] for r in rest] for k in (2, 0, 1)]
    if chunked:
        q = jnp.stack([place(rep, order) for order in orders(R)]).astype(jnp.int32)
        part = swap_shards(part, me, S, FL // R)
        hs, y_got[:-1], g_got[:-1], part = lax.optimization_barrier((hs, y_got[:-1], g_got[:-1], part))
        gmlp_all = lax.all_gather(part, "rep", axis=0, tiled=False)
        gatt = attn_grads(S, R, q, hs, dls, ctxs, [DY[m][j] for m in range(MB) for j in range(S)])
        dls_own, _ = lax.optimization_barrier(([r[0] for r in rest], gatt))
        for m in range(MB):
            rest[m][0] = dls_own[m]
        mine = [own(m) for m in range(MB)]
        beside = {1: mine}
        levels = R.bit_length() - 1
        path = hops(vectors(mine), R)
        late_hops = {}
        for n, v in enumerate(path):
            at = 2 + n
            (beside if at < levels else late_hops).setdefault(at if at < levels else max(2 * levels - 1 - at, 0), []).append(v)
        outs = None
        for m in range(MB - 1):
            outs = finals(m, mine[m], outs)
        whole_outs = finals(MB - 1, mine[-1], outs)
        beside[levels - 1] = beside.get(levels - 1, []) + [y_got[-1], g_got[-1]]
        half = halving([gatt[:2], gatt[2:]], R, beside)
        k = D // CW * (D // S // R)
        finished = mlp_finish(S, gmlp_all, FL)
        after = {3: (outs, late_hops.get(3, [])), 2: (finished, late_hops.get(2, [])), 1: (whole_outs, late_hops.get(1, []))}
        g1, g2 = doubling([swap_shards(half[0], me, S, 0), swap_shards(half[1], me, S, k)], R, after)
        outs = after[1][0]
        g_down, g_up = after[2][0]
        vecs = path[-1]
        g_out, g_qkv = attn_finish(S, q, g1, g2)
    else:
        dls, ctxs, hs = [[r[k] for r in rest] for k in (0, 1, 2)]
        mine = [own(m) for m in range(MB)]
        g_down = reduce_rows(tn_sum(of(every, 0), [DY[m][j] for m, j in every], 256))
        g_up = reduce_columns(tn_sum(of(every, 2), of(every, 1), 256), me, S, 1)
        dycs = [jnp.concatenate(DY[m], axis=0) for m in range(MB)]
        g_out = reduce_rows(tn_sum(ctxs, dycs, 256))
        g_qkv = reduce_columns(tn_sum(hs, dls, 256), me, S, 3)
        vecs = sum_all(vectors(mine), S, R)
        outs = None
        for m in range(MB):
            outs = finals(m, mine[m], outs)
    tot = vecs + sum(shifted(vecs, S, j) for j in range(1, S))
    held = lambda a, n: lax.dynamic_slice_in_dim(tot, a + me * n, n, 0).reshape(-1)
    v_ln1g, v_ln1b, v_ln2g, v_ln2b, v_out = [held(k * S, 1) for k in range(5)]
    v_qkv = held(5 * S, 3)
    v_up = held(8 * S, FL // CW)

    po, co, pg, cg = outs
    return (
        po.reshape(MB, 1, PD, D),
        co.reshape(MB, 1, CD, CL, D),
        pg.reshape(MB, 1, PD, D),
        cg.reshape(MB, 1, CD, CL, D),
        v_ln1g,
        v_ln1b,
        v_ln2g,
        v_ln2b,
        g_qkv,
        v_qkv,
        g_out,
        v_out,
        g_up,
        v_up,
        g_down,
        v_out,
    )


def solution(mesh):
    tokens = (
        P(None, "rep", "shard", None),
        P(None, "rep", "shard", None, None),
        P(None, "rep", "shard", None),
        P(None, "rep", "shard", None, None),
    )
    vec = P("shard")
    mat = P("shard", None)
    params = (vec, vec, vec, vec, mat, vec, mat, vec, mat, vec, mat, vec)
    return jax.shard_map(
        per_device, mesh=mesh, in_specs=tokens + params, out_specs=tokens + params, check_vma=False
    )
```

```python
import functools
import math

import jax
import jax.numpy as jnp
import numpy as np
from jax import lax
from jax.experimental import pallas as pl
from jax.experimental.pallas import tpu as pltpu
from jax.sharding import PartitionSpec as P

H = 16
HD = 64
ROT = 16
EPS = 1e-05
F32 = jnp.float32
BF = jnp.bfloat16
MIB = 1024 * 1024
SD = jax.ShapeDtypeStruct
SMALL = pl.CostEstimate(flops=1000000, bytes_accessed=100000, transcendentals=0)


def dnn(a, b):
    return lax.dot_general(a, b, (((1,), (0,)), ((), ())), preferred_element_type=F32)


def dnt(a, b):
    return lax.dot_general(a, b, (((1,), (1,)), ((), ())), preferred_element_type=F32)


def dtn(a, b):
    return lax.dot_general(a, b, (((0,), (0,)), ((), ())), preferred_element_type=F32)


def normed(rows):
    x = rows.astype(F32)
    c = x - jnp.mean(x, axis=-1, keepdims=True)
    inv = lax.rsqrt(jnp.mean(c * c, axis=-1, keepdims=True) + EPS)
    return c * inv, inv


def tile(i, n):
    return pl.ds(pl.multiple_of(i * n, n), n)


def rows_tile(n, most):
    t = most
    while n % t:
        t -= 8
    return t


def mlp_kernel(rt, x_ref, dy_ref, wu_ref, bu_ref, wd_ref, gb_ref, act_ref, dpre_ref, h_ref, bu_out, *back):
    f = pl.program_id(0)
    if back:
        yp_ref, g2_ref, ln_ref, yacc, dacc = back
    last = pl.num_programs(0) - 1
    rows = x_ref.shape[0]

    @pl.when(f == 0)
    def _():
        @pl.loop(0, rows // 128)
        def _(i):
            r = tile(i, 128)
            xh, _ = normed(x_ref[r, :])
            h_ref[r, :] = (xh * gb_ref[0:1, :] + gb_ref[1:2, :]).astype(BF)
            if back:
                yacc[r, :] = jnp.zeros((128, yacc.shape[1]), F32)
                dacc[r, :] = jnp.zeros((128, dacc.shape[1]), F32)

    def step(i, bsum):
        r = tile(i, rt)
        pre = dnn(h_ref[r, :], wu_ref[...]) + bu_ref[...]
        da = dnt(dy_ref[r, :], wd_ref[...])
        cdf = 0.5 * (1.0 + lax.erf(pre * 0.7071067811865476))
        act = (pre * cdf).astype(BF)
        dpre = (da * (cdf + pre * jnp.exp(-0.5 * pre * pre) * 0.3989422804014327)).astype(BF)
        act_ref[r, :] = act
        dpre_ref[r, :] = dpre
        if back:
            yacc[r, :] += dnn(act, wd_ref[...])
            dacc[r, :] += dnt(dpre, wu_ref[...])
        return bsum + jnp.sum(dpre.astype(F32), axis=0, keepdims=True)

    bu_out[...] = lax.fori_loop(0, rows // rt, step, jnp.zeros(bu_out.shape, F32))
    if not back:
        return

    @pl.when(f == last)
    def _():
        ln_ref[...] = jnp.zeros_like(ln_ref)

        @pl.loop(0, rows // 128)
        def _(i):
            r = tile(i, 128)
            xh, _ = normed(x_ref[r, :])
            dh = dacc[r, :]
            yp_ref[r, :] = yacc[r, :].astype(BF)
            g2_ref[r, :] = (dh * gb_ref[0:1, :]).astype(BF)
            ln_ref[0:1, :] += jnp.sum(dh * xh, axis=0, keepdims=True)
            ln_ref[1:2, :] += jnp.sum(dh, axis=0, keepdims=True)


def mlp_rows(x, dy, wu, bu, wd, gb, back):
    rows, width = x.shape
    hidden = wu.shape[1]
    fb = min(512, hidden)
    full = lambda s: pl.BlockSpec(s, lambda f: (0,) * len(s))
    return pl.pallas_call(
        functools.partial(mlp_kernel, rows_tile(rows, 640)),
        grid=(hidden // fb,),
        in_specs=[
            full((rows, width)),
            full((rows, width)),
            pl.BlockSpec((width, fb), lambda f: (0, f)),
            pl.BlockSpec((1, fb), lambda f: (0, f)),
            pl.BlockSpec((fb, width), lambda f: (f, 0)),
            full((2, width)),
        ],
        out_specs=[
            pl.BlockSpec((rows, fb), lambda f: (0, f)),
            pl.BlockSpec((rows, fb), lambda f: (0, f)),
            full((rows, width)),
            pl.BlockSpec((1, fb), lambda f: (0, f)),
        ]
        + [full((rows, width)), full((rows, width)), full((2, width))] * back,
        out_shape=[SD((rows, hidden), BF), SD((rows, hidden), BF), SD((rows, width), BF), SD((1, hidden), F32)]
        + [SD((rows, width), BF), SD((rows, width), BF), SD((2, width), F32)] * back,
        scratch_shapes=[pltpu.VMEM((rows, width), F32)] * (2 * back),
        compiler_params=pltpu.CompilerParams(vmem_limit_bytes=60 * MIB),
        cost_estimate=SMALL,
    )(x, dy, wu, bu, wd, gb)


def roll8(x, left):
    w = x.shape[-1]
    return pltpu.roll(x, (w - 8) if left else 8, 1)


def attn_kernel(S, PD, CL, QB, HG, adding, me_ref, *refs):
    it = iter(refs)
    take = lambda n: [next(it) for _ in range(n)]
    stacked = S > 2
    per = 1 if stacked else S
    xs = take(per)
    dys = take(per)
    far = 1 if stacked else S - 1
    yps = take(far * adding)
    g2s = take(far * adding)
    wq, wk, wv = take(3)
    bq, bk, bv = take(3)
    wo, gb = take(2)
    cr, s1r, s2r = take(3)
    ys = take(far)
    gs = take(far)
    dl, ctx, h1, ln, db = take(5)
    yacc, dacc, q_s, k_s, v_s, dc_s, kT, vT, dk_s, dv_s = take(10)
    g = pl.program_id(0)
    last = pl.num_programs(0) - 1
    me = me_ref[0]
    N = xs[0].shape[-2]
    T = N * S
    PR = PD * S
    CR = N - PD
    W = HG * HD

    def every_slot(fn, start=0):
        if stacked:

            @pl.loop(start, S)
            def _(j):
                fn(j, lambda refs: refs[0].at[j], lambda refs: refs[0].at[j - 1])

        else:
            for j in range(start, S):
                fn(j, lambda refs: refs[j], lambda refs: refs[j - 1])

    def slot_rows(start, n):
        if start < PR:
            s, off = start // PD, start % PD
        else:
            s, off = (start - PR) // CR, PD + (start - PR) % CR
        return pl.ds(pl.multiple_of(lax.rem(s - me + S, S) * N + off, 128), n)

    def pieces(start, n):
        step = min(n, PD if start < PR else CR)
        return [(i, step) for i in range(0, n, step)]

    @pl.when(g == 0)
    def _():
        def load(j, of, away):
            x = of(xs)

            @pl.loop(0, N // 128)
            def _(i):
                xh, _ = normed(x[tile(i, 128), :])
                h1[pl.ds(pl.multiple_of(j * N + i * 128, 128), 128), :] = (xh * gb[0:1, :] + gb[1:2, :]).astype(BF)

        every_slot(load)

    def rot(y, r, scale):
        c = cr[r, :]
        s1 = s1r[r, :]
        s2 = s2r[r, :]
        out = []
        for p in range(W // 128):
            z = y[:, p * 128 : (p + 1) * 128]
            z = (z * c + roll8(z, True) * s1 + roll8(z, False) * s2).astype(BF)
            out.append(z * jnp.asarray(scale, BF) if scale != 1.0 else z)
        return jnp.concatenate(out, axis=1) if len(out) > 1 else out[0]

    def proj(j, of, away):
        s = lax.rem(me + j, S)
        rp = pl.ds(pl.multiple_of(s * PD, 128), PD)
        rc = pl.ds(pl.multiple_of(PR + s * CR, 128), CR)
        hh = h1[pl.ds(pl.multiple_of(j * N, 128), N), :]
        y = dnn(hh, wq[...]) + bq[...]
        q_s[rp, :] = rot(y[:PD], rp, HD**-0.5)
        q_s[rc, :] = rot(y[PD:], rc, HD**-0.5)
        y = dnn(hh, wk[...]) + bk[...]
        k_s[rp, :] = rot(y[:PD], rp, 1.0)
        k_s[rc, :] = rot(y[PD:], rc, 1.0)
        y = (dnn(hh, wv[...]) + bv[...]).astype(BF)
        v_s[rp, :] = y[:PD]
        v_s[rc, :] = y[PD:]
        y = dnt(of(dys)[...], wo[...]).astype(BF)
        dc_s[rp, :] = y[:PD]
        dc_s[rc, :] = y[PD:]

    def bring(j, of, away):
        nb = away(yps).shape[0]
        r = pl.ds(pl.multiple_of(g * nb, 16), nb)
        away(ys)[r, :] = away(yps)[...]
        away(gs)[r, :] = away(g2s)[...]

    every_slot(proj)
    if adding:
        every_slot(bring, 1)
    lane = lax.broadcasted_iota(jnp.int32, (1, 128), 1)
    row_i = lax.broadcasted_iota(jnp.int32, (QB, QB), 0)
    col_i = lax.broadcasted_iota(jnp.int32, (QB, QB), 1)
    causal = row_i <= col_i
    cmask = causal & ((row_i // CL) == (col_i // CL))
    blocks = []
    for i in range(PR // QB):
        blocks.append((i * QB, [(0, i * QB, None)] * (i > 0) + [(i * QB, QB, causal)]))
    for c in range((T - PR) // QB):
        blocks.append((PR + c * QB, [(0, PR, None), (PR + c * QB, QB, cmask)]))

    @pl.loop(0, W // 128)
    def _(p):
        lanes = tile(p, 128)
        kT[...] = k_s[:, lanes].T
        vT[...] = v_s[:, lanes].T
        dk_s[...] = jnp.zeros_like(dk_s)
        dv_s[...] = jnp.zeros_like(dv_s)
        def begin(q0, parts):
            qb = q_s[pl.ds(q0, QB), lanes]
            dcb = dc_s[pl.ds(q0, QB), lanes]
            out = []
            for h in range(2):
                sel = (lane >= HD * h) & (lane < HD * h + HD)
                qm = jnp.where(sel, qb, jnp.zeros_like(qb))
                dm = jnp.where(sel, dcb, jnp.zeros_like(dcb))
                ss = []
                for k0, n, mask in parts:
                    s = dnt(k_s[k0 : k0 + n, lanes], qm)
                    ss.append(s if mask is None else jnp.where(mask, s, -1e30))
                out.append((qm, dm, ss, [dnt(v_s[k0 : k0 + n, lanes], dm) for k0, n, _ in parts]))
            return out

        ahead = begin(*blocks[0])
        for b, (q0, parts) in enumerate(blocks):
            now = ahead
            if b + 1 < len(blocks):
                ahead = begin(*blocks[b + 1])
            rq = pl.ds(q0, QB)
            P_, DS, cT, dqT = [], [], [], []
            qh = [t[0] for t in now]
            dch = [t[1] for t in now]
            for h in range(2):
                _, _, ss, dps = now[h]
                m = functools.reduce(jnp.maximum, [jnp.max(s, axis=0, keepdims=True) for s in ss])
                es = [jnp.exp(s - m) for s in ss]
                rl = 1.0 / sum(jnp.sum(e, axis=0, keepdims=True) for e in es)
                ps = [e * rl for e in es]
                delta = sum(jnp.sum(a * b, axis=0, keepdims=True) for a, b in zip(ps, dps))
                P_.append([a.astype(BF) for a in ps])
                DS.append([(a * (b - delta)).astype(BF) for a, b in zip(ps, dps)])
                hr = slice(HD * h, HD * h + HD)
                cT.append(sum(dnn(vT[hr, k0 : k0 + n], a) for (k0, n, _), a in zip(parts, P_[h])))
                dqT.append(sum(dnn(kT[hr, k0 : k0 + n], a) for (k0, n, _), a in zip(parts, DS[h])))
            q2 = jnp.concatenate(qh, axis=0)
            dc2 = jnp.concatenate(dch, axis=0)
            for i, (k0, n, _) in enumerate(parts):
                dv_s[k0 : k0 + n, :] += dnn(jnp.concatenate([P_[0][i], P_[1][i]], axis=1), dc2)
                dk_s[k0 : k0 + n, :] += dnn(jnp.concatenate([DS[0][i], DS[1][i]], axis=1), q2)
            co = jnp.concatenate(cT, axis=0).T.astype(BF)
            z = jnp.concatenate(dqT, axis=0).T * (HD**-0.5)
            z = (z * cr[rq, :] - roll8(z, True) * s1r[rq, :] - roll8(z, False) * s2r[rq, :]).astype(BF)
            for o, n in pieces(q0, QB):
                ctx[slot_rows(q0 + o, n), lanes] = co[o : o + n]
                dl[0, slot_rows(q0 + o, n), lanes] = z[o : o + n]

        @pl.loop(0, S)
        def _(s):
            to = lax.rem(s - me + S, S) * N
            for src, off, n in ((s * PD, 0, PD), (PR + s * CR, PD, CR)):
                r = pl.ds(pl.multiple_of(src, 128), n)
                w = pl.ds(pl.multiple_of(to + off, 128), n)
                z = dk_s[r, :]
                z = z * cr[r, :] - roll8(z, True) * s1r[r, :] - roll8(z, False) * s2r[r, :]
                dl[1, w, lanes] = z.astype(BF)
                dl[2, w, lanes] = dv_s[r, :].astype(BF)

    for c in range(3):
        db[c : c + 1, :] = jnp.sum(dl[c].astype(F32), axis=0, keepdims=True)

    @pl.loop(1, S)
    def _(j):
        r = pl.ds(pl.multiple_of(j * N, 128), N)
        w = pl.ds(pl.multiple_of((j - 1) * N, 128), N)
        y = dnn(ctx[r, :], wo[...])
        d = dnt(dl[0, r, :], wq[...]) + dnt(dl[1, r, :], wk[...]) + dnt(dl[2, r, :], wv[...])

        @pl.when(g == 0)
        def _():
            yacc[w, :] = y
            dacc[w, :] = d

        @pl.when(g > 0)
        def _():
            yacc[w, :] += y
            dacc[w, :] += d

    @pl.when(g == last)
    def _():
        ln[...] = jnp.zeros_like(ln)

        def store(j, of, away):
            x, yo, go = of(xs), away(ys), away(gs)

            @pl.loop(0, N // 128)
            def _(i):
                r = tile(i, 128)
                w = pl.ds(pl.multiple_of((j - 1) * N + i * 128, 128), 128)
                xh, _ = normed(x[r, :])
                d = dacc[w, :]
                y = yacc[w, :]
                gg = d * gb[0:1, :]
                if adding:
                    y = y + yo[r, :].astype(F32)
                    gg = gg + go[r, :].astype(F32)
                yo[r, :] = y.astype(BF)
                go[r, :] = gg.astype(BF)
                ln[0:1, :] += jnp.sum(d * xh, axis=0, keepdims=True)
                ln[1:2, :] += jnp.sum(d, axis=0, keepdims=True)

        every_slot(store, 1)


def attn_group(S, PD, CL, me, xs, dys, yps, g2s, wqkv, bqkv, wo, gb, tabs):
    N, D = xs[0].shape
    CW = wo.shape[0]
    T = N * S
    HG = 4 if CW % 256 == 0 else 2
    QB = 256
    W = HG * HD
    G = CW // W
    full = lambda s: pl.BlockSpec(s, lambda g, m: (0,) * len(s), pipeline_mode=pl.Buffered(1))
    keep = lambda s: pl.BlockSpec(s, lambda g, m: (0,) * len(s))
    tok, tok_out, per, far = full((N, D)), keep((N, D)), S, S - 1
    adding = int(T * D <= 1536 * 1024)
    others = (yps, g2s)
    if not adding:
        yps, g2s = [], []
    out_tok = SD((N, D), BF)
    part = pl.BlockSpec((N // G, D), lambda g, m: (g, 0))
    if S > 2:
        xs, dys, yps, g2s = [[jnp.stack(v, axis=0)] if v else v for v in (xs, dys, yps, g2s)]
        tok, tok_out, per, far = full((S, N, D)), keep((S - 1, N, D)), 1, 1
        out_tok = SD((S - 1, N, D), BF)
        part = pl.BlockSpec((S - 1, N // G, D), lambda g, m: (0, g, 0))
    wspec = lambda c: pl.BlockSpec((D, W), lambda g, m: (0, c * G + g))
    bspec = lambda c: pl.BlockSpec((1, W), lambda g, m: (0, c * G + g))
    outs = pl.pallas_call(
        functools.partial(attn_kernel, S, PD, CL, QB, HG, adding),
        grid_spec=pltpu.PrefetchScalarGridSpec(
            num_scalar_prefetch=1,
            grid=(G,),
            in_specs=[tok] * (2 * per)
            + [part] * (2 * adding * far)
            + [wspec(0), wspec(1), wspec(2), bspec(0), bspec(1), bspec(2)]
            + [pl.BlockSpec((W, D), lambda g, m: (g, 0)), full((2, D))]
            + [full((T, 128))] * 3,
            out_specs=[tok_out] * (2 * far)
            + [
                pl.BlockSpec((3, T, W), lambda g, m: (0, 0, g)),
                pl.BlockSpec((T, W), lambda g, m: (0, g)),
                keep((T, D)),
                keep((2, D)),
                pl.BlockSpec((3, W), lambda g, m: (0, g)),
            ],
            scratch_shapes=[pltpu.VMEM((T - N, D), F32)] * 2
            + [pltpu.VMEM((T, W), BF)] * 4
            + [pltpu.VMEM((128, T), BF)] * 2
            + [pltpu.VMEM((T, 128), F32)] * 2,
        ),
        out_shape=[out_tok] * (2 * far)
        + [SD((3, T, CW), BF), SD((T, CW), BF), SD((T, D), BF), SD((2, D), F32), SD((3, CW), F32)],
        compiler_params=pltpu.CompilerParams(vmem_limit_bytes=62 * MIB),
        cost_estimate=SMALL,
    )(me, *xs, *dys, *yps, *g2s, wqkv, wqkv, wqkv, bqkv, bqkv, bqkv, wo, gb, *tabs)
    ys, gs = outs[:far], outs[far : 2 * far]
    if S > 2:
        ys, gs = [[v[0][j] for j in range(S - 1)] for v in (ys, gs)]
    if not adding:
        ys, gs = [[a + b for a, b in zip(p, q)] for p, q in zip((ys, gs), others)]
    return ys, gs, outs[2 * far :]


def tn_kernel(n, wide, *refs):
    a = refs[:n]
    b = refs[n : 2 * n]
    o = refs[2 * n]
    if wide == 0:
        o[...] = sum(dtn(x[...], y[...]) for x, y in zip(a, b)).astype(BF)
    else:
        w = b[0].shape[2]
        for c in range(wide):
            o[:, c * w : (c + 1) * w] = sum(dtn(x[...], y[c]) for x, y in zip(a, b)).astype(BF)


def tn_sum(a, b, block):
    n = len(a)
    rows, da = a[0].shape
    block = min(block, da)
    wide = b[0].shape[0] if b[0].ndim == 3 else 0
    db = b[0].shape[-1] * max(wide, 1)
    keep = lambda s: pl.BlockSpec(s, lambda i: (0,) * len(s), pipeline_mode=pl.Buffered(1))
    return pl.pallas_call(
        functools.partial(tn_kernel, n, wide),
        grid=(da // block,),
        in_specs=[pl.BlockSpec((rows, block), lambda i: (0, i))] * n + [keep(b[0].shape)] * n,
        out_specs=pl.BlockSpec((block, db), lambda i: (i, 0)),
        out_shape=SD((da, db), BF),
        compiler_params=pltpu.CompilerParams(vmem_limit_bytes=60 * MIB),
        cost_estimate=SMALL,
    )(*a, *b)


def joined(refs):
    return jnp.concatenate([r[...] for r in refs], axis=0)


def down_kernel(n, more, *refs):
    o = refs[-1]
    t = dtn(joined(refs[:n]), joined(refs[n : 2 * n])).reshape(o.shape)
    o[...] = (t + refs[2 * n][...].astype(F32) if more else t).astype(BF)


def up_kernel(n, more, *refs):
    o = refs[-1]
    c, rows, w = o.shape
    t = dtn(joined(refs[:n]), joined(refs[n : 2 * n]))
    k = t.shape[1] // w
    for i in range(k):
        r = slice(i * (rows // k), (i + 1) * (rows // k))
        p = t[:, i * w : (i + 1) * w].reshape(c, rows // k, w)
        o[:, r, :] = (p + refs[2 * n][:, r, :].astype(F32) if more else p).astype(BF)


def mlp_grads(S, R, acts, dys, hs, dpres, g=None):
    n = len(acts)
    rows, FL = acts[0].shape
    D = dys[0].shape[1]
    DR = D // S
    blk = 256
    rd = FL // R
    ru = DR // R
    k = FL // D
    per = rd + S * ru * k
    keep = lambda s: pl.BlockSpec(s, lambda i: (0,) * len(s), pipeline_mode=pl.Buffered(1))
    steps = DR // blk
    more = g is not None
    hbm = pl.BlockSpec(memory_space=pl.ANY)

    def call(kernel, a, b, spec, g):
        width = b[0].shape[1]
        prior = [] if g is None else [g]
        return pl.pallas_call(
            functools.partial(kernel, n, more),
            grid=(a[0].shape[1] // blk,),
            in_specs=[pl.BlockSpec((rows, blk), lambda i: (0, i))] * n
            + [keep((rows, width))] * n
            + ([spec if more else hbm] if prior else []),
            out_specs=spec,
            out_shape=SD((R, per, D), BF),
            input_output_aliases={2 * n: 0} if prior else {},
            compiler_params=pltpu.CompilerParams(vmem_limit_bytes=60 * MIB),
            cost_estimate=SMALL,
        )(*a, *b, *prior)

    g = call(down_kernel, acts, dys, pl.BlockSpec((blk // rd, rd, D), lambda i: (i, 0, 0)), g)
    spec = pl.BlockSpec((blk // ru, ru * k, D), lambda i: (i % steps, rd // (ru * k) + i // steps, 0))
    return call(up_kernel, hs, dpres, spec, g)


def mlp_finish_kernel(S, rd, ru, g, down, up):
    n, per, D = g.shape
    k = (per - rd) // (S * ru)
    for c in range(n):
        down[c * rd : (c + 1) * rd, :] = g[c, :rd, :].astype(F32)
        for t in range(S * k):
            a = rd + t * ru
            up[c * ru : (c + 1) * ru, t * D : (t + 1) * D] = g[c, a : a + ru, :].astype(F32)


def mlp_finish(S, g, FL):
    R, per, D = g.shape
    rd = FL // R
    ru = D // S // R
    n = 4
    return pl.pallas_call(
        functools.partial(mlp_finish_kernel, S, rd, ru),
        grid=(R // n,),
        in_specs=[pl.BlockSpec((n, per, D), lambda c: (c, 0, 0))],
        out_specs=[pl.BlockSpec((n * rd, D), lambda c: (c, 0)), pl.BlockSpec((n * ru, S * FL), lambda c: (c, 0))],
        out_shape=[SD((FL, D), F32), SD((D // S, S * FL), F32)],
        compiler_params=pltpu.CompilerParams(vmem_limit_bytes=40 * MIB),
        cost_estimate=SMALL,
    )(g)


def attn_grads_kernel(n, S, R, q_ref, *refs):
    h = refs[:n]
    dl = refs[n : 2 * n]
    ctx = refs[2 * n : 3 * n]
    dy = refs[3 * n : -2]
    first, second = refs[-2:-1], refs[-1:]
    i = pl.program_id(0)
    q1 = q_ref[0]
    q2 = q_ref[1]
    blk = h[0].shape[1]
    D = dy[0].shape[1]
    DR = D // S
    CW = dl[0].shape[2]
    ru = DR // R
    k = D // CW
    steps = DR // blk
    s = i // steps
    base = (i % steps) * (blk // ru)

    def put(pair, pos, rows, v):
        pair[0][pos, rows, :] = v

    for p in range(3):
        t = dtn(joined(h), jnp.concatenate([y[p] for y in dl], axis=0)).astype(BF)
        for c in range(blk // ru):
            v = t[c * ru : (c + 1) * ru, :]
            if p < 2:
                put(first, (base + c) ^ q1, pl.ds(s * 2 * ru + p * ru, ru), v)
            else:
                put(second, (base + c) ^ q2, pl.ds(k * ru + s * ru, ru), v)
    t = dtn(joined(ctx), joined(dy)).astype(BF)
    m = ctx[0].shape[1] // ru
    for c in range(m):
        for j in range(k):
            put(second, (i * m + c) ^ q2, pl.ds(j * ru, ru), t[c * ru : (c + 1) * ru, j * CW : (j + 1) * CW])


def attn_grads(S, R, q, hs, dls, ctxs, dys):
    n = len(hs)
    T, D = hs[0].shape
    CW = ctxs[0].shape[1]
    DR = D // S
    ru = DR // R
    blk = 256
    G = D // blk
    keep = lambda s: pl.BlockSpec(s, lambda i, q: (0,) * len(s), pipeline_mode=pl.Buffered(1))
    shapes = [(R, S * 2 * ru, CW), (R, (D // CW + S) * ru, CW)]
    return pl.pallas_call(
        functools.partial(attn_grads_kernel, n, S, R),
        grid_spec=pltpu.PrefetchScalarGridSpec(
            num_scalar_prefetch=1,
            grid=(G,),
            in_specs=[pl.BlockSpec((T, blk), lambda i, q: (0, i))] * n
            + [keep((3, T, CW))] * n
            + [pl.BlockSpec((T, CW // G), lambda i, q: (0, i))] * n
            + [keep(dys[0].shape)] * len(dys),
            out_specs=[pl.BlockSpec(s, lambda i, q: (0, 0, 0)) for s in shapes],
        ),
        out_shape=[SD(s, BF) for s in shapes],
        compiler_params=pltpu.CompilerParams(vmem_limit_bytes=60 * MIB),
        cost_estimate=SMALL,
    )(q, *hs, *dls, *ctxs, *dys)


def attn_finish_kernel(S, ru, k, n, half, q_ref, *refs):
    out, qkv = refs[4 * n :]
    CW = refs[0].shape[2]
    D = out.shape[1]
    i = pl.program_id(0)

    def piece(which, c, a):
        low, high = refs[2 * which * n + c], refs[(2 * which + 1) * n + c]
        here = ((i * n + c) ^ q_ref[which]) < half
        rows = pl.ds(a, ru)
        return jnp.where(here, low[0, rows, :].astype(F32), high[0, rows, :].astype(F32))

    for c in range(n):
        r = slice(c * ru, (c + 1) * ru)
        for j in range(k):
            out[r, j * CW : (j + 1) * CW] = piece(1, c, j * ru)
        for t in range(S):
            for p in range(3):
                v = piece(0, c, (t * 2 + p) * ru) if p < 2 else piece(1, c, (k + t) * ru)
                qkv[r, p * D + t * CW : p * D + (t + 1) * CW] = v


def attn_finish(S, q, one, two):
    half, per1, CW = one[0].shape
    per2 = two[0].shape[1]
    R = 2 * half
    D = CW * S
    ru = D // S // R
    n = 4
    place_of = lambda i, q, k, c: (i * n + c) ^ q[k]
    low = lambda per, k, c: pl.BlockSpec((1, per, CW), lambda i, q: (jnp.minimum(place_of(i, q, k, c), half - 1), 0, 0))
    high = lambda per, k, c: pl.BlockSpec((1, per, CW), lambda i, q: (jnp.maximum(place_of(i, q, k, c) - half, 0), 0, 0))
    specs = [f(per, k, c) for k, per in ((0, per1), (1, per2)) for f in (low, high) for c in range(n)]
    return pl.pallas_call(
        functools.partial(attn_finish_kernel, S, ru, S, n, half),
        grid_spec=pltpu.PrefetchScalarGridSpec(
            num_scalar_prefetch=1,
            grid=(R // n,),
            in_specs=specs,
            out_specs=[pl.BlockSpec((n * ru, D), lambda c, q: (c, 0)), pl.BlockSpec((n * ru, 3 * D), lambda c, q: (c, 0))],
        ),
        out_shape=[SD((CW, D), F32), SD((D // S, 3 * D), F32)],
        compiler_params=pltpu.CompilerParams(vmem_limit_bytes=40 * MIB),
        cost_estimate=SMALL,
    )(q, *[a for pair in (one, two) for arr in pair for a in [arr] * n])


def own_kernel(dl, ctx, wqkv, wo, x, yp, g2, gb, y, g, ln, d1):
    N = x.shape[0]
    CW = ctx.shape[1]
    d1[...] = sum(dnt(dl[p], wqkv[:, p * CW : (p + 1) * CW]) for p in range(3))
    y[...] = (yp[...].astype(F32) + dnn(ctx[...], wo[...])).astype(BF)
    ln[...] = jnp.zeros_like(ln)

    @pl.loop(0, N // 128)
    def _(i):
        r = tile(i, 128)
        xh, _ = normed(x[r, :])
        a = d1[r, :]
        g[r, :] = (a * gb[0:1, :] + g2[r, :].astype(F32)).astype(BF)
        ln[0:1, :] += jnp.sum(a * xh, axis=0, keepdims=True)
        ln[1:2, :] += jnp.sum(a, axis=0, keepdims=True)


def own_rows(x, yp, g2, dl, ctx, wqkv, wo, gb):
    N, D = x.shape
    CW = wo.shape[0]
    full = lambda s: pl.BlockSpec(s, lambda f: (0,) * len(s))
    return pl.pallas_call(
        own_kernel,
        grid=(1,),
        in_specs=[full((3, N, CW)), full((N, CW)), full((D, 3 * CW)), full((CW, D))] + [full((N, D))] * 3 + [full((2, D))],
        out_specs=[full((N, D)), full((N, D)), full((2, D))],
        out_shape=[SD((N, D), BF), SD((N, D), BF), SD((2, D), F32)],
        scratch_shapes=[pltpu.VMEM((N, D), F32)],
        compiler_params=pltpu.CompilerParams(vmem_limit_bytes=60 * MIB),
        cost_estimate=SMALL,
    )(dl, ctx, wqkv, wo, x, yp, g2, gb)


def final_kernel(S, first, PT, *refs):
    it = iter(refs)
    take = lambda n: [next(it) for _ in range(n)]
    x, dy = take(2)
    ys = take(S)
    gs = take(S)
    (vb,) = take(1)
    if not first:
        take(4)
    po, co, pg, cg = take(4)
    i = pl.program_id(0)
    xv = x[...].astype(F32)
    xh, inv = normed(xv)
    y = xv + vb[0:1, :] + sum(r[...].astype(F32) for r in ys) + vb[1:2, :]
    gsum = sum(r[...].astype(F32) for r in gs)
    dx = (gsum - jnp.mean(gsum, axis=-1, keepdims=True) - xh * jnp.mean(gsum * xh, axis=-1, keepdims=True)) * inv
    out = y.astype(BF)
    grad = dy[...].astype(F32) + dx

    @pl.when(i < PT)
    def _():
        po[0] = out
        pg[0] = grad

    @pl.when(i >= PT)
    def _():
        co[0] = out
        cg[0] = grad


def final_rows(m, MB, PD, x, dy, ys, gs, vb, prior):
    S = len(ys)
    N, D = x.shape
    CR = N - PD
    RT = 128
    PT = PD // RT
    first = prior is None
    row = pl.BlockSpec((RT, D), lambda i: (i, 0))
    pspec = pl.BlockSpec((1, RT, D), lambda i: (m, jnp.minimum(i, PT - 1), 0))
    cspec = pl.BlockSpec((1, RT, D), lambda i: (m, jnp.maximum(i - PT, 0), 0))
    hbm = pl.BlockSpec(memory_space=pl.ANY)
    n_in = 2 * S + 3
    return pl.pallas_call(
        functools.partial(final_kernel, S, first, PT),
        grid=(N // RT,),
        in_specs=[row] * (2 * S + 2) + [pl.BlockSpec((2, D), lambda i: (0, 0))] + ([] if first else [hbm] * 4),
        out_specs=[pspec, cspec, pspec, cspec],
        out_shape=[SD((MB, PD, D), BF), SD((MB, CR, D), BF), SD((MB, PD, D), F32), SD((MB, CR, D), F32)],
        input_output_aliases={} if first else {n_in + k: k for k in range(4)},
        compiler_params=pltpu.CompilerParams(vmem_limit_bytes=32 * MIB),
        cost_estimate=SMALL,
    )(x, dy, *ys, *gs, vb, *(() if first else prior))


def shifted(value, S, j):
    return lax.ppermute(value, "shard", [(i, (i + j) % S) for i in range(S)])


def canonical(slots, me, S, back):
    if S == 1:
        return slots
    if S == 2:
        a, b = slots
        return [jnp.where(me == 0, a, b), jnp.where(me == 0, b, a)]
    stacked = jnp.stack(slots, axis=0)
    return [
        lax.dynamic_index_in_dim(stacked, lax.rem((me - s if back else s - me) + S, S), 0, keepdims=False) for s in range(S)
    ]


def exchanged(value, R, bit):
    return lax.ppermute(value, "rep", [(i, i ^ bit) for i in range(R)])


def columns_for(weight, me, S, j, parts, row=0, rows=None):
    cols = weight.shape[1] // parts
    rows = weight.shape[0] if rows is None else rows
    w = cols // S
    at = lax.rem(me + j, S) * w
    got = [lax.dynamic_slice(weight, (row, p * cols + at), (rows, w)) for p in range(parts)]
    return got[0] if parts == 1 else jnp.concatenate(got, axis=1)


def half_pieces(weight, me, S):
    n = weight.shape[0] // 2
    at = lax.axis_index("rep") % 2 * n
    return [columns_for(weight, me, S, j, 1, at, n) for j in range(1, S)]


def from_halves(weight, pieces, me, S, R):
    first = lax.axis_index("rep") % 2 == 0
    slots = [columns_for(weight, me, S, 0, 1)]
    for piece in pieces:
        other = exchanged(piece, R, 1)
        slots.append(jnp.concatenate([jnp.where(first, piece, other), jnp.where(first, other, piece)], axis=0))
    return jnp.concatenate(canonical(slots, me, S, True), axis=0)


def rep_pieces(weight, me, S, R, parts):
    n = weight.shape[0] // R
    rep = lax.axis_index("rep")
    return [columns_for(weight, me, S, j, parts, rep * n, n) for j in range(1, S)]


def from_rep(weight, pieces, me, S, parts):
    others = lax.all_gather(jnp.stack(pieces, axis=0), "rep", axis=1, tiled=True)
    slots = [columns_for(weight, me, S, 0, parts)] + [others[j] for j in range(S - 1)]
    return jnp.concatenate(canonical(slots, me, S, True), axis=0)


def add_low(a, b):
    return (a.astype(F32) + b.astype(F32)).astype(BF)


def orders(R):
    bits = [1 << i for i in range(R.bit_length() - 1)]
    return bits, bits[:1] + bits[2:] + bits[1:2]


def place(rep, order):
    q = jnp.zeros((), jnp.int32)
    for bit in order:
        q = 2 * q + (rep & bit) // bit
    return q


def beside_it(got, key, beside):
    if key in beside:
        got, beside[key] = lax.optimization_barrier((got, beside[key]))
    return got


def halving(pairs, R, beside):
    for i, bits in enumerate(zip(*orders(R))):
        got = beside_it([exchanged(p[1], R, bit) for p, bit in zip(pairs, bits)], i, beside)
        h = got[0].shape[0] // 2
        if h:
            pairs = [(add_low(p[0][:h], t[:h]), add_low(p[0][h:], t[h:])) for p, t in zip(pairs, got)]
        else:
            pairs = [add_low(p[0], t) for p, t in zip(pairs, got)]
    return [p[0] for p in pairs]


def doubling(parts, R, beside):
    pair = [p[None] for p in parts]
    for i, bits in reversed(list(enumerate(zip(*orders(R))))):
        got = beside_it([exchanged(g, R, bit) for g, bit in zip(pair, bits)], i, beside)
        if i:
            pair = [jnp.concatenate([g, t], axis=0) for g, t in zip(pair, got)]
    return list(zip(pair, got))


def hops(v, R):
    out = []
    for b in range(R.bit_length() - 1):
        v = v + exchanged(v, R, 1 << b)
        out.append(v)
    return out


def sum_all(v, S, R):
    bit = 1
    while bit < R:
        v = v + exchanged(v, R, bit)
        bit *= 2
    return v


def swap_shards(part, me, S, head):
    n = (part.shape[0] - head) // S
    slots = []
    for j in range(S):
        b = lax.dynamic_slice_in_dim(part, head + lax.rem(me + j, S) * n, n, 0)
        slots.append(shifted(b, S, j) if j else b)
    return jnp.concatenate(([part[:head]] if head else []) + canonical(slots, me, S, True), axis=0)


def reduce_rows(grad):
    part = lax.psum_scatter(grad, "rep", scatter_dimension=0, tiled=True)
    return lax.all_gather(part, "rep", axis=0, tiled=True).astype(F32)


def reduce_columns(grad, me, S, parts):
    rows, cols = grad.shape
    part = lax.psum_scatter(grad.reshape(S, rows // S, cols), "rep", scatter_dimension=1, tiled=True)
    slots = [lax.dynamic_index_in_dim(part, me, 0, keepdims=False)]
    for j in range(1, S):
        slots.append(shifted(lax.dynamic_index_in_dim(part, lax.rem(me + j, S), 0, keepdims=False), S, j))
    slots = [s.reshape(s.shape[0], parts, cols // parts) for s in slots]
    whole = jnp.stack(canonical(slots, me, S, True), axis=2).reshape(-1, S * cols)
    return lax.all_gather(whole, "rep", axis=0, tiled=True).astype(F32)


def rotary_tables(PR, CR, CL):
    pos = np.concatenate([np.arange(PR), PR + np.arange(CR) % CL]).astype(np.float32)
    half = ROT // 2
    freq = np.exp(np.arange(half, dtype=np.float32) * np.float32(-2.0 * math.log(10000.0) / ROT)).astype(np.float32)
    ang = (pos[:, None] * freq[None, :]).astype(np.float32)
    c = np.cos(ang)
    s = np.sin(ang)
    n = pos.shape[0]
    one = np.ones((n, HD - ROT), np.float32)
    zero = np.zeros((n, HD - ROT), np.float32)
    z8 = np.zeros((n, half), np.float32)
    tabs = ([c, c, one], [-s, z8, zero], [z8, s, zero])
    return [jnp.asarray(np.tile(np.concatenate(t, axis=1), (1, 128 // HD)), F32) for t in tabs]


def per_device(
    prompt_in,
    cont_in,
    prompt_cot,
    cont_cot,
    ln1_gain,
    ln1_bias,
    ln2_gain,
    ln2_bias,
    qkv_weight,
    qkv_bias,
    out_weight,
    out_bias,
    up_weight,
    up_bias,
    down_weight,
    down_bias,
):
    S = lax.axis_size("shard")
    R = lax.axis_size("rep")
    me = lax.axis_index("shard")
    MB, _, PD, D = prompt_in.shape
    CD, CL = cont_in.shape[2:4]
    CR = CD * CL
    N = PD + CR
    CW = D // S
    FL = up_weight.shape[1] // S
    me_arr = jnp.reshape(me, (1,)).astype(jnp.int32)

    X = [[jnp.concatenate([prompt_in[m, 0], cont_in[m, 0].reshape(CR, D)], axis=0)] for m in range(MB)]
    DY = [[jnp.concatenate([prompt_cot[m, 0], cont_cot[m, 0].reshape(CR, D)], axis=0)] for m in range(MB)]
    away = lambda values: [shifted(v, S, j + 1) for j, v in enumerate(values)]
    cut = half_pieces(up_weight, me, S)
    vectors_in = (ln1_gain, ln1_bias, ln2_gain, ln2_bias, out_bias, down_bias, qkv_bias)
    (vectors_in, qkv_weight), cut = lax.optimization_barrier(((vectors_in, qkv_weight), cut))
    small = jnp.concatenate([v.astype(F32).reshape(-1, CW) for v in vectors_in], axis=0)
    slots = [small] + away([small] * (S - 1))
    pieces_qkv = away(rep_pieces(qkv_weight, me, S, R, 3))
    pieces_up = away(cut)
    src = [(X[m][0], DY[m][0]) for m in range(MB)]
    src[1:], _ = lax.optimization_barrier((src[1:], pieces_up))
    pieces_up, _ = lax.optimization_barrier((pieces_up, (small, X, DY)))
    src[0], _ = lax.optimization_barrier((src[0], (slots[1:])))
    w_up = from_halves(up_weight, pieces_up, me, S, R)
    w_qkv = from_rep(qkv_weight, pieces_qkv, me, S, 3)

    whole = jnp.stack(canonical(slots, me, S, True), axis=0)
    vec = whole[:, :6].transpose(1, 0, 2).reshape(6, D)
    gb1 = vec[0:2]
    gb2 = vec[2:4]
    vb = vec[4:6]
    bqkv = whole[:, 6:].reshape(3, S, CW)
    bqkv = lax.dynamic_index_in_dim(bqkv, me, 1, keepdims=False).reshape(1, 3 * CW)
    bup = up_bias.astype(F32).reshape(1, FL)

    tabs = rotary_tables(PD * S, CR * S, CL)
    for m in range(MB):
        for j in range(1, S):
            X[m].append(shifted(src[m][0], S, S - j))
            DY[m].append(shifted(src[m][1], S, S - j))

    ff = [[None] * S for _ in range(MB)]

    def mlp(m, j):
        ff[m][j] = mlp_rows(X[m][j], DY[m][j], w_up, bup, down_weight, gb2, 1)

    for m in range(MB):
        mlp(m, 0)
    rest = []
    y_got, g_got = [], []

    def attend(m):
        ys, gs, more = attn_group(
            S, PD, CL, me_arr, X[m], DY[m], [f[4] for f in ff[m][1:]], [f[5] for f in ff[m][1:]], w_qkv, bqkv, out_weight, gb1, tabs
        )
        rest.append(list(more))
        y_got.append([shifted(ys[j - 1], S, j) for j in range(1, S)])
        g_got.append([shifted(gs[j - 1], S, j) for j in range(1, S)])

    def own(m):
        f = ff[m][0]
        return own_rows(X[m][0], f[4], f[5], rest[m][0], rest[m][1], w_qkv, out_weight, gb1)

    chunked = (D // S // R) % 16 == 0 and R & (R - 1) == 0
    rep = lax.axis_index("rep")
    late = [(MB - 1, j) for j in range(1, S)]
    early = [(m, j) for m in range(MB) for j in range(S) if (m, j) not in late]
    of = lambda set_, k: [ff[m][j][k] for m, j in set_]
    for m, j in early:
        if j:
            mlp(m, j)
    if chunked:
        gmlp = mlp_grads(S, R, of(early, 0), [DY[m][j] for m, j in early], of(early, 2), of(early, 1))
        w_up, gmlp, w_qkv = lax.optimization_barrier((w_up, gmlp, w_qkv))
    for m, j in late:
        mlp(m, j)
    if chunked:
        if late:
            gmlp = mlp_grads(S, R, of(late, 0), [DY[m][j] for m, j in late], of(late, 2), of(late, 1), gmlp)
        part = lax.psum_scatter(gmlp, "rep", scatter_dimension=0, tiled=True)[0]
        w_qkv, gmlp = lax.optimization_barrier((w_qkv, gmlp))
    for m in range(MB):
        attend(m)
        if m + 1 < MB:
            w_qkv, rest[m][3] = lax.optimization_barrier((w_qkv, rest[m][3]))
    every = early + late
    def vectors(mine_):
        ln1 = sum(r[3] for r in rest) + sum(o[2] for o in mine_)
        ln2 = sum(of(every, 6))
        db_out = sum(jnp.sum(DY[m][0].astype(F32), axis=0) for m in range(MB)).reshape(-1, CW)
        mine = (jnp.arange(S) == me).astype(F32)
        db_qkv = (sum(r[4] for r in rest)[:, None, :] * mine[None, :, None]).reshape(-1, CW)
        db_up = (sum(of(every, 3)) * mine[:, None]).reshape(-1, CW)
        return jnp.concatenate([ln1.reshape(-1, CW), ln2.reshape(-1, CW), db_out, db_qkv, db_up], axis=0)

    finals = lambda m, o, prior: final_rows(m, MB, PD, X[m][0], DY[m][0], [o[0]] + y_got[m], [o[1]] + g_got[m], vb, prior)
    hs, dls, ctxs = [[r[k] for r in rest] for k in (2, 0, 1)]
    if chunked:
        q = jnp.stack([place(rep, order) for order in orders(R)]).astype(jnp.int32)
        part = swap_shards(part, me, S, FL // R)
        hs, y_got[:-1], g_got[:-1], part = lax.optimization_barrier((hs, y_got[:-1], g_got[:-1], part))
        gmlp_all = lax.all_gather(part, "rep", axis=0, tiled=False)
        gatt = attn_grads(S, R, q, hs, dls, ctxs, [DY[m][j] for m in range(MB) for j in range(S)])
        dls_own, _ = lax.optimization_barrier(([r[0] for r in rest], gatt))
        for m in range(MB):
            rest[m][0] = dls_own[m]
        mine = [own(m) for m in range(MB)]
        beside = {1: mine}
        levels = R.bit_length() - 1
        path = hops(vectors(mine), R)
        late_hops = {}
        for n, v in enumerate(path):
            at = 2 + n
            (beside if at < levels else late_hops).setdefault(at if at < levels else max(2 * levels - 1 - at, 0), []).append(v)
        outs = None
        for m in range(MB - 1):
            outs = finals(m, mine[m], outs)
        whole_outs = finals(MB - 1, mine[-1], outs)
        beside[levels - 1] = beside.get(levels - 1, []) + [y_got[-1], g_got[-1]]
        half = halving([(g[: R // 2], g[R // 2 :]) for g in gatt], R, beside)
        k = D // CW * (D // S // R)
        finished = mlp_finish(S, gmlp_all, FL)
        after = {3: (outs, late_hops.get(3, [])), 2: (finished, late_hops.get(2, [])), 1: (whole_outs, late_hops.get(1, []))}
        g1, g2 = doubling([swap_shards(half[0], me, S, 0), swap_shards(half[1], me, S, k)], R, after)
        outs = after[1][0]
        g_down, g_up = after[2][0]
        vecs = path[-1]
        g_out, g_qkv = attn_finish(S, q, g1, g2)
    else:
        dls, ctxs, hs = [[r[k] for r in rest] for k in (0, 1, 2)]
        mine = [own(m) for m in range(MB)]
        g_down = reduce_rows(tn_sum(of(every, 0), [DY[m][j] for m, j in every], 256))
        g_up = reduce_columns(tn_sum(of(every, 2), of(every, 1), 256), me, S, 1)
        dycs = [jnp.concatenate(DY[m], axis=0) for m in range(MB)]
        g_out = reduce_rows(tn_sum(ctxs, dycs, 256))
        g_qkv = reduce_columns(tn_sum(hs, dls, 256), me, S, 3)
        vecs = sum_all(vectors(mine), S, R)
        outs = None
        for m in range(MB):
            outs = finals(m, mine[m], outs)
    tot = vecs + sum(shifted(vecs, S, j) for j in range(1, S))
    held = lambda a, n: lax.dynamic_slice_in_dim(tot, a + me * n, n, 0).reshape(-1)
    v_ln1g, v_ln1b, v_ln2g, v_ln2b, v_out = [held(k * S, 1) for k in range(5)]
    v_qkv = held(5 * S, 3)
    v_up = held(8 * S, FL // CW)

    po, co, pg, cg = outs
    return (
        po.reshape(MB, 1, PD, D),
        co.reshape(MB, 1, CD, CL, D),
        pg.reshape(MB, 1, PD, D),
        cg.reshape(MB, 1, CD, CL, D),
        v_ln1g,
        v_ln1b,
        v_ln2g,
        v_ln2b,
        g_qkv,
        v_qkv,
        g_out,
        v_out,
        g_up,
        v_up,
        g_down,
        v_out,
    )


def solution(mesh):
    tokens = (
        P(None, "rep", "shard", None),
        P(None, "rep", "shard", None, None),
        P(None, "rep", "shard", None),
        P(None, "rep", "shard", None, None),
    )
    vec = P("shard")
    mat = P("shard", None)
    params = (vec, vec, vec, vec, mat, vec, mat, vec, mat, vec, mat, vec)
    return jax.shard_map(
        per_device, mesh=mesh, in_specs=tokens + params, out_specs=tokens + params, check_vma=False
    )
```

```python
import functools
import math

import jax
import jax.numpy as jnp
import numpy as np
from jax import lax
from jax.experimental import pallas as pl
from jax.experimental.pallas import tpu as pltpu
from jax.sharding import PartitionSpec as P

H = 16
HD = 64
ROT = 16
EPS = 1e-05
F32 = jnp.float32
BF = jnp.bfloat16
MIB = 1024 * 1024
SD = jax.ShapeDtypeStruct
SMALL = pl.CostEstimate(flops=1000000, bytes_accessed=100000, transcendentals=0)


def dnn(a, b):
    return lax.dot_general(a, b, (((1,), (0,)), ((), ())), preferred_element_type=F32)


def dnt(a, b):
    return lax.dot_general(a, b, (((1,), (1,)), ((), ())), preferred_element_type=F32)


def dtn(a, b):
    return lax.dot_general(a, b, (((0,), (0,)), ((), ())), preferred_element_type=F32)


def normed(rows):
    x = rows.astype(F32)
    c = x - jnp.mean(x, axis=-1, keepdims=True)
    inv = lax.rsqrt(jnp.mean(c * c, axis=-1, keepdims=True) + EPS)
    return c * inv, inv


def tile(i, n):
    return pl.ds(pl.multiple_of(i * n, n), n)


def rows_tile(n, most):
    t = most
    while n % t:
        t -= 8
    return t


def mlp_kernel(rt, x_ref, dy_ref, wu_ref, bu_ref, wd_ref, gb_ref, act_ref, dpre_ref, h_ref, bu_out, *back):
    f = pl.program_id(0)
    if back:
        yp_ref, g2_ref, ln_ref, yacc, dacc = back
    last = pl.num_programs(0) - 1
    rows = x_ref.shape[0]

    @pl.when(f == 0)
    def _():
        @pl.loop(0, rows // 128)
        def _(i):
            r = tile(i, 128)
            xh, _ = normed(x_ref[r, :])
            h_ref[r, :] = (xh * gb_ref[0:1, :] + gb_ref[1:2, :]).astype(BF)
            if back:
                yacc[r, :] = jnp.zeros((128, yacc.shape[1]), F32)
                dacc[r, :] = jnp.zeros((128, dacc.shape[1]), F32)

    def step(i, bsum):
        r = tile(i, rt)
        pre = dnn(h_ref[r, :], wu_ref[...]) + bu_ref[...]
        da = dnt(dy_ref[r, :], wd_ref[...])
        cdf = 0.5 * (1.0 + lax.erf(pre * 0.7071067811865476))
        act = (pre * cdf).astype(BF)
        dpre = (da * (cdf + pre * jnp.exp(-0.5 * pre * pre) * 0.3989422804014327)).astype(BF)
        act_ref[r, :] = act
        dpre_ref[r, :] = dpre
        if back:
            yacc[r, :] += dnn(act, wd_ref[...])
            dacc[r, :] += dnt(dpre, wu_ref[...])
        return bsum + jnp.sum(dpre.astype(F32), axis=0, keepdims=True)

    bu_out[...] = lax.fori_loop(0, rows // rt, step, jnp.zeros(bu_out.shape, F32))
    if not back:
        return

    @pl.when(f == last)
    def _():
        ln_ref[...] = jnp.zeros_like(ln_ref)

        @pl.loop(0, rows // 128)
        def _(i):
            r = tile(i, 128)
            xh, _ = normed(x_ref[r, :])
            dh = dacc[r, :]
            yp_ref[r, :] = yacc[r, :].astype(BF)
            g2_ref[r, :] = (dh * gb_ref[0:1, :]).astype(BF)
            ln_ref[0:1, :] += jnp.sum(dh * xh, axis=0, keepdims=True)
            ln_ref[1:2, :] += jnp.sum(dh, axis=0, keepdims=True)


def mlp_rows(x, dy, wu, bu, wd, gb, back):
    rows, width = x.shape
    hidden = wu.shape[1]
    fb = min(512, hidden)
    full = lambda s: pl.BlockSpec(s, lambda f: (0,) * len(s))
    return pl.pallas_call(
        functools.partial(mlp_kernel, rows_tile(rows, 640)),
        grid=(hidden // fb,),
        in_specs=[
            full((rows, width)),
            full((rows, width)),
            pl.BlockSpec((width, fb), lambda f: (0, f)),
            pl.BlockSpec((1, fb), lambda f: (0, f)),
            pl.BlockSpec((fb, width), lambda f: (f, 0)),
            full((2, width)),
        ],
        out_specs=[
            pl.BlockSpec((rows, fb), lambda f: (0, f)),
            pl.BlockSpec((rows, fb), lambda f: (0, f)),
            full((rows, width)),
            pl.BlockSpec((1, fb), lambda f: (0, f)),
        ]
        + [full((rows, width)), full((rows, width)), full((2, width))] * back,
        out_shape=[SD((rows, hidden), BF), SD((rows, hidden), BF), SD((rows, width), BF), SD((1, hidden), F32)]
        + [SD((rows, width), BF), SD((rows, width), BF), SD((2, width), F32)] * back,
        scratch_shapes=[pltpu.VMEM((rows, width), F32)] * (2 * back),
        compiler_params=pltpu.CompilerParams(vmem_limit_bytes=60 * MIB),
        cost_estimate=pl.CostEstimate(flops=4 * rows * width * hidden, bytes_accessed=4 * (width * hidden + rows * hidden) + 6 * rows * width, transcendentals=2 * rows * hidden),
    )(x, dy, wu, bu, wd, gb)


def roll8(x, left):
    w = x.shape[-1]
    return pltpu.roll(x, (w - 8) if left else 8, 1)


def attn_kernel(S, PD, CL, QB, HG, adding, me_ref, *refs):
    it = iter(refs)
    take = lambda n: [next(it) for _ in range(n)]
    stacked = S > 2
    per = 1 if stacked else S
    xs = take(per)
    dys = take(per)
    far = 1 if stacked else S - 1
    yps = take(far * adding)
    g2s = take(far * adding)
    wq, wk, wv = take(3)
    bq, bk, bv = take(3)
    wo, gb = take(2)
    cr, s1r, s2r = take(3)
    ys = take(far)
    gs = take(far)
    dl, ctx, h1, ln, db = take(5)
    yacc, dacc, q_s, k_s, v_s, dc_s, kT, vT, dk_s, dv_s = take(10)
    g = pl.program_id(0)
    last = pl.num_programs(0) - 1
    me = me_ref[0]
    N = xs[0].shape[-2]
    T = N * S
    PR = PD * S
    CR = N - PD
    W = HG * HD

    def every_slot(fn, start=0):
        if stacked:

            @pl.loop(start, S)
            def _(j):
                fn(j, lambda refs: refs[0].at[j], lambda refs: refs[0].at[j - 1])

        else:
            for j in range(start, S):
                fn(j, lambda refs: refs[j], lambda refs: refs[j - 1])

    def slot_rows(start, n):
        if start < PR:
            s, off = start // PD, start % PD
        else:
            s, off = (start - PR) // CR, PD + (start - PR) % CR
        return pl.ds(pl.multiple_of(lax.rem(s - me + S, S) * N + off, 128), n)

    def pieces(start, n):
        step = min(n, PD if start < PR else CR)
        return [(i, step) for i in range(0, n, step)]

    @pl.when(g == 0)
    def _():
        def load(j, of, away):
            x = of(xs)

            @pl.loop(0, N // 128)
            def _(i):
                xh, _ = normed(x[tile(i, 128), :])
                h1[pl.ds(pl.multiple_of(j * N + i * 128, 128), 128), :] = (xh * gb[0:1, :] + gb[1:2, :]).astype(BF)

        every_slot(load)

    def rot(y, r, scale):
        c = cr[r, :]
        s1 = s1r[r, :]
        s2 = s2r[r, :]
        out = []
        for p in range(W // 128):
            z = y[:, p * 128 : (p + 1) * 128]
            z = (z * c + roll8(z, True) * s1 + roll8(z, False) * s2).astype(BF)
            out.append(z * jnp.asarray(scale, BF) if scale != 1.0 else z)
        return jnp.concatenate(out, axis=1) if len(out) > 1 else out[0]

    def proj(j, of, away):
        s = lax.rem(me + j, S)
        rp = pl.ds(pl.multiple_of(s * PD, 128), PD)
        rc = pl.ds(pl.multiple_of(PR + s * CR, 128), CR)
        hh = h1[pl.ds(pl.multiple_of(j * N, 128), N), :]
        y = dnn(hh, wq[...]) + bq[...]
        q_s[rp, :] = rot(y[:PD], rp, HD**-0.5)
        q_s[rc, :] = rot(y[PD:], rc, HD**-0.5)
        y = dnn(hh, wk[...]) + bk[...]
        k_s[rp, :] = rot(y[:PD], rp, 1.0)
        k_s[rc, :] = rot(y[PD:], rc, 1.0)
        y = (dnn(hh, wv[...]) + bv[...]).astype(BF)
        v_s[rp, :] = y[:PD]
        v_s[rc, :] = y[PD:]
        y = dnt(of(dys)[...], wo[...]).astype(BF)
        dc_s[rp, :] = y[:PD]
        dc_s[rc, :] = y[PD:]

    def bring(j, of, away):
        nb = away(yps).shape[0]
        r = pl.ds(pl.multiple_of(g * nb, 16), nb)
        away(ys)[r, :] = away(yps)[...]
        away(gs)[r, :] = away(g2s)[...]

    every_slot(proj)
    if adding:
        every_slot(bring, 1)
    lane = lax.broadcasted_iota(jnp.int32, (1, 128), 1)
    row_i = lax.broadcasted_iota(jnp.int32, (QB, QB), 0)
    col_i = lax.broadcasted_iota(jnp.int32, (QB, QB), 1)
    causal = row_i <= col_i
    cmask = causal & ((row_i // CL) == (col_i // CL))
    blocks = []
    for i in range(PR // QB):
        blocks.append((i * QB, [(0, i * QB, None)] * (i > 0) + [(i * QB, QB, causal)]))
    for c in range((T - PR) // QB):
        blocks.append((PR + c * QB, [(0, PR, None), (PR + c * QB, QB, cmask)]))

    @pl.loop(0, W // 128)
    def _(p):
        lanes = tile(p, 128)
        kT[...] = k_s[:, lanes].T
        vT[...] = v_s[:, lanes].T
        dk_s[...] = jnp.zeros_like(dk_s)
        dv_s[...] = jnp.zeros_like(dv_s)
        def begin(q0, parts):
            qb = q_s[pl.ds(q0, QB), lanes]
            dcb = dc_s[pl.ds(q0, QB), lanes]
            out = []
            for h in range(2):
                sel = (lane >= HD * h) & (lane < HD * h + HD)
                qm = jnp.where(sel, qb, jnp.zeros_like(qb))
                dm = jnp.where(sel, dcb, jnp.zeros_like(dcb))
                ss = []
                for k0, n, mask in parts:
                    s = dnt(k_s[k0 : k0 + n, lanes], qm)
                    ss.append(s if mask is None else jnp.where(mask, s, -1e30))
                out.append((qm, dm, ss, [dnt(v_s[k0 : k0 + n, lanes], dm) for k0, n, _ in parts]))
            return out

        ahead = begin(*blocks[0])
        for b, (q0, parts) in enumerate(blocks):
            now = ahead
            if b + 1 < len(blocks):
                ahead = begin(*blocks[b + 1])
            rq = pl.ds(q0, QB)
            P_, DS, cT, dqT = [], [], [], []
            qh = [t[0] for t in now]
            dch = [t[1] for t in now]
            for h in range(2):
                _, _, ss, dps = now[h]
                m = functools.reduce(jnp.maximum, [jnp.max(s, axis=0, keepdims=True) for s in ss])
                es = [jnp.exp(s - m) for s in ss]
                rl = 1.0 / sum(jnp.sum(e, axis=0, keepdims=True) for e in es)
                ps = [e * rl for e in es]
                delta = sum(jnp.sum(a * b, axis=0, keepdims=True) for a, b in zip(ps, dps))
                P_.append([a.astype(BF) for a in ps])
                DS.append([(a * (b - delta)).astype(BF) for a, b in zip(ps, dps)])
                hr = slice(HD * h, HD * h + HD)
                cT.append(sum(dnn(vT[hr, k0 : k0 + n], a) for (k0, n, _), a in zip(parts, P_[h])))
                dqT.append(sum(dnn(kT[hr, k0 : k0 + n], a) for (k0, n, _), a in zip(parts, DS[h])))
            q2 = jnp.concatenate(qh, axis=0)
            dc2 = jnp.concatenate(dch, axis=0)
            for i, (k0, n, _) in enumerate(parts):
                dv_s[k0 : k0 + n, :] += dnn(jnp.concatenate([P_[0][i], P_[1][i]], axis=1), dc2)
                dk_s[k0 : k0 + n, :] += dnn(jnp.concatenate([DS[0][i], DS[1][i]], axis=1), q2)
            co = jnp.concatenate(cT, axis=0).T.astype(BF)
            z = jnp.concatenate(dqT, axis=0).T * (HD**-0.5)
            z = (z * cr[rq, :] - roll8(z, True) * s1r[rq, :] - roll8(z, False) * s2r[rq, :]).astype(BF)
            for o, n in pieces(q0, QB):
                ctx[slot_rows(q0 + o, n), lanes] = co[o : o + n]
                dl[0, slot_rows(q0 + o, n), lanes] = z[o : o + n]

        @pl.loop(0, S)
        def _(s):
            to = lax.rem(s - me + S, S) * N
            for src, off, n in ((s * PD, 0, PD), (PR + s * CR, PD, CR)):
                r = pl.ds(pl.multiple_of(src, 128), n)
                w = pl.ds(pl.multiple_of(to + off, 128), n)
                z = dk_s[r, :]
                z = z * cr[r, :] - roll8(z, True) * s1r[r, :] - roll8(z, False) * s2r[r, :]
                dl[1, w, lanes] = z.astype(BF)
                dl[2, w, lanes] = dv_s[r, :].astype(BF)

    for c in range(3):
        db[c : c + 1, :] = jnp.sum(dl[c].astype(F32), axis=0, keepdims=True)

    @pl.loop(1, S)
    def _(j):
        r = pl.ds(pl.multiple_of(j * N, 128), N)
        w = pl.ds(pl.multiple_of((j - 1) * N, 128), N)
        y = dnn(ctx[r, :], wo[...])
        d = dnt(dl[0, r, :], wq[...]) + dnt(dl[1, r, :], wk[...]) + dnt(dl[2, r, :], wv[...])

        @pl.when(g == 0)
        def _():
            yacc[w, :] = y
            dacc[w, :] = d

        @pl.when(g > 0)
        def _():
            yacc[w, :] += y
            dacc[w, :] += d

    @pl.when(g == last)
    def _():
        ln[...] = jnp.zeros_like(ln)

        def store(j, of, away):
            x, yo, go = of(xs), away(ys), away(gs)

            @pl.loop(0, N // 128)
            def _(i):
                r = tile(i, 128)
                w = pl.ds(pl.multiple_of((j - 1) * N + i * 128, 128), 128)
                xh, _ = normed(x[r, :])
                d = dacc[w, :]
                y = yacc[w, :]
                gg = d * gb[0:1, :]
                if adding:
                    y = y + yo[r, :].astype(F32)
                    gg = gg + go[r, :].astype(F32)
                yo[r, :] = y.astype(BF)
                go[r, :] = gg.astype(BF)
                ln[0:1, :] += jnp.sum(d * xh, axis=0, keepdims=True)
                ln[1:2, :] += jnp.sum(d, axis=0, keepdims=True)

        every_slot(store, 1)


def attn_group(S, PD, CL, me, xs, dys, yps, g2s, wqkv, bqkv, wo, gb, tabs):
    N, D = xs[0].shape
    CW = wo.shape[0]
    T = N * S
    HG = 4 if CW % 256 == 0 else 2
    QB = 256
    W = HG * HD
    G = CW // W
    full = lambda s: pl.BlockSpec(s, lambda g, m: (0,) * len(s), pipeline_mode=pl.Buffered(1))
    keep = lambda s: pl.BlockSpec(s, lambda g, m: (0,) * len(s))
    tok, tok_out, per, far = full((N, D)), keep((N, D)), S, S - 1
    adding = int(T * D <= 1536 * 1024)
    others = (yps, g2s)
    if not adding:
        yps, g2s = [], []
    out_tok = SD((N, D), BF)
    part = pl.BlockSpec((N // G, D), lambda g, m: (g, 0))
    if S > 2:
        xs, dys, yps, g2s = [[jnp.stack(v, axis=0)] if v else v for v in (xs, dys, yps, g2s)]
        tok, tok_out, per, far = full((S, N, D)), keep((S - 1, N, D)), 1, 1
        out_tok = SD((S - 1, N, D), BF)
        part = pl.BlockSpec((S - 1, N // G, D), lambda g, m: (0, g, 0))
    wspec = lambda c: pl.BlockSpec((D, W), lambda g, m: (0, c * G + g))
    bspec = lambda c: pl.BlockSpec((1, W), lambda g, m: (0, c * G + g))
    outs = pl.pallas_call(
        functools.partial(attn_kernel, S, PD, CL, QB, HG, adding),
        grid_spec=pltpu.PrefetchScalarGridSpec(
            num_scalar_prefetch=1,
            grid=(G,),
            in_specs=[tok] * (2 * per)
            + [part] * (2 * adding * far)
            + [wspec(0), wspec(1), wspec(2), bspec(0), bspec(1), bspec(2)]
            + [pl.BlockSpec((W, D), lambda g, m: (g, 0)), full((2, D))]
            + [full((T, 128))] * 3,
            out_specs=[tok_out] * (2 * far)
            + [
                pl.BlockSpec((3, T, W), lambda g, m: (0, 0, g)),
                pl.BlockSpec((T, W), lambda g, m: (0, g)),
                keep((T, D)),
                keep((2, D)),
                pl.BlockSpec((3, W), lambda g, m: (0, g)),
            ],
            scratch_shapes=[pltpu.VMEM((T - N, D), F32)] * 2
            + [pltpu.VMEM((T, W), BF)] * 4
            + [pltpu.VMEM((128, T), BF)] * 2
            + [pltpu.VMEM((T, 128), F32)] * 2,
        ),
        out_shape=[out_tok] * (2 * far)
        + [SD((3, T, CW), BF), SD((T, CW), BF), SD((T, D), BF), SD((2, D), F32), SD((3, CW), F32)],
        compiler_params=pltpu.CompilerParams(vmem_limit_bytes=62 * MIB),
        cost_estimate=SMALL,
    )(me, *xs, *dys, *yps, *g2s, wqkv, wqkv, wqkv, bqkv, bqkv, bqkv, wo, gb, *tabs)
    ys, gs = outs[:far], outs[far : 2 * far]
    if S > 2:
        ys, gs = [[v[0][j] for j in range(S - 1)] for v in (ys, gs)]
    if not adding:
        ys, gs = [[a + b for a, b in zip(p, q)] for p, q in zip((ys, gs), others)]
    return ys, gs, outs[2 * far :]


def tn_kernel(n, wide, *refs):
    a = refs[:n]
    b = refs[n : 2 * n]
    o = refs[2 * n]
    if wide == 0:
        o[...] = sum(dtn(x[...], y[...]) for x, y in zip(a, b)).astype(BF)
    else:
        w = b[0].shape[2]
        for c in range(wide):
            o[:, c * w : (c + 1) * w] = sum(dtn(x[...], y[c]) for x, y in zip(a, b)).astype(BF)


def tn_sum(a, b, block):
    n = len(a)
    rows, da = a[0].shape
    block = min(block, da)
    wide = b[0].shape[0] if b[0].ndim == 3 else 0
    db = b[0].shape[-1] * max(wide, 1)
    keep = lambda s: pl.BlockSpec(s, lambda i: (0,) * len(s), pipeline_mode=pl.Buffered(1))
    return pl.pallas_call(
        functools.partial(tn_kernel, n, wide),
        grid=(da // block,),
        in_specs=[pl.BlockSpec((rows, block), lambda i: (0, i))] * n + [keep(b[0].shape)] * n,
        out_specs=pl.BlockSpec((block, db), lambda i: (i, 0)),
        out_shape=SD((da, db), BF),
        compiler_params=pltpu.CompilerParams(vmem_limit_bytes=60 * MIB),
        cost_estimate=SMALL,
    )(*a, *b)


def joined(refs):
    return jnp.concatenate([r[...] for r in refs], axis=0)


def down_kernel(n, more, *refs):
    o = refs[-1]
    t = dtn(joined(refs[:n]), joined(refs[n : 2 * n])).reshape(o.shape)
    o[...] = (t + refs[2 * n][...].astype(F32) if more else t).astype(BF)


def up_kernel(n, more, *refs):
    o = refs[-1]
    c, rows, w = o.shape
    t = dtn(joined(refs[:n]), joined(refs[n : 2 * n]))
    k = t.shape[1] // w
    for i in range(k):
        r = slice(i * (rows // k), (i + 1) * (rows // k))
        p = t[:, i * w : (i + 1) * w].reshape(c, rows // k, w)
        o[:, r, :] = (p + refs[2 * n][:, r, :].astype(F32) if more else p).astype(BF)


def mlp_grads(S, R, acts, dys, hs, dpres, g=None):
    n = len(acts)
    rows, FL = acts[0].shape
    D = dys[0].shape[1]
    DR = D // S
    blk = 256
    rd = FL // R
    ru = DR // R
    k = FL // D
    per = rd + S * ru * k
    keep = lambda s: pl.BlockSpec(s, lambda i: (0,) * len(s), pipeline_mode=pl.Buffered(1))
    steps = DR // blk
    more = g is not None
    hbm = pl.BlockSpec(memory_space=pl.ANY)

    def call(kernel, a, b, spec, g):
        width = b[0].shape[1]
        prior = [] if g is None else [g]
        return pl.pallas_call(
            functools.partial(kernel, n, more),
            grid=(a[0].shape[1] // blk,),
            in_specs=[pl.BlockSpec((rows, blk), lambda i: (0, i))] * n
            + [keep((rows, width))] * n
            + ([spec if more else hbm] if prior else []),
            out_specs=spec,
            out_shape=SD((R, per, D), BF),
            input_output_aliases={2 * n: 0} if prior else {},
            compiler_params=pltpu.CompilerParams(vmem_limit_bytes=60 * MIB),
            cost_estimate=SMALL,
        )(*a, *b, *prior)

    g = call(down_kernel, acts, dys, pl.BlockSpec((blk // rd, rd, D), lambda i: (i, 0, 0)), g)
    spec = pl.BlockSpec((blk // ru, ru * k, D), lambda i: (i % steps, rd // (ru * k) + i // steps, 0))
    return call(up_kernel, hs, dpres, spec, g)


def mlp_finish_kernel(S, rd, ru, g, down, up):
    n, per, D = g.shape
    k = (per - rd) // (S * ru)
    for c in range(n):
        down[c * rd : (c + 1) * rd, :] = g[c, :rd, :].astype(F32)
        for t in range(S * k):
            a = rd + t * ru
            up[c * ru : (c + 1) * ru, t * D : (t + 1) * D] = g[c, a : a + ru, :].astype(F32)


def mlp_finish(S, g, FL):
    R, per, D = g.shape
    rd = FL // R
    ru = D // S // R
    n = 4
    return pl.pallas_call(
        functools.partial(mlp_finish_kernel, S, rd, ru),
        grid=(R // n,),
        in_specs=[pl.BlockSpec((n, per, D), lambda c: (c, 0, 0))],
        out_specs=[pl.BlockSpec((n * rd, D), lambda c: (c, 0)), pl.BlockSpec((n * ru, S * FL), lambda c: (c, 0))],
        out_shape=[SD((FL, D), F32), SD((D // S, S * FL), F32)],
        compiler_params=pltpu.CompilerParams(vmem_limit_bytes=40 * MIB),
        cost_estimate=SMALL,
    )(g)


def attn_grads_kernel(n, S, R, q_ref, *refs):
    h = refs[:n]
    dl = refs[n : 2 * n]
    ctx = refs[2 * n : 3 * n]
    dy = refs[3 * n : -2]
    first, second = refs[-2:-1], refs[-1:]
    i = pl.program_id(0)
    q1 = q_ref[0]
    q2 = q_ref[1]
    blk = h[0].shape[1]
    D = dy[0].shape[1]
    DR = D // S
    CW = dl[0].shape[2]
    ru = DR // R
    k = D // CW
    steps = DR // blk
    s = i // steps
    base = (i % steps) * (blk // ru)

    def put(pair, pos, rows, v):
        pair[0][pos, rows, :] = v

    for p in range(3):
        t = dtn(joined(h), jnp.concatenate([y[p] for y in dl], axis=0)).astype(BF)
        for c in range(blk // ru):
            v = t[c * ru : (c + 1) * ru, :]
            if p < 2:
                put(first, (base + c) ^ q1, pl.ds(s * 2 * ru + p * ru, ru), v)
            else:
                put(second, (base + c) ^ q2, pl.ds(k * ru + s * ru, ru), v)
    t = dtn(joined(ctx), joined(dy)).astype(BF)
    m = ctx[0].shape[1] // ru
    for c in range(m):
        for j in range(k):
            put(second, (i * m + c) ^ q2, pl.ds(j * ru, ru), t[c * ru : (c + 1) * ru, j * CW : (j + 1) * CW])


def attn_grads(S, R, q, hs, dls, ctxs, dys):
    n = len(hs)
    T, D = hs[0].shape
    CW = ctxs[0].shape[1]
    DR = D // S
    ru = DR // R
    blk = 256
    G = D // blk
    keep = lambda s: pl.BlockSpec(s, lambda i, q: (0,) * len(s), pipeline_mode=pl.Buffered(1))
    shapes = [(R, S * 2 * ru, CW), (R, (D // CW + S) * ru, CW)]
    return pl.pallas_call(
        functools.partial(attn_grads_kernel, n, S, R),
        grid_spec=pltpu.PrefetchScalarGridSpec(
            num_scalar_prefetch=1,
            grid=(G,),
            in_specs=[pl.BlockSpec((T, blk), lambda i, q: (0, i))] * n
            + [keep((3, T, CW))] * n
            + [pl.BlockSpec((T, CW // G), lambda i, q: (0, i))] * n
            + [keep(dys[0].shape)] * len(dys),
            out_specs=[pl.BlockSpec(s, lambda i, q: (0, 0, 0)) for s in shapes],
        ),
        out_shape=[SD(s, BF) for s in shapes],
        compiler_params=pltpu.CompilerParams(vmem_limit_bytes=60 * MIB),
        cost_estimate=SMALL,
    )(q, *hs, *dls, *ctxs, *dys)


def attn_finish_kernel(S, ru, k, n, half, q_ref, *refs):
    out, qkv = refs[4 * n :]
    CW = refs[0].shape[2]
    D = out.shape[1]
    i = pl.program_id(0)

    def piece(which, c, a):
        low, high = refs[2 * which * n + c], refs[(2 * which + 1) * n + c]
        here = ((i * n + c) ^ q_ref[which]) < half
        rows = pl.ds(a, ru)
        return jnp.where(here, low[0, rows, :].astype(F32), high[0, rows, :].astype(F32))

    for c in range(n):
        r = slice(c * ru, (c + 1) * ru)
        for j in range(k):
            out[r, j * CW : (j + 1) * CW] = piece(1, c, j * ru)
        for t in range(S):
            for p in range(3):
                v = piece(0, c, (t * 2 + p) * ru) if p < 2 else piece(1, c, (k + t) * ru)
                qkv[r, p * D + t * CW : p * D + (t + 1) * CW] = v


def attn_finish(S, q, one, two):
    half, per1, CW = one[0].shape
    per2 = two[0].shape[1]
    R = 2 * half
    D = CW * S
    ru = D // S // R
    n = 4
    place_of = lambda i, q, k, c: (i * n + c) ^ q[k]
    low = lambda per, k, c: pl.BlockSpec((1, per, CW), lambda i, q: (jnp.minimum(place_of(i, q, k, c), half - 1), 0, 0))
    high = lambda per, k, c: pl.BlockSpec((1, per, CW), lambda i, q: (jnp.maximum(place_of(i, q, k, c) - half, 0), 0, 0))
    specs = [f(per, k, c) for k, per in ((0, per1), (1, per2)) for f in (low, high) for c in range(n)]
    return pl.pallas_call(
        functools.partial(attn_finish_kernel, S, ru, S, n, half),
        grid_spec=pltpu.PrefetchScalarGridSpec(
            num_scalar_prefetch=1,
            grid=(R // n,),
            in_specs=specs,
            out_specs=[pl.BlockSpec((n * ru, D), lambda c, q: (c, 0)), pl.BlockSpec((n * ru, 3 * D), lambda c, q: (c, 0))],
        ),
        out_shape=[SD((CW, D), F32), SD((D // S, 3 * D), F32)],
        compiler_params=pltpu.CompilerParams(vmem_limit_bytes=40 * MIB),
        cost_estimate=SMALL,
    )(q, *[a for pair in (one, two) for arr in pair for a in [arr] * n])


def own_kernel(dl, ctx, wqkv, wo, x, yp, g2, gb, y, g, ln, d1):
    N = x.shape[0]
    CW = ctx.shape[1]
    d1[...] = sum(dnt(dl[p], wqkv[:, p * CW : (p + 1) * CW]) for p in range(3))
    y[...] = (yp[...].astype(F32) + dnn(ctx[...], wo[...])).astype(BF)
    ln[...] = jnp.zeros_like(ln)

    @pl.loop(0, N // 128)
    def _(i):
        r = tile(i, 128)
        xh, _ = normed(x[r, :])
        a = d1[r, :]
        g[r, :] = (a * gb[0:1, :] + g2[r, :].astype(F32)).astype(BF)
        ln[0:1, :] += jnp.sum(a * xh, axis=0, keepdims=True)
        ln[1:2, :] += jnp.sum(a, axis=0, keepdims=True)


def own_rows(x, yp, g2, dl, ctx, wqkv, wo, gb):
    N, D = x.shape
    CW = wo.shape[0]
    full = lambda s: pl.BlockSpec(s, lambda f: (0,) * len(s))
    return pl.pallas_call(
        own_kernel,
        grid=(1,),
        in_specs=[full((3, N, CW)), full((N, CW)), full((D, 3 * CW)), full((CW, D))] + [full((N, D))] * 3 + [full((2, D))],
        out_specs=[full((N, D)), full((N, D)), full((2, D))],
        out_shape=[SD((N, D), BF), SD((N, D), BF), SD((2, D), F32)],
        scratch_shapes=[pltpu.VMEM((N, D), F32)],
        compiler_params=pltpu.CompilerParams(vmem_limit_bytes=60 * MIB),
        cost_estimate=SMALL,
    )(dl, ctx, wqkv, wo, x, yp, g2, gb)


def final_kernel(S, first, PT, *refs):
    it = iter(refs)
    take = lambda n: [next(it) for _ in range(n)]
    x, dy = take(2)
    ys = take(S)
    gs = take(S)
    (vb,) = take(1)
    if not first:
        take(4)
    po, co, pg, cg = take(4)
    i = pl.program_id(0)
    xv = x[...].astype(F32)
    xh, inv = normed(xv)
    y = xv + vb[0:1, :] + sum(r[...].astype(F32) for r in ys) + vb[1:2, :]
    gsum = sum(r[...].astype(F32) for r in gs)
    dx = (gsum - jnp.mean(gsum, axis=-1, keepdims=True) - xh * jnp.mean(gsum * xh, axis=-1, keepdims=True)) * inv
    out = y.astype(BF)
    grad = dy[...].astype(F32) + dx

    @pl.when(i < PT)
    def _():
        po[0] = out
        pg[0] = grad

    @pl.when(i >= PT)
    def _():
        co[0] = out
        cg[0] = grad


def final_rows(m, MB, PD, x, dy, ys, gs, vb, prior):
    S = len(ys)
    N, D = x.shape
    CR = N - PD
    RT = 128
    PT = PD // RT
    first = prior is None
    row = pl.BlockSpec((RT, D), lambda i: (i, 0))
    pspec = pl.BlockSpec((1, RT, D), lambda i: (m, jnp.minimum(i, PT - 1), 0))
    cspec = pl.BlockSpec((1, RT, D), lambda i: (m, jnp.maximum(i - PT, 0), 0))
    hbm = pl.BlockSpec(memory_space=pl.ANY)
    n_in = 2 * S + 3
    return pl.pallas_call(
        functools.partial(final_kernel, S, first, PT),
        grid=(N // RT,),
        in_specs=[row] * (2 * S + 2) + [pl.BlockSpec((2, D), lambda i: (0, 0))] + ([] if first else [hbm] * 4),
        out_specs=[pspec, cspec, pspec, cspec],
        out_shape=[SD((MB, PD, D), BF), SD((MB, CR, D), BF), SD((MB, PD, D), F32), SD((MB, CR, D), F32)],
        input_output_aliases={} if first else {n_in + k: k for k in range(4)},
        compiler_params=pltpu.CompilerParams(vmem_limit_bytes=32 * MIB),
        cost_estimate=SMALL,
    )(x, dy, *ys, *gs, vb, *(() if first else prior))


def shifted(value, S, j):
    return lax.ppermute(value, "shard", [(i, (i + j) % S) for i in range(S)])


def canonical(slots, me, S, back):
    if S == 1:
        return slots
    if S == 2:
        a, b = slots
        return [jnp.where(me == 0, a, b), jnp.where(me == 0, b, a)]
    stacked = jnp.stack(slots, axis=0)
    return [
        lax.dynamic_index_in_dim(stacked, lax.rem((me - s if back else s - me) + S, S), 0, keepdims=False) for s in range(S)
    ]


def exchanged(value, R, bit):
    return lax.ppermute(value, "rep", [(i, i ^ bit) for i in range(R)])


def columns_for(weight, me, S, j, parts, row=0, rows=None):
    cols = weight.shape[1] // parts
    rows = weight.shape[0] if rows is None else rows
    w = cols // S
    at = lax.rem(me + j, S) * w
    got = [lax.dynamic_slice(weight, (row, p * cols + at), (rows, w)) for p in range(parts)]
    return got[0] if parts == 1 else jnp.concatenate(got, axis=1)


def quarter_pieces(weight, me, S):
    n = weight.shape[0] // 4
    rep = lax.axis_index("rep")
    at = (2 * (rep % 2) + (rep // 2) % 2) * n
    return [columns_for(weight, me, S, j, 1, at, n) for j in range(1, S)]


def from_quarters(weight, pieces, me, S, R):
    rep = lax.axis_index("rep")

    def both(piece, other, first):
        return jnp.concatenate([jnp.where(first, piece, other), jnp.where(first, other, piece)], axis=0)

    slots = [columns_for(weight, me, S, 0, 1)]
    for piece in pieces:
        pair = both(piece, exchanged(piece, R, 2), (rep // 2) % 2 == 0)
        slots.append(both(pair, exchanged(pair, R, 1), rep % 2 == 0))
    return jnp.concatenate(canonical(slots, me, S, True), axis=0)


def from_rep(weight, pieces, me, S, parts):
    others = lax.all_gather(jnp.stack(pieces, axis=0), "rep", axis=1, tiled=True)
    slots = [columns_for(weight, me, S, 0, parts)] + [others[j] for j in range(S - 1)]
    return jnp.concatenate(canonical(slots, me, S, True), axis=0)


def add_low(a, b):
    return (a.astype(F32) + b.astype(F32)).astype(BF)


def orders(R):
    bits = [1 << i for i in range(R.bit_length() - 1)]
    return bits, bits[:1] + bits[2:] + bits[1:2]


def place(rep, order):
    q = jnp.zeros((), jnp.int32)
    for bit in order:
        q = 2 * q + (rep & bit) // bit
    return q


def beside_it(got, key, beside):
    if key in beside:
        got, beside[key] = lax.optimization_barrier((got, beside[key]))
    return got


def halving(pairs, R, beside):
    for i, bits in enumerate(zip(*orders(R))):
        got = beside_it([exchanged(p[1], R, bit) for p, bit in zip(pairs, bits)], i, beside)
        h = got[0].shape[0] // 2
        if h:
            pairs = [(add_low(p[0][:h], t[:h]), add_low(p[0][h:], t[h:])) for p, t in zip(pairs, got)]
        else:
            pairs = [add_low(p[0], t) for p, t in zip(pairs, got)]
    return [p[0] for p in pairs]


def doubling(parts, R, beside):
    pair = [p[None] for p in parts]
    for i, bits in reversed(list(enumerate(zip(*orders(R))))):
        got = beside_it([exchanged(g, R, bit) for g, bit in zip(pair, bits)], i, beside)
        if i:
            pair = [jnp.concatenate([g, t], axis=0) for g, t in zip(pair, got)]
    return list(zip(pair, got))


def hops(v, R):
    out = []
    for b in range(R.bit_length() - 1):
        v = v + exchanged(v, R, 1 << b)
        out.append(v)
    return out


def sum_all(v, S, R):
    bit = 1
    while bit < R:
        v = v + exchanged(v, R, bit)
        bit *= 2
    return v


def swap_shards(part, me, S, head):
    n = (part.shape[0] - head) // S
    slots = []
    for j in range(S):
        b = lax.dynamic_slice_in_dim(part, head + lax.rem(me + j, S) * n, n, 0)
        slots.append(shifted(b, S, j) if j else b)
    return jnp.concatenate(([part[:head]] if head else []) + canonical(slots, me, S, True), axis=0)


def reduce_rows(grad):
    part = lax.psum_scatter(grad, "rep", scatter_dimension=0, tiled=True)
    return lax.all_gather(part, "rep", axis=0, tiled=True).astype(F32)


def reduce_columns(grad, me, S, parts):
    rows, cols = grad.shape
    part = lax.psum_scatter(grad.reshape(S, rows // S, cols), "rep", scatter_dimension=1, tiled=True)
    slots = [lax.dynamic_index_in_dim(part, me, 0, keepdims=False)]
    for j in range(1, S):
        slots.append(shifted(lax.dynamic_index_in_dim(part, lax.rem(me + j, S), 0, keepdims=False), S, j))
    slots = [s.reshape(s.shape[0], parts, cols // parts) for s in slots]
    whole = jnp.stack(canonical(slots, me, S, True), axis=2).reshape(-1, S * cols)
    return lax.all_gather(whole, "rep", axis=0, tiled=True).astype(F32)


def rotary_tables(PR, CR, CL):
    pos = np.concatenate([np.arange(PR), PR + np.arange(CR) % CL]).astype(np.float32)
    half = ROT // 2
    freq = np.exp(np.arange(half, dtype=np.float32) * np.float32(-2.0 * math.log(10000.0) / ROT)).astype(np.float32)
    ang = (pos[:, None] * freq[None, :]).astype(np.float32)
    c = np.cos(ang)
    s = np.sin(ang)
    n = pos.shape[0]
    one = np.ones((n, HD - ROT), np.float32)
    zero = np.zeros((n, HD - ROT), np.float32)
    z8 = np.zeros((n, half), np.float32)
    tabs = ([c, c, one], [-s, z8, zero], [z8, s, zero])
    return [jnp.asarray(np.tile(np.concatenate(t, axis=1), (1, 128 // HD)), F32) for t in tabs]


def per_device(
    prompt_in,
    cont_in,
    prompt_cot,
    cont_cot,
    ln1_gain,
    ln1_bias,
    ln2_gain,
    ln2_bias,
    qkv_weight,
    qkv_bias,
    out_weight,
    out_bias,
    up_weight,
    up_bias,
    down_weight,
    down_bias,
):
    S = lax.axis_size("shard")
    R = lax.axis_size("rep")
    me = lax.axis_index("shard")
    MB, _, PD, D = prompt_in.shape
    CD, CL = cont_in.shape[2:4]
    CR = CD * CL
    N = PD + CR
    CW = D // S
    FL = up_weight.shape[1] // S
    me_arr = jnp.reshape(me, (1,)).astype(jnp.int32)

    X = [[jnp.concatenate([prompt_in[m, 0], cont_in[m, 0].reshape(CR, D)], axis=0)] for m in range(MB)]
    DY = [[jnp.concatenate([prompt_cot[m, 0], cont_cot[m, 0].reshape(CR, D)], axis=0)] for m in range(MB)]
    away = lambda values: [shifted(v, S, j + 1) for j, v in enumerate(values)]
    cut = quarter_pieces(up_weight, me, S)
    vectors_in = (ln1_gain, ln1_bias, ln2_gain, ln2_bias, out_bias, down_bias, qkv_bias)
    (vectors_in, qkv_weight), cut = lax.optimization_barrier(((vectors_in, qkv_weight), cut))
    small = jnp.concatenate([v.reshape(-1, CW) for v in vectors_in], axis=0)
    n = D // S // R
    rep = lax.axis_index("rep")
    at = lambda j, p: (rep * n, p * D + lax.rem(me + j, S) * CW)
    pack = lambda j: jnp.concatenate([lax.dynamic_slice(qkv_weight, at(j, p), (n, CW)) for p in range(3)] + [small], axis=0)
    packs = away([pack(j) for j in range(1, S)])
    slots = [small.astype(F32)] + [g[3 * n :].astype(F32) for g in packs]
    pieces_qkv = [jnp.concatenate([g[p * n : (p + 1) * n] for p in range(3)], axis=1) for g in packs]
    pieces_up = away(cut)
    src = [(X[m][0], DY[m][0]) for m in range(MB)]
    src[1:], _ = lax.optimization_barrier((src[1:], pieces_up))
    pieces_up, _ = lax.optimization_barrier((pieces_up, (packs, X[0], DY[0])))
    w_up = from_quarters(up_weight, pieces_up, me, S, R)
    w_qkv = from_rep(qkv_weight, pieces_qkv, me, S, 3)

    whole = jnp.stack(canonical(slots, me, S, True), axis=0)
    vec = whole[:, :6].transpose(1, 0, 2).reshape(6, D)
    gb1 = vec[0:2]
    gb2 = vec[2:4]
    vb = vec[4:6]
    bqkv = whole[:, 6:].reshape(3, S, CW)
    bqkv = lax.dynamic_index_in_dim(bqkv, me, 1, keepdims=False).reshape(1, 3 * CW)
    bup = up_bias.astype(F32).reshape(1, FL)

    tabs = rotary_tables(PD * S, CR * S, CL)
    for m in range(MB):
        for j in range(1, S):
            X[m].append(shifted(src[m][0], S, S - j))
            DY[m].append(shifted(src[m][1], S, S - j))

    ff = [[None] * S for _ in range(MB)]

    def mlp(m, j):
        ff[m][j] = mlp_rows(X[m][j], DY[m][j], w_up, bup, down_weight, gb2, 1)

    for m in range(MB):
        mlp(m, 0)
    rest = []
    y_got, g_got = [], []

    def attend(m):
        ys, gs, more = attn_group(
            S, PD, CL, me_arr, X[m], DY[m], [f[4] for f in ff[m][1:]], [f[5] for f in ff[m][1:]], w_qkv, bqkv, out_weight, gb1, tabs
        )
        rest.append(list(more))
        y_got.append([shifted(ys[j - 1], S, j) for j in range(1, S)])
        g_got.append([shifted(gs[j - 1], S, j) for j in range(1, S)])

    def own(m):
        f = ff[m][0]
        return own_rows(X[m][0], f[4], f[5], rest[m][0], rest[m][1], w_qkv, out_weight, gb1)

    chunked = (D // S // R) % 16 == 0 and R & (R - 1) == 0
    rep = lax.axis_index("rep")
    late = [(MB - 1, j) for j in range(1, S)]
    early = [(m, j) for m in range(MB) for j in range(S) if (m, j) not in late]
    of = lambda set_, k: [ff[m][j][k] for m, j in set_]
    for m, j in early:
        if j:
            mlp(m, j)
    if chunked:
        gmlp = mlp_grads(S, R, of(early, 0), [DY[m][j] for m, j in early], of(early, 2), of(early, 1))
        w_up, gmlp, w_qkv = lax.optimization_barrier((w_up, gmlp, w_qkv))
    for m, j in late:
        mlp(m, j)
    if chunked:
        if late:
            gmlp = mlp_grads(S, R, of(late, 0), [DY[m][j] for m, j in late], of(late, 2), of(late, 1), gmlp)
        part = lax.psum_scatter(gmlp, "rep", scatter_dimension=0, tiled=True)[0]
        w_qkv, gmlp = lax.optimization_barrier((w_qkv, gmlp))
    for m in range(MB):
        attend(m)
        if m + 1 < MB:
            w_qkv, rest[m][3] = lax.optimization_barrier((w_qkv, rest[m][3]))
    every = early + late
    def vectors(mine_):
        ln1 = sum(r[3] for r in rest) + sum(o[2] for o in mine_)
        ln2 = sum(of(every, 6))
        db_out = sum(jnp.sum(DY[m][0].astype(F32), axis=0) for m in range(MB)).reshape(-1, CW)
        mine = (jnp.arange(S) == me).astype(F32)
        db_qkv = (sum(r[4] for r in rest)[:, None, :] * mine[None, :, None]).reshape(-1, CW)
        db_up = (sum(of(every, 3)) * mine[:, None]).reshape(-1, CW)
        return jnp.concatenate([ln1.reshape(-1, CW), ln2.reshape(-1, CW), db_out, db_qkv, db_up], axis=0)

    finals = lambda m, o, prior: final_rows(m, MB, PD, X[m][0], DY[m][0], [o[0]] + y_got[m], [o[1]] + g_got[m], vb, prior)
    hs, dls, ctxs = [[r[k] for r in rest] for k in (2, 0, 1)]
    if chunked:
        q = jnp.stack([place(rep, order) for order in orders(R)]).astype(jnp.int32)
        part = swap_shards(part, me, S, FL // R)
        hs, y_got[:-1], g_got[:-1], part = lax.optimization_barrier((hs, y_got[:-1], g_got[:-1], part))
        gmlp_all = lax.all_gather(part, "rep", axis=0, tiled=False)
        gatt = attn_grads(S, R, q, hs, dls, ctxs, [DY[m][j] for m in range(MB) for j in range(S)])
        dls_own, _ = lax.optimization_barrier(([r[0] for r in rest], gatt))
        for m in range(MB):
            rest[m][0] = dls_own[m]
        mine = [own(m) for m in range(MB)]
        beside = {1: mine}
        levels = R.bit_length() - 1
        path = hops(vectors(mine), R)
        late_hops = {}
        for n, v in enumerate(path):
            at = 2 + n
            (beside if at < levels else late_hops).setdefault(at if at < levels else max(2 * levels - 1 - at, 0), []).append(v)
        outs = None
        for m in range(MB - 1):
            outs = finals(m, mine[m], outs)
        whole_outs = finals(MB - 1, mine[-1], outs)
        beside[levels - 1] = beside.get(levels - 1, []) + [y_got[-1], g_got[-1]]
        half = halving([(g[: R // 2], g[R // 2 :]) for g in gatt], R, beside)
        k = D // CW * (D // S // R)
        finished = mlp_finish(S, gmlp_all, FL)
        after = {3: (outs, late_hops.get(3, [])), 2: (finished, late_hops.get(2, [])), 1: (whole_outs, late_hops.get(1, []))}
        g1, g2 = doubling([swap_shards(half[0], me, S, 0), swap_shards(half[1], me, S, k)], R, after)
        outs = after[1][0]
        g_down, g_up = after[2][0]
        vecs = path[-1]
        g_out, g_qkv = attn_finish(S, q, g1, g2)
    else:
        dls, ctxs, hs = [[r[k] for r in rest] for k in (0, 1, 2)]
        mine = [own(m) for m in range(MB)]
        g_down = reduce_rows(tn_sum(of(every, 0), [DY[m][j] for m, j in every], 256))
        g_up = reduce_columns(tn_sum(of(every, 2), of(every, 1), 256), me, S, 1)
        dycs = [jnp.concatenate(DY[m], axis=0) for m in range(MB)]
        g_out = reduce_rows(tn_sum(ctxs, dycs, 256))
        g_qkv = reduce_columns(tn_sum(hs, dls, 256), me, S, 3)
        vecs = sum_all(vectors(mine), S, R)
        outs = None
        for m in range(MB):
            outs = finals(m, mine[m], outs)
    tot = vecs + sum(shifted(vecs, S, j) for j in range(1, S))
    held = lambda a, n: lax.dynamic_slice_in_dim(tot, a + me * n, n, 0).reshape(-1)
    v_ln1g, v_ln1b, v_ln2g, v_ln2b, v_out = [held(k * S, 1) for k in range(5)]
    v_qkv = held(5 * S, 3)
    v_up = held(8 * S, FL // CW)

    po, co, pg, cg = outs
    return (
        po.reshape(MB, 1, PD, D),
        co.reshape(MB, 1, CD, CL, D),
        pg.reshape(MB, 1, PD, D),
        cg.reshape(MB, 1, CD, CL, D),
        v_ln1g,
        v_ln1b,
        v_ln2g,
        v_ln2b,
        g_qkv,
        v_qkv,
        g_out,
        v_out,
        g_up,
        v_up,
        g_down,
        v_out,
    )


def solution(mesh):
    tokens = (
        P(None, "rep", "shard", None),
        P(None, "rep", "shard", None, None),
        P(None, "rep", "shard", None),
        P(None, "rep", "shard", None, None),
    )
    vec = P("shard")
    mat = P("shard", None)
    params = (vec, vec, vec, vec, mat, vec, mat, vec, mat, vec, mat, vec)
    return jax.shard_map(
        per_device, mesh=mesh, in_specs=tokens + params, out_specs=tokens + params, check_vma=False
    )
```

```python
import functools
import math

import jax
import jax.numpy as jnp
import numpy as np
from jax import lax
from jax.experimental import pallas as pl
from jax.experimental.pallas import tpu as pltpu
from jax.sharding import PartitionSpec as P

H = 16
HD = 64
ROT = 16
EPS = 1e-05
F32 = jnp.float32
BF = jnp.bfloat16
MIB = 1024 * 1024
SD = jax.ShapeDtypeStruct
SMALL = pl.CostEstimate(flops=1000000, bytes_accessed=100000, transcendentals=0)


def dnn(a, b):
    return lax.dot_general(a, b, (((1,), (0,)), ((), ())), preferred_element_type=F32)


def dnt(a, b):
    return lax.dot_general(a, b, (((1,), (1,)), ((), ())), preferred_element_type=F32)


def dtn(a, b):
    return lax.dot_general(a, b, (((0,), (0,)), ((), ())), preferred_element_type=F32)


def normed(rows):
    x = rows.astype(F32)
    c = x - jnp.mean(x, axis=-1, keepdims=True)
    inv = lax.rsqrt(jnp.mean(c * c, axis=-1, keepdims=True) + EPS)
    return c * inv, inv


def tile(i, n):
    return pl.ds(pl.multiple_of(i * n, n), n)


def rows_tile(n, most):
    t = most
    while n % t:
        t -= 8
    return t


def mlp_kernel(rt, x_ref, dy_ref, wu_ref, bu_ref, wd_ref, gb_ref, act_ref, dpre_ref, h_ref, bu_out, *back):
    f = pl.program_id(0)
    if back:
        yp_ref, g2_ref, ln_ref, yacc, dacc = back
    last = pl.num_programs(0) - 1
    rows = x_ref.shape[0]

    @pl.when(f == 0)
    def _():
        @pl.loop(0, rows // 128)
        def _(i):
            r = tile(i, 128)
            xh, _ = normed(x_ref[r, :])
            h_ref[r, :] = (xh * gb_ref[0:1, :] + gb_ref[1:2, :]).astype(BF)
            if back:
                yacc[r, :] = jnp.zeros((128, yacc.shape[1]), F32)
                dacc[r, :] = jnp.zeros((128, dacc.shape[1]), F32)

    def step(i, bsum):
        r = tile(i, rt)
        pre = dnn(h_ref[r, :], wu_ref[...]) + bu_ref[...]
        da = dnt(dy_ref[r, :], wd_ref[...])
        cdf = 0.5 * (1.0 + lax.erf(pre * 0.7071067811865476))
        act = (pre * cdf).astype(BF)
        dpre = (da * (cdf + pre * jnp.exp(-0.5 * pre * pre) * 0.3989422804014327)).astype(BF)
        act_ref[r, :] = act
        dpre_ref[r, :] = dpre
        if back:
            yacc[r, :] += dnn(act, wd_ref[...])
            dacc[r, :] += dnt(dpre, wu_ref[...])
        return bsum + jnp.sum(dpre.astype(F32), axis=0, keepdims=True)

    bu_out[...] = lax.fori_loop(0, rows // rt, step, jnp.zeros(bu_out.shape, F32))
    if not back:
        return

    @pl.when(f == last)
    def _():
        ln_ref[...] = jnp.zeros_like(ln_ref)

        @pl.loop(0, rows // 128)
        def _(i):
            r = tile(i, 128)
            xh, _ = normed(x_ref[r, :])
            dh = dacc[r, :]
            yp_ref[r, :] = yacc[r, :].astype(BF)
            g2_ref[r, :] = (dh * gb_ref[0:1, :]).astype(BF)
            ln_ref[0:1, :] += jnp.sum(dh * xh, axis=0, keepdims=True)
            ln_ref[1:2, :] += jnp.sum(dh, axis=0, keepdims=True)


def mlp_rows(x, dy, wu, bu, wd, gb, back):
    rows, width = x.shape
    hidden = wu.shape[1]
    fb = min(512, hidden)
    full = lambda s: pl.BlockSpec(s, lambda f: (0,) * len(s))
    return pl.pallas_call(
        functools.partial(mlp_kernel, rows_tile(rows, 640)),
        grid=(hidden // fb,),
        in_specs=[
            full((rows, width)),
            full((rows, width)),
            pl.BlockSpec((width, fb), lambda f: (0, f)),
            pl.BlockSpec((1, fb), lambda f: (0, f)),
            pl.BlockSpec((fb, width), lambda f: (f, 0)),
            full((2, width)),
        ],
        out_specs=[
            pl.BlockSpec((rows, fb), lambda f: (0, f)),
            pl.BlockSpec((rows, fb), lambda f: (0, f)),
            full((rows, width)),
            pl.BlockSpec((1, fb), lambda f: (0, f)),
        ]
        + [full((rows, width)), full((rows, width)), full((2, width))] * back,
        out_shape=[SD((rows, hidden), BF), SD((rows, hidden), BF), SD((rows, width), BF), SD((1, hidden), F32)]
        + [SD((rows, width), BF), SD((rows, width), BF), SD((2, width), F32)] * back,
        scratch_shapes=[pltpu.VMEM((rows, width), F32)] * (2 * back),
        compiler_params=pltpu.CompilerParams(vmem_limit_bytes=60 * MIB),
        cost_estimate=pl.CostEstimate(flops=4 * rows * width * hidden, bytes_accessed=4 * (width * hidden + rows * hidden) + 6 * rows * width, transcendentals=2 * rows * hidden),
    )(x, dy, wu, bu, wd, gb)


def roll8(x, left):
    w = x.shape[-1]
    return pltpu.roll(x, (w - 8) if left else 8, 1)


def attn_kernel(S, PD, CL, QB, HG, adding, me_ref, *refs):
    it = iter(refs)
    take = lambda n: [next(it) for _ in range(n)]
    stacked = S > 2
    per = 1 if stacked else S
    xs = take(per)
    dys = take(per)
    far = 1 if stacked else S - 1
    yps = take(far * adding)
    g2s = take(far * adding)
    wq, wk, wv = take(3)
    bq, bk, bv = take(3)
    wo, gb = take(2)
    cr, s1r, s2r = take(3)
    ys = take(far)
    gs = take(far)
    dl, ctx, h1, ln, db = take(5)
    yacc, dacc, q_s, k_s, v_s, dc_s, kT, vT, dk_s, dv_s = take(10)
    g = pl.program_id(0)
    last = pl.num_programs(0) - 1
    me = me_ref[0]
    N = xs[0].shape[-2]
    T = N * S
    PR = PD * S
    CR = N - PD
    W = HG * HD

    def every_slot(fn, start=0):
        if stacked:

            @pl.loop(start, S)
            def _(j):
                fn(j, lambda refs: refs[0].at[j], lambda refs: refs[0].at[j - 1])

        else:
            for j in range(start, S):
                fn(j, lambda refs: refs[j], lambda refs: refs[j - 1])

    def slot_rows(start, n):
        if start < PR:
            s, off = start // PD, start % PD
        else:
            s, off = (start - PR) // CR, PD + (start - PR) % CR
        return pl.ds(pl.multiple_of(lax.rem(s - me + S, S) * N + off, 128), n)

    def pieces(start, n):
        step = min(n, PD if start < PR else CR)
        return [(i, step) for i in range(0, n, step)]

    @pl.when(g == 0)
    def _():
        def load(j, of, away):
            x = of(xs)

            @pl.loop(0, N // 128)
            def _(i):
                xh, _ = normed(x[tile(i, 128), :])
                h1[pl.ds(pl.multiple_of(j * N + i * 128, 128), 128), :] = (xh * gb[0:1, :] + gb[1:2, :]).astype(BF)

        every_slot(load)

    def rot(y, r, scale):
        c = cr[r, :]
        s1 = s1r[r, :]
        s2 = s2r[r, :]
        out = []
        for p in range(W // 128):
            z = y[:, p * 128 : (p + 1) * 128]
            z = (z * c + roll8(z, True) * s1 + roll8(z, False) * s2).astype(BF)
            out.append(z * jnp.asarray(scale, BF) if scale != 1.0 else z)
        return jnp.concatenate(out, axis=1) if len(out) > 1 else out[0]

    def proj(j, of, away):
        s = lax.rem(me + j, S)
        rp = pl.ds(pl.multiple_of(s * PD, 128), PD)
        rc = pl.ds(pl.multiple_of(PR + s * CR, 128), CR)
        hh = h1[pl.ds(pl.multiple_of(j * N, 128), N), :]
        y = dnn(hh, wq[...]) + bq[...]
        q_s[rp, :] = rot(y[:PD], rp, HD**-0.5)
        q_s[rc, :] = rot(y[PD:], rc, HD**-0.5)
        y = dnn(hh, wk[...]) + bk[...]
        k_s[rp, :] = rot(y[:PD], rp, 1.0)
        k_s[rc, :] = rot(y[PD:], rc, 1.0)
        y = (dnn(hh, wv[...]) + bv[...]).astype(BF)
        v_s[rp, :] = y[:PD]
        v_s[rc, :] = y[PD:]
        y = dnt(of(dys)[...], wo[...]).astype(BF)
        dc_s[rp, :] = y[:PD]
        dc_s[rc, :] = y[PD:]

    def bring(j, of, away):
        nb = away(yps).shape[0]
        r = pl.ds(pl.multiple_of(g * nb, 16), nb)
        away(ys)[r, :] = away(yps)[...]
        away(gs)[r, :] = away(g2s)[...]

    every_slot(proj)
    if adding:
        every_slot(bring, 1)
    lane = lax.broadcasted_iota(jnp.int32, (1, 128), 1)
    row_i = lax.broadcasted_iota(jnp.int32, (QB, QB), 0)
    col_i = lax.broadcasted_iota(jnp.int32, (QB, QB), 1)
    causal = row_i <= col_i
    cmask = causal & ((row_i // CL) == (col_i // CL))
    blocks = []
    for i in range(PR // QB):
        blocks.append((i * QB, [(0, i * QB, None)] * (i > 0) + [(i * QB, QB, causal)]))
    for c in range((T - PR) // QB):
        blocks.append((PR + c * QB, [(0, PR, None), (PR + c * QB, QB, cmask)]))

    @pl.loop(0, W // 128)
    def _(p):
        lanes = tile(p, 128)
        kT[...] = k_s[:, lanes].T
        vT[...] = v_s[:, lanes].T
        dk_s[...] = jnp.zeros_like(dk_s)
        dv_s[...] = jnp.zeros_like(dv_s)
        def begin(q0, parts):
            qb = q_s[pl.ds(q0, QB), lanes]
            dcb = dc_s[pl.ds(q0, QB), lanes]
            out = []
            for h in range(2):
                sel = (lane >= HD * h) & (lane < HD * h + HD)
                qm = jnp.where(sel, qb, jnp.zeros_like(qb))
                dm = jnp.where(sel, dcb, jnp.zeros_like(dcb))
                ss = []
                for k0, n, mask in parts:
                    s = dnt(k_s[k0 : k0 + n, lanes], qm)
                    ss.append(s if mask is None else jnp.where(mask, s, -1e30))
                out.append((qm, dm, ss, [dnt(v_s[k0 : k0 + n, lanes], dm) for k0, n, _ in parts]))
            return out

        ahead = begin(*blocks[0])
        for b, (q0, parts) in enumerate(blocks):
            now = ahead
            if b + 1 < len(blocks):
                ahead = begin(*blocks[b + 1])
            rq = pl.ds(q0, QB)
            P_, DS, cT, dqT = [], [], [], []
            qh = [t[0] for t in now]
            dch = [t[1] for t in now]
            for h in range(2):
                _, _, ss, dps = now[h]
                m = functools.reduce(jnp.maximum, [jnp.max(s, axis=0, keepdims=True) for s in ss])
                es = [jnp.exp(s - m) for s in ss]
                rl = 1.0 / sum(jnp.sum(e, axis=0, keepdims=True) for e in es)
                ps = [e * rl for e in es]
                delta = sum(jnp.sum(a * b, axis=0, keepdims=True) for a, b in zip(ps, dps))
                P_.append([a.astype(BF) for a in ps])
                DS.append([(a * (b - delta)).astype(BF) for a, b in zip(ps, dps)])
                hr = slice(HD * h, HD * h + HD)
                cT.append(sum(dnn(vT[hr, k0 : k0 + n], a) for (k0, n, _), a in zip(parts, P_[h])))
                dqT.append(sum(dnn(kT[hr, k0 : k0 + n], a) for (k0, n, _), a in zip(parts, DS[h])))
            q2 = jnp.concatenate(qh, axis=0)
            dc2 = jnp.concatenate(dch, axis=0)
            for i, (k0, n, _) in enumerate(parts):
                dv_s[k0 : k0 + n, :] += dnn(jnp.concatenate([P_[0][i], P_[1][i]], axis=1), dc2)
                dk_s[k0 : k0 + n, :] += dnn(jnp.concatenate([DS[0][i], DS[1][i]], axis=1), q2)
            co = jnp.concatenate(cT, axis=0).T.astype(BF)
            z = jnp.concatenate(dqT, axis=0).T * (HD**-0.5)
            z = (z * cr[rq, :] - roll8(z, True) * s1r[rq, :] - roll8(z, False) * s2r[rq, :]).astype(BF)
            for o, n in pieces(q0, QB):
                ctx[slot_rows(q0 + o, n), lanes] = co[o : o + n]
                dl[0, slot_rows(q0 + o, n), lanes] = z[o : o + n]

        @pl.loop(0, S)
        def _(s):
            to = lax.rem(s - me + S, S) * N
            for src, off, n in ((s * PD, 0, PD), (PR + s * CR, PD, CR)):
                r = pl.ds(pl.multiple_of(src, 128), n)
                w = pl.ds(pl.multiple_of(to + off, 128), n)
                z = dk_s[r, :]
                z = z * cr[r, :] - roll8(z, True) * s1r[r, :] - roll8(z, False) * s2r[r, :]
                dl[1, w, lanes] = z.astype(BF)
                dl[2, w, lanes] = dv_s[r, :].astype(BF)

    for c in range(3):
        db[c : c + 1, :] = jnp.sum(dl[c].astype(F32), axis=0, keepdims=True)

    @pl.loop(1, S)
    def _(j):
        r = pl.ds(pl.multiple_of(j * N, 128), N)
        w = pl.ds(pl.multiple_of((j - 1) * N, 128), N)
        y = dnn(ctx[r, :], wo[...])
        d = dnt(dl[0, r, :], wq[...]) + dnt(dl[1, r, :], wk[...]) + dnt(dl[2, r, :], wv[...])

        @pl.when(g == 0)
        def _():
            yacc[w, :] = y
            dacc[w, :] = d

        @pl.when(g > 0)
        def _():
            yacc[w, :] += y
            dacc[w, :] += d

    @pl.when(g == last)
    def _():
        ln[...] = jnp.zeros_like(ln)

        def store(j, of, away):
            x, yo, go = of(xs), away(ys), away(gs)

            @pl.loop(0, N // 128)
            def _(i):
                r = tile(i, 128)
                w = pl.ds(pl.multiple_of((j - 1) * N + i * 128, 128), 128)
                xh, _ = normed(x[r, :])
                d = dacc[w, :]
                y = yacc[w, :]
                gg = d * gb[0:1, :]
                if adding:
                    y = y + yo[r, :].astype(F32)
                    gg = gg + go[r, :].astype(F32)
                yo[r, :] = y.astype(BF)
                go[r, :] = gg.astype(BF)
                ln[0:1, :] += jnp.sum(d * xh, axis=0, keepdims=True)
                ln[1:2, :] += jnp.sum(d, axis=0, keepdims=True)

        every_slot(store, 1)


def attn_group(S, PD, CL, me, xs, dys, yps, g2s, wqkv, bqkv, wo, gb, tabs):
    N, D = xs[0].shape
    CW = wo.shape[0]
    T = N * S
    HG = 4 if CW % 256 == 0 else 2
    QB = 256
    W = HG * HD
    G = CW // W
    full = lambda s: pl.BlockSpec(s, lambda g, m: (0,) * len(s), pipeline_mode=pl.Buffered(1))
    keep = lambda s: pl.BlockSpec(s, lambda g, m: (0,) * len(s))
    tok, tok_out, per, far = full((N, D)), keep((N, D)), S, S - 1
    adding = int(T * D <= 1536 * 1024)
    others = (yps, g2s)
    if not adding:
        yps, g2s = [], []
    out_tok = SD((N, D), BF)
    part = pl.BlockSpec((N // G, D), lambda g, m: (g, 0))
    if S > 2:
        xs, dys, yps, g2s = [[jnp.stack(v, axis=0)] if v else v for v in (xs, dys, yps, g2s)]
        tok, tok_out, per, far = full((S, N, D)), keep((S - 1, N, D)), 1, 1
        out_tok = SD((S - 1, N, D), BF)
        part = pl.BlockSpec((S - 1, N // G, D), lambda g, m: (0, g, 0))
    wspec = lambda c: pl.BlockSpec((D, W), lambda g, m: (0, c * G + g))
    bspec = lambda c: pl.BlockSpec((1, W), lambda g, m: (0, c * G + g))
    outs = pl.pallas_call(
        functools.partial(attn_kernel, S, PD, CL, QB, HG, adding),
        grid_spec=pltpu.PrefetchScalarGridSpec(
            num_scalar_prefetch=1,
            grid=(G,),
            in_specs=[tok] * (2 * per)
            + [part] * (2 * adding * far)
            + [wspec(0), wspec(1), wspec(2), bspec(0), bspec(1), bspec(2)]
            + [pl.BlockSpec((W, D), lambda g, m: (g, 0)), full((2, D))]
            + [full((T, 128))] * 3,
            out_specs=[tok_out] * (2 * far)
            + [
                pl.BlockSpec((3, T, W), lambda g, m: (0, 0, g)),
                pl.BlockSpec((T, W), lambda g, m: (0, g)),
                keep((T, D)),
                keep((2, D)),
                pl.BlockSpec((3, W), lambda g, m: (0, g)),
            ],
            scratch_shapes=[pltpu.VMEM((T - N, D), F32)] * 2
            + [pltpu.VMEM((T, W), BF)] * 4
            + [pltpu.VMEM((128, T), BF)] * 2
            + [pltpu.VMEM((T, 128), F32)] * 2,
        ),
        out_shape=[out_tok] * (2 * far)
        + [SD((3, T, CW), BF), SD((T, CW), BF), SD((T, D), BF), SD((2, D), F32), SD((3, CW), F32)],
        compiler_params=pltpu.CompilerParams(vmem_limit_bytes=62 * MIB),
        cost_estimate=SMALL,
    )(me, *xs, *dys, *yps, *g2s, wqkv, wqkv, wqkv, bqkv, bqkv, bqkv, wo, gb, *tabs)
    ys, gs = outs[:far], outs[far : 2 * far]
    if S > 2:
        ys, gs = [[v[0][j] for j in range(S - 1)] for v in (ys, gs)]
    if not adding:
        ys, gs = [[a + b for a, b in zip(p, q)] for p, q in zip((ys, gs), others)]
    return ys, gs, outs[2 * far :]


def tn_kernel(n, wide, *refs):
    a = refs[:n]
    b = refs[n : 2 * n]
    o = refs[2 * n]
    if wide == 0:
        o[...] = sum(dtn(x[...], y[...]) for x, y in zip(a, b)).astype(BF)
    else:
        w = b[0].shape[2]
        for c in range(wide):
            o[:, c * w : (c + 1) * w] = sum(dtn(x[...], y[c]) for x, y in zip(a, b)).astype(BF)


def tn_sum(a, b, block):
    n = len(a)
    rows, da = a[0].shape
    block = min(block, da)
    wide = b[0].shape[0] if b[0].ndim == 3 else 0
    db = b[0].shape[-1] * max(wide, 1)
    keep = lambda s: pl.BlockSpec(s, lambda i: (0,) * len(s), pipeline_mode=pl.Buffered(1))
    return pl.pallas_call(
        functools.partial(tn_kernel, n, wide),
        grid=(da // block,),
        in_specs=[pl.BlockSpec((rows, block), lambda i: (0, i))] * n + [keep(b[0].shape)] * n,
        out_specs=pl.BlockSpec((block, db), lambda i: (i, 0)),
        out_shape=SD((da, db), BF),
        compiler_params=pltpu.CompilerParams(vmem_limit_bytes=60 * MIB),
        cost_estimate=SMALL,
    )(*a, *b)


def joined(refs):
    return jnp.concatenate([r[...] for r in refs], axis=0)


def down_kernel(n, more, *refs):
    o = refs[-1]
    t = dtn(joined(refs[:n]), joined(refs[n : 2 * n])).reshape(o.shape)
    o[...] = (t + refs[2 * n][...].astype(F32) if more else t).astype(BF)


def up_kernel(n, more, *refs):
    o = refs[-1]
    c, rows, w = o.shape
    t = dtn(joined(refs[:n]), joined(refs[n : 2 * n]))
    k = t.shape[1] // w
    for i in range(k):
        r = slice(i * (rows // k), (i + 1) * (rows // k))
        p = t[:, i * w : (i + 1) * w].reshape(c, rows // k, w)
        o[:, r, :] = (p + refs[2 * n][:, r, :].astype(F32) if more else p).astype(BF)


def mlp_grads(S, R, acts, dys, hs, dpres, g=None):
    n = len(acts)
    rows, FL = acts[0].shape
    D = dys[0].shape[1]
    DR = D // S
    blk = 256
    rd = FL // R
    ru = DR // R
    k = FL // D
    per = rd + S * ru * k
    keep = lambda s: pl.BlockSpec(s, lambda i: (0,) * len(s), pipeline_mode=pl.Buffered(1))
    steps = DR // blk
    more = g is not None
    hbm = pl.BlockSpec(memory_space=pl.ANY)

    def call(kernel, a, b, spec, g):
        width = b[0].shape[1]
        prior = [] if g is None else [g]
        return pl.pallas_call(
            functools.partial(kernel, n, more),
            grid=(a[0].shape[1] // blk,),
            in_specs=[pl.BlockSpec((rows, blk), lambda i: (0, i))] * n
            + [keep((rows, width))] * n
            + ([spec if more else hbm] if prior else []),
            out_specs=spec,
            out_shape=SD((R, per, D), BF),
            input_output_aliases={2 * n: 0} if prior else {},
            compiler_params=pltpu.CompilerParams(vmem_limit_bytes=60 * MIB),
            cost_estimate=SMALL,
        )(*a, *b, *prior)

    g = call(down_kernel, acts, dys, pl.BlockSpec((blk // rd, rd, D), lambda i: (i, 0, 0)), g)
    spec = pl.BlockSpec((blk // ru, ru * k, D), lambda i: (i % steps, rd // (ru * k) + i // steps, 0))
    return call(up_kernel, hs, dpres, spec, g)


def mlp_finish_kernel(S, rd, ru, g, down, up):
    n, per, D = g.shape
    k = (per - rd) // (S * ru)
    for c in range(n):
        down[c * rd : (c + 1) * rd, :] = g[c, :rd, :].astype(F32)
        for t in range(S * k):
            a = rd + t * ru
            up[c * ru : (c + 1) * ru, t * D : (t + 1) * D] = g[c, a : a + ru, :].astype(F32)


def mlp_finish(S, g, FL):
    R, per, D = g.shape
    rd = FL // R
    ru = D // S // R
    n = 4
    return pl.pallas_call(
        functools.partial(mlp_finish_kernel, S, rd, ru),
        grid=(R // n,),
        in_specs=[pl.BlockSpec((n, per, D), lambda c: (c, 0, 0))],
        out_specs=[pl.BlockSpec((n * rd, D), lambda c: (c, 0)), pl.BlockSpec((n * ru, S * FL), lambda c: (c, 0))],
        out_shape=[SD((FL, D), F32), SD((D // S, S * FL), F32)],
        compiler_params=pltpu.CompilerParams(vmem_limit_bytes=40 * MIB),
        cost_estimate=SMALL,
    )(g)


def attn_grads_kernel(n, S, R, q_ref, *refs):
    h = refs[:n]
    dl = refs[n : 2 * n]
    ctx = refs[2 * n : 3 * n]
    dy = refs[3 * n : -2]
    first, second = refs[-2:-1], refs[-1:]
    i = pl.program_id(0)
    q1 = q_ref[0]
    q2 = q_ref[1]
    blk = h[0].shape[1]
    D = dy[0].shape[1]
    DR = D // S
    CW = dl[0].shape[2]
    ru = DR // R
    k = D // CW
    steps = DR // blk
    s = i // steps
    base = (i % steps) * (blk // ru)

    def put(pair, pos, rows, v):
        pair[0][pos, rows, :] = v

    for p in range(3):
        t = dtn(joined(h), jnp.concatenate([y[p] for y in dl], axis=0)).astype(BF)
        for c in range(blk // ru):
            v = t[c * ru : (c + 1) * ru, :]
            if p < 2:
                put(first, (base + c) ^ q1, pl.ds(s * 2 * ru + p * ru, ru), v)
            else:
                put(second, (base + c) ^ q2, pl.ds(k * ru + s * ru, ru), v)
    t = dtn(joined(ctx), joined(dy)).astype(BF)
    m = ctx[0].shape[1] // ru
    for c in range(m):
        for j in range(k):
            put(second, (i * m + c) ^ q2, pl.ds(j * ru, ru), t[c * ru : (c + 1) * ru, j * CW : (j + 1) * CW])


def attn_grads(S, R, q, hs, dls, ctxs, dys):
    n = len(hs)
    T, D = hs[0].shape
    CW = ctxs[0].shape[1]
    DR = D // S
    ru = DR // R
    blk = 256
    G = D // blk
    keep = lambda s: pl.BlockSpec(s, lambda i, q: (0,) * len(s), pipeline_mode=pl.Buffered(1))
    shapes = [(R, S * 2 * ru, CW), (R, (D // CW + S) * ru, CW)]
    return pl.pallas_call(
        functools.partial(attn_grads_kernel, n, S, R),
        grid_spec=pltpu.PrefetchScalarGridSpec(
            num_scalar_prefetch=1,
            grid=(G,),
            in_specs=[pl.BlockSpec((T, blk), lambda i, q: (0, i))] * n
            + [keep((3, T, CW))] * n
            + [pl.BlockSpec((T, CW // G), lambda i, q: (0, i))] * n
            + [keep(dys[0].shape)] * len(dys),
            out_specs=[pl.BlockSpec(s, lambda i, q: (0, 0, 0)) for s in shapes],
        ),
        out_shape=[SD(s, BF) for s in shapes],
        compiler_params=pltpu.CompilerParams(vmem_limit_bytes=60 * MIB),
        cost_estimate=SMALL,
    )(q, *hs, *dls, *ctxs, *dys)


def attn_finish_kernel(S, ru, k, n, half, q_ref, *refs):
    out, qkv = refs[4 * n :]
    CW = refs[0].shape[2]
    D = out.shape[1]
    i = pl.program_id(0)

    def piece(which, c, a):
        low, high = refs[2 * which * n + c], refs[(2 * which + 1) * n + c]
        here = ((i * n + c) ^ q_ref[which]) < half
        rows = pl.ds(a, ru)
        return jnp.where(here, low[0, rows, :].astype(F32), high[0, rows, :].astype(F32))

    for c in range(n):
        r = slice(c * ru, (c + 1) * ru)
        for j in range(k):
            out[r, j * CW : (j + 1) * CW] = piece(1, c, j * ru)
        for t in range(S):
            for p in range(3):
                v = piece(0, c, (t * 2 + p) * ru) if p < 2 else piece(1, c, (k + t) * ru)
                qkv[r, p * D + t * CW : p * D + (t + 1) * CW] = v


def attn_finish(S, q, one, two):
    half, per1, CW = one[0].shape
    per2 = two[0].shape[1]
    R = 2 * half
    D = CW * S
    ru = D // S // R
    n = 4
    place_of = lambda i, q, k, c: (i * n + c) ^ q[k]
    low = lambda per, k, c: pl.BlockSpec((1, per, CW), lambda i, q: (jnp.minimum(place_of(i, q, k, c), half - 1), 0, 0))
    high = lambda per, k, c: pl.BlockSpec((1, per, CW), lambda i, q: (jnp.maximum(place_of(i, q, k, c) - half, 0), 0, 0))
    specs = [f(per, k, c) for k, per in ((0, per1), (1, per2)) for f in (low, high) for c in range(n)]
    return pl.pallas_call(
        functools.partial(attn_finish_kernel, S, ru, S, n, half),
        grid_spec=pltpu.PrefetchScalarGridSpec(
            num_scalar_prefetch=1,
            grid=(R // n,),
            in_specs=specs,
            out_specs=[pl.BlockSpec((n * ru, D), lambda c, q: (c, 0)), pl.BlockSpec((n * ru, 3 * D), lambda c, q: (c, 0))],
        ),
        out_shape=[SD((CW, D), F32), SD((D // S, 3 * D), F32)],
        compiler_params=pltpu.CompilerParams(vmem_limit_bytes=40 * MIB),
        cost_estimate=SMALL,
    )(q, *[a for pair in (one, two) for arr in pair for a in [arr] * n])


def own_kernel(dl, ctx, wqkv, wo, x, yp, g2, gb, y, g, ln, d1):
    N = x.shape[0]
    CW = ctx.shape[1]
    d1[...] = sum(dnt(dl[p], wqkv[:, p * CW : (p + 1) * CW]) for p in range(3))
    y[...] = (yp[...].astype(F32) + dnn(ctx[...], wo[...])).astype(BF)
    ln[...] = jnp.zeros_like(ln)

    @pl.loop(0, N // 128)
    def _(i):
        r = tile(i, 128)
        xh, _ = normed(x[r, :])
        a = d1[r, :]
        g[r, :] = (a * gb[0:1, :] + g2[r, :].astype(F32)).astype(BF)
        ln[0:1, :] += jnp.sum(a * xh, axis=0, keepdims=True)
        ln[1:2, :] += jnp.sum(a, axis=0, keepdims=True)


def own_rows(x, yp, g2, dl, ctx, wqkv, wo, gb):
    N, D = x.shape
    CW = wo.shape[0]
    full = lambda s: pl.BlockSpec(s, lambda f: (0,) * len(s))
    return pl.pallas_call(
        own_kernel,
        grid=(1,),
        in_specs=[full((3, N, CW)), full((N, CW)), full((D, 3 * CW)), full((CW, D))] + [full((N, D))] * 3 + [full((2, D))],
        out_specs=[full((N, D)), full((N, D)), full((2, D))],
        out_shape=[SD((N, D), BF), SD((N, D), BF), SD((2, D), F32)],
        scratch_shapes=[pltpu.VMEM((N, D), F32)],
        compiler_params=pltpu.CompilerParams(vmem_limit_bytes=60 * MIB),
        cost_estimate=SMALL,
    )(dl, ctx, wqkv, wo, x, yp, g2, gb)


def own_both_kernel(act, dpre, wu, wd, dl, ctx, wqkv, wo, x, gb, y, g, ln, yacc, d1, d2):
    f = pl.program_id(0)
    last = pl.num_programs(0) - 1
    N = x.shape[0]
    CW = ctx.shape[1]

    @pl.when(f == 0)
    def _():
        yacc[...] = dnn(ctx[...], wo[...])
        d1[...] = sum(dnt(dl[p], wqkv[:, p * CW : (p + 1) * CW]) for p in range(3))
        d2[...] = jnp.zeros_like(d2)

    yacc[...] += dnn(act[...], wd[...])
    d2[...] += dnt(dpre[...], wu[...])

    @pl.when(f == last)
    def _():
        ln[...] = jnp.zeros_like(ln)

        @pl.loop(0, N // 128)
        def _(i):
            r = tile(i, 128)
            xh, _ = normed(x[r, :])
            a = d1[r, :]
            b = d2[r, :]
            y[r, :] = yacc[r, :].astype(BF)
            g[r, :] = (a * gb[0:1, :] + b * gb[2:3, :]).astype(BF)
            ln[0:1, :] += jnp.sum(a * xh, axis=0, keepdims=True)
            ln[1:2, :] += jnp.sum(a, axis=0, keepdims=True)
            ln[2:3, :] += jnp.sum(b * xh, axis=0, keepdims=True)
            ln[3:4, :] += jnp.sum(b, axis=0, keepdims=True)


def own_both_rows(x, act, dpre, wu, wd, dl, ctx, wqkv, wo, gb):
    N, D = x.shape
    FL = wu.shape[1]
    CW = wo.shape[0]
    fb = min(512, FL)
    full = lambda s: pl.BlockSpec(s, lambda f: (0,) * len(s), pipeline_mode=pl.Buffered(1))
    keep = lambda s: pl.BlockSpec(s, lambda f: (0,) * len(s))
    rows = pl.BlockSpec((N, fb), lambda f: (0, f))
    return pl.pallas_call(
        own_both_kernel,
        grid=(FL // fb,),
        in_specs=[rows, rows, pl.BlockSpec((D, fb), lambda f: (0, f)), pl.BlockSpec((fb, D), lambda f: (f, 0))]
        + [full((3, N, CW)), full((N, CW)), full((D, 3 * CW)), full((CW, D)), full((N, D)), full((4, D))],
        out_specs=[keep((N, D)), keep((N, D)), keep((4, D))],
        out_shape=[SD((N, D), BF), SD((N, D), BF), SD((4, D), F32)],
        scratch_shapes=[pltpu.VMEM((N, D), F32)] * 3,
        compiler_params=pltpu.CompilerParams(vmem_limit_bytes=60 * MIB),
        cost_estimate=SMALL,
    )(act, dpre, wu, wd, dl, ctx, wqkv, wo, x, gb)


def final_kernel(S, first, PT, *refs):
    it = iter(refs)
    take = lambda n: [next(it) for _ in range(n)]
    x, dy = take(2)
    ys = take(S)
    gs = take(S)
    (vb,) = take(1)
    if not first:
        take(4)
    po, co, pg, cg = take(4)
    i = pl.program_id(0)
    xv = x[...].astype(F32)
    xh, inv = normed(xv)
    y = xv + vb[0:1, :] + sum(r[...].astype(F32) for r in ys) + vb[1:2, :]
    gsum = sum(r[...].astype(F32) for r in gs)
    dx = (gsum - jnp.mean(gsum, axis=-1, keepdims=True) - xh * jnp.mean(gsum * xh, axis=-1, keepdims=True)) * inv
    out = y.astype(BF)
    grad = dy[...].astype(F32) + dx

    @pl.when(i < PT)
    def _():
        po[0] = out
        pg[0] = grad

    @pl.when(i >= PT)
    def _():
        co[0] = out
        cg[0] = grad


def final_rows(m, MB, PD, x, dy, ys, gs, vb, prior):
    S = len(ys)
    N, D = x.shape
    CR = N - PD
    RT = 128
    PT = PD // RT
    first = prior is None
    row = pl.BlockSpec((RT, D), lambda i: (i, 0))
    pspec = pl.BlockSpec((1, RT, D), lambda i: (m, jnp.minimum(i, PT - 1), 0))
    cspec = pl.BlockSpec((1, RT, D), lambda i: (m, jnp.maximum(i - PT, 0), 0))
    hbm = pl.BlockSpec(memory_space=pl.ANY)
    n_in = 2 * S + 3
    return pl.pallas_call(
        functools.partial(final_kernel, S, first, PT),
        grid=(N // RT,),
        in_specs=[row] * (2 * S + 2) + [pl.BlockSpec((2, D), lambda i: (0, 0))] + ([] if first else [hbm] * 4),
        out_specs=[pspec, cspec, pspec, cspec],
        out_shape=[SD((MB, PD, D), BF), SD((MB, CR, D), BF), SD((MB, PD, D), F32), SD((MB, CR, D), F32)],
        input_output_aliases={} if first else {n_in + k: k for k in range(4)},
        compiler_params=pltpu.CompilerParams(vmem_limit_bytes=32 * MIB),
        cost_estimate=SMALL,
    )(x, dy, *ys, *gs, vb, *(() if first else prior))


def shifted(value, S, j):
    return lax.ppermute(value, "shard", [(i, (i + j) % S) for i in range(S)])


def canonical(slots, me, S, back):
    if S == 1:
        return slots
    if S == 2:
        a, b = slots
        return [jnp.where(me == 0, a, b), jnp.where(me == 0, b, a)]
    stacked = jnp.stack(slots, axis=0)
    return [
        lax.dynamic_index_in_dim(stacked, lax.rem((me - s if back else s - me) + S, S), 0, keepdims=False) for s in range(S)
    ]


def exchanged(value, R, bit):
    return lax.ppermute(value, "rep", [(i, i ^ bit) for i in range(R)])


def columns_for(weight, me, S, j, parts, row=0, rows=None):
    cols = weight.shape[1] // parts
    rows = weight.shape[0] if rows is None else rows
    w = cols // S
    at = lax.rem(me + j, S) * w
    got = [lax.dynamic_slice(weight, (row, p * cols + at), (rows, w)) for p in range(parts)]
    return got[0] if parts == 1 else jnp.concatenate(got, axis=1)


def quarter_pieces(weight, me, S):
    n = weight.shape[0] // 4
    rep = lax.axis_index("rep")
    at = (2 * (rep % 2) + (rep // 2) % 2) * n
    return [columns_for(weight, me, S, j, 1, at, n) for j in range(1, S)]


def from_quarters(weight, pieces, me, S, R):
    rep = lax.axis_index("rep")

    def both(piece, other, first):
        return jnp.concatenate([jnp.where(first, piece, other), jnp.where(first, other, piece)], axis=0)

    slots = [columns_for(weight, me, S, 0, 1)]
    for piece in pieces:
        pair = both(piece, exchanged(piece, R, 2), (rep // 2) % 2 == 0)
        slots.append(both(pair, exchanged(pair, R, 1), rep % 2 == 0))
    return jnp.concatenate(canonical(slots, me, S, True), axis=0)


def from_rep(weight, pieces, me, S, parts):
    others = lax.all_gather(jnp.stack(pieces, axis=0), "rep", axis=1, tiled=True)
    slots = [columns_for(weight, me, S, 0, parts)] + [others[j] for j in range(S - 1)]
    return jnp.concatenate(canonical(slots, me, S, True), axis=0)


def add_low(a, b):
    return (a.astype(F32) + b.astype(F32)).astype(BF)


def orders(R):
    bits = [1 << i for i in range(R.bit_length() - 1)]
    return bits, bits[:1] + bits[2:] + bits[1:2]


def place(rep, order):
    q = jnp.zeros((), jnp.int32)
    for bit in order:
        q = 2 * q + (rep & bit) // bit
    return q


def beside_it(got, key, beside):
    if key in beside:
        got, beside[key] = lax.optimization_barrier((got, beside[key]))
    return got


def halving(pairs, R, beside):
    for i, bits in enumerate(zip(*orders(R))):
        got = beside_it([exchanged(p[1], R, bit) for p, bit in zip(pairs, bits)], i, beside)
        h = got[0].shape[0] // 2
        if h:
            pairs = [(add_low(p[0][:h], t[:h]), add_low(p[0][h:], t[h:])) for p, t in zip(pairs, got)]
        else:
            pairs = [add_low(p[0], t) for p, t in zip(pairs, got)]
    return [p[0] for p in pairs]


def doubling(parts, R, beside):
    pair = [p[None] for p in parts]
    for i, bits in reversed(list(enumerate(zip(*orders(R))))):
        got = beside_it([exchanged(g, R, bit) for g, bit in zip(pair, bits)], i, beside)
        if i:
            pair = [jnp.concatenate([g, t], axis=0) for g, t in zip(pair, got)]
    return list(zip(pair, got))


def hops(v, R):
    out = []
    for b in range(R.bit_length() - 1):
        v = v + exchanged(v, R, 1 << b)
        out.append(v)
    return out


def sum_all(v, S, R):
    bit = 1
    while bit < R:
        v = v + exchanged(v, R, bit)
        bit *= 2
    return v


def swap_shards(part, me, S, head):
    n = (part.shape[0] - head) // S
    slots = []
    for j in range(S):
        b = lax.dynamic_slice_in_dim(part, head + lax.rem(me + j, S) * n, n, 0)
        slots.append(shifted(b, S, j) if j else b)
    return jnp.concatenate(([part[:head]] if head else []) + canonical(slots, me, S, True), axis=0)


def reduce_rows(grad):
    part = lax.psum_scatter(grad, "rep", scatter_dimension=0, tiled=True)
    return lax.all_gather(part, "rep", axis=0, tiled=True).astype(F32)


def reduce_columns(grad, me, S, parts):
    rows, cols = grad.shape
    part = lax.psum_scatter(grad.reshape(S, rows // S, cols), "rep", scatter_dimension=1, tiled=True)
    slots = [lax.dynamic_index_in_dim(part, me, 0, keepdims=False)]
    for j in range(1, S):
        slots.append(shifted(lax.dynamic_index_in_dim(part, lax.rem(me + j, S), 0, keepdims=False), S, j))
    slots = [s.reshape(s.shape[0], parts, cols // parts) for s in slots]
    whole = jnp.stack(canonical(slots, me, S, True), axis=2).reshape(-1, S * cols)
    return lax.all_gather(whole, "rep", axis=0, tiled=True).astype(F32)


def rotary_tables(PR, CR, CL):
    pos = np.concatenate([np.arange(PR), PR + np.arange(CR) % CL]).astype(np.float32)
    half = ROT // 2
    freq = np.exp(np.arange(half, dtype=np.float32) * np.float32(-2.0 * math.log(10000.0) / ROT)).astype(np.float32)
    ang = (pos[:, None] * freq[None, :]).astype(np.float32)
    c = np.cos(ang)
    s = np.sin(ang)
    n = pos.shape[0]
    one = np.ones((n, HD - ROT), np.float32)
    zero = np.zeros((n, HD - ROT), np.float32)
    z8 = np.zeros((n, half), np.float32)
    tabs = ([c, c, one], [-s, z8, zero], [z8, s, zero])
    return [jnp.asarray(np.tile(np.concatenate(t, axis=1), (1, 128 // HD)), F32) for t in tabs]


def per_device(
    prompt_in,
    cont_in,
    prompt_cot,
    cont_cot,
    ln1_gain,
    ln1_bias,
    ln2_gain,
    ln2_bias,
    qkv_weight,
    qkv_bias,
    out_weight,
    out_bias,
    up_weight,
    up_bias,
    down_weight,
    down_bias,
):
    S = lax.axis_size("shard")
    R = lax.axis_size("rep")
    me = lax.axis_index("shard")
    MB, _, PD, D = prompt_in.shape
    CD, CL = cont_in.shape[2:4]
    CR = CD * CL
    N = PD + CR
    CW = D // S
    FL = up_weight.shape[1] // S
    me_arr = jnp.reshape(me, (1,)).astype(jnp.int32)

    X = [[jnp.concatenate([prompt_in[m, 0], cont_in[m, 0].reshape(CR, D)], axis=0)] for m in range(MB)]
    DY = [[jnp.concatenate([prompt_cot[m, 0], cont_cot[m, 0].reshape(CR, D)], axis=0)] for m in range(MB)]
    away = lambda values: [shifted(v, S, j + 1) for j, v in enumerate(values)]
    cut = quarter_pieces(up_weight, me, S)
    vectors_in = (ln1_gain, ln1_bias, ln2_gain, ln2_bias, out_bias, down_bias, qkv_bias)
    (vectors_in, qkv_weight), _ = lax.optimization_barrier(((vectors_in, qkv_weight), (cut, X[0], DY[0])))
    small = jnp.concatenate([v.reshape(-1, CW) for v in vectors_in], axis=0)
    n = D // S // R
    rep = lax.axis_index("rep")
    at = lambda j, p: (rep * n, p * D + lax.rem(me + j, S) * CW)
    pack = lambda j: jnp.concatenate([lax.dynamic_slice(qkv_weight, at(j, p), (n, CW)) for p in range(3)] + [small], axis=0)
    packs = away([pack(j) for j in range(1, S)])
    slots = [small.astype(F32)] + [g[3 * n :].astype(F32) for g in packs]
    pieces_qkv = [jnp.concatenate([g[p * n : (p + 1) * n] for p in range(3)], axis=1) for g in packs]
    pieces_up = away(cut)
    src = [(X[m][0], DY[m][0]) for m in range(MB)]
    src[1:], _ = lax.optimization_barrier((src[1:], pieces_up))
    pieces_up, _ = lax.optimization_barrier((pieces_up, (packs, X[0], DY[0])))
    w_up = from_quarters(up_weight, pieces_up, me, S, R)
    w_qkv = from_rep(qkv_weight, pieces_qkv, me, S, 3)

    whole = jnp.stack(canonical(slots, me, S, True), axis=0)
    vec = whole[:, :6].transpose(1, 0, 2).reshape(6, D)
    gb = vec[0:4]
    gb1 = vec[0:2]
    gb2 = vec[2:4]
    vb = vec[4:6]
    bqkv = whole[:, 6:].reshape(3, S, CW)
    bqkv = lax.dynamic_index_in_dim(bqkv, me, 1, keepdims=False).reshape(1, 3 * CW)
    bup = up_bias.astype(F32).reshape(1, FL)

    tabs = rotary_tables(PD * S, CR * S, CL)
    for m in range(MB):
        for j in range(1, S):
            X[m].append(shifted(src[m][0], S, S - j))
            DY[m].append(shifted(src[m][1], S, S - j))

    ff = [[None] * S for _ in range(MB)]

    def mlp(m, j):
        ff[m][j] = mlp_rows(X[m][j], DY[m][j], w_up, bup, down_weight, gb2, int((m, j) != (MB - 1, 0)))

    for m in range(MB):
        mlp(m, 0)
    rest = []
    y_got, g_got = [], []

    def attend(m):
        ys, gs, more = attn_group(
            S, PD, CL, me_arr, X[m], DY[m], [f[4] for f in ff[m][1:]], [f[5] for f in ff[m][1:]], w_qkv, bqkv, out_weight, gb1, tabs
        )
        rest.append(list(more))
        y_got.append([shifted(ys[j - 1], S, j) for j in range(1, S)])
        g_got.append([shifted(gs[j - 1], S, j) for j in range(1, S)])

    def own(m):
        f = ff[m][0]
        if len(f) == 4:
            return own_both_rows(X[m][0], f[0], f[1], w_up, down_weight, rest[m][0], rest[m][1], w_qkv, out_weight, gb)
        return own_rows(X[m][0], f[4], f[5], rest[m][0], rest[m][1], w_qkv, out_weight, gb1)

    chunked = (D // S // R) % 16 == 0 and R & (R - 1) == 0
    rep = lax.axis_index("rep")
    late = [(MB - 1, j) for j in range(1, S)]
    early = [(m, j) for m in range(MB) for j in range(S) if (m, j) not in late]
    of = lambda set_, k: [ff[m][j][k] for m, j in set_]
    for m, j in early:
        if j:
            mlp(m, j)
    if chunked:
        gmlp = mlp_grads(S, R, of(early, 0), [DY[m][j] for m, j in early], of(early, 2), of(early, 1))
        w_up, gmlp, w_qkv = lax.optimization_barrier((w_up, gmlp, w_qkv))
    for m, j in late:
        mlp(m, j)
    if chunked:
        if late:
            gmlp = mlp_grads(S, R, of(late, 0), [DY[m][j] for m, j in late], of(late, 2), of(late, 1), gmlp)
        part = lax.psum_scatter(gmlp, "rep", scatter_dimension=0, tiled=True)[0]
        w_qkv, gmlp = lax.optimization_barrier((w_qkv, gmlp))
    for m in range(MB):
        attend(m)
        if m + 1 < MB:
            w_qkv, rest[m][3] = lax.optimization_barrier((w_qkv, rest[m][3]))
    every = early + late
    def vectors(mine_):
        ln1 = sum(r[3] for r in rest) + sum(o[2][0:2] for o in mine_)
        ln2 = sum(f[6] for f in (ff[m][j] for m, j in every) if len(f) > 4) + sum(o[2][2:4] for o in mine_ if o[2].shape[0] > 2)
        db_out = sum(jnp.sum(DY[m][0].astype(F32), axis=0) for m in range(MB)).reshape(-1, CW)
        mine = (jnp.arange(S) == me).astype(F32)
        db_qkv = (sum(r[4] for r in rest)[:, None, :] * mine[None, :, None]).reshape(-1, CW)
        db_up = (sum(of(every, 3)) * mine[:, None]).reshape(-1, CW)
        return jnp.concatenate([ln1.reshape(-1, CW), ln2.reshape(-1, CW), db_out, db_qkv, db_up], axis=0)

    finals = lambda m, o, prior: final_rows(m, MB, PD, X[m][0], DY[m][0], [o[0]] + y_got[m], [o[1]] + g_got[m], vb, prior)
    hs, dls, ctxs = [[r[k] for r in rest] for k in (2, 0, 1)]
    if chunked:
        q = jnp.stack([place(rep, order) for order in orders(R)]).astype(jnp.int32)
        part = swap_shards(part, me, S, FL // R)
        hs, y_got[:-1], g_got[:-1], part = lax.optimization_barrier((hs, y_got[:-1], g_got[:-1], part))
        gmlp_all = lax.all_gather(part, "rep", axis=0, tiled=False)
        gatt = attn_grads(S, R, q, hs, dls, ctxs, [DY[m][j] for m in range(MB) for j in range(S)])
        dls_own, _ = lax.optimization_barrier(([r[0] for r in rest], gatt))
        for m in range(MB):
            rest[m][0] = dls_own[m]
        mine = [own(m) for m in range(MB)]
        beside = {1: mine[:-1]}
        beside[2] = mine[-1:]
        levels = R.bit_length() - 1
        path = hops(vectors(mine), R)
        late_hops = {}
        for n, v in enumerate(path):
            at = 3 + n
            (beside if at < levels else late_hops).setdefault(at if at < levels else max(2 * levels - 1 - at, 0), []).append(v)
        outs = None
        for m in range(MB - 1):
            outs = finals(m, mine[m], outs)
        whole_outs = finals(MB - 1, mine[-1], outs)
        beside[levels - 1] = beside.get(levels - 1, []) + [y_got[-1], g_got[-1]]
        half = halving([(g[: R // 2], g[R // 2 :]) for g in gatt], R, beside)
        k = D // CW * (D // S // R)
        finished = mlp_finish(S, gmlp_all, FL)
        after = {3: (outs, late_hops.get(3, [])), 2: (finished, late_hops.get(2, [])), 1: (whole_outs, late_hops.get(1, []))}
        g1, g2 = doubling([swap_shards(half[0], me, S, 0), swap_shards(half[1], me, S, k)], R, after)
        outs = after[1][0]
        g_down, g_up = after[2][0]
        vecs = path[-1]
        g_out, g_qkv = attn_finish(S, q, g1, g2)
    else:
        dls, ctxs, hs = [[r[k] for r in rest] for k in (0, 1, 2)]
        mine = [own(m) for m in range(MB)]
        g_down = reduce_rows(tn_sum(of(every, 0), [DY[m][j] for m, j in every], 256))
        g_up = reduce_columns(tn_sum(of(every, 2), of(every, 1), 256), me, S, 1)
        dycs = [jnp.concatenate(DY[m], axis=0) for m in range(MB)]
        g_out = reduce_rows(tn_sum(ctxs, dycs, 256))
        g_qkv = reduce_columns(tn_sum(hs, dls, 256), me, S, 3)
        vecs = sum_all(vectors(mine), S, R)
        outs = None
        for m in range(MB):
            outs = finals(m, mine[m], outs)
    tot = vecs + sum(shifted(vecs, S, j) for j in range(1, S))
    held = lambda a, n: lax.dynamic_slice_in_dim(tot, a + me * n, n, 0).reshape(-1)
    v_ln1g, v_ln1b, v_ln2g, v_ln2b, v_out = [held(k * S, 1) for k in range(5)]
    v_qkv = held(5 * S, 3)
    v_up = held(8 * S, FL // CW)

    po, co, pg, cg = outs
    return (
        po.reshape(MB, 1, PD, D),
        co.reshape(MB, 1, CD, CL, D),
        pg.reshape(MB, 1, PD, D),
        cg.reshape(MB, 1, CD, CL, D),
        v_ln1g,
        v_ln1b,
        v_ln2g,
        v_ln2b,
        g_qkv,
        v_qkv,
        g_out,
        v_out,
        g_up,
        v_up,
        g_down,
        v_out,
    )


def solution(mesh):
    tokens = (
        P(None, "rep", "shard", None),
        P(None, "rep", "shard", None, None),
        P(None, "rep", "shard", None),
        P(None, "rep", "shard", None, None),
    )
    vec = P("shard")
    mat = P("shard", None)
    params = (vec, vec, vec, vec, mat, vec, mat, vec, mat, vec, mat, vec)
    return jax.shard_map(
        per_device, mesh=mesh, in_specs=tokens + params, out_specs=tokens + params, check_vma=False
    )
```

```python
import functools
import math

import jax
import jax.numpy as jnp
import numpy as np
from jax import lax
from jax.experimental import pallas as pl
from jax.experimental.pallas import tpu as pltpu
from jax.sharding import PartitionSpec as P

H = 16
HD = 64
ROT = 16
EPS = 1e-05
F32 = jnp.float32
BF = jnp.bfloat16
MIB = 1024 * 1024
SD = jax.ShapeDtypeStruct
SMALL = pl.CostEstimate(flops=1000000, bytes_accessed=100000, transcendentals=0)


def dnn(a, b):
    return lax.dot_general(a, b, (((1,), (0,)), ((), ())), preferred_element_type=F32)


def dnt(a, b):
    return lax.dot_general(a, b, (((1,), (1,)), ((), ())), preferred_element_type=F32)


def dtn(a, b):
    return lax.dot_general(a, b, (((0,), (0,)), ((), ())), preferred_element_type=F32)


def normed(rows):
    x = rows.astype(F32)
    c = x - jnp.mean(x, axis=-1, keepdims=True)
    inv = lax.rsqrt(jnp.mean(c * c, axis=-1, keepdims=True) + EPS)
    return c * inv, inv


def tile(i, n):
    return pl.ds(pl.multiple_of(i * n, n), n)


def rows_tile(n, most):
    t = most
    while n % t:
        t -= 8
    return t


def mlp_kernel(rt, x_ref, dy_ref, wu_ref, bu_ref, wd_ref, gb_ref, act_ref, dpre_ref, h_ref, bu_out, *back):
    f = pl.program_id(0)
    if back:
        yp_ref, g2_ref, ln_ref, yacc, dacc = back
    last = pl.num_programs(0) - 1
    rows = x_ref.shape[0]

    @pl.when(f == 0)
    def _():
        @pl.loop(0, rows // 128)
        def _(i):
            r = tile(i, 128)
            xh, _ = normed(x_ref[r, :])
            h_ref[r, :] = (xh * gb_ref[0:1, :] + gb_ref[1:2, :]).astype(BF)
            if back:
                yacc[r, :] = jnp.zeros((128, yacc.shape[1]), F32)
                dacc[r, :] = jnp.zeros((128, dacc.shape[1]), F32)

    def step(i, bsum):
        r = tile(i, rt)
        pre = dnn(h_ref[r, :], wu_ref[...]) + bu_ref[...]
        da = dnt(dy_ref[r, :], wd_ref[...])
        cdf = 0.5 * (1.0 + lax.erf(pre * 0.7071067811865476))
        act = (pre * cdf).astype(BF)
        dpre = (da * (cdf + pre * jnp.exp(-0.5 * pre * pre) * 0.3989422804014327)).astype(BF)
        act_ref[r, :] = act
        dpre_ref[r, :] = dpre
        if back:
            yacc[r, :] += dnn(act, wd_ref[...])
            dacc[r, :] += dnt(dpre, wu_ref[...])
        return bsum + jnp.sum(dpre.astype(F32), axis=0, keepdims=True)

    bu_out[...] = lax.fori_loop(0, rows // rt, step, jnp.zeros(bu_out.shape, F32))
    if not back:
        return

    @pl.when(f == last)
    def _():
        ln_ref[...] = jnp.zeros_like(ln_ref)

        @pl.loop(0, rows // 128)
        def _(i):
            r = tile(i, 128)
            xh, _ = normed(x_ref[r, :])
            dh = dacc[r, :]
            yp_ref[r, :] = yacc[r, :].astype(BF)
            g2_ref[r, :] = (dh * gb_ref[0:1, :]).astype(BF)
            ln_ref[0:1, :] += jnp.sum(dh * xh, axis=0, keepdims=True)
            ln_ref[1:2, :] += jnp.sum(dh, axis=0, keepdims=True)


def mlp_rows(x, dy, wu, bu, wd, gb, back):
    rows, width = x.shape
    hidden = wu.shape[1]
    fb = min(512, hidden)
    full = lambda s: pl.BlockSpec(s, lambda f: (0,) * len(s))
    return pl.pallas_call(
        functools.partial(mlp_kernel, rows_tile(rows, 640)),
        grid=(hidden // fb,),
        in_specs=[
            full((rows, width)),
            full((rows, width)),
            pl.BlockSpec((width, fb), lambda f: (0, f)),
            pl.BlockSpec((1, fb), lambda f: (0, f)),
            pl.BlockSpec((fb, width), lambda f: (f, 0)),
            full((2, width)),
        ],
        out_specs=[
            pl.BlockSpec((rows, fb), lambda f: (0, f)),
            pl.BlockSpec((rows, fb), lambda f: (0, f)),
            full((rows, width)),
            pl.BlockSpec((1, fb), lambda f: (0, f)),
        ]
        + [full((rows, width)), full((rows, width)), full((2, width))] * back,
        out_shape=[SD((rows, hidden), BF), SD((rows, hidden), BF), SD((rows, width), BF), SD((1, hidden), F32)]
        + [SD((rows, width), BF), SD((rows, width), BF), SD((2, width), F32)] * back,
        scratch_shapes=[pltpu.VMEM((rows, width), F32)] * (2 * back),
        compiler_params=pltpu.CompilerParams(vmem_limit_bytes=60 * MIB),
        cost_estimate=pl.CostEstimate(flops=4 * rows * width * hidden, bytes_accessed=4 * (width * hidden + rows * hidden) + 6 * rows * width, transcendentals=2 * rows * hidden),
    )(x, dy, wu, bu, wd, gb)


def roll8(x, left):
    w = x.shape[-1]
    return pltpu.roll(x, (w - 8) if left else 8, 1)


def attn_kernel(S, PD, CL, QB, HG, adding, back, me_ref, *refs):
    it = iter(refs)
    take = lambda n: [next(it) for _ in range(n)]
    stacked = S > 2
    per = 1 if stacked else S
    xs = take(per)
    dys = take(per)
    far = back * (1 if stacked else S - 1)
    yps = take(far * adding)
    g2s = take(far * adding)
    wq, wk, wv = take(3)
    bq, bk, bv = take(3)
    wo, gb = take(2)
    cr, s1r, s2r = take(3)
    ys = take(far)
    gs = take(far)
    dl, ctx, h1 = take(3)
    ln = take(back)
    (db,) = take(1)
    sums = take(2 * back)
    if back:
        (ln,) = ln
        yacc, dacc = sums
    q_s, k_s, v_s, dc_s, kT, vT, dk_s, dv_s = take(8)
    g = pl.program_id(0)
    last = pl.num_programs(0) - 1
    me = me_ref[0]
    N = xs[0].shape[-2]
    T = N * S
    PR = PD * S
    CR = N - PD
    W = HG * HD

    def every_slot(fn, start=0):
        if stacked:

            @pl.loop(start, S)
            def _(j):
                fn(j, lambda refs: refs[0].at[j], lambda refs: refs[0].at[j - 1])

        else:
            for j in range(start, S):
                fn(j, lambda refs: refs[j], lambda refs: refs[j - 1])

    def slot_rows(start, n):
        if start < PR:
            s, off = start // PD, start % PD
        else:
            s, off = (start - PR) // CR, PD + (start - PR) % CR
        return pl.ds(pl.multiple_of(lax.rem(s - me + S, S) * N + off, 128), n)

    def pieces(start, n):
        step = min(n, PD if start < PR else CR)
        return [(i, step) for i in range(0, n, step)]

    @pl.when(g == 0)
    def _():
        def load(j, of, away):
            x = of(xs)

            @pl.loop(0, N // 128)
            def _(i):
                xh, _ = normed(x[tile(i, 128), :])
                h1[pl.ds(pl.multiple_of(j * N + i * 128, 128), 128), :] = (xh * gb[0:1, :] + gb[1:2, :]).astype(BF)

        every_slot(load)

    def rot(y, r, scale):
        c = cr[r, :]
        s1 = s1r[r, :]
        s2 = s2r[r, :]
        out = []
        for p in range(W // 128):
            z = y[:, p * 128 : (p + 1) * 128]
            z = (z * c + roll8(z, True) * s1 + roll8(z, False) * s2).astype(BF)
            out.append(z * jnp.asarray(scale, BF) if scale != 1.0 else z)
        return jnp.concatenate(out, axis=1) if len(out) > 1 else out[0]

    def proj(j, of, away):
        s = lax.rem(me + j, S)
        rp = pl.ds(pl.multiple_of(s * PD, 128), PD)
        rc = pl.ds(pl.multiple_of(PR + s * CR, 128), CR)
        hh = h1[pl.ds(pl.multiple_of(j * N, 128), N), :]
        y = dnn(hh, wq[...]) + bq[...]
        q_s[rp, :] = rot(y[:PD], rp, HD**-0.5)
        q_s[rc, :] = rot(y[PD:], rc, HD**-0.5)
        y = dnn(hh, wk[...]) + bk[...]
        k_s[rp, :] = rot(y[:PD], rp, 1.0)
        k_s[rc, :] = rot(y[PD:], rc, 1.0)
        y = (dnn(hh, wv[...]) + bv[...]).astype(BF)
        v_s[rp, :] = y[:PD]
        v_s[rc, :] = y[PD:]
        y = dnt(of(dys)[...], wo[...]).astype(BF)
        dc_s[rp, :] = y[:PD]
        dc_s[rc, :] = y[PD:]

    def bring(j, of, away):
        nb = away(yps).shape[0]
        r = pl.ds(pl.multiple_of(g * nb, 16), nb)
        away(ys)[r, :] = away(yps)[...]
        away(gs)[r, :] = away(g2s)[...]

    every_slot(proj)
    if adding and back:
        every_slot(bring, 1)
    lane = lax.broadcasted_iota(jnp.int32, (1, 128), 1)
    row_i = lax.broadcasted_iota(jnp.int32, (QB, QB), 0)
    col_i = lax.broadcasted_iota(jnp.int32, (QB, QB), 1)
    causal = row_i <= col_i
    cmask = causal & ((row_i // CL) == (col_i // CL))
    blocks = []
    for i in range(PR // QB):
        blocks.append((i * QB, [(0, i * QB, None)] * (i > 0) + [(i * QB, QB, causal)]))
    for c in range((T - PR) // QB):
        blocks.append((PR + c * QB, [(0, PR, None), (PR + c * QB, QB, cmask)]))

    @pl.loop(0, W // 128)
    def _(p):
        lanes = tile(p, 128)
        kT[...] = k_s[:, lanes].T
        vT[...] = v_s[:, lanes].T
        dk_s[...] = jnp.zeros_like(dk_s)
        dv_s[...] = jnp.zeros_like(dv_s)
        def begin(q0, parts):
            qb = q_s[pl.ds(q0, QB), lanes]
            dcb = dc_s[pl.ds(q0, QB), lanes]
            out = []
            for h in range(2):
                sel = (lane >= HD * h) & (lane < HD * h + HD)
                qm = jnp.where(sel, qb, jnp.zeros_like(qb))
                dm = jnp.where(sel, dcb, jnp.zeros_like(dcb))
                ss = []
                for k0, n, mask in parts:
                    s = dnt(k_s[k0 : k0 + n, lanes], qm)
                    ss.append(s if mask is None else jnp.where(mask, s, -1e30))
                out.append((qm, dm, ss, [dnt(v_s[k0 : k0 + n, lanes], dm) for k0, n, _ in parts]))
            return out

        ahead = begin(*blocks[0])
        for b, (q0, parts) in enumerate(blocks):
            now = ahead
            if b + 1 < len(blocks):
                ahead = begin(*blocks[b + 1])
            rq = pl.ds(q0, QB)
            P_, DS, cT, dqT = [], [], [], []
            qh = [t[0] for t in now]
            dch = [t[1] for t in now]
            for h in range(2):
                _, _, ss, dps = now[h]
                m = functools.reduce(jnp.maximum, [jnp.max(s, axis=0, keepdims=True) for s in ss])
                es = [jnp.exp(s - m) for s in ss]
                rl = 1.0 / sum(jnp.sum(e, axis=0, keepdims=True) for e in es)
                ps = [e * rl for e in es]
                delta = sum(jnp.sum(a * b, axis=0, keepdims=True) for a, b in zip(ps, dps))
                P_.append([a.astype(BF) for a in ps])
                DS.append([(a * (b - delta)).astype(BF) for a, b in zip(ps, dps)])
                hr = slice(HD * h, HD * h + HD)
                cT.append(sum(dnn(vT[hr, k0 : k0 + n], a) for (k0, n, _), a in zip(parts, P_[h])))
                dqT.append(sum(dnn(kT[hr, k0 : k0 + n], a) for (k0, n, _), a in zip(parts, DS[h])))
            q2 = jnp.concatenate(qh, axis=0)
            dc2 = jnp.concatenate(dch, axis=0)
            for i, (k0, n, _) in enumerate(parts):
                dv_s[k0 : k0 + n, :] += dnn(jnp.concatenate([P_[0][i], P_[1][i]], axis=1), dc2)
                dk_s[k0 : k0 + n, :] += dnn(jnp.concatenate([DS[0][i], DS[1][i]], axis=1), q2)
            co = jnp.concatenate(cT, axis=0).T.astype(BF)
            z = jnp.concatenate(dqT, axis=0).T * (HD**-0.5)
            z = (z * cr[rq, :] - roll8(z, True) * s1r[rq, :] - roll8(z, False) * s2r[rq, :]).astype(BF)
            for o, n in pieces(q0, QB):
                ctx[slot_rows(q0 + o, n), lanes] = co[o : o + n]
                dl[0, slot_rows(q0 + o, n), lanes] = z[o : o + n]

        @pl.loop(0, S)
        def _(s):
            to = lax.rem(s - me + S, S) * N
            for src, off, n in ((s * PD, 0, PD), (PR + s * CR, PD, CR)):
                r = pl.ds(pl.multiple_of(src, 128), n)
                w = pl.ds(pl.multiple_of(to + off, 128), n)
                z = dk_s[r, :]
                z = z * cr[r, :] - roll8(z, True) * s1r[r, :] - roll8(z, False) * s2r[r, :]
                dl[1, w, lanes] = z.astype(BF)
                dl[2, w, lanes] = dv_s[r, :].astype(BF)

    for c in range(3):
        db[c : c + 1, :] = jnp.sum(dl[c].astype(F32), axis=0, keepdims=True)
    if not back:
        return

    @pl.loop(1, S)
    def _(j):
        r = pl.ds(pl.multiple_of(j * N, 128), N)
        w = pl.ds(pl.multiple_of((j - 1) * N, 128), N)
        y = dnn(ctx[r, :], wo[...])
        d = dnt(dl[0, r, :], wq[...]) + dnt(dl[1, r, :], wk[...]) + dnt(dl[2, r, :], wv[...])

        @pl.when(g == 0)
        def _():
            yacc[w, :] = y
            dacc[w, :] = d

        @pl.when(g > 0)
        def _():
            yacc[w, :] += y
            dacc[w, :] += d

    @pl.when(g == last)
    def _():
        ln[...] = jnp.zeros_like(ln)

        def store(j, of, away):
            x, yo, go = of(xs), away(ys), away(gs)

            @pl.loop(0, N // 128)
            def _(i):
                r = tile(i, 128)
                w = pl.ds(pl.multiple_of((j - 1) * N + i * 128, 128), 128)
                xh, _ = normed(x[r, :])
                d = dacc[w, :]
                y = yacc[w, :]
                gg = d * gb[0:1, :]
                if adding:
                    y = y + yo[r, :].astype(F32)
                    gg = gg + go[r, :].astype(F32)
                yo[r, :] = y.astype(BF)
                go[r, :] = gg.astype(BF)
                ln[0:1, :] += jnp.sum(d * xh, axis=0, keepdims=True)
                ln[1:2, :] += jnp.sum(d, axis=0, keepdims=True)

        every_slot(store, 1)


def attn_group(S, PD, CL, me, xs, dys, yps, g2s, wqkv, bqkv, wo, gb, tabs, back):
    N, D = xs[0].shape
    CW = wo.shape[0]
    T = N * S
    HG = 4 if CW % 256 == 0 else 2
    QB = 256
    W = HG * HD
    G = CW // W
    full = lambda s: pl.BlockSpec(s, lambda g, m: (0,) * len(s), pipeline_mode=pl.Buffered(1))
    keep = lambda s: pl.BlockSpec(s, lambda g, m: (0,) * len(s))
    tok, tok_out, per, far = full((N, D)), keep((N, D)), S, S - 1
    adding = int(T * D <= 1536 * 1024)
    others = (yps, g2s)
    if not adding:
        yps, g2s = [], []
    if not back:
        yps, g2s, far = [], [], 0
    out_tok = SD((N, D), BF)
    part = pl.BlockSpec((N // G, D), lambda g, m: (g, 0))
    if S > 2:
        xs, dys, yps, g2s = [[jnp.stack(v, axis=0)] if v else v for v in (xs, dys, yps, g2s)]
        tok, tok_out, per, far = full((S, N, D)), keep((S - 1, N, D)), 1, back
        out_tok = SD((S - 1, N, D), BF)
        part = pl.BlockSpec((S - 1, N // G, D), lambda g, m: (0, g, 0))
    wspec = lambda c: pl.BlockSpec((D, W), lambda g, m: (0, c * G + g))
    bspec = lambda c: pl.BlockSpec((1, W), lambda g, m: (0, c * G + g))
    outs = pl.pallas_call(
        functools.partial(attn_kernel, S, PD, CL, QB, HG, adding, back),
        grid_spec=pltpu.PrefetchScalarGridSpec(
            num_scalar_prefetch=1,
            grid=(G,),
            in_specs=[tok] * (2 * per)
            + [part] * (2 * adding * far)
            + [wspec(0), wspec(1), wspec(2), bspec(0), bspec(1), bspec(2)]
            + [pl.BlockSpec((W, D), lambda g, m: (g, 0)), full((2, D))]
            + [full((T, 128))] * 3,
            out_specs=[tok_out] * (2 * far)
            + [
                pl.BlockSpec((3, T, W), lambda g, m: (0, 0, g)),
                pl.BlockSpec((T, W), lambda g, m: (0, g)),
                keep((T, D)),
            ]
            + [keep((2, D))] * back
            + [pl.BlockSpec((3, W), lambda g, m: (0, g))],
            scratch_shapes=[pltpu.VMEM((T - N, D), F32)] * (2 * back)
            + [pltpu.VMEM((T, W), BF)] * 4
            + [pltpu.VMEM((128, T), BF)] * 2
            + [pltpu.VMEM((T, 128), F32)] * 2,
        ),
        out_shape=[out_tok] * (2 * far)
        + [SD((3, T, CW), BF), SD((T, CW), BF), SD((T, D), BF)] + [SD((2, D), F32)] * back + [SD((3, CW), F32)],
        compiler_params=pltpu.CompilerParams(vmem_limit_bytes=62 * MIB),
        cost_estimate=SMALL,
    )(me, *xs, *dys, *yps, *g2s, wqkv, wqkv, wqkv, bqkv, bqkv, bqkv, wo, gb, *tabs)
    if not back:
        dl, ctx, h1, db = outs
        return [], [], [dl, ctx, h1, 0.0, db]
    ys, gs = outs[:far], outs[far : 2 * far]
    if S > 2:
        ys, gs = [[v[0][j] for j in range(S - 1)] for v in (ys, gs)]
    if not adding:
        ys, gs = [[a + b for a, b in zip(p, q)] for p, q in zip((ys, gs), others)]
    return ys, gs, outs[2 * far :]


def tn_kernel(n, wide, *refs):
    a = refs[:n]
    b = refs[n : 2 * n]
    o = refs[2 * n]
    if wide == 0:
        o[...] = sum(dtn(x[...], y[...]) for x, y in zip(a, b)).astype(BF)
    else:
        w = b[0].shape[2]
        for c in range(wide):
            o[:, c * w : (c + 1) * w] = sum(dtn(x[...], y[c]) for x, y in zip(a, b)).astype(BF)


def tn_sum(a, b, block):
    n = len(a)
    rows, da = a[0].shape
    block = min(block, da)
    wide = b[0].shape[0] if b[0].ndim == 3 else 0
    db = b[0].shape[-1] * max(wide, 1)
    keep = lambda s: pl.BlockSpec(s, lambda i: (0,) * len(s), pipeline_mode=pl.Buffered(1))
    return pl.pallas_call(
        functools.partial(tn_kernel, n, wide),
        grid=(da // block,),
        in_specs=[pl.BlockSpec((rows, block), lambda i: (0, i))] * n + [keep(b[0].shape)] * n,
        out_specs=pl.BlockSpec((block, db), lambda i: (i, 0)),
        out_shape=SD((da, db), BF),
        compiler_params=pltpu.CompilerParams(vmem_limit_bytes=60 * MIB),
        cost_estimate=SMALL,
    )(*a, *b)


def joined(refs):
    return jnp.concatenate([r[...] for r in refs], axis=0)


def down_kernel(n, more, *refs):
    o = refs[-1]
    t = dtn(joined(refs[:n]), joined(refs[n : 2 * n])).reshape(o.shape)
    o[...] = (t + refs[2 * n][...].astype(F32) if more else t).astype(BF)


def up_kernel(n, more, *refs):
    o = refs[-1]
    c, rows, w = o.shape
    t = dtn(joined(refs[:n]), joined(refs[n : 2 * n]))
    k = t.shape[1] // w
    for i in range(k):
        r = slice(i * (rows // k), (i + 1) * (rows // k))
        p = t[:, i * w : (i + 1) * w].reshape(c, rows // k, w)
        o[:, r, :] = (p + refs[2 * n][:, r, :].astype(F32) if more else p).astype(BF)


def mlp_grads(S, R, acts, dys, hs, dpres, g=None):
    n = len(acts)
    rows, FL = acts[0].shape
    D = dys[0].shape[1]
    DR = D // S
    blk = 256
    rd = FL // R
    ru = DR // R
    k = FL // D
    per = rd + S * ru * k
    keep = lambda s: pl.BlockSpec(s, lambda i: (0,) * len(s), pipeline_mode=pl.Buffered(1))
    steps = DR // blk
    more = g is not None
    hbm = pl.BlockSpec(memory_space=pl.ANY)

    def call(kernel, a, b, spec, g):
        width = b[0].shape[1]
        prior = [] if g is None else [g]
        return pl.pallas_call(
            functools.partial(kernel, n, more),
            grid=(a[0].shape[1] // blk,),
            in_specs=[pl.BlockSpec((rows, blk), lambda i: (0, i))] * n
            + [keep((rows, width))] * n
            + ([spec if more else hbm] if prior else []),
            out_specs=spec,
            out_shape=SD((R, per, D), BF),
            input_output_aliases={2 * n: 0} if prior else {},
            compiler_params=pltpu.CompilerParams(vmem_limit_bytes=60 * MIB),
            cost_estimate=SMALL,
        )(*a, *b, *prior)

    g = call(down_kernel, acts, dys, pl.BlockSpec((blk // rd, rd, D), lambda i: (i, 0, 0)), g)
    spec = pl.BlockSpec((blk // ru, ru * k, D), lambda i: (i % steps, rd // (ru * k) + i // steps, 0))
    return call(up_kernel, hs, dpres, spec, g)


def mlp_finish_kernel(S, rd, ru, g, down, up):
    n, per, D = g.shape
    k = (per - rd) // (S * ru)
    for c in range(n):
        down[c * rd : (c + 1) * rd, :] = g[c, :rd, :].astype(F32)
        for t in range(S * k):
            a = rd + t * ru
            up[c * ru : (c + 1) * ru, t * D : (t + 1) * D] = g[c, a : a + ru, :].astype(F32)


def mlp_finish(S, g, FL):
    R, per, D = g.shape
    rd = FL // R
    ru = D // S // R
    n = 4
    return pl.pallas_call(
        functools.partial(mlp_finish_kernel, S, rd, ru),
        grid=(R // n,),
        in_specs=[pl.BlockSpec((n, per, D), lambda c: (c, 0, 0))],
        out_specs=[pl.BlockSpec((n * rd, D), lambda c: (c, 0)), pl.BlockSpec((n * ru, S * FL), lambda c: (c, 0))],
        out_shape=[SD((FL, D), F32), SD((D // S, S * FL), F32)],
        compiler_params=pltpu.CompilerParams(vmem_limit_bytes=40 * MIB),
        cost_estimate=SMALL,
    )(g)


def attn_grads_kernel(n, S, R, q_ref, *refs):
    h = refs[:n]
    dl = refs[n : 2 * n]
    ctx = refs[2 * n : 3 * n]
    dy = refs[3 * n : -2]
    first, second = refs[-2:-1], refs[-1:]
    i = pl.program_id(0)
    q1 = q_ref[0]
    q2 = q_ref[1]
    blk = h[0].shape[1]
    D = dy[0].shape[1]
    DR = D // S
    CW = dl[0].shape[2]
    ru = DR // R
    k = D // CW
    steps = DR // blk
    s = i // steps
    base = (i % steps) * (blk // ru)

    def put(pair, pos, rows, v):
        pair[0][pos, rows, :] = v

    for p in range(3):
        t = dtn(joined(h), jnp.concatenate([y[p] for y in dl], axis=0)).astype(BF)
        for c in range(blk // ru):
            v = t[c * ru : (c + 1) * ru, :]
            if p < 2:
                put(first, (base + c) ^ q1, pl.ds(s * 2 * ru + p * ru, ru), v)
            else:
                put(second, (base + c) ^ q2, pl.ds(k * ru + s * ru, ru), v)
    t = dtn(joined(ctx), joined(dy)).astype(BF)
    m = ctx[0].shape[1] // ru
    for c in range(m):
        for j in range(k):
            put(second, (i * m + c) ^ q2, pl.ds(j * ru, ru), t[c * ru : (c + 1) * ru, j * CW : (j + 1) * CW])


def attn_grads(S, R, q, hs, dls, ctxs, dys):
    n = len(hs)
    T, D = hs[0].shape
    CW = ctxs[0].shape[1]
    DR = D // S
    ru = DR // R
    blk = 256
    G = D // blk
    keep = lambda s: pl.BlockSpec(s, lambda i, q: (0,) * len(s), pipeline_mode=pl.Buffered(1))
    shapes = [(R, S * 2 * ru, CW), (R, (D // CW + S) * ru, CW)]
    return pl.pallas_call(
        functools.partial(attn_grads_kernel, n, S, R),
        grid_spec=pltpu.PrefetchScalarGridSpec(
            num_scalar_prefetch=1,
            grid=(G,),
            in_specs=[pl.BlockSpec((T, blk), lambda i, q: (0, i))] * n
            + [keep((3, T, CW))] * n
            + [pl.BlockSpec((T, CW // G), lambda i, q: (0, i))] * n
            + [keep(dys[0].shape)] * len(dys),
            out_specs=[pl.BlockSpec(s, lambda i, q: (0, 0, 0)) for s in shapes],
        ),
        out_shape=[SD(s, BF) for s in shapes],
        compiler_params=pltpu.CompilerParams(vmem_limit_bytes=60 * MIB),
        cost_estimate=SMALL,
    )(q, *hs, *dls, *ctxs, *dys)


def attn_finish_kernel(S, ru, k, n, half, q_ref, *refs):
    out, qkv = refs[4 * n :]
    CW = refs[0].shape[2]
    D = out.shape[1]
    i = pl.program_id(0)

    def piece(which, c, a):
        low, high = refs[2 * which * n + c], refs[(2 * which + 1) * n + c]
        here = ((i * n + c) ^ q_ref[which]) < half
        rows = pl.ds(a, ru)
        return jnp.where(here, low[0, rows, :].astype(F32), high[0, rows, :].astype(F32))

    for c in range(n):
        r = slice(c * ru, (c + 1) * ru)
        for j in range(k):
            out[r, j * CW : (j + 1) * CW] = piece(1, c, j * ru)
        for t in range(S):
            for p in range(3):
                v = piece(0, c, (t * 2 + p) * ru) if p < 2 else piece(1, c, (k + t) * ru)
                qkv[r, p * D + t * CW : p * D + (t + 1) * CW] = v


def attn_finish(S, q, one, two):
    half, per1, CW = one[0].shape
    per2 = two[0].shape[1]
    R = 2 * half
    D = CW * S
    ru = D // S // R
    n = 4
    place_of = lambda i, q, k, c: (i * n + c) ^ q[k]
    low = lambda per, k, c: pl.BlockSpec((1, per, CW), lambda i, q: (jnp.minimum(place_of(i, q, k, c), half - 1), 0, 0))
    high = lambda per, k, c: pl.BlockSpec((1, per, CW), lambda i, q: (jnp.maximum(place_of(i, q, k, c) - half, 0), 0, 0))
    specs = [f(per, k, c) for k, per in ((0, per1), (1, per2)) for f in (low, high) for c in range(n)]
    return pl.pallas_call(
        functools.partial(attn_finish_kernel, S, ru, S, n, half),
        grid_spec=pltpu.PrefetchScalarGridSpec(
            num_scalar_prefetch=1,
            grid=(R // n,),
            in_specs=specs,
            out_specs=[pl.BlockSpec((n * ru, D), lambda c, q: (c, 0)), pl.BlockSpec((n * ru, 3 * D), lambda c, q: (c, 0))],
        ),
        out_shape=[SD((CW, D), F32), SD((D // S, 3 * D), F32)],
        compiler_params=pltpu.CompilerParams(vmem_limit_bytes=40 * MIB),
        cost_estimate=SMALL,
    )(q, *[a for pair in (one, two) for arr in pair for a in [arr] * n])


def own_kernel(dl, ctx, wqkv, wo, x, yp, g2, gb, y, g, ln, d1):
    N = x.shape[0]
    CW = ctx.shape[1]
    d1[...] = sum(dnt(dl[p], wqkv[:, p * CW : (p + 1) * CW]) for p in range(3))
    y[...] = (yp[...].astype(F32) + dnn(ctx[...], wo[...])).astype(BF)
    ln[...] = jnp.zeros_like(ln)

    @pl.loop(0, N // 128)
    def _(i):
        r = tile(i, 128)
        xh, _ = normed(x[r, :])
        a = d1[r, :]
        g[r, :] = (a * gb[0:1, :] + g2[r, :].astype(F32)).astype(BF)
        ln[0:1, :] += jnp.sum(a * xh, axis=0, keepdims=True)
        ln[1:2, :] += jnp.sum(a, axis=0, keepdims=True)


def own_rows(x, yp, g2, dl, ctx, wqkv, wo, gb):
    N, D = x.shape
    CW = wo.shape[0]
    full = lambda s: pl.BlockSpec(s, lambda f: (0,) * len(s))
    return pl.pallas_call(
        own_kernel,
        grid=(1,),
        in_specs=[full((3, N, CW)), full((N, CW)), full((D, 3 * CW)), full((CW, D))] + [full((N, D))] * 3 + [full((2, D))],
        out_specs=[full((N, D)), full((N, D)), full((2, D))],
        out_shape=[SD((N, D), BF), SD((N, D), BF), SD((2, D), F32)],
        scratch_shapes=[pltpu.VMEM((N, D), F32)],
        compiler_params=pltpu.CompilerParams(vmem_limit_bytes=60 * MIB),
        cost_estimate=SMALL,
    )(dl, ctx, wqkv, wo, x, yp, g2, gb)


def own_both_kernel(act, dpre, wu, wd, dl, ctx, wqkv, wo, x, gb, y, g, ln, yacc, d1, d2):
    f = pl.program_id(0)
    last = pl.num_programs(0) - 1
    N = x.shape[0]
    CW = ctx.shape[1]

    @pl.when(f == 0)
    def _():
        yacc[...] = dnn(ctx[...], wo[...])
        d1[...] = sum(dnt(dl[p], wqkv[:, p * CW : (p + 1) * CW]) for p in range(3))
        d2[...] = jnp.zeros_like(d2)

    yacc[...] += dnn(act[...], wd[...])
    d2[...] += dnt(dpre[...], wu[...])

    @pl.when(f == last)
    def _():
        ln[...] = jnp.zeros_like(ln)

        @pl.loop(0, N // 128)
        def _(i):
            r = tile(i, 128)
            xh, _ = normed(x[r, :])
            a = d1[r, :]
            b = d2[r, :]
            y[r, :] = yacc[r, :].astype(BF)
            g[r, :] = (a * gb[0:1, :] + b * gb[2:3, :]).astype(BF)
            ln[0:1, :] += jnp.sum(a * xh, axis=0, keepdims=True)
            ln[1:2, :] += jnp.sum(a, axis=0, keepdims=True)
            ln[2:3, :] += jnp.sum(b * xh, axis=0, keepdims=True)
            ln[3:4, :] += jnp.sum(b, axis=0, keepdims=True)


def own_both_rows(j, x, act, dpre, wu, wd, dl, ctx, wqkv, wo, gb):
    N, D = x.shape
    FL = wu.shape[1]
    CW = wo.shape[0]
    fb = min(512, FL)
    full = lambda s: pl.BlockSpec(s, lambda f: (0,) * len(s), pipeline_mode=pl.Buffered(1))
    keep = lambda s: pl.BlockSpec(s, lambda f: (0,) * len(s))
    rows = pl.BlockSpec((N, fb), lambda f: (0, f))
    return pl.pallas_call(
        own_both_kernel,
        grid=(FL // fb,),
        in_specs=[rows, rows, pl.BlockSpec((D, fb), lambda f: (0, f)), pl.BlockSpec((fb, D), lambda f: (f, 0))]
        + [
            pl.BlockSpec((3, N, CW), lambda f: (0, j, 0), pipeline_mode=pl.Buffered(1)),
            pl.BlockSpec((N, CW), lambda f: (j, 0), pipeline_mode=pl.Buffered(1)),
        ]
        + [full((D, 3 * CW)), full((CW, D)), full((N, D)), full((4, D))],
        out_specs=[keep((N, D)), keep((N, D)), keep((4, D))],
        out_shape=[SD((N, D), BF), SD((N, D), BF), SD((4, D), F32)],
        scratch_shapes=[pltpu.VMEM((N, D), F32)] * 3,
        compiler_params=pltpu.CompilerParams(vmem_limit_bytes=60 * MIB),
        cost_estimate=SMALL,
    )(act, dpre, wu, wd, dl, ctx, wqkv, wo, x, gb)


def final_kernel(S, first, PT, *refs):
    it = iter(refs)
    take = lambda n: [next(it) for _ in range(n)]
    x, dy = take(2)
    ys = take(S)
    gs = take(S)
    (vb,) = take(1)
    if not first:
        take(4)
    po, co, pg, cg = take(4)
    i = pl.program_id(0)
    xv = x[...].astype(F32)
    xh, inv = normed(xv)
    y = xv + vb[0:1, :] + sum(r[...].astype(F32) for r in ys) + vb[1:2, :]
    gsum = sum(r[...].astype(F32) for r in gs)
    dx = (gsum - jnp.mean(gsum, axis=-1, keepdims=True) - xh * jnp.mean(gsum * xh, axis=-1, keepdims=True)) * inv
    out = y.astype(BF)
    grad = dy[...].astype(F32) + dx

    @pl.when(i < PT)
    def _():
        po[0] = out
        pg[0] = grad

    @pl.when(i >= PT)
    def _():
        co[0] = out
        cg[0] = grad


def final_rows(m, MB, PD, x, dy, ys, gs, vb, prior):
    S = len(ys)
    N, D = x.shape
    CR = N - PD
    RT = 128
    PT = PD // RT
    first = prior is None
    row = pl.BlockSpec((RT, D), lambda i: (i, 0))
    pspec = pl.BlockSpec((1, RT, D), lambda i: (m, jnp.minimum(i, PT - 1), 0))
    cspec = pl.BlockSpec((1, RT, D), lambda i: (m, jnp.maximum(i - PT, 0), 0))
    hbm = pl.BlockSpec(memory_space=pl.ANY)
    n_in = 2 * S + 3
    return pl.pallas_call(
        functools.partial(final_kernel, S, first, PT),
        grid=(N // RT,),
        in_specs=[row] * (2 * S + 2) + [pl.BlockSpec((2, D), lambda i: (0, 0))] + ([] if first else [hbm] * 4),
        out_specs=[pspec, cspec, pspec, cspec],
        out_shape=[SD((MB, PD, D), BF), SD((MB, CR, D), BF), SD((MB, PD, D), F32), SD((MB, CR, D), F32)],
        input_output_aliases={} if first else {n_in + k: k for k in range(4)},
        compiler_params=pltpu.CompilerParams(vmem_limit_bytes=32 * MIB),
        cost_estimate=SMALL,
    )(x, dy, *ys, *gs, vb, *(() if first else prior))


def shifted(value, S, j):
    return lax.ppermute(value, "shard", [(i, (i + j) % S) for i in range(S)])


def canonical(slots, me, S, back):
    if S == 1:
        return slots
    if S == 2:
        a, b = slots
        return [jnp.where(me == 0, a, b), jnp.where(me == 0, b, a)]
    stacked = jnp.stack(slots, axis=0)
    return [
        lax.dynamic_index_in_dim(stacked, lax.rem((me - s if back else s - me) + S, S), 0, keepdims=False) for s in range(S)
    ]


def exchanged(value, R, bit):
    return lax.ppermute(value, "rep", [(i, i ^ bit) for i in range(R)])


def columns_for(weight, me, S, j, parts, row=0, rows=None):
    cols = weight.shape[1] // parts
    rows = weight.shape[0] if rows is None else rows
    w = cols // S
    at = lax.rem(me + j, S) * w
    got = [lax.dynamic_slice(weight, (row, p * cols + at), (rows, w)) for p in range(parts)]
    return got[0] if parts == 1 else jnp.concatenate(got, axis=1)


def quarter_pieces(weight, me, S):
    n = weight.shape[0] // 4
    rep = lax.axis_index("rep")
    at = (2 * (rep % 2) + (rep // 2) % 2) * n
    return [columns_for(weight, me, S, j, 1, at, n) for j in range(1, S)]


def from_quarters(weight, pieces, me, S, R):
    rep = lax.axis_index("rep")

    def both(piece, other, first):
        return jnp.concatenate([jnp.where(first, piece, other), jnp.where(first, other, piece)], axis=0)

    slots = [columns_for(weight, me, S, 0, 1)]
    for piece in pieces:
        pair = both(piece, exchanged(piece, R, 2), (rep // 2) % 2 == 0)
        slots.append(both(pair, exchanged(pair, R, 1), rep % 2 == 0))
    return jnp.concatenate(canonical(slots, me, S, True), axis=0)


def from_rep(weight, pieces, me, S, parts):
    others = lax.all_gather(jnp.stack(pieces, axis=0), "rep", axis=1, tiled=True)
    slots = [columns_for(weight, me, S, 0, parts)] + [others[j] for j in range(S - 1)]
    return jnp.concatenate(canonical(slots, me, S, True), axis=0)


def add_low(a, b):
    return (a.astype(F32) + b.astype(F32)).astype(BF)


def orders(R):
    bits = [1 << i for i in range(R.bit_length() - 1)]
    return bits, bits[:1] + bits[2:] + bits[1:2]


def place(rep, order):
    q = jnp.zeros((), jnp.int32)
    for bit in order:
        q = 2 * q + (rep & bit) // bit
    return q


def beside_it(got, key, beside):
    if key in beside:
        got, beside[key] = lax.optimization_barrier((got, beside[key]))
    return got


def halving(pairs, R, beside):
    for i, bits in enumerate(zip(*orders(R))):
        got = beside_it([exchanged(p[1], R, bit) for p, bit in zip(pairs, bits)], i, beside)
        h = got[0].shape[0] // 2
        if h:
            pairs = [(add_low(p[0][:h], t[:h]), add_low(p[0][h:], t[h:])) for p, t in zip(pairs, got)]
        else:
            pairs = [add_low(p[0], t) for p, t in zip(pairs, got)]
    return [p[0] for p in pairs]


def doubling(parts, R, beside):
    pair = [p[None] for p in parts]
    for i, bits in reversed(list(enumerate(zip(*orders(R))))):
        got = beside_it([exchanged(g, R, bit) for g, bit in zip(pair, bits)], i, beside)
        if i:
            pair = [jnp.concatenate([g, t], axis=0) for g, t in zip(pair, got)]
    return list(zip(pair, got))


def hops(v, R):
    out = []
    for b in range(R.bit_length() - 1):
        v = v + exchanged(v, R, 1 << b)
        out.append(v)
    return out


def sum_all(v, S, R):
    bit = 1
    while bit < R:
        v = v + exchanged(v, R, bit)
        bit *= 2
    return v


def swap_shards(part, me, S, head):
    n = (part.shape[0] - head) // S
    slots = []
    for j in range(S):
        b = lax.dynamic_slice_in_dim(part, head + lax.rem(me + j, S) * n, n, 0)
        slots.append(shifted(b, S, j) if j else b)
    return jnp.concatenate(([part[:head]] if head else []) + canonical(slots, me, S, True), axis=0)


def reduce_rows(grad):
    part = lax.psum_scatter(grad, "rep", scatter_dimension=0, tiled=True)
    return lax.all_gather(part, "rep", axis=0, tiled=True).astype(F32)


def reduce_columns(grad, me, S, parts):
    rows, cols = grad.shape
    part = lax.psum_scatter(grad.reshape(S, rows // S, cols), "rep", scatter_dimension=1, tiled=True)
    slots = [lax.dynamic_index_in_dim(part, me, 0, keepdims=False)]
    for j in range(1, S):
        slots.append(shifted(lax.dynamic_index_in_dim(part, lax.rem(me + j, S), 0, keepdims=False), S, j))
    slots = [s.reshape(s.shape[0], parts, cols // parts) for s in slots]
    whole = jnp.stack(canonical(slots, me, S, True), axis=2).reshape(-1, S * cols)
    return lax.all_gather(whole, "rep", axis=0, tiled=True).astype(F32)


def rotary_tables(PR, CR, CL):
    pos = np.concatenate([np.arange(PR), PR + np.arange(CR) % CL]).astype(np.float32)
    half = ROT // 2
    freq = np.exp(np.arange(half, dtype=np.float32) * np.float32(-2.0 * math.log(10000.0) / ROT)).astype(np.float32)
    ang = (pos[:, None] * freq[None, :]).astype(np.float32)
    c = np.cos(ang)
    s = np.sin(ang)
    n = pos.shape[0]
    one = np.ones((n, HD - ROT), np.float32)
    zero = np.zeros((n, HD - ROT), np.float32)
    z8 = np.zeros((n, half), np.float32)
    tabs = ([c, c, one], [-s, z8, zero], [z8, s, zero])
    return [jnp.asarray(np.tile(np.concatenate(t, axis=1), (1, 128 // HD)), F32) for t in tabs]


def per_device(
    prompt_in,
    cont_in,
    prompt_cot,
    cont_cot,
    ln1_gain,
    ln1_bias,
    ln2_gain,
    ln2_bias,
    qkv_weight,
    qkv_bias,
    out_weight,
    out_bias,
    up_weight,
    up_bias,
    down_weight,
    down_bias,
):
    S = lax.axis_size("shard")
    R = lax.axis_size("rep")
    me = lax.axis_index("shard")
    MB, _, PD, D = prompt_in.shape
    CD, CL = cont_in.shape[2:4]
    CR = CD * CL
    N = PD + CR
    CW = D // S
    FL = up_weight.shape[1] // S
    me_arr = jnp.reshape(me, (1,)).astype(jnp.int32)

    X = [[jnp.concatenate([prompt_in[m, 0], cont_in[m, 0].reshape(CR, D)], axis=0)] for m in range(MB)]
    DY = [[jnp.concatenate([prompt_cot[m, 0], cont_cot[m, 0].reshape(CR, D)], axis=0)] for m in range(MB)]
    away = lambda values: [shifted(v, S, j + 1) for j, v in enumerate(values)]
    cut = quarter_pieces(up_weight, me, S)
    vectors_in = (ln1_gain, ln1_bias, ln2_gain, ln2_bias, out_bias, down_bias, qkv_bias)
    (vectors_in, qkv_weight), _ = lax.optimization_barrier(((vectors_in, qkv_weight), (cut, X[0], DY[0])))
    small = jnp.concatenate([v.reshape(-1, CW) for v in vectors_in], axis=0)
    n = D // S // R
    rep = lax.axis_index("rep")
    at = lambda j, p: (rep * n, p * D + lax.rem(me + j, S) * CW)
    pack = lambda j: jnp.concatenate([lax.dynamic_slice(qkv_weight, at(j, p), (n, CW)) for p in range(3)] + [small], axis=0)
    packs = away([pack(j) for j in range(1, S)])
    slots = [small.astype(F32)] + [g[3 * n :].astype(F32) for g in packs]
    pieces_qkv = [jnp.concatenate([g[p * n : (p + 1) * n] for p in range(3)], axis=1) for g in packs]
    pieces_up = away(cut)
    src = [(X[m][0], DY[m][0]) for m in range(MB)]
    src[1:], _ = lax.optimization_barrier((src[1:], pieces_up))
    pieces_up, _ = lax.optimization_barrier((pieces_up, (packs, X[0], DY[0])))
    w_up = from_quarters(up_weight, pieces_up, me, S, R)
    w_qkv = from_rep(qkv_weight, pieces_qkv, me, S, 3)

    whole = jnp.stack(canonical(slots, me, S, True), axis=0)
    vec = whole[:, :6].transpose(1, 0, 2).reshape(6, D)
    gb = vec[0:4]
    gb1 = vec[0:2]
    gb2 = vec[2:4]
    vb = vec[4:6]
    bqkv = whole[:, 6:].reshape(3, S, CW)
    bqkv = lax.dynamic_index_in_dim(bqkv, me, 1, keepdims=False).reshape(1, 3 * CW)
    bup = up_bias.astype(F32).reshape(1, FL)

    tabs = rotary_tables(PD * S, CR * S, CL)
    for m in range(MB):
        for j in range(1, S):
            X[m].append(shifted(src[m][0], S, S - j))
            DY[m].append(shifted(src[m][1], S, S - j))

    chunked = (D // S // R) % 16 == 0 and R & (R - 1) == 0
    ff = [[None] * S for _ in range(MB)]

    def mlp(m, j):
        ff[m][j] = mlp_rows(X[m][j], DY[m][j], w_up, bup, down_weight, gb2, int((m, j) != (MB - 1, 0) and not (chunked and m == MB - 1)))

    for m in range(MB):
        mlp(m, 0)
    rest = []
    y_got, g_got = [], []

    def attend(m):
        ys, gs, more = attn_group(
            S, PD, CL, me_arr, X[m], DY[m], [f[4] for f in ff[m][1:] if len(f) > 4], [f[5] for f in ff[m][1:] if len(f) > 4], w_qkv, bqkv, out_weight, gb1, tabs, int(m < MB - 1 or not chunked)
        )
        rest.append(list(more))
        y_got.append([shifted(v, S, j + 1) for j, v in enumerate(ys)])
        g_got.append([shifted(v, S, j + 1) for j, v in enumerate(gs)])

    def both_rows(m, j):
        f = ff[m][j]
        return own_both_rows(j, X[m][j], f[0], f[1], w_up, down_weight, rest[m][0], rest[m][1], w_qkv, out_weight, gb)

    def own(m):
        f = ff[m][0]
        if len(f) == 4:
            return both_rows(m, 0)
        return own_rows(X[m][0], f[4], f[5], rest[m][0], rest[m][1], w_qkv, out_weight, gb1)

    rep = lax.axis_index("rep")
    late = [(MB - 1, j) for j in range(1, S)]
    early = [(m, j) for m in range(MB) for j in range(S) if (m, j) not in late]
    of = lambda set_, k: [ff[m][j][k] for m, j in set_]
    for m, j in early:
        if j:
            mlp(m, j)
    if chunked:
        gmlp = mlp_grads(S, R, of(early, 0), [DY[m][j] for m, j in early], of(early, 2), of(early, 1))
        w_up, gmlp, w_qkv = lax.optimization_barrier((w_up, gmlp, w_qkv))
    for m, j in late:
        mlp(m, j)
    if chunked:
        if late:
            gmlp = mlp_grads(S, R, of(late, 0), [DY[m][j] for m, j in late], of(late, 2), of(late, 1), gmlp)
        part = lax.psum_scatter(gmlp, "rep", scatter_dimension=0, tiled=True)[0]
        w_qkv, gmlp = lax.optimization_barrier((w_qkv, gmlp))
    for m in range(MB):
        attend(m)
        if m + 1 < MB:
            w_qkv, rest[m][3] = lax.optimization_barrier((w_qkv, rest[m][3]))
    every = early + late
    def vectors(mine_):
        ln1 = sum(r[3] for r in rest) + sum(o[2][0:2] for o in mine_)
        ln2 = sum(f[6] for f in (ff[m][j] for m, j in every) if len(f) > 4) + sum(o[2][2:4] for o in mine_ if o[2].shape[0] > 2)
        db_out = sum(jnp.sum(DY[m][0].astype(F32), axis=0) for m in range(MB)).reshape(-1, CW)
        mine = (jnp.arange(S) == me).astype(F32)
        db_qkv = (sum(r[4] for r in rest)[:, None, :] * mine[None, :, None]).reshape(-1, CW)
        db_up = (sum(of(every, 3)) * mine[:, None]).reshape(-1, CW)
        return jnp.concatenate([ln1.reshape(-1, CW), ln2.reshape(-1, CW), db_out, db_qkv, db_up], axis=0)

    finals = lambda m, o, prior: final_rows(m, MB, PD, X[m][0], DY[m][0], [o[0]] + y_got[m], [o[1]] + g_got[m], vb, prior)
    hs, dls, ctxs = [[r[k] for r in rest] for k in (2, 0, 1)]
    if chunked:
        q = jnp.stack([place(rep, order) for order in orders(R)]).astype(jnp.int32)
        part = swap_shards(part, me, S, FL // R)
        hs, y_got[:-1], g_got[:-1], part = lax.optimization_barrier((hs, y_got[:-1], g_got[:-1], part))
        gmlp_all = lax.all_gather(part, "rep", axis=0, tiled=False)
        gatt = attn_grads(S, R, q, hs, dls, ctxs, [DY[m][j] for m in range(MB) for j in range(S)])
        dls_own, _ = lax.optimization_barrier(([r[0] for r in rest], gatt))
        for m in range(MB):
            rest[m][0] = dls_own[m]
        far = [both_rows(MB - 1, j) for j in range(1, S)]
        y_got[-1], g_got[-1] = [[shifted(r[i], S, j + 1) for j, r in enumerate(far)] for i in range(2)]
        dls_own, far_sums = lax.optimization_barrier(([r[0] for r in rest], [r[2] for r in far]))
        for m in range(MB):
            rest[m][0] = dls_own[m]
        mine = [own(m) for m in range(MB)]
        beside = {1: [far_sums] + mine[:-1]}
        beside[2] = mine[-1:]
        levels = R.bit_length() - 1
        beside[levels - 1] = beside.get(levels - 1, []) + [y_got[-1], g_got[-1]]
        path = hops(vectors(mine + far), R)
        late_hops = {}
        for n, v in enumerate(path):
            at = 3 + n
            (beside if at < levels else late_hops).setdefault(at if at < levels else max(2 * levels - 1 - at, 0), []).append(v)
        outs = None
        for m in range(MB - 1):
            outs = finals(m, mine[m], outs)
        whole_outs = finals(MB - 1, mine[-1], outs)
        half = halving([(g[: R // 2], g[R // 2 :]) for g in gatt], R, beside)
        k = D // CW * (D // S // R)
        finished = mlp_finish(S, gmlp_all, FL)
        after = {3: (outs, late_hops.get(3, [])), 2: (finished, late_hops.get(2, [])), 1: (whole_outs, late_hops.get(1, []))}
        g1, g2 = doubling([swap_shards(half[0], me, S, 0), swap_shards(half[1], me, S, k)], R, after)
        outs = after[1][0]
        g_down, g_up = after[2][0]
        vecs = path[-1]
        g_out, g_qkv = attn_finish(S, q, g1, g2)
    else:
        dls, ctxs, hs = [[r[k] for r in rest] for k in (0, 1, 2)]
        mine = [own(m) for m in range(MB)]
        g_down = reduce_rows(tn_sum(of(every, 0), [DY[m][j] for m, j in every], 256))
        g_up = reduce_columns(tn_sum(of(every, 2), of(every, 1), 256), me, S, 1)
        dycs = [jnp.concatenate(DY[m], axis=0) for m in range(MB)]
        g_out = reduce_rows(tn_sum(ctxs, dycs, 256))
        g_qkv = reduce_columns(tn_sum(hs, dls, 256), me, S, 3)
        vecs = sum_all(vectors(mine), S, R)
        outs = None
        for m in range(MB):
            outs = finals(m, mine[m], outs)
    tot = vecs + sum(shifted(vecs, S, j) for j in range(1, S))
    held = lambda a, n: lax.dynamic_slice_in_dim(tot, a + me * n, n, 0).reshape(-1)
    v_ln1g, v_ln1b, v_ln2g, v_ln2b, v_out = [held(k * S, 1) for k in range(5)]
    v_qkv = held(5 * S, 3)
    v_up = held(8 * S, FL // CW)

    po, co, pg, cg = outs
    return (
        po.reshape(MB, 1, PD, D),
        co.reshape(MB, 1, CD, CL, D),
        pg.reshape(MB, 1, PD, D),
        cg.reshape(MB, 1, CD, CL, D),
        v_ln1g,
        v_ln1b,
        v_ln2g,
        v_ln2b,
        g_qkv,
        v_qkv,
        g_out,
        v_out,
        g_up,
        v_up,
        g_down,
        v_out,
    )


def solution(mesh):
    tokens = (
        P(None, "rep", "shard", None),
        P(None, "rep", "shard", None, None),
        P(None, "rep", "shard", None),
        P(None, "rep", "shard", None, None),
    )
    vec = P("shard")
    mat = P("shard", None)
    params = (vec, vec, vec, vec, mat, vec, mat, vec, mat, vec, mat, vec)
    return jax.shard_map(
        per_device, mesh=mesh, in_specs=tokens + params, out_specs=tokens + params, check_vma=False
    )
```
